32 devices in a mesh: seq: 16 (over z, y, x), fsdp: 2 (over core).
Axes of the slice: x: 2, y: 2, z: 4, core: 2. Of those that a mesh axis runs over, the one named last changes fastest.
Arguments:
- tokens: bfloat16 [4096, 2048], P(('seq', 'fsdp')), may hold values from -6 to 6
- w_mixer: bfloat16 [2048, 8192], P(('seq', 'fsdp')), may hold values from -0.125 to 0.125
- w_rates: bfloat16 [2048, 32], P(('seq', 'fsdp')), may hold values from -0.125 to 0.125
- w_project: bfloat16 [2048, 2048], P(('seq', 'fsdp')), may hold values from -0.125 to 0.125
- w_gate_up: bfloat16 [2048, 11264], P(('seq', 'fsdp')), may hold values from -0.125 to 0.125
- w_down: bfloat16 [2048, 5632], P(('seq', 'fsdp')), may hold values from -0.078125 to 0.078125
- conv_kernel: float32 [4, 6144], replicated, may hold values from -3 to 3
- decay_log: float32 [16], replicated, may hold values from -8 to 0
- decay_bias: float32 [16], replicated, may hold values from -4 to -2
- head_gain: float32 [128], replicated, may hold values from 0.5 to 1.5
- gain_mixer: float32 [2048], replicated, may hold values from 0.5 to 1.5
- gain_mlp: float32 [2048], replicated, may hold values from 0.5 to 1.5
- cotangent: bfloat16 [4096, 2048], P(('seq', 'fsdp')), may hold values from -6 to 6
Outputs:
- output: bfloat16 [4096, 2048], P(('seq', 'fsdp'))
- grad_tokens: bfloat16 [4096, 2048], P(('seq', 'fsdp'))
- grad_mixer: float32 [2048, 8192], P(('seq', 'fsdp'))
- grad_rates: float32 [2048, 32], P(('seq', 'fsdp'))
- grad_project: float32 [2048, 2048], P(('seq', 'fsdp'))
- grad_gate_up: float32 [2048, 11264], P(('seq', 'fsdp'))
- grad_down: float32 [2048, 5632], P(('seq', 'fsdp'))
- grad_kernel: float32 [4, 6144], replicated
- grad_decay_log: float32 [16], replicated
- grad_decay_bias: float32 [16], replicated
- grad_head_gain: float32 [128], replicated
- grad_gain_mixer: float32 [2048], replicated
- grad_gain_mlp: float32 [2048], replicated
The draws below stay inside these ranges and needn't reach their ends.
All inputs are finite; a program needn't handle non-finite values.
Results may differ from the reference program's by a relative error of at most 0.015.
Values may be sent and summed in bfloat16 or wider, within the bound.
A program may use at most 832 MiB of HBM per device.

```python
import jax
import jax.numpy as jnp
from jax import lax

D = 2048
H = 16
DK = 128
FF = 5632
BLOCK = 64
TOKENS = 4096


def block_scale(key, shape, shards, least, top_value):
    def one(axis_at, shards_of):
        steps = jax.random.uniform(jax.random.fold_in(jax.random.fold_in(key, 6), axis_at), (shards_of,), jnp.float32, least / len(shards), top_value / len(shards))
        return jnp.repeat(jnp.exp(steps), shape[axis_at] // shards_of).reshape((-1,) + (1,) * (len(shape) - axis_at - 1))

    factor_of = one(*shards[0])
    for cut in shards[1:]:
        factor_of = factor_of * one(*cut)
    return factor_of


def gaussian(key, dims, deviation, most, pieces=(), dtype=jnp.bfloat16):
    loudness = block_scale(key, dims, pieces, -0.22, 0.18) if pieces else 1.0
    drawn = jax.random.normal(key, dims, jnp.float32) * deviation * loudness
    return jnp.minimum(jnp.maximum(drawn, -most), most).astype(dtype)


def setup_inputs(seed: int = 0) -> dict:
    arg_keys = jax.random.split(jax.random.key(seed), 14)
    return {
        "tokens": gaussian(arg_keys[0], (TOKENS, D), 1.0, 6.0, ((0, 32),)),
        "w_mixer": gaussian(arg_keys[1], (D, 4 * D), D ** -0.5, 0.125, ((0, 32),)),
        "w_rates": gaussian(arg_keys[2], (D, 2 * H), D ** -0.5, 0.125, ((0, 32),)),
        "w_project": gaussian(arg_keys[3], (D, D), D ** -0.5, 0.125, ((0, 32),)),
        "w_gate_up": gaussian(arg_keys[4], (D, 2 * FF), D ** -0.5, 0.125, ((0, 32),)),
        "w_down": gaussian(arg_keys[5], (D, FF), FF ** -0.5, 0.078125, ((0, 32),)),
        "conv_kernel": gaussian(arg_keys[6], (4, 3 * D), 0.5, 3.0, (), jnp.float32),
        "decay_log": jnp.clip(jax.random.uniform(arg_keys[7], (H,), jnp.float32, -8.0, 0.0), -8.0, 0.0),
        "decay_bias": jnp.clip(jax.random.uniform(arg_keys[8], (H,), jnp.float32, -4.0, -2.0), -4.0, -2.0),
        "head_gain": jnp.clip(1.0 + 0.1 * jax.random.normal(arg_keys[9], (DK,), jnp.float32), 0.5, 1.5),
        "gain_mixer": jnp.clip(1.0 + 0.1 * jax.random.normal(arg_keys[10], (D,), jnp.float32), 0.5, 1.5),
        "gain_mlp": jnp.clip(1.0 + 0.1 * jax.random.normal(arg_keys[11], (D,), jnp.float32), 0.5, 1.5),
        "cotangent": gaussian(arg_keys[12], (TOKENS, D), 1.0, 6.0, ((0, 32),)),
    }


highest = lax.Precision.HIGHEST

@jax.custom_vjp
def low(v):
    return lax.optimization_barrier(v.astype(jnp.bfloat16)).astype(jnp.float32)

@jax.custom_vjp
def low_back(v):
    return v

def low_keep(v):
    return (low(v), None)

def low_pass(kept, grad):
    return (grad,)

def back_keep(v):
    return (v, None)

def back_low(kept, grad):
    return (low(grad),)
low.defvjp(low_keep, low_pass)
low_back.defvjp(back_keep, back_low)

def hdot(left, right):
    return jnp.dot(left, right, precision=highest)

def norm_scale(values_in, scales):
    return values_in * lax.rsqrt(lax.optimization_barrier(jnp.mean(values_in * values_in, axis=-1, keepdims=True)) + 1e-06) * scales

def features(extended, kernel, head_count):
    length = extended.shape[0] - 3
    summed = kernel[0] * extended[0:length]
    for offset in range(1, 4):
        summed = summed + kernel[offset] * extended[offset:offset + length]
    active = jax.nn.silu(summed)
    model_width = active.shape[1] // 3

    def unit_rows(member):
        shaped = member.reshape(length, head_count, -1)
        return shaped * lax.rsqrt(lax.optimization_barrier(jnp.sum(shaped * shaped, axis=-1, keepdims=True)) + 1e-06)
    queries = unit_rows(active[:, :model_width])
    queries = queries * queries.shape[-1] ** (-0.5)
    keys_all = unit_rows(active[:, model_width:2 * model_width])
    values_all = active[:, 2 * model_width:].reshape(length, head_count, -1)
    return (queries, keys_all, values_all)

def rates_of(rate_inputs, decay_log, decay_bias):
    head_count = decay_log.shape[0]
    strength = jax.nn.sigmoid(rate_inputs[:, :head_count])
    decays = -jnp.exp(decay_log) * jax.nn.softplus(rate_inputs[:, head_count:] + decay_bias)
    return (strength, decays)

def head_output(outputs, gate_part, head_gain):
    normed_heads = outputs * lax.rsqrt(lax.optimization_barrier(jnp.mean(outputs * outputs, axis=-1, keepdims=True)) + 1e-05) * head_gain
    return normed_heads.reshape(outputs.shape[0], -1) * jax.nn.silu(gate_part)

def swiglu(gate_up):
    half_width = gate_up.shape[1] // 2
    return jax.nn.silu(gate_up[:, :half_width]) * gate_up[:, half_width:]

def token_step(carried, element):
    query_now, key_now, value_now, strength_now, decay_now = element
    retain = jnp.exp(decay_now)
    recalled = jnp.einsum('hvd,hd->hv', carried, key_now, precision=highest)
    written = strength_now[:, None] * (value_now - retain[:, None] * recalled)
    carried = retain[:, None, None] * carried + written[:, :, None] * key_now[:, None, :]
    return (carried, jnp.einsum('hvd,hd->hv', carried, query_now, precision=highest))

def block_step(carried, element):
    return lax.scan(token_step, carried, element)

def recurrence(queries, keys_all, values_all, strength, decays):
    block_count = queries.shape[0] // BLOCK
    blocks = tuple((member.reshape((block_count, BLOCK) + member.shape[1:]) for member in (queries, keys_all, values_all, strength, decays)))
    head_count = queries.shape[1]
    head_size = queries.shape[2]
    initial = jnp.zeros((head_count, head_size, head_size), jnp.float32)
    produced = lax.scan(jax.checkpoint(block_step), initial, blocks)[1]
    return produced.reshape(queries.shape)

def forward(tokens, w_mixer, w_rates, w_project, w_gate_up, w_down, conv_kernel, decay_log, decay_bias, head_gain, gain_mixer, gain_mlp):
    model_width = tokens.shape[1]
    head_count = decay_log.shape[0]
    normed = low(norm_scale(tokens, gain_mixer))
    mixed = low_back(low(hdot(normed, w_mixer)))
    padded = jnp.concatenate([jnp.zeros((3, 3 * model_width), jnp.float32), mixed[:, :3 * model_width]], 0)
    queries, keys_all, values_all = features(padded, conv_kernel, head_count)
    queries = low_back(low(queries))
    keys_all = low_back(low(keys_all))
    values_all = low_back(low(values_all))
    strength, decays = rates_of(hdot(normed, w_rates), decay_log, decay_bias)
    outputs = recurrence(queries, keys_all, values_all, strength, decays)
    gated = low(head_output(outputs, mixed[:, 3 * model_width:], head_gain))
    hidden_state = tokens + low_back(hdot(gated, w_project))
    normed_two = low(norm_scale(hidden_state, gain_mlp))
    gate_up = low_back(hdot(normed_two, w_gate_up))
    inner_act = low(swiglu(gate_up))
    return hidden_state + low_back(hdot(inner_act, w_down.T))

def reference(tokens, w_mixer, w_rates, w_project, w_gate_up, w_down, conv_kernel, decay_log, decay_bias, head_gain, gain_mixer, gain_mlp, cotangent):
    primals = tuple((member.astype(jnp.float32) for member in (tokens, w_mixer, w_rates, w_project, w_gate_up, w_down, conv_kernel, decay_log, decay_bias, head_gain, gain_mixer, gain_mlp)))
    result, pullback = jax.vjp(forward, *primals)
    gradients = pullback(cotangent.astype(jnp.float32))
    return (result.astype(jnp.bfloat16), gradients[0].astype(jnp.bfloat16), gradients[1], gradients[2], gradients[3], gradients[4], gradients[5], gradients[6], gradients[7], gradients[8], gradients[9], gradients[10], gradients[11])
```

```python
from functools import partial

import jax
import jax.numpy as jnp
from jax import lax
from jax.sharding import PartitionSpec as P

BLOCK = 64


highest = lax.Precision.HIGHEST


def shifted(value, axis, by):
    length = lax.axis_size(axis)
    pairs = [(i, i + by) for i in range(length) if 0 <= i + by < length]
    return lax.ppermute(value, axis, pairs)


def prefix_2(value, axis, join, neutral):
    place = lax.axis_index(axis)
    gathered = jax.tree.map(
        lambda a, kind: lax.all_gather(a.astype(kind), axis), value, (jnp.bfloat16, jnp.bfloat16)
    )
    state = jax.tree.map(lambda a, e: jnp.zeros_like(a) + jnp.asarray(e, a.dtype), value, neutral)

    def one(turn, state):
        return join(
            state,
            jax.tree.map(
                lambda a, own: lax.dynamic_index_in_dim(a, turn, 0, False).astype(own.dtype),
                gathered,
                value,
            ),
        )

    return lax.fori_loop(0, place, one, state)


def entering(value, axis, combine, identity):
    length, place = (lax.axis_size(axis), lax.axis_index(axis))
    everything = jax.tree.map(
        lambda part, kind: lax.all_gather(part.astype(kind), axis),
        value,
        jax.tree.map(lambda a: jnp.bfloat16 if a.dtype == jnp.float32 else a.dtype, value),
    )
    start = jax.tree.map(
        lambda part, zero: jnp.broadcast_to(jnp.asarray(zero, part.dtype), part.shape),
        value,
        identity,
    )

    def turn(k, before):
        at = length - 1 - k
        reached = at > place
        new = combine(
            before, jax.tree.map(lambda part, own: part[at].astype(own.dtype), everything, value)
        )
        return jax.tree.map(lambda a, b: jnp.where(reached, a, b), new, before)

    return lax.fori_loop(0, length, turn, start)


def round_trip(values_in):
    return lax.optimization_barrier(values_in.astype(jnp.bfloat16)).astype(jnp.float32)


def norm_scale(values_in, scales):
    return (
        values_in
        * lax.rsqrt(jnp.mean(values_in * values_in, axis=-1, keepdims=True) + 1e-06)
        * scales
    )


def features(extended, kernel, head_count):
    length = extended.shape[0] - 3
    summed = kernel[0] * extended[0:length]
    for offset in range(1, 4):
        summed = summed + kernel[offset] * extended[offset : offset + length]
    active = jax.nn.silu(summed)
    model_width = active.shape[1] // 3

    def unit_rows(member):
        shaped = member.reshape(length, head_count, -1)
        return shaped * lax.rsqrt(jnp.sum(shaped * shaped, axis=-1, keepdims=True) + 1e-06)

    queries = unit_rows(active[:, :model_width])
    queries = queries * queries.shape[-1] ** (-0.5)
    keys_all = unit_rows(active[:, model_width : 2 * model_width])
    values_all = active[:, 2 * model_width :].reshape(length, head_count, -1)
    return (queries, keys_all, values_all)


def rates_of(rate_inputs, decay_log, decay_bias):
    head_count = decay_log.shape[0]
    strength = jax.nn.sigmoid(rate_inputs[:, :head_count])
    decays = -jnp.exp(decay_log) * jax.nn.softplus(rate_inputs[:, head_count:] + decay_bias)
    return (strength, decays)


def head_output(outputs, gate_part, head_gain):
    normed_heads = (
        outputs * lax.rsqrt(jnp.mean(outputs * outputs, axis=-1, keepdims=True) + 1e-05) * head_gain
    )
    return normed_heads.reshape(outputs.shape[0], -1) * jax.nn.silu(gate_part)


def swiglu(gate_up):
    half_width = gate_up.shape[1] // 2
    return jax.nn.silu(gate_up[:, :half_width]) * gate_up[:, half_width:]


def to_blocks(member):
    block_count = member.shape[0] // BLOCK
    shaped = member.reshape((block_count, BLOCK) + member.shape[1:])
    return jnp.moveaxis(shaped, 2, 1)


def from_blocks(member):
    shaped = jnp.moveaxis(member, 1, 2)
    return shaped.reshape((-1,) + shaped.shape[2:])


def unit_pair(head_count, head_size):
    identity_matrix = jnp.eye(head_size, dtype=jnp.float32)
    return (
        jnp.broadcast_to(identity_matrix, (head_count, head_size, head_size)),
        jnp.zeros((head_count, head_size, head_size), jnp.float32),
    )


def combine(earlier, later):
    product = jnp.einsum("hab,hbc->hac", earlier[0], later[0], precision=highest)
    carried = jnp.einsum("hab,hbc->hac", earlier[1], later[0], precision=highest) + later[1]
    return (product, carried)


def block_terms(query_block, key_block, value_block, strength_block, decay_block):
    block_size = key_block.shape[1]
    lower_ones = jnp.tril(jnp.ones((block_size, block_size), jnp.float32))
    cumulative = jnp.einsum("hd,cd->hc", decay_block, lower_ones, precision=highest)
    positions = jnp.arange(block_size)
    causal = positions[:, None] >= positions[None, :]
    strict = positions[:, None] > positions[None, :]
    spread = cumulative[:, :, None] - cumulative[:, None, :]
    ratios = jnp.where(causal, jnp.exp(jnp.where(causal, spread, 0.0)), 0.0)
    key_products = jnp.einsum("hcd,hed->hce", key_block, key_block, precision=highest)
    lower_part = jnp.where(strict, strength_block[:, :, None] * ratios * key_products, 0.0)
    system = lower_part + jnp.eye(block_size, dtype=jnp.float32)
    gammas = jnp.exp(cumulative)
    updates = lax.linalg.triangular_solve(
        system,
        strength_block[:, :, None] * value_block,
        left_side=True,
        lower=True,
        unit_diagonal=True,
    )
    erasers = lax.linalg.triangular_solve(
        system,
        (strength_block * gammas)[:, :, None] * key_block,
        left_side=True,
        lower=True,
        unit_diagonal=True,
    )
    scores = jnp.einsum("hcd,hed->hce", query_block, key_block, precision=highest) * ratios
    tail_keys = jnp.exp(cumulative[:, -1:] - cumulative)[:, :, None] * key_block
    return (gammas, scores, updates, erasers, tail_keys)


def run_blocks(query_blocks, block_parts, start_state):

    def advance(carried, element):
        query_block, gammas, scores, updates, erasers, tail_keys = element
        fresh_values = updates - jnp.einsum("hcd,hvd->hcv", erasers, carried, precision=highest)
        produced = gammas[:, :, None] * jnp.einsum(
            "hcd,hvd->hcv", query_block, carried, precision=highest
        )
        produced = produced + jnp.einsum("hce,hev->hcv", scores, fresh_values, precision=highest)
        carried = gammas[:, -1][:, None, None] * carried + jnp.einsum(
            "hcv,hcd->hvd", fresh_values, tail_keys, precision=highest
        )
        return (carried, produced)

    end_state, produced = lax.scan(advance, start_state, (query_blocks,) + tuple(block_parts))
    return (produced, end_state)


def span(query_blocks, key_blocks, value_blocks, strength_blocks, decay_blocks, start_state):
    block_parts = jax.vmap(block_terms)(
        query_blocks, key_blocks, value_blocks, strength_blocks, decay_blocks
    )
    return run_blocks(query_blocks, block_parts, start_state)


def block_maps(block_parts, head_size):
    gammas, scores, updates, erasers, tail_keys = block_parts
    identity_matrix = jnp.eye(head_size, dtype=jnp.float32)
    transitions = gammas[:, :, -1][:, :, None, None] * identity_matrix - jnp.einsum(
        "nhcd,nhce->nhde", erasers, tail_keys, precision=highest
    )
    writes = jnp.einsum("nhcv,nhce->nhve", updates, tail_keys, precision=highest)

    def compose(carried, element):
        return (combine(carried, element), None)

    initial = unit_pair(transitions.shape[1], head_size)
    return lax.scan(compose, initial, (transitions, writes))[0]


def term_rows(left, right, precise):
    if precise:
        return jnp.einsum(
            "tr,tc->rc", left, right, precision=highest, preferred_element_type=jnp.float32
        )
    return jnp.einsum("tr,tc->rc", left, right, preferred_element_type=jnp.float32)


def on_device(
    tokens,
    w_mixer,
    w_rates,
    w_project,
    w_gate_up,
    w_down,
    conv_kernel,
    decay_log,
    decay_bias,
    head_gain,
    gain_mixer,
    gain_mlp,
    cotangent,
):
    length, model_width = tokens.shape
    head_count = decay_log.shape[0]
    head_size = head_gain.shape[0]
    conv_width = 3 * model_width
    full_mixer, full_rates, full_project, full_gate_up, full_down = (
        lax.all_gather(w_mixer, ("seq", "fsdp"), axis=0, tiled=True),
        lax.all_gather(w_rates, ("seq", "fsdp"), axis=0, tiled=True),
        lax.all_gather(w_project, ("seq", "fsdp"), axis=0, tiled=True),
        lax.all_gather(w_gate_up, ("seq", "fsdp"), axis=0, tiled=True),
        lax.all_gather(w_down, ("seq", "fsdp"), axis=0, tiled=True),
    )
    source = tokens.astype(jnp.float32)
    normed, norm_pull = jax.vjp(norm_scale, source, gain_mixer)
    normed_low = normed.astype(jnp.bfloat16)
    mixed_low = jnp.dot(normed_low, full_mixer, preferred_element_type=jnp.float32).astype(
        jnp.bfloat16
    )
    rate_inputs = jnp.dot(normed_low, full_rates, preferred_element_type=jnp.float32)
    previous = shifted(mixed_low[length - 3 :, :conv_width], ("seq", "fsdp"), 1)
    extended = jnp.concatenate([previous, mixed_low[:, :conv_width]], 0).astype(jnp.float32)
    triple, feature_pull = jax.vjp(partial(features, head_count=head_count), extended, conv_kernel)
    queries, keys_all, values_all = (round_trip(member) for member in triple)
    (strength, decays), rate_pull = jax.vjp(rates_of, rate_inputs, decay_log, decay_bias)
    blocks = tuple(
        (to_blocks(member) for member in (queries, keys_all, values_all, strength, decays))
    )
    block_parts = jax.vmap(block_terms)(*blocks)
    span_trans, span_writes = block_maps(block_parts, head_size)
    identity = unit_pair(head_count, head_size)
    prefix = prefix_2((span_trans, span_writes), ("seq", "fsdp"), combine, identity)
    start_state = prefix[1]
    output_blocks = run_blocks(blocks[0], block_parts, start_state)[0]
    outputs = from_blocks(output_blocks)
    gate_part = mixed_low[:, conv_width:].astype(jnp.float32)
    gated, head_pull = jax.vjp(head_output, outputs, gate_part, head_gain)
    gated_low = gated.astype(jnp.bfloat16)
    hidden_state = source + jnp.dot(gated_low, full_project, preferred_element_type=jnp.float32)
    normed_two, norm_two_pull = jax.vjp(norm_scale, hidden_state, gain_mlp)
    normed_two_low = normed_two.astype(jnp.bfloat16)
    gate_up = jnp.dot(normed_two_low, full_gate_up, preferred_element_type=jnp.float32)
    inner_act, inner_pull = jax.vjp(swiglu, gate_up)
    inner_low = inner_act.astype(jnp.bfloat16)
    result = hidden_state + jnp.einsum(
        "tf,df->td", inner_low, full_down, preferred_element_type=jnp.float32
    )
    upstream = cotangent.astype(jnp.float32)
    grad_inner = jnp.dot(cotangent, full_down, preferred_element_type=jnp.float32)
    grad_swiglu_low = inner_pull(grad_inner)[0].astype(jnp.bfloat16)
    grad_normed_two = jnp.einsum(
        "tc,dc->td", grad_swiglu_low, full_gate_up, preferred_element_type=jnp.float32
    )
    grad_hidden_part, grad_gain_mlp = norm_two_pull(grad_normed_two)
    grad_hidden = upstream + grad_hidden_part
    grad_hidden_low = grad_hidden.astype(jnp.bfloat16)
    grad_gated = jnp.einsum(
        "te,de->td", grad_hidden_low, full_project, preferred_element_type=jnp.float32
    )
    grad_outputs, grad_gate, grad_head_gain = head_pull(grad_gated)
    grad_out_blocks = to_blocks(grad_outputs)
    primal_pair, span_pull = jax.vjp(span, *blocks, start_state)
    local_grads = span_pull((grad_out_blocks, jnp.zeros_like(start_state)))
    suffix = entering(
        (jnp.swapaxes(span_trans, 1, 2), local_grads[5]), ("seq", "fsdp"), combine, identity
    )
    later_grads = span_pull((jnp.zeros_like(grad_out_blocks), suffix[1]))
    grad_blocks = [
        from_blocks(front_grad + back_grad)
        for front_grad, back_grad in zip(local_grads[:5], later_grads[:5])
    ]
    grad_triple = tuple((round_trip(member) for member in grad_blocks[:3]))
    grad_extended, grad_kernel = feature_pull(grad_triple)
    grad_inputs, grad_decay_log, grad_decay_bias = rate_pull((grad_blocks[3], grad_blocks[4]))
    following = shifted(grad_extended[:3].astype(jnp.bfloat16), ("seq", "fsdp"), -1).astype(
        jnp.float32
    )
    grad_conv = grad_extended[3:] + jnp.pad(following, ((length - 3, 0), (0, 0)))
    grad_mixed_low = jnp.concatenate([grad_conv, grad_gate], 1).astype(jnp.bfloat16)
    grad_normed = jnp.einsum(
        "tc,dc->td", grad_mixed_low, full_mixer, preferred_element_type=jnp.float32
    )
    grad_normed = grad_normed + jnp.dot(
        grad_inputs, full_rates.astype(jnp.float32).T, precision=highest
    )
    grad_source, grad_gain_mixer = norm_pull(grad_normed)
    grad_tokens = (grad_hidden + grad_source).astype(jnp.bfloat16)
    normed_wide = normed_low.astype(jnp.float32)
    grad_mixer = lax.psum_scatter(
        term_rows(normed_low, grad_mixed_low, False),
        ("seq", "fsdp"),
        scatter_dimension=0,
        tiled=True,
    )
    grad_rates = lax.psum_scatter(
        term_rows(normed_wide, grad_inputs, True), ("seq", "fsdp"), scatter_dimension=0, tiled=True
    )
    grad_project = lax.psum_scatter(
        term_rows(gated_low, grad_hidden_low, False),
        ("seq", "fsdp"),
        scatter_dimension=0,
        tiled=True,
    )
    grad_gate_up = lax.psum_scatter(
        term_rows(normed_two_low, grad_swiglu_low, False),
        ("seq", "fsdp"),
        scatter_dimension=0,
        tiled=True,
    )
    grad_down = lax.psum_scatter(
        term_rows(cotangent, inner_low, False), ("seq", "fsdp"), scatter_dimension=0, tiled=True
    )
    small_sums = lax.psum(
        (
            grad_kernel,
            grad_decay_log,
            grad_decay_bias,
            grad_head_gain,
            grad_gain_mixer,
            grad_gain_mlp,
        ),
        ("seq", "fsdp"),
    )
    return (
        result.astype(jnp.bfloat16),
        grad_tokens,
        grad_mixer,
        grad_rates,
        grad_project,
        grad_gate_up,
        grad_down,
        small_sums[0],
        small_sums[1],
        small_sums[2],
        small_sums[3],
        small_sums[4],
        small_sums[5],
    )


def dot_bf16(left, right):
    return jnp.dot(left, right, preferred_element_type=jnp.float32)


def dot_nt(left, right):
    return lax.dot_general(
        left, right, (((1,), (1,)), ((), ())), preferred_element_type=jnp.float32
    )


def dot_tn(left, right):
    return lax.dot_general(
        left, right, (((0,), (0,)), ((), ())), preferred_element_type=jnp.float32
    )


def exact(left, right, dims=((1,), (0,))):
    return lax.dot_general(
        left, right, (dims, ((), ())), precision=highest, preferred_element_type=jnp.float32
    )


NT = ((1,), (1,))
TN = ((0,), (0,))


def unit_lower_inverse(strict_lower):
    size = strict_lower.shape[0]
    rows = lax.broadcasted_iota(jnp.int32, (size, size), 0)
    columns = lax.broadcasted_iota(jnp.int32, (size, size), 1)
    identity = jnp.where(rows == columns, 1.0, 0.0)
    inverse = identity - jnp.where(rows // 2 == columns // 2, strict_lower, 0.0)
    width = 2
    while width < size:
        off = (rows // (2 * width) == columns // (2 * width)) & (rows // width != columns // width)
        below = jnp.where(off, strict_lower, 0.0)
        inverse = inverse - exact(inverse, exact(below, inverse))
        width *= 2
    return inverse


def block_prepare(query, key, value, strength, decay):
    size = key.shape[0]
    rows = lax.broadcasted_iota(jnp.int32, (size, size), 0)
    columns = lax.broadcasted_iota(jnp.int32, (size, size), 1)
    causal = rows >= columns
    ones = jnp.where(causal, 1.0, 0.0)
    cumulative = exact(ones, decay)
    across = exact(decay, ones, ((0,), (1,)))
    ratios = jnp.where(causal, jnp.exp(jnp.where(causal, cumulative - across, 0.0)), 0.0)
    lower = jnp.where(rows > columns, strength * ratios * exact(key, key, NT), 0.0)
    scores = ratios * exact(query, key, NT)
    inverse = unit_lower_inverse(lower)
    gammas = jnp.exp(cumulative)
    last = cumulative[size - 1 :, :]
    updates = exact(inverse, strength * value)
    erasers = exact(inverse, (strength * gammas) * key)
    tails = jnp.exp(last - cumulative) * key
    identity = jnp.where(rows == columns, 1.0, 0.0)
    step = jnp.exp(last) * identity - exact(tails, erasers, TN)
    write = exact(tails, updates, TN)
    return ratios, lower, scores, inverse, gammas, updates, erasers, tails, step, write


def block_output(query, terms, state):
    ratios, lower, scores, inverse, gammas, updates, erasers, tails, step, write = terms
    fresh = updates - exact(erasers, state)
    return gammas * exact(query, state) + exact(scores, fresh), fresh


def block_return(query, terms, grad_out):
    gammas, scores, erasers = terms[4], terms[2], terms[6]
    return exact(gammas * query - exact(scores, erasers), grad_out, TN)


def block_backward(query, key, value, strength, terms, state, fresh, grad_out, grad_state):
    ratios, lower, scores, inverse, gammas, updates, erasers, tails, step, write = terms
    size = key.shape[0]
    rows = lax.broadcasted_iota(jnp.int32, (size, size), 0)
    columns = lax.broadcasted_iota(jnp.int32, (size, size), 1)
    grad_fresh = exact(scores, grad_out, TN) + exact(tails, grad_state)
    solved = exact(inverse, grad_fresh, TN)
    grad_lower = jnp.where(rows > columns, -exact(solved, fresh, NT), 0.0)
    grad_scores = jnp.where(rows >= columns, exact(grad_out, fresh, NT), 0.0)
    grad_erase = -exact(solved, state, NT)
    grad_decayed = exact(grad_out, state, NT)
    grad_tails = exact(fresh, grad_state, NT)
    score_part = grad_scores * ratios
    lower_part = grad_lower * ratios
    weighed = strength * lower_part
    grad_query = gammas * grad_decayed + exact(score_part, key)
    spread = gammas[size - 1 :, :]
    tail_scale = ratios[size - 1 :, :]
    tail_column = jnp.sum(jnp.where(rows == columns, tail_scale, 0.0), axis=1, keepdims=True)
    grad_key = (
        exact(score_part, query, TN)
        + exact(weighed, key)
        + exact(weighed, key, TN)
        + (strength * gammas) * grad_erase
        + tail_column * grad_tails
    )
    grad_value = strength * solved
    erase_key = jnp.sum(grad_erase * key, axis=1, keepdims=True) * gammas
    products = exact(key, key, NT)
    grad_strength = (
        jnp.sum(lower_part * products, axis=1, keepdims=True)
        + jnp.sum(solved * value, axis=1, keepdims=True)
        + erase_key
    )
    both = grad_scores * scores + grad_lower * lower
    ones_column = jnp.ones((size, 1), jnp.float32)
    tail_sum = jnp.sum(grad_tails * tails, axis=1, keepdims=True)
    grad_cumulative = (
        jnp.sum(both, axis=1, keepdims=True)
        - exact(both, ones_column, TN)
        + gammas * jnp.sum(grad_decayed * query, axis=1, keepdims=True)
        + strength * erase_key
        - tail_sum
    )
    end = jnp.sum(tail_sum) + jnp.sum(spread) * jnp.sum(state * grad_state)
    ones_upper = jnp.where(rows <= columns, 1.0, 0.0)
    grad_decay = exact(ones_upper, grad_cumulative) + end
    return grad_query, grad_key, grad_value, grad_strength, grad_decay


def conv_features(extended, kernel):
    size = extended.shape[0] - 3
    width = kernel.shape[1] // 3
    summed = kernel[0:1] * extended[0:size]
    for offset in range(1, 4):
        summed = summed + kernel[offset : offset + 1] * extended[offset : offset + size]
    active = jax.nn.silu(summed)

    def unit(part):
        return part * lax.rsqrt(jnp.sum(part * part, axis=-1, keepdims=True) + 1e-06)

    return (
        unit(active[:, :width]) * width**-0.5,
        unit(active[:, width : 2 * width]),
        active[:, 2 * width :],
    )


def rates_one(rate_inputs, log_rate, bias):
    strength = jax.nn.sigmoid(rate_inputs[:, 0:1])
    return strength, -jnp.exp(log_rate) * jax.nn.softplus(rate_inputs[:, 1:2] + bias)


def head_norm(outputs, gate_part, head_gain):
    normed = outputs * lax.rsqrt(jnp.mean(outputs * outputs, -1, keepdims=True) + 1e-05)
    return normed * head_gain * jax.nn.silu(gate_part)


def head_on_chip(
    tokens,
    w_mixer,
    w_rates,
    w_project,
    w_gate_up,
    w_down,
    conv_kernel,
    decay_log,
    decay_bias,
    head_gain,
    gain_mixer,
    gain_mlp,
    cotangent,
):
    length, width = tokens.shape
    heads = decay_log.shape[0]
    size = head_gain.shape[0]
    rows = w_mixer.shape[0]
    hidden = w_down.shape[1]
    chip, core = lax.axis_index("seq"), lax.axis_index("fsdp")
    low = jnp.bfloat16
    part = -(-hidden // (heads * 128)) * 128
    padding = heads * part - hidden

    def to_chips(columns):
        moved = lax.all_to_all(jnp.swapaxes(columns, 0, 1), "seq", 0, 0)
        both = lax.all_gather(moved, "fsdp", axis=1)
        return both.reshape(-1, columns.shape[2])

    def from_chips(grad):
        split = grad.reshape(heads, 2, rows, -1)
        summed = lax.psum_scatter(split, "fsdp", scatter_dimension=1).astype(low)
        return jnp.swapaxes(lax.all_to_all(summed, "seq", 0, 0), 0, 1).astype(jnp.float32)

    def gather(rows_here):
        return lax.all_gather(rows_here, "seq").reshape(-1, rows_here.shape[1])

    def scatter(terms):
        split = terms.astype(low).reshape(heads, length, -1)
        return lax.psum_scatter(split, "seq", scatter_dimension=0).astype(jnp.float32)

    rate_columns = jnp.swapaxes(w_rates.reshape(rows, 2, heads), 1, 2)
    mixer_columns = jnp.swapaxes(w_mixer.reshape(rows, 4, heads, size), 1, 2)
    mixer_columns = jnp.concatenate(
        [
            mixer_columns.reshape(rows, heads, 4 * size),
            jnp.pad(rate_columns, ((0, 0), (0, 0), (0, size - 2))),
        ],
        2,
    )
    mixer = to_chips(mixer_columns)
    gate_up_columns = jnp.pad(w_gate_up.reshape(rows, 2, hidden), ((0, 0), (0, 0), (0, padding)))
    gate_up_columns = jnp.swapaxes(gate_up_columns.reshape(rows, 2, heads, part), 1, 2)
    down_columns = jnp.pad(w_down, ((0, 0), (0, padding))).reshape(rows, heads, part)
    later_columns = jnp.concatenate(
        [gate_up_columns.reshape(rows, heads, 2 * part), down_columns], 2
    )
    later = to_chips(later_columns)
    gate_up_weight, down_weight = later[:, : 2 * part], later[:, 2 * part :]
    project = lax.all_gather(w_project, "fsdp", axis=0, tiled=True)
    kernel = lax.dynamic_index_in_dim(
        conv_kernel.reshape(4, 3, heads, size), chip, 2, False
    ).reshape(4, 3 * size)
    log_rate, bias = decay_log[chip], decay_bias[chip]

    source = tokens.astype(jnp.float32)
    normed, norm_pull = jax.vjp(norm_scale, source, gain_mixer)
    normed_all = gather(normed.astype(low))
    cotangent_all = gather(cotangent)
    mixed = dot_bf16(normed_all, mixer)
    mixed_low = mixed[:, : 4 * size].astype(low)
    rate_inputs = mixed[:, 4 * size : 4 * size + 2].reshape(heads, length, 2)

    def from_before(tail):
        other = lax.ppermute(tail, "fsdp", [(0, 1), (1, 0)])
        earlier = jnp.concatenate([jnp.zeros_like(other[:1]), other[:-1]], 0)
        return jnp.where(core == 0, earlier, other)

    def from_after(front):
        other = lax.ppermute(front, "fsdp", [(0, 1), (1, 0)])
        nextone = jnp.concatenate([other[1:], jnp.zeros_like(other[:1])], 0)
        return jnp.where(core == 0, other, nextone)

    blocks = mixed_low.reshape(heads, length, 4 * size)
    conv_in = blocks[:, :, : 3 * size]
    extended = jnp.concatenate([from_before(conv_in[:, length - 3 :]), conv_in], 1)
    triple, feature_pull = jax.vjp(
        jax.vmap(conv_features, (0, None)), extended.astype(jnp.float32), kernel
    )
    query, key, value = (round_trip(member) for member in triple)
    (strength, decay), rate_pull = jax.vjp(
        jax.vmap(rates_one, (0, None, None)), rate_inputs, log_rate, bias
    )
    terms = jax.vmap(block_prepare)(query, key, value, strength, decay)

    def in_order(member):
        both = lax.all_gather(member, "fsdp", axis=1)
        return both.reshape((-1,) + member.shape[1:])

    def own(member):
        return lax.dynamic_index_in_dim(
            member.reshape((-1, 2) + member.shape[1:]), core, 1, False
        )

    steps, writes = in_order(terms[8]), in_order(terms[9])

    def forward_step(state, element):
        return exact(element[0], state) + element[1], state

    states = own(lax.scan(forward_step, jnp.zeros_like(steps[0]), (steps, writes))[1])
    outputs, fresh = jax.vmap(block_output)(query, terms, states)
    gate_part = blocks[:, :, 3 * size :].astype(jnp.float32)
    gated, head_pull = jax.vjp(head_norm, outputs, gate_part, head_gain)
    gated_low = gated.astype(low).reshape(-1, size)
    hidden_state = source + scatter(dot_bf16(gated_low, project))
    normed_two, norm_two_pull = jax.vjp(norm_scale, hidden_state, gain_mlp)
    normed_two_all = gather(normed_two.astype(low))
    gate_up = dot_bf16(normed_two_all, gate_up_weight)
    inner_act, inner_pull = jax.vjp(swiglu, gate_up)
    inner_low = inner_act.astype(low)
    result = hidden_state + scatter(dot_nt(inner_low, down_weight))
    grad_inner = dot_bf16(cotangent_all, down_weight)
    grad_swiglu = inner_pull(grad_inner)[0].astype(low)
    grad_hidden_part, grad_gain_mlp = norm_two_pull(scatter(dot_nt(grad_swiglu, gate_up_weight)))
    grad_hidden = cotangent.astype(jnp.float32) + grad_hidden_part
    grad_branch = gather(grad_hidden.astype(low))
    grad_down = dot_tn(cotangent_all, inner_low)
    grad_gate_up = dot_tn(normed_two_all, grad_swiglu)
    grad_gated = dot_nt(grad_branch, project).reshape(heads, length, size)
    grad_outputs, grad_gate, grad_head_gain = head_pull(grad_gated)
    returns = in_order(jax.vmap(block_return)(query, terms, grad_outputs))

    def backward_step(grad, element):
        return exact(element[0], grad, TN) + element[1], grad

    grad_states = own(
        lax.scan(backward_step, jnp.zeros_like(steps[0]), (steps, returns), reverse=True)[1]
    )
    grad_query, grad_key, grad_value, grad_strength, grad_decay = jax.vmap(block_backward)(
        query, key, value, strength, terms, states, fresh, grad_outputs, grad_states
    )
    grad_triple = tuple(round_trip(member) for member in (grad_query, grad_key, grad_value))
    grad_extended, grad_kernel = feature_pull(grad_triple)
    grad_rate_inputs, grad_log_rate, grad_bias = rate_pull((grad_strength, grad_decay))
    following = from_after(grad_extended[:, :3].astype(low)).astype(jnp.float32)
    grad_conv = grad_extended[:, 3:] + jnp.pad(following, ((0, 0), (length - 3, 0), (0, 0)))
    grad_mixed = (
        jnp.concatenate(
            [
                grad_conv,
                grad_gate,
                jnp.pad(grad_rate_inputs, ((0, 0), (0, 0), (0, size - 2))),
            ],
            2,
        )
        .astype(low)
        .reshape(-1, 5 * size)
    )
    grad_source, grad_gain_mixer = norm_pull(scatter(dot_nt(grad_mixed, mixer)))
    grad_tokens = (grad_hidden + grad_source).astype(low)
    grad_mixer = from_chips(dot_tn(normed_all, grad_mixed))
    grad_later = from_chips(jnp.concatenate([grad_gate_up, grad_down], 1))
    grad_project = lax.psum_scatter(
        dot_tn(gated_low, grad_branch), "fsdp", scatter_dimension=0, tiled=True
    )
    grad_gate_up = jnp.swapaxes(
        grad_later[:, :, : 2 * part].reshape(rows, heads, 2, part), 1, 2
    ).reshape(rows, 2, -1)[:, :, :hidden]
    place = jax.nn.one_hot(chip, heads, dtype=jnp.float32)
    small = lax.psum(
        (
            (place[:, None] * grad_kernel.reshape(4, 3, 1, size)).reshape(4, -1),
            place * grad_log_rate,
            place * grad_bias,
            grad_head_gain,
            grad_gain_mixer,
            grad_gain_mlp,
        ),
        ("seq", "fsdp"),
    )
    return (
        result.astype(low),
        grad_tokens,
        jnp.swapaxes(grad_mixer[:, :, : 4 * size].reshape(rows, heads, 4, size), 1, 2).reshape(
            rows, -1
        ),
        jnp.swapaxes(grad_mixer[:, :, 4 * size : 4 * size + 2], 1, 2).reshape(rows, -1),
        grad_project,
        grad_gate_up.reshape(rows, -1),
        grad_later[:, :, 2 * part :].reshape(rows, -1)[:, :hidden],
    ) + small


def solution(mesh):
    placed = (
        P(("seq", "fsdp"), None),
        P(("seq", "fsdp"), None),
        P(("seq", "fsdp"), None),
        P(("seq", "fsdp"), None),
        P(("seq", "fsdp"), None),
        P(("seq", "fsdp"), None),
        P(),
        P(),
        P(),
        P(),
        P(),
        P(),
        P(("seq", "fsdp"), None),
    )
    def body(*members):
        one_head = members[7].shape[0] == mesh.shape["seq"] and mesh.shape["fsdp"] == 2
        one_block = members[0].shape[0] == 2 * BLOCK == members[9].shape[0]
        return (head_on_chip if one_head and one_block else on_device)(*members)

    return jax.shard_map(
        body,
        mesh=mesh,
        in_specs=placed,
        out_specs=(
            P(("seq", "fsdp"), None),
            P(("seq", "fsdp"), None),
            P(("seq", "fsdp"), None),
            P(("seq", "fsdp"), None),
            P(("seq", "fsdp"), None),
            P(("seq", "fsdp"), None),
            P(("seq", "fsdp"), None),
            P(),
            P(),
            P(),
            P(),
            P(),
            P(),
        ),
        check_vma=False,
    )
```

```python
from functools import partial

import jax
import jax.numpy as jnp
from jax import lax
from jax.experimental import pallas as pl
from jax.experimental.pallas import tpu as pltpu
from jax.sharding import Mesh
from jax.sharding import PartitionSpec as P

BLOCK = 64


highest = lax.Precision.HIGHEST


def shifted(value, axis, by):
    length = lax.axis_size(axis)
    pairs = [(i, i + by) for i in range(length) if 0 <= i + by < length]
    return lax.ppermute(value, axis, pairs)


def prefix_2(value, axis, join, neutral):
    place = lax.axis_index(axis)
    gathered = jax.tree.map(
        lambda a, kind: lax.all_gather(a.astype(kind), axis), value, (jnp.bfloat16, jnp.bfloat16)
    )
    state = jax.tree.map(lambda a, e: jnp.zeros_like(a) + jnp.asarray(e, a.dtype), value, neutral)

    def one(turn, state):
        return join(
            state,
            jax.tree.map(
                lambda a, own: lax.dynamic_index_in_dim(a, turn, 0, False).astype(own.dtype),
                gathered,
                value,
            ),
        )

    return lax.fori_loop(0, place, one, state)


def entering(value, axis, combine, identity):
    length, place = (lax.axis_size(axis), lax.axis_index(axis))
    everything = jax.tree.map(
        lambda part, kind: lax.all_gather(part.astype(kind), axis),
        value,
        jax.tree.map(lambda a: jnp.bfloat16 if a.dtype == jnp.float32 else a.dtype, value),
    )
    start = jax.tree.map(
        lambda part, zero: jnp.broadcast_to(jnp.asarray(zero, part.dtype), part.shape),
        value,
        identity,
    )

    def turn(k, before):
        at = length - 1 - k
        reached = at > place
        new = combine(
            before, jax.tree.map(lambda part, own: part[at].astype(own.dtype), everything, value)
        )
        return jax.tree.map(lambda a, b: jnp.where(reached, a, b), new, before)

    return lax.fori_loop(0, length, turn, start)


def round_trip(values_in):
    return lax.optimization_barrier(values_in.astype(jnp.bfloat16)).astype(jnp.float32)


def norm_scale(values_in, scales):
    return (
        values_in
        * lax.rsqrt(jnp.mean(values_in * values_in, axis=-1, keepdims=True) + 1e-06)
        * scales
    )


def features(extended, kernel, head_count):
    length = extended.shape[0] - 3
    summed = kernel[0] * extended[0:length]
    for offset in range(1, 4):
        summed = summed + kernel[offset] * extended[offset : offset + length]
    active = jax.nn.silu(summed)
    model_width = active.shape[1] // 3

    def unit_rows(member):
        shaped = member.reshape(length, head_count, -1)
        return shaped * lax.rsqrt(jnp.sum(shaped * shaped, axis=-1, keepdims=True) + 1e-06)

    queries = unit_rows(active[:, :model_width])
    queries = queries * queries.shape[-1] ** (-0.5)
    keys_all = unit_rows(active[:, model_width : 2 * model_width])
    values_all = active[:, 2 * model_width :].reshape(length, head_count, -1)
    return (queries, keys_all, values_all)


def rates_of(rate_inputs, decay_log, decay_bias):
    head_count = decay_log.shape[0]
    strength = jax.nn.sigmoid(rate_inputs[:, :head_count])
    decays = -jnp.exp(decay_log) * jax.nn.softplus(rate_inputs[:, head_count:] + decay_bias)
    return (strength, decays)


def head_output(outputs, gate_part, head_gain):
    normed_heads = (
        outputs * lax.rsqrt(jnp.mean(outputs * outputs, axis=-1, keepdims=True) + 1e-05) * head_gain
    )
    return normed_heads.reshape(outputs.shape[0], -1) * jax.nn.silu(gate_part)


def swiglu(gate_up):
    half_width = gate_up.shape[1] // 2
    return jax.nn.silu(gate_up[:, :half_width]) * gate_up[:, half_width:]


def to_blocks(member):
    block_count = member.shape[0] // BLOCK
    shaped = member.reshape((block_count, BLOCK) + member.shape[1:])
    return jnp.moveaxis(shaped, 2, 1)


def from_blocks(member):
    shaped = jnp.moveaxis(member, 1, 2)
    return shaped.reshape((-1,) + shaped.shape[2:])


def unit_pair(head_count, head_size):
    identity_matrix = jnp.eye(head_size, dtype=jnp.float32)
    return (
        jnp.broadcast_to(identity_matrix, (head_count, head_size, head_size)),
        jnp.zeros((head_count, head_size, head_size), jnp.float32),
    )


def combine(earlier, later):
    product = jnp.einsum("hab,hbc->hac", earlier[0], later[0], precision=highest)
    carried = jnp.einsum("hab,hbc->hac", earlier[1], later[0], precision=highest) + later[1]
    return (product, carried)


def block_terms(query_block, key_block, value_block, strength_block, decay_block):
    block_size = key_block.shape[1]
    lower_ones = jnp.tril(jnp.ones((block_size, block_size), jnp.float32))
    cumulative = jnp.einsum("hd,cd->hc", decay_block, lower_ones, precision=highest)
    positions = jnp.arange(block_size)
    causal = positions[:, None] >= positions[None, :]
    strict = positions[:, None] > positions[None, :]
    spread = cumulative[:, :, None] - cumulative[:, None, :]
    ratios = jnp.where(causal, jnp.exp(jnp.where(causal, spread, 0.0)), 0.0)
    key_products = jnp.einsum("hcd,hed->hce", key_block, key_block, precision=highest)
    lower_part = jnp.where(strict, strength_block[:, :, None] * ratios * key_products, 0.0)
    system = lower_part + jnp.eye(block_size, dtype=jnp.float32)
    gammas = jnp.exp(cumulative)
    updates = lax.linalg.triangular_solve(
        system,
        strength_block[:, :, None] * value_block,
        left_side=True,
        lower=True,
        unit_diagonal=True,
    )
    erasers = lax.linalg.triangular_solve(
        system,
        (strength_block * gammas)[:, :, None] * key_block,
        left_side=True,
        lower=True,
        unit_diagonal=True,
    )
    scores = jnp.einsum("hcd,hed->hce", query_block, key_block, precision=highest) * ratios
    tail_keys = jnp.exp(cumulative[:, -1:] - cumulative)[:, :, None] * key_block
    return (gammas, scores, updates, erasers, tail_keys)


def run_blocks(query_blocks, block_parts, start_state):

    def advance(carried, element):
        query_block, gammas, scores, updates, erasers, tail_keys = element
        fresh_values = updates - jnp.einsum("hcd,hvd->hcv", erasers, carried, precision=highest)
        produced = gammas[:, :, None] * jnp.einsum(
            "hcd,hvd->hcv", query_block, carried, precision=highest
        )
        produced = produced + jnp.einsum("hce,hev->hcv", scores, fresh_values, precision=highest)
        carried = gammas[:, -1][:, None, None] * carried + jnp.einsum(
            "hcv,hcd->hvd", fresh_values, tail_keys, precision=highest
        )
        return (carried, produced)

    end_state, produced = lax.scan(advance, start_state, (query_blocks,) + tuple(block_parts))
    return (produced, end_state)


def span(query_blocks, key_blocks, value_blocks, strength_blocks, decay_blocks, start_state):
    block_parts = jax.vmap(block_terms)(
        query_blocks, key_blocks, value_blocks, strength_blocks, decay_blocks
    )
    return run_blocks(query_blocks, block_parts, start_state)


def block_maps(block_parts, head_size):
    gammas, scores, updates, erasers, tail_keys = block_parts
    identity_matrix = jnp.eye(head_size, dtype=jnp.float32)
    transitions = gammas[:, :, -1][:, :, None, None] * identity_matrix - jnp.einsum(
        "nhcd,nhce->nhde", erasers, tail_keys, precision=highest
    )
    writes = jnp.einsum("nhcv,nhce->nhve", updates, tail_keys, precision=highest)

    def compose(carried, element):
        return (combine(carried, element), None)

    initial = unit_pair(transitions.shape[1], head_size)
    return lax.scan(compose, initial, (transitions, writes))[0]


def term_rows(left, right, precise):
    if precise:
        return jnp.einsum(
            "tr,tc->rc", left, right, precision=highest, preferred_element_type=jnp.float32
        )
    return jnp.einsum("tr,tc->rc", left, right, preferred_element_type=jnp.float32)


def on_device(
    tokens,
    w_mixer,
    w_rates,
    w_project,
    w_gate_up,
    w_down,
    conv_kernel,
    decay_log,
    decay_bias,
    head_gain,
    gain_mixer,
    gain_mlp,
    cotangent,
):
    length, model_width = tokens.shape
    head_count = decay_log.shape[0]
    head_size = head_gain.shape[0]
    conv_width = 3 * model_width
    full_mixer, full_rates, full_project, full_gate_up, full_down = (
        lax.all_gather(w_mixer, ("seq", "fsdp"), axis=0, tiled=True),
        lax.all_gather(w_rates, ("seq", "fsdp"), axis=0, tiled=True),
        lax.all_gather(w_project, ("seq", "fsdp"), axis=0, tiled=True),
        lax.all_gather(w_gate_up, ("seq", "fsdp"), axis=0, tiled=True),
        lax.all_gather(w_down, ("seq", "fsdp"), axis=0, tiled=True),
    )
    source = tokens.astype(jnp.float32)
    normed, norm_pull = jax.vjp(norm_scale, source, gain_mixer)
    normed_low = normed.astype(jnp.bfloat16)
    mixed_low = jnp.dot(normed_low, full_mixer, preferred_element_type=jnp.float32).astype(
        jnp.bfloat16
    )
    rate_inputs = jnp.dot(normed_low, full_rates, preferred_element_type=jnp.float32)
    previous = shifted(mixed_low[length - 3 :, :conv_width], ("seq", "fsdp"), 1)
    extended = jnp.concatenate([previous, mixed_low[:, :conv_width]], 0).astype(jnp.float32)
    triple, feature_pull = jax.vjp(partial(features, head_count=head_count), extended, conv_kernel)
    queries, keys_all, values_all = (round_trip(member) for member in triple)
    (strength, decays), rate_pull = jax.vjp(rates_of, rate_inputs, decay_log, decay_bias)
    blocks = tuple(
        (to_blocks(member) for member in (queries, keys_all, values_all, strength, decays))
    )
    block_parts = jax.vmap(block_terms)(*blocks)
    span_trans, span_writes = block_maps(block_parts, head_size)
    identity = unit_pair(head_count, head_size)
    prefix = prefix_2((span_trans, span_writes), ("seq", "fsdp"), combine, identity)
    start_state = prefix[1]
    output_blocks = run_blocks(blocks[0], block_parts, start_state)[0]
    outputs = from_blocks(output_blocks)
    gate_part = mixed_low[:, conv_width:].astype(jnp.float32)
    gated, head_pull = jax.vjp(head_output, outputs, gate_part, head_gain)
    gated_low = gated.astype(jnp.bfloat16)
    hidden_state = source + jnp.dot(gated_low, full_project, preferred_element_type=jnp.float32)
    normed_two, norm_two_pull = jax.vjp(norm_scale, hidden_state, gain_mlp)
    normed_two_low = normed_two.astype(jnp.bfloat16)
    gate_up = jnp.dot(normed_two_low, full_gate_up, preferred_element_type=jnp.float32)
    inner_act, inner_pull = jax.vjp(swiglu, gate_up)
    inner_low = inner_act.astype(jnp.bfloat16)
    result = hidden_state + jnp.einsum(
        "tf,df->td", inner_low, full_down, preferred_element_type=jnp.float32
    )
    upstream = cotangent.astype(jnp.float32)
    grad_inner = jnp.dot(cotangent, full_down, preferred_element_type=jnp.float32)
    grad_swiglu_low = inner_pull(grad_inner)[0].astype(jnp.bfloat16)
    grad_normed_two = jnp.einsum(
        "tc,dc->td", grad_swiglu_low, full_gate_up, preferred_element_type=jnp.float32
    )
    grad_hidden_part, grad_gain_mlp = norm_two_pull(grad_normed_two)
    grad_hidden = upstream + grad_hidden_part
    grad_hidden_low = grad_hidden.astype(jnp.bfloat16)
    grad_gated = jnp.einsum(
        "te,de->td", grad_hidden_low, full_project, preferred_element_type=jnp.float32
    )
    grad_outputs, grad_gate, grad_head_gain = head_pull(grad_gated)
    grad_out_blocks = to_blocks(grad_outputs)
    primal_pair, span_pull = jax.vjp(span, *blocks, start_state)
    local_grads = span_pull((grad_out_blocks, jnp.zeros_like(start_state)))
    suffix = entering(
        (jnp.swapaxes(span_trans, 1, 2), local_grads[5]), ("seq", "fsdp"), combine, identity
    )
    later_grads = span_pull((jnp.zeros_like(grad_out_blocks), suffix[1]))
    grad_blocks = [
        from_blocks(front_grad + back_grad)
        for front_grad, back_grad in zip(local_grads[:5], later_grads[:5])
    ]
    grad_triple = tuple((round_trip(member) for member in grad_blocks[:3]))
    grad_extended, grad_kernel = feature_pull(grad_triple)
    grad_inputs, grad_decay_log, grad_decay_bias = rate_pull((grad_blocks[3], grad_blocks[4]))
    following = shifted(grad_extended[:3].astype(jnp.bfloat16), ("seq", "fsdp"), -1).astype(
        jnp.float32
    )
    grad_conv = grad_extended[3:] + jnp.pad(following, ((length - 3, 0), (0, 0)))
    grad_mixed_low = jnp.concatenate([grad_conv, grad_gate], 1).astype(jnp.bfloat16)
    grad_normed = jnp.einsum(
        "tc,dc->td", grad_mixed_low, full_mixer, preferred_element_type=jnp.float32
    )
    grad_normed = grad_normed + jnp.dot(
        grad_inputs, full_rates.astype(jnp.float32).T, precision=highest
    )
    grad_source, grad_gain_mixer = norm_pull(grad_normed)
    grad_tokens = (grad_hidden + grad_source).astype(jnp.bfloat16)
    normed_wide = normed_low.astype(jnp.float32)
    grad_mixer = lax.psum_scatter(
        term_rows(normed_low, grad_mixed_low, False),
        ("seq", "fsdp"),
        scatter_dimension=0,
        tiled=True,
    )
    grad_rates = lax.psum_scatter(
        term_rows(normed_wide, grad_inputs, True), ("seq", "fsdp"), scatter_dimension=0, tiled=True
    )
    grad_project = lax.psum_scatter(
        term_rows(gated_low, grad_hidden_low, False),
        ("seq", "fsdp"),
        scatter_dimension=0,
        tiled=True,
    )
    grad_gate_up = lax.psum_scatter(
        term_rows(normed_two_low, grad_swiglu_low, False),
        ("seq", "fsdp"),
        scatter_dimension=0,
        tiled=True,
    )
    grad_down = lax.psum_scatter(
        term_rows(cotangent, inner_low, False), ("seq", "fsdp"), scatter_dimension=0, tiled=True
    )
    small_sums = lax.psum(
        (
            grad_kernel,
            grad_decay_log,
            grad_decay_bias,
            grad_head_gain,
            grad_gain_mixer,
            grad_gain_mlp,
        ),
        ("seq", "fsdp"),
    )
    return (
        result.astype(jnp.bfloat16),
        grad_tokens,
        grad_mixer,
        grad_rates,
        grad_project,
        grad_gate_up,
        grad_down,
        small_sums[0],
        small_sums[1],
        small_sums[2],
        small_sums[3],
        small_sums[4],
        small_sums[5],
    )


def dot_bf16(left, right):
    return jnp.dot(left, right, preferred_element_type=jnp.float32)


def dot_nt(left, right):
    return lax.dot_general(
        left, right, (((1,), (1,)), ((), ())), preferred_element_type=jnp.float32
    )


def dot_tn(left, right):
    return lax.dot_general(
        left, right, (((0,), (0,)), ((), ())), preferred_element_type=jnp.float32
    )


def exact(left, right, dims=((1,), (0,))):
    return lax.dot_general(
        left, right, (dims, ((), ())), precision=highest, preferred_element_type=jnp.float32
    )


NT = ((1,), (1,))
TN = ((0,), (0,))


PLANE = ("y", "x", "core")
ALL = ("z",) + PLANE


LOW, WIDE = jnp.bfloat16, jnp.float32
NN = ((1,), (0,))
VMEM_MOST = 56 << 20


def once(left, right, dims=NN):
    return lax.dot_general(
        left.astype(LOW), right.astype(LOW), (dims, ((), ())), preferred_element_type=WIDE
    )


def halves(value):
    high = value.astype(LOW)
    return high, (value - high.astype(WIDE)).astype(LOW)


def thrice(left, right, dims=NN):
    if not isinstance(left, tuple):
        left = halves(left)
    if not isinstance(right, tuple):
        right = halves(right)
    return (
        once(left[0], right[0], dims) + once(left[0], right[1], dims) + once(left[1], right[0], dims)
    )


def pair_rows(first, second):
    return jnp.concatenate([first, second], 0)


def pair_diagonal(first, second):
    zero = jnp.zeros_like(first)
    return pair_rows(
        jnp.concatenate([first, zero], 1), jnp.concatenate([zero, second], 1)
    )


def square_iotas(size):
    return (
        lax.broadcasted_iota(jnp.int32, (size, size), 0),
        lax.broadcasted_iota(jnp.int32, (size, size), 1),
    )


def decay_ratios(column, row, causal):
    return jnp.where(causal, jnp.exp(jnp.minimum(column - row, 0.0)), 0.0)


def inverses(lowers, differ):
    size = lowers[0].shape[0]
    results = [
        jnp.where(differ == 0, 1.0, 0.0) - jnp.where(differ == 1, lower, 0.0) for lower in lowers
    ]
    for level in range(1, 7):
        parts = [halves(result) for result in results]
        below = [jnp.where((differ >> level) == 1, lower, 0.0) for lower in lowers]
        inner = [thrice(b, p) for b, p in zip(below, parts)]
        results = [r - thrice(p, i) for r, p, i in zip(results, parts, inner)]
    return results


def silu_unit(summed):
    active = summed * jax.nn.sigmoid(summed)
    scale = lax.rsqrt(jnp.sum(active * active, axis=-1, keepdims=True) + 1e-06)
    return active, scale


def conv_of(ext, kernel, column, offset, count):
    at = pl.ds(column, 128)
    summed = kernel[0:1, at] * ext[pl.ds(offset, count), at]
    for j in range(1, 4):
        summed = summed + kernel[j : j + 1, at] * ext[pl.ds(offset + j, count), at]
    return summed


def softplus(value):
    return jnp.maximum(value, 0.0) + jnp.log1p(jnp.exp(-jnp.abs(value)))


def prepare_kernel(
    normed, mixer, all_rates, pick, tail, kernel, rates, mixed, gates, rate_in, ue, inverse, scores, steps, before,
    qk, columns, total, rate_weight, ext, carry
):
    step = pl.program_id(0)
    size = 128
    span = normed.shape[0]
    count = span // size
    conv = 6 * size

    @pl.when(step == 0)
    def _():
        rate_weight[...] = once(all_rates[...], pick[...]).astype(LOW)
        first = once(tail[...], mixer[...])
        low = first.astype(LOW)
        mixed[pl.ds(0, 16), :] = low[:, :conv]
        ext[pl.ds(0, 8), :] = low.astype(WIDE)[8:16, :conv]
        rows, cols = square_iotas(size)
        one = jnp.where(rows == cols, 1.0, 0.0)
        zero = jnp.zeros_like(one)
        carry[...] = pair_rows(
            jnp.concatenate([one, zero], 1), jnp.concatenate([one, zero], 1)
        )

    products = once(normed[...], mixer[...])
    low = products.astype(LOW)
    mixed[pl.ds(pl.multiple_of(16 + step * span, 16), span), :] = low[:, :conv]
    gates[...] = low[:, conv:]
    ext[pl.ds(8, span), :] = low[:, :conv].astype(WIDE)
    rate = once(normed[...], rate_weight[...])
    rate_in[...] = rate
    strength = jax.nn.sigmoid(rate)
    decay = rates[0:1, :] * softplus(rate + rates[1:2, :])
    unit = []
    for part in range(3):
        unit.append([])
        for head in range(2):
            summed = conv_of(ext, kernel, part * 256 + head * size, 5, span)
            active, scale = silu_unit(summed)
            if part == 0:
                active = active * scale * size**-0.5
            if part == 1:
                active = active * scale
            unit[part].append(active.astype(LOW))
    ext[pl.ds(0, 8), :] = ext[pl.ds(span, 8), :]
    small_rows, small_cols = square_iotas(size)
    causal = small_rows >= small_cols
    ones = jnp.where(causal, 1.0, 0.0)
    rows, cols = square_iotas(2 * size)
    differ = rows ^ cols
    lowers, keep = [], []
    for b in range(count):
        at = slice(b * size, (b + 1) * size)
        cumulative = lax.dot_general(
            ones, decay[at], (NN, ((), ())), precision=highest, preferred_element_type=WIDE
        )
        across = cumulative.T
        ratios = pair_diagonal(
            *(
                decay_ratios(cumulative[:, 2 + h : 3 + h], across[2 + h : 3 + h, :], causal)
                for h in range(2)
            )
        )
        query, key, value = (pair_rows(unit[p][0][at], unit[p][1][at]) for p in range(3))
        beta = pair_rows(strength[at, 0:1], strength[at, 1:2])
        column = pair_rows(cumulative[:, 2:3], cumulative[:, 3:4])
        lower = jnp.where(rows > cols, beta * ratios * once(key, key, NT), 0.0)
        lowers.append(lower)
        score = ratios * once(query, key, NT)
        scores[b] = score.astype(LOW)
        qk[b] = jnp.concatenate([query, key], 1)
        lanes = lax.broadcasted_iota(jnp.int32, (2 * size, 128), 1)
        columns[b] = jnp.where(lanes == 0, beta, jnp.where(lanes == 1, column, 0.0))
        keep.append((key.astype(WIDE), value.astype(WIDE), beta, column))
    for b, inv in enumerate(inverses(lowers, differ)):
        key, value, beta, column = keep[b]
        inverse[b] = inv.astype(LOW)
        gammas = jnp.exp(column)
        both = thrice(inv, jnp.concatenate([beta * value, (beta * gammas) * key], 1))
        ue[b] = both
        before[b] = carry[...]
        next_rows = []
        for h in range(2):
            at = slice(h * size, (h + 1) * size)
            last = column[(h + 1) * size - 1 : (h + 1) * size, :]
            tails = jnp.exp(last - column[at]) * key[at]
            made = thrice(tails, both[at], TN)
            advance = jnp.where(small_rows == small_cols, jnp.exp(last), 0.0) - made[:, size:]
            steps[b, at, :] = advance
            moved = thrice(advance, carry[at, :])
            next_rows.append(
                jnp.concatenate([moved[:, :size], moved[:, size:] + made[:, :size]], 1)
            )
        carry[...] = pair_rows(*next_rows)

    @pl.when(step == pl.num_programs(0) - 1)
    def _():
        total[...] = carry[...]


def output_kernel(
    start, before, ue, scores, qk, columns, mixed, gain, project, partial_out, gated_out,
    fresh_out, state_out, out_out
):
    size = 128
    count = ue.shape[0]
    for b in range(count):
        gated = []
        tokens = pl.ds(b * size, size)
        fresh_parts, queried = [], []
        for h in range(2):
            at = slice(h * size, (h + 1) * size)
            pre = before[b, at, :]
            state = thrice(pre[:, :size], start[at, :]) + pre[:, size:]
            state_out[b, at, :] = state
            seen = thrice(
                pair_rows(ue[b, at, size:], qk[b, at, :size].astype(WIDE)), state
            )
            fresh_parts.append(ue[b, at, :size] - seen[:size])
            queried.append(jnp.exp(columns[b, at, 1:2]) * seen[size:])
        fresh = pair_rows(*fresh_parts)
        fresh_out[b] = fresh.astype(LOW)
        outputs = pair_rows(*queried) + once(scores[b], fresh)
        out_out[b] = outputs
        for h in range(2):
            at = slice(h * size, (h + 1) * size)
            one = outputs[at]
            scale = lax.rsqrt(jnp.mean(one * one, axis=-1, keepdims=True) + 1e-05)
            gate = mixed[tokens, pl.ds(h * size, size)].astype(WIDE)
            gated.append((one * scale * gain[0:1, :] * (gate * jax.nn.sigmoid(gate))).astype(LOW))
        both = jnp.concatenate(gated, 1)
        gated_out[tokens, :] = both
        partial_out[tokens, :] = once(both, project[...]).astype(LOW)


def return_kernel(
    branch, project, mixed, gain, out, scores, ue, qk, columns, steps, grad_out, back_scores,
    returns, grad_gate, total, grad_gain, carry
):
    size = 128
    count = ue.shape[0]

    @pl.when(pl.program_id(0) == 0)
    def _():
        carry[...] = jnp.zeros_like(carry)
        grad_gain[...] = jnp.zeros_like(grad_gain)

    grad_gated = once(branch[...], project[...], NT)
    for b in reversed(range(count)):
        tokens = pl.ds(b * size, size)
        grads = []
        for h in range(2):
            at, wide = slice(h * size, (h + 1) * size), pl.ds(h * size, size)
            one = out[b, at, :]
            scale = lax.rsqrt(jnp.mean(one * one, axis=-1, keepdims=True) + 1e-05)
            gate = mixed[tokens, wide].astype(WIDE)
            open_ = jax.nn.sigmoid(gate)
            given = grad_gated[b * size : (b + 1) * size, at]
            normal = one * scale
            through = given * gate * open_
            grad_gain[0:1, :] += jnp.sum(through * normal, axis=0, keepdims=True)
            grad_gate[tokens, wide] = (
                given * normal * gain[0:1, :] * (open_ * (1.0 + gate * (1.0 - open_)))
            ).astype(LOW)
            f = through * gain[0:1, :]
            grads.append(
                scale * f
                - one * (scale * scale * scale) * jnp.mean(f * one, axis=-1, keepdims=True)
            )
        grad = pair_rows(*grads)
        grad_out[b] = grad
        back = once(scores[b], grad, TN)
        back_scores[b] = back
        for h in range(2):
            at = slice(h * size, (h + 1) * size)
            scaled = jnp.exp(columns[b, at, 1:2]) * qk[b, at, :size].astype(WIDE)
            given = once(
                pair_rows(scaled, -ue[b, at, size:]), pair_rows(grad[at], back[at]), TN
            )
            returns[b, at, :] = given
            carry[at, :] = thrice(steps[b, at, :], carry[at, :], TN) + given

    @pl.when(pl.program_id(0) == pl.num_programs(0) - 1)
    def _():
        total[...] = carry[...]


def gradient_kernel(
    end, returns, steps, grad_out, back_scores, fresh, states, inverse, scores, qk, columns,
    mixed, rate_in, grad_gate, kernel, rates, grad_mixed, grad_rates, grad_kernel, sums, front,
    edge, ext, gext, carry
):
    size = 128
    count = fresh.shape[0]
    span = count * size
    conv = 6 * size
    turn = pl.program_id(0)
    step = pl.num_programs(0) - 1 - turn

    @pl.when(turn == 0)
    def _():
        carry[...] = end[...]
        grad_kernel[...] = jnp.zeros_like(grad_kernel)
        sums[...] = jnp.zeros_like(sums)
        gext[pl.ds(span, 8), :] = jnp.zeros((8, conv), WIDE)

    ext[...] = mixed[pl.ds(pl.multiple_of(step * span, 16), span + 16), :].astype(WIDE)
    small_rows, small_cols = square_iotas(size)
    causal = small_rows >= small_cols
    upper = jnp.where(small_rows <= small_cols, 1.0, 0.0)
    rows, cols = square_iotas(2 * size)
    lanes = lax.broadcasted_iota(jnp.int32, (size, 128), 1)
    values = []
    for h in range(2):
        summed = conv_of(ext, kernel, 512 + h * size, 13, span)
        values.append(summed * jax.nn.sigmoid(summed))
    unit_grads = [[None] * count for _ in range(6)]
    for b in reversed(range(count)):
        tokens = slice(b * size, (b + 1) * size)
        grad_state = carry[...]
        after = [
            thrice(steps[b, h * size : (h + 1) * size, :], grad_state[h * size : (h + 1) * size], TN)
            for h in range(2)
        ]
        carry[...] = pair_rows(*after) + returns[b]
        beta, column = columns[b, :, 0:1], columns[b, :, 1:2]
        across = [columns[b, pl.ds(h * size, size), :].T[1:2, :] for h in range(2)]
        ratios = pair_diagonal(
            *(
                decay_ratios(column[h * size : (h + 1) * size], across[h], causal)
                for h in range(2)
            )
        )
        query, key = qk[b, :, :size].astype(WIDE), qk[b, :, size:].astype(WIDE)
        value = pair_rows(
            *(values[h][tokens].astype(LOW).astype(WIDE) for h in range(2))
        )
        gammas = jnp.exp(column)
        last = [column[(h + 1) * size - 1 : (h + 1) * size] for h in range(2)]
        tail_scale = pair_rows(
            *(jnp.exp(last[h] - column[h * size : (h + 1) * size]) for h in range(2))
        )
        tails = tail_scale * key
        grad = grad_out[b]
        from_tails = [
            once(tails[h * size : (h + 1) * size], grad_state[h * size : (h + 1) * size])
            for h in range(2)
        ]
        grad_fresh = back_scores[b] + pair_rows(*from_tails)
        solved = once(inverse[b], grad_fresh, TN)
        made = fresh[b].astype(WIDE)
        pairs = once(pair_rows(-solved, grad), made, NT)
        score = scores[b].astype(WIDE)
        lower_part = jnp.where(rows > cols, pairs[: 2 * size] * ratios, 0.0)
        score_part = pairs[2 * size :] * ratios
        products = once(key, key, NT)
        weighed = beta * lower_part
        grad_decayed, grad_erase, grad_tails = [], [], []
        for h in range(2):
            at = slice(h * size, (h + 1) * size)
            state = states[b, at, :]
            both = once(pair_rows(grad[at], -solved[at]), state, NT)
            grad_decayed.append(both[:size])
            grad_erase.append(both[size:])
            grad_tails.append(once(made[at], grad_state[at], NT))
        grad_decayed, grad_erase, grad_tails = (
            pair_rows(*m) for m in (grad_decayed, grad_erase, grad_tails)
        )
        stacked = pair_rows(score_part, weighed)
        with_key = once(stacked, key)
        turned = once(stacked, pair_rows(query, key), TN)
        grad_query = gammas * grad_decayed + with_key[: 2 * size]
        grad_key = (
            turned
            + with_key[2 * size :]
            + (beta * gammas) * grad_erase
            + tail_scale * grad_tails
        )
        grad_value = beta * solved
        erase_key = jnp.sum(grad_erase * key, axis=1, keepdims=True) * gammas
        lower_products = lower_part * products
        grad_beta = (
            jnp.sum(lower_products, axis=1, keepdims=True)
            + jnp.sum(solved * value, axis=1, keepdims=True)
            + erase_key
        )
        both = pairs[2 * size :] * score + beta * lower_products
        tail_sum = jnp.sum(grad_tails * tails, axis=1, keepdims=True)
        to_column = jnp.sum(both, axis=0, keepdims=True)
        grad_column = (
            jnp.sum(both, axis=1, keepdims=True)
            + gammas * jnp.sum(grad_decayed * query, axis=1, keepdims=True)
            + beta * erase_key
            - tail_sum
        )
        grad_rate = jnp.zeros((size, 128), WIDE)
        grad_step = jnp.zeros((size, 128), WIDE)
        for h in range(2):
            at = slice(h * size, (h + 1) * size)
            kept = jnp.sum(states[b, at, :] * grad_state[at]) * jnp.exp(last[h])
            finish = kept + jnp.sum(tail_sum[at], axis=0, keepdims=True)
            turned_row = jnp.broadcast_to(to_column[:, at], (size, size)).T
            cumulated = grad_column[at] - turned_row
            summed = lax.dot_general(
                upper, cumulated, (NN, ((), ())), precision=highest, preferred_element_type=WIDE
            )
            grad_step = jnp.where(lanes == 2 + h, summed + finish, grad_step)
            grad_rate = jnp.where(lanes == h, grad_beta[at], grad_rate)
        rate = rate_in[tokens, :]
        strength = jax.nn.sigmoid(rate)
        slope = jax.nn.sigmoid(rate + rates[1:2, :])
        grad_in = grad_rate * strength * (1.0 - strength) + grad_step * rates[0:1, :] * slope
        decay = rates[0:1, :] * softplus(rate + rates[1:2, :])
        sums[0:1, :] += jnp.sum(grad_in, axis=0, keepdims=True)
        sums[1:2, :] += jnp.sum(grad_step * decay, axis=0, keepdims=True)
        grad_rates[tokens, :] = grad_in.astype(LOW)
        grad_mixed[tokens, conv:] = grad_gate[tokens, :]
        for part, member in enumerate((grad_query, grad_key, grad_value)):
            rounded = member.astype(LOW).astype(WIDE)
            for h in range(2):
                unit_grads[2 * part + h][b] = rounded[h * size : (h + 1) * size]
    for part in range(3):
        for h in range(2):
            at = part * 256 + h * size
            wide = pl.ds(at, size)
            given = jnp.concatenate(unit_grads[2 * part + h], 0)
            summed = conv_of(ext, kernel, at, 13, span)
            open_ = jax.nn.sigmoid(summed)
            if part < 2:
                active, scale = silu_unit(summed)
                if part == 0:
                    given = given * size**-0.5
                inner = jnp.sum(active * given, axis=-1, keepdims=True)
                given = scale * given - (scale * scale * scale) * inner * active
            slope = open_ * (1.0 + summed * (1.0 - open_))
            grad_conv = given * slope
            gext[pl.ds(0, span), wide] = grad_conv
            for j in range(4):
                grad_kernel[j : j + 1, wide] += jnp.sum(
                    grad_conv * ext[pl.ds(13 + j, span), wide], axis=0, keepdims=True
                )
            moved = kernel[0:1, wide] * gext[pl.ds(3, span), wide]
            for j in range(1, 4):
                moved = moved + kernel[j : j + 1, wide] * gext[pl.ds(3 - j, span), wide]
            grad_mixed[:, wide] = moved.astype(LOW)

            @pl.when(turn == 0)
            def _():
                edge[:, wide] = moved[span - 16 :]

    gext[pl.ds(span, 8), :] = gext[pl.ds(0, 8), :]

    @pl.when(turn == pl.num_programs(0) - 1)
    def _():
        front[...] = gext[pl.ds(0, 8), :]


def whole_spec(shape):
    return pl.BlockSpec(shape, lambda i: (0,) * len(shape))


def rows_spec(shape, turn=None):
    zeros = (0,) * (len(shape) - 1)
    if turn is None:
        return pl.BlockSpec(shape, lambda i: (i,) + zeros)
    return pl.BlockSpec(shape, lambda i: (turn - 1 - i,) + zeros)


GROUP = 2


def cost(flops, touched):
    return pl.CostEstimate(flops=int(flops), bytes_accessed=int(touched), transcendentals=0)


def prepare(normed, mixer, all_rates, pick, tail, kernel, rates):
    total, width = normed.shape
    blocks = total // 128
    steps = blocks // GROUP
    span = GROUP * 128
    like = jax.ShapeDtypeStruct
    return pl.pallas_call(
        prepare_kernel,
        grid=(steps,),
        in_specs=[
            rows_spec((span, width)),
            whole_spec(mixer.shape),
            whole_spec(all_rates.shape),
            whole_spec(pick.shape),
            whole_spec(tail.shape),
            whole_spec(kernel.shape),
            whole_spec(rates.shape),
        ],
        out_specs=[
            whole_spec((total + 16, 768)),
            rows_spec((span, 256)),
            rows_spec((span, 128)),
            rows_spec((GROUP, 256, 256)),
            rows_spec((GROUP, 256, 256)),
            rows_spec((GROUP, 256, 256)),
            rows_spec((GROUP, 256, 128)),
            rows_spec((GROUP, 256, 256)),
            rows_spec((GROUP, 256, 256)),
            rows_spec((GROUP, 256, 128)),
            whole_spec((256, 256)),
            whole_spec(all_rates.shape),
        ],
        out_shape=[
            like((total + 16, 768), LOW),
            like((total, 256), LOW),
            like((total, 128), WIDE),
            like((blocks, 256, 256), WIDE),
            like((blocks, 256, 256), LOW),
            like((blocks, 256, 256), LOW),
            like((blocks, 256, 128), WIDE),
            like((blocks, 256, 256), WIDE),
            like((blocks, 256, 256), LOW),
            like((blocks, 256, 128), WIDE),
            like((256, 256), WIDE),
            like(all_rates.shape, LOW),
        ],
        scratch_shapes=[pltpu.VMEM((span + 8, 768), WIDE), pltpu.VMEM((256, 256), WIDE)],
        compiler_params=pltpu.CompilerParams(vmem_limit_bytes=VMEM_MOST),
        cost_estimate=cost(4e10, 2e7),
        name="prepare",
    )(normed, mixer, all_rates, pick, tail, kernel, rates)


def finish(start, before, ue, scores, qk, columns, gates, gain, project):
    blocks = ue.shape[0]
    total, width = blocks * 128, project.shape[1]
    span = GROUP * 128
    like = jax.ShapeDtypeStruct
    return pl.pallas_call(
        output_kernel,
        grid=(blocks // GROUP,),
        in_specs=[
            whole_spec(start.shape),
            rows_spec((GROUP, 256, 256)),
            rows_spec((GROUP, 256, 256)),
            rows_spec((GROUP, 256, 256)),
            rows_spec((GROUP, 256, 256)),
            rows_spec((GROUP, 256, 128)),
            rows_spec((span, 256)),
            whole_spec(gain.shape),
            whole_spec(project.shape),
        ],
        out_specs=[
            rows_spec((span, width)),
            rows_spec((span, 256)),
            rows_spec((GROUP, 256, 128)),
            rows_spec((GROUP, 256, 128)),
            rows_spec((GROUP, 256, 128)),
        ],
        out_shape=[
            like((total, width), LOW),
            like((total, 256), LOW),
            like((blocks, 256, 128), LOW),
            like((blocks, 256, 128), WIDE),
            like((blocks, 256, 128), WIDE),
        ],
        compiler_params=pltpu.CompilerParams(vmem_limit_bytes=VMEM_MOST),
        cost_estimate=cost(1e10, 1e7),
        name="finish",
    )(start, before, ue, scores, qk, columns, gates, gain, project)


def give_back(branch, project, gates, gain, out, scores, ue, qk, columns, steps):
    blocks = ue.shape[0]
    total, width = branch.shape
    turns = blocks // GROUP
    span = GROUP * 128
    like = jax.ShapeDtypeStruct
    block = lambda *shape: rows_spec((GROUP,) + shape, turns)
    return pl.pallas_call(
        return_kernel,
        grid=(turns,),
        in_specs=[
            rows_spec((span, width), turns),
            whole_spec(project.shape),
            rows_spec((span, 256), turns),
            whole_spec(gain.shape),
            block(256, 128),
            block(256, 256),
            block(256, 256),
            block(256, 256),
            block(256, 128),
            block(256, 128),
        ],
        out_specs=[
            block(256, 128),
            block(256, 128),
            block(256, 128),
            rows_spec((span, 256), turns),
            whole_spec((256, 128)),
            whole_spec((8, 128)),
        ],
        out_shape=[
            like((blocks, 256, 128), WIDE),
            like((blocks, 256, 128), WIDE),
            like((blocks, 256, 128), WIDE),
            like((total, 256), LOW),
            like((256, 128), WIDE),
            like((8, 128), WIDE),
        ],
        scratch_shapes=[pltpu.VMEM((256, 128), WIDE)],
        compiler_params=pltpu.CompilerParams(vmem_limit_bytes=VMEM_MOST),
        cost_estimate=cost(1e10, 1e7),
        name="give_back",
    )(branch, project, gates, gain, out, scores, ue, qk, columns, steps)


def gradients(
    end, returns, steps, grad_out, back_scores, fresh, states, inverse, scores, qk, columns,
    mixed, rate_in, grad_gate, kernel, rates, after=()
):
    blocks = fresh.shape[0]
    total = blocks * 128
    turns = blocks // GROUP
    span = GROUP * 128
    like = jax.ShapeDtypeStruct
    block = lambda *shape: rows_spec((GROUP,) + shape, turns)
    return pl.pallas_call(
        behind(gradient_kernel, len(after)),
        grid=(turns,),
        in_specs=[pl.BlockSpec(memory_space=pl.ANY)] * len(after)
        + [
            whole_spec(end.shape),
            block(256, 128),
            block(256, 128),
            block(256, 128),
            block(256, 128),
            block(256, 128),
            block(256, 128),
            block(256, 256),
            block(256, 256),
            block(256, 256),
            block(256, 128),
            whole_spec(mixed.shape),
            rows_spec((span, 128), turns),
            rows_spec((span, 256), turns),
            whole_spec(kernel.shape),
            whole_spec(rates.shape),
        ],
        out_specs=[
            rows_spec((span, 1024), turns),
            rows_spec((span, 128), turns),
            whole_spec((8, 768)),
            whole_spec((8, 128)),
            whole_spec((8, 768)),
            whole_spec((16, 768)),
        ],
        out_shape=[
            like((total, 1024), LOW),
            like((total, 128), LOW),
            like((8, 768), WIDE),
            like((8, 128), WIDE),
            like((8, 768), WIDE),
            like((16, 768), WIDE),
        ],
        scratch_shapes=[
            pltpu.VMEM((span + 16, 768), WIDE),
            pltpu.VMEM((span + 8, 768), WIDE),
            pltpu.VMEM((256, 128), WIDE),
        ],
        compiler_params=pltpu.CompilerParams(vmem_limit_bytes=VMEM_MOST),
        cost_estimate=cost(2e10, 1e7),
        name="gradients",
    )(
        *after, end, returns, steps, grad_out, back_scores, fresh, states, inverse, scores, qk, columns,
        mixed, rate_in, grad_gate, kernel, rates
    )


MESH = pl.DeviceIdType.MESH
DMA = pltpu.SemaphoreType.DMA


def neighbours():
    z, y, x, core = (lax.axis_index(name) for name in ALL)
    over_x, over_y, sibling = (z, y, 1 - x, core), (z, 1 - y, x, core), (z, y, x, 1 - core)
    return z, y, x, core, over_x, over_y, sibling


def rank_of(y, x, core):
    return (y * 2 + x) * 2 + core


def greet(others):
    barrier = pltpu.get_barrier_semaphore()
    for other in others:
        pl.semaphore_signal(barrier, inc=1, device_id=other, device_id_type=MESH)
    pl.semaphore_wait(barrier, len(others))


def remote(source, target, sent, arrived, device):
    return pltpu.make_async_remote_copy(
        source, target, sent, arrived, device_id=device, device_id_type=MESH
    )


class Gather:
    def __init__(
        self, mine, out, own_sem, sent, arrived, across_sent, across_arrived, core_sent, core_arrived
    ):
        z, y, x, core, over_x, over_y, sibling = neighbours()
        half = mine.shape[0] // 2
        me, other = rank_of(y, x, core), 1 - core
        piece = lambda slot, p: out.at[slot, pl.ds(p * half, half)]
        from_axis = [rank_of(y, 1 - x, core), rank_of(1 - y, x, core)]
        theirs = [rank_of(y, 1 - x, other), rank_of(1 - y, x, other)]
        over = [over_x, over_y]
        self.own = pltpu.make_async_copy(mine, out.at[me], own_sem)

        def to_core(slot, p, k):
            place = piece(slot, p)
            return remote(place, place, core_sent.at[k], core_arrived.at[k], sibling)

        self.first = [
            remote(
                mine.at[pl.ds(p * half, half)], piece(me, p), sent.at[axis, p],
                arrived.at[axis, p], over[axis]
            )
            for axis, p in ((0, 0), (1, 1), (0, 1), (1, 0))
        ]
        self.first_core = remote(mine, out.at[me], core_sent.at[6], core_arrived.at[6], sibling)
        self.onward = [
            remote(
                piece(from_axis[axis], axis), piece(from_axis[axis], axis),
                across_sent.at[axis], across_arrived.at[axis], over[1 - axis]
            )
            for axis in range(2)
        ]
        self.shared = [
            to_core(from_axis[axis], p, 2 * axis + p)
            for axis, p in ((0, 0), (1, 1), (0, 1), (1, 0))
        ]
        mine_across = rank_of(1 - y, 1 - x, core)
        self.across = [
            remote(
                piece(mine_across, p), piece(mine_across, p), across_sent.at[p],
                across_arrived.at[p], over_x
            )
            for p in range(2)
        ]
        self.shared_across = [to_core(mine_across, p, 4 + p) for p in range(2)]
        self.last = [to_core(theirs[axis], p, 2 * axis + p) for axis in range(2) for p in range(2)]
        self.last += [to_core(rank_of(1 - y, 1 - x, other), p, 4 + p) for p in range(2)]
        place = out.at[rank_of(y, x, other)]
        self.last.append(remote(place, place, core_sent.at[6], core_arrived.at[6], sibling))

    def start(self):
        self.own.start()
        for copy in self.first:
            copy.start()
        self.first_core.start()

    def forward(self):
        for i in range(4):
            self.first[i].wait_recv()
            if i < 2:
                self.onward[i].start()
            self.shared[i].start()

    def finish(self):
        for p in range(2):
            self.across[p].wait_recv()
            self.shared_across[p].start()
        for copy in self.last:
            copy.wait_recv()
        self.own.wait()
        for copy in self.first + [self.first_core] + self.onward + self.shared + self.shared_across:
            copy.wait_send()


def gather_kernel(mine, out, *semaphores):
    greet(neighbours()[4:])
    gather = Gather(mine, out, *semaphores)
    gather.start()
    gather.forward()
    gather.finish()


GATHER_SEMAPHORES = [DMA, DMA((2, 2)), DMA((2, 2)), DMA((2,)), DMA((2,)), DMA((7,)), DMA((7,))]


def plane_gather(rows_here, place):
    rows, width = rows_here.shape
    out = pl.pallas_call(
        gather_kernel,
        out_shape=jax.ShapeDtypeStruct((8, rows, width), rows_here.dtype),
        in_specs=[pl.BlockSpec(memory_space=pltpu.VMEM)],
        out_specs=pl.BlockSpec(memory_space=pltpu.VMEM),
        scratch_shapes=GATHER_SEMAPHORES,
        compiler_params=pltpu.CompilerParams(
            collective_id=place, has_side_effects=True, vmem_limit_bytes=VMEM_MOST
        ),
        cost_estimate=pl.CostEstimate(flops=0, bytes_accessed=70_000_000, transcendentals=0),
        name="plane_gather",
    )(rows_here)
    return out.reshape(8 * rows, width)

def turned(place, flip):
    return place + flip - 2 * place * flip


def units_of(hidden, core, half):
    tiles = hidden // 4 // 128
    most = -(-tiles // 2)
    first = -(-most // 2)
    begin = core * most + half * first
    end = min(begin + first, tiles if core else most)
    return begin * 128, (end - begin) * 128, first * 128


def front_kernel(
    w_mixer, w_gate_up, w_down, w_project, normed, cotangent, zeros, w_rates, mixer, later_a,
    later_b, project, normed_all, cotangent_all, tail, rates, project_own, project_sent,
    project_arrived, rates_own, rates_z_sent, rates_z, rates_sent,
    rates_arrived, mixer_own, mixer_sent, mixer_arrived, up_sent, down_sent, z_arrived,
    later_own, later_sent, later_arrived, zero_sem, tail_sent, tail_arrived, *gather_semaphores
):
    z, y, x, core, over_x, over_y, sibling = neighbours()
    layers = lax.axis_size("z")
    rows, width = w_mixer.shape[0], w_mixer.shape[1] // 4
    wide = width // 8
    hidden = w_down.shape[1]
    per_chip = hidden // 4
    laters = (later_a, later_b)
    block = 8 * rows
    me = rank_of(y, x, core)
    low_z, high_z = jnp.maximum(z - 1, 0), jnp.minimum(z + 1, layers - 1)
    below, above = (low_z, y, x, core), (high_z, y, x, core)
    last = (me == 7) & (z < layers - 1)
    flips = [(k >> 2, (k >> 1) & 1, k & 1) for k in range(8)]
    ranks = [rank_of(turned(y, a), turned(x, b), turned(core, c)) for a, b, c in flips]
    devices = [(z, turned(y, a), turned(x, b), turned(core, c)) for a, b, c in flips]

    barrier = pltpu.get_barrier_semaphore()
    for k in range(1, 8):
        pl.semaphore_signal(barrier, inc=1, device_id=devices[k], device_id_type=MESH)

    @pl.when(z > 0)
    def _():
        pl.semaphore_signal(barrier, inc=1, device_id=below, device_id_type=MESH)
        pl.semaphore_signal(barrier, inc=1, device_id=(low_z, 1, 1, 1), device_id_type=MESH)

    @pl.when(z < layers - 1)
    def _():
        pl.semaphore_signal(barrier, inc=1, device_id=above, device_id_type=MESH)

    others_z = [(lax.rem(z + k, layers), y, x, core) for k in range(1, layers)]
    for other in others_z:
        pl.semaphore_signal(barrier, inc=1, device_id=other, device_id_type=MESH)
    keeps = (y == z // 2) & (x == lax.rem(z, 2)) & (core == y)
    own_j = 2 * x + core
    for j in range(4):

        @pl.when(jnp.logical_not(keeps & (own_j == j)))
        def _():
            pl.semaphore_signal(
                barrier, inc=1, device_id=(2 * y + x, core, j // 2, j % 2), device_id_type=MESH
            )

    pl.semaphore_wait(
        barrier,
        10 + layers - jnp.where(keeps, 1, 0) + jnp.where(z > 0, 1, 0) + jnp.where(z < layers - 1, 1, 0) + jnp.where(last, 8, 0),
    )

    def columns(p, rank):
        return w_mixer.at[:, pl.ds(pl.multiple_of(p * width + rank * wide, 128), wide)]

    def mixer_rows(layer, rank):
        return mixer.at[pl.ds(pl.multiple_of(layer * block + rank * rows, rows), rows)]

    mine = mixer_rows(z, me)
    owns = [
        pltpu.make_async_copy(columns(p, me), mine.at[:, pl.ds(p * wide, wide)], mixer_own.at[p])
        for p in range(4)
    ]
    for copy in owns:
        copy.start()
    for k in (2, 4, 6, 1, 3, 5, 7):
        for p in range(4):
            remote(
                columns(p, ranks[k]), mine.at[:, pl.ds(p * wide, wide)], mixer_sent.at[k],
                mixer_arrived.at[k], devices[k]
            ).start()

    def along(layer, rank, upward):
        place = mixer_rows(layer, rank)
        return remote(
            place, place, (up_sent if upward else down_sent).at[layer, rank],
            z_arrived.at[layer, rank], above if upward else below
        )

    def spread(rank):
        @pl.when(z < layers - 1)
        def _():
            along(z, rank, True).start()

        @pl.when(z > 0)
        def _():
            along(z, rank, False).start()

    count = len(gather_semaphores) // 2
    gather_normed = Gather(normed, normed_all, *gather_semaphores[:count])
    gather_cotangent = Gather(cotangent, cotangent_all, *gather_semaphores[count:])
    for copy in owns:
        copy.wait()
    spread(me)
    gather_normed.start()
    rate_copies = [
        remote(w_rates, rates.at[me, z], rates_z_sent.at[k], rates_z.at[k], other)
        for k, other in enumerate(others_z)
    ]
    for copy in rate_copies:
        copy.start()
    rate_own = pltpu.make_async_copy(w_rates, rates.at[me, z], rates_own)
    rate_own.start()

    def tails(a, b, c):
        k = (a * 2 + b) * 2 + c
        return remote(
            normed.at[pl.ds(normed.shape[0] - 16, 16)], tail, tail_sent.at[k], tail_arrived,
            (high_z, a, b, c)
        )

    @pl.when(last)
    def _():
        for a, b, c in flips:
            tails(a, b, c).start()

    for k in (1, 2, 4, 3, 5, 6, 7):
        place = mixer_rows(z, ranks[k])
        remote(place, place, mixer_sent.at[k], mixer_arrived.at[k], devices[k]).wait_recv()
        spread(ranks[k])

    def pass_on(far):
        @pl.loop(0, 8)
        def _(rank):
            @pl.when(z - far >= 0)
            def _():
                copy = along(jnp.maximum(z - far, 0), rank, True)
                copy.wait_recv()

                @pl.when(z < layers - 1)
                def _():
                    copy.start()

            @pl.when(z + far <= layers - 1)
            def _():
                copy = along(jnp.minimum(z + far, layers - 1), rank, False)
                copy.wait_recv()

                @pl.when(z > 0)
                def _():
                    copy.start()

    here = pl.ds(pl.multiple_of(me * rows, rows), rows)

    def shares(chip, t):
        found = []
        for half, later in enumerate(laters):
            begin, size, slot = units_of(hidden, t, half)
            first = pl.multiple_of(chip * per_chip + begin, 128)
            up = pl.multiple_of(hidden + first, 128)
            found += [
                (w_gate_up.at[:, pl.ds(first, size)], later.at[here, pl.ds(0, size)]),
                (w_gate_up.at[:, pl.ds(up, size)], later.at[here, pl.ds(slot, size)]),
                (w_down.at[:, pl.ds(first, size)], later.at[here, pl.ds(2 * slot, size)]),
            ]
        return found

    def later_wait(t, semaphore, arrival):
        for half, later in enumerate(laters):
            place = later.at[pl.ds(0, rows), pl.ds(0, 3 * units_of(hidden, t, half)[1])]
            copy = remote(place, place, semaphore.at[half], semaphore.at[half], sibling)
            if arrival:
                copy.wait_recv()
            else:
                copy.wait_send()

    def send_later(f, t):
        a, b = f >> 1, f & 1
        for i, (source, target) in enumerate(shares(turned(y, a) * 2 + turned(x, b), t)):
            remote(
                source, target, later_sent.at[f, t, i // 3], later_arrived.at[f, core, i // 3],
                (z, turned(y, a), turned(x, b), t)
            ).start()

    for f in (1, 2, 3):
        for t in range(2):
            send_later(f, t)
    for t in range(2):

        @pl.when(core == t)
        def _():
            for i, (source, target) in enumerate(shares(y * 2 + x, t)):
                pltpu.make_async_copy(source, target, later_own.at[i]).start()

        @pl.when(core != t)
        def _():
            send_later(0, t)

    _, least, slot = units_of(hidden, 1, 1)
    pads = [
        pltpu.make_async_copy(
            zeros, later_b.at[:, pl.ds(i * slot + least, slot - least)], zero_sem.at[i]
        )
        for i in range(3)
    ]

    @pl.when(core == 1)
    def _():
        for copy in pads:
            copy.start()

    pass_on(1)
    rows_of = lambda j: project.at[pl.ds(pl.multiple_of(j * rows, rows), rows)]
    project_copies = [
        remote(
            w_project, rows_of(own_j), project_sent.at[k], project_arrived.at[own_j],
            (lax.rem(z + k, layers), z // 2, lax.rem(z, 2), y)
        )
        for k in range(4)
    ]
    project_kept = pltpu.make_async_copy(w_project, rows_of(own_j), project_own)

    @pl.when(keeps)
    def _():
        project_kept.start()

    @pl.when(jnp.logical_not(keeps))
    def _():
        project_copies[0].start()

    for copy in project_copies[1:]:
        copy.start()
    gather_normed.forward()
    gather_cotangent.start()
    pass_on(2)
    rate_own.wait()
    for copy in rate_copies:
        copy.wait_recv()
    for k in range(1, 8):
        place = rates.at[me]
        copy = remote(place, place, rates_sent.at[k], rates_arrived.at[k], devices[k])
        copy.start()
        rate_copies.append(copy)
    gather_normed.finish()
    gather_cotangent.forward()
    pass_on(3)
    gather_cotangent.finish()
    for j in range(4):

        @pl.when(jnp.logical_not(keeps & (own_j == j)))
        def _():
            remote(
                rows_of(j), rows_of(j), project_sent.at[0], project_arrived.at[j], sibling
            ).wait_recv()

    @pl.when(keeps)
    def _():
        project_kept.wait()

    @pl.when(jnp.logical_not(keeps))
    def _():
        project_copies[0].wait_send()

    for copy in project_copies[1:]:
        copy.wait_send()

    for t in range(2):

        @pl.when(core == t)
        def _():
            for f in range(4):
                for s in range(2):
                    if f or s != t:
                        later_wait(t, later_arrived.at[f, s], True)
            for i, (source, target) in enumerate(shares(y * 2 + x, t)):
                pltpu.make_async_copy(source, target, later_own.at[i]).wait()

    @pl.when(core == 1)
    def _():
        for copy in pads:
            copy.wait()

    for t in range(2):
        for f in range(1, 4):
            later_wait(t, later_sent.at[f, t], False)

        @pl.when(core != t)
        def _():
            later_wait(t, later_sent.at[0, t], False)

    for k in range(1, 8):
        remote(mine, mine, mixer_sent.at[k], mixer_arrived.at[k], devices[k]).wait_send()
        place = rates.at[ranks[k]]
        remote(place, place, rates_sent.at[k], rates_arrived.at[k], devices[k]).wait_recv()
    for copy in rate_copies:
        copy.wait_send()

    @pl.when(z == 0)
    def _():
        tail[...] = jnp.zeros_like(tail)

    @pl.when(z > 0)
    def _():
        tails(0, 0, 0).wait_recv()

    @pl.when(last)
    def _():
        for a, b, c in flips:
            tails(a, b, c).wait_send()

    for layer in range(4):

        @pl.loop(0, 8)
        def _(rank):
            @pl.when((z < layers - 1) & (layer <= z))
            def _():
                along(layer, rank, True).wait_send()

            @pl.when((z > 0) & (layer >= z))
            def _():
                along(layer, rank, False).wait_send()


def front(w_mixer, w_gate_up, w_down, w_project, w_rates, normed, cotangent, place):
    rows, columns = w_mixer.shape
    layers = lax.axis_size("z")
    hidden = w_down.shape[1]
    _, least, slot = units_of(hidden, 1, 1)
    length, width = normed.shape
    like = jax.ShapeDtypeStruct
    any_, vmem = pl.BlockSpec(memory_space=pl.ANY), pl.BlockSpec(memory_space=pltpu.VMEM)
    return pl.pallas_call(
        front_kernel,
        out_shape=[
            like((8 * layers * rows, columns // 8), LOW),
            like((8 * rows, 3 * slot), LOW),
            like((8 * rows, 3 * slot), LOW),
            like((4 * rows, w_project.shape[1]), LOW),
            like((8, length, width), LOW),
            like((8, length, width), LOW),
            like((16, width), LOW),
            like((8, layers, rows, 128), LOW),
        ],
        in_specs=[any_, any_, any_, any_, vmem, vmem, vmem, vmem],
        out_specs=[any_, any_, any_, any_, vmem, vmem, vmem, vmem],
        scratch_shapes=[
            DMA, DMA((4,)), DMA((4,)), DMA, DMA((layers - 1,)), DMA((layers - 1,)), DMA((8,)), DMA((8,)),
            DMA((4,)), DMA((8,)), DMA((8,)), DMA((4, 8)), DMA((4, 8)), DMA((4, 8)),
            DMA((6,)), DMA((4, 2, 2)), DMA((4, 2, 2)), DMA((3,)), DMA((8,)), DMA,
        ]
        + GATHER_SEMAPHORES * 2,
        compiler_params=pltpu.CompilerParams(
            collective_id=place, has_side_effects=True, vmem_limit_bytes=VMEM_MOST
        ),
        cost_estimate=pl.CostEstimate(flops=0, bytes_accessed=250_000_000, transcendentals=0),
        name="front",
    )(
        w_mixer, w_gate_up, w_down, w_project, normed, cotangent, jnp.zeros((8 * rows, slot - least), LOW),
        jnp.pad(w_rates, ((0, 0), (0, 128 - w_rates.shape[1]))),
    )


def scatter_steps(
    terms, out, held, from_core, over_a, over_b, side_x, side_y, core_sent, core_arrived,
    across_sent, across_arrived, sent, arrived
):
    z, y, x, core, over_x, over_y, sibling = neighbours()
    rows = terms.shape[1]
    half, step = rows // 2, 16
    chunks = lambda c: [
        rank_of(1 - y, 1 - x, c), rank_of(y, 1 - x, c), rank_of(1 - y, x, c), rank_of(y, x, c)
    ]
    mine, theirs = chunks(core), chunks(1 - core)
    to_core = [
        remote(terms.at[theirs[i]], from_core.at[i], core_sent.at[i], core_arrived.at[i], sibling)
        for i in range(4)
    ]
    for copy in to_core:
        copy.start()
    yield

    def add(target, at, count, more=None):
        @pl.loop(0, count, step=step)
        def _(r):
            here = pl.ds(pl.multiple_of(at + r, step), step)
            total = terms[mine[target], here, :].astype(WIDE) + from_core[target, here, :].astype(WIDE)
            if more is not None:
                total = total + more[pl.ds(pl.multiple_of(r, step), step), :].astype(WIDE)
            held[target, here, :] = total.astype(LOW)

    top, bottom = pl.ds(0, half), pl.ds(half, half)
    to_core[0].wait_recv()
    add(0, 0, rows)
    top_y = remote(held.at[0, top], over_a, across_sent.at[0], across_arrived.at[0], over_y)
    bottom_x = remote(held.at[0, bottom], over_b, across_sent.at[1], across_arrived.at[1], over_x)
    top_y.start()
    bottom_x.start()
    yield
    to_core[1].wait_recv()
    add(1, half, half)
    x_bottom = remote(held.at[1, bottom], side_x.at[bottom], sent.at[0, 1], arrived.at[0, 1], over_x)
    x_bottom.start()
    to_core[2].wait_recv()
    add(2, 0, half)
    y_top = remote(held.at[2, top], side_y.at[top], sent.at[1, 0], arrived.at[1, 0], over_y)
    y_top.start()
    yield
    top_y.wait_recv()
    add(1, 0, half, over_a)
    x_top = remote(held.at[1, top], side_x.at[top], sent.at[0, 0], arrived.at[0, 0], over_x)
    x_top.start()
    bottom_x.wait_recv()
    add(2, half, half, over_b)
    y_bottom = remote(held.at[2, bottom], side_y.at[bottom], sent.at[1, 1], arrived.at[1, 1], over_y)
    y_bottom.start()
    yield
    to_core[3].wait_recv()
    for copy in (x_bottom, y_top, x_top, y_bottom):
        copy.wait_recv()

    @pl.loop(0, rows, step=step)
    def _(r):
        here = pl.ds(pl.multiple_of(r, step), step)
        out[here, :] = (
            terms[mine[3], here, :].astype(WIDE)
            + from_core[3, here, :].astype(WIDE)
            + (side_x[here, :].astype(WIDE) + side_y[here, :].astype(WIDE))
        )

    for copy in to_core + [top_y, bottom_x, x_bottom, y_top, x_top, y_bottom]:
        copy.wait_send()


def scatter_kernel(*refs):
    greet(neighbours()[4:])
    for _ in scatter_steps(*refs):
        pass


def scatter_scratch(rows, width):
    block = lambda *shape: pltpu.VMEM(shape, LOW)
    return [
        block(3, rows, width),
        block(4, rows, width),
        block(rows // 2, width),
        block(rows // 2, width),
        block(rows, width),
        block(rows, width),
        DMA((4,)),
        DMA((4,)),
        DMA((2,)),
        DMA((2,)),
        DMA((2, 2)),
        DMA((2, 2)),
    ]


def behind(kernel, count):
    return lambda *refs: kernel(*refs[count:])


def plane_scatter(terms, place, after=()):
    rows, width = terms.shape[0] // 8, terms.shape[1]
    return pl.pallas_call(
        behind(scatter_kernel, len(after)),
        out_shape=jax.ShapeDtypeStruct((rows, width), WIDE),
        in_specs=[pl.BlockSpec(memory_space=pl.ANY)] * len(after)
        + [pl.BlockSpec(memory_space=pltpu.VMEM)],
        out_specs=pl.BlockSpec(memory_space=pltpu.VMEM),
        scratch_shapes=scatter_scratch(rows, width),
        compiler_params=pltpu.CompilerParams(
            collective_id=place, has_side_effects=True, vmem_limit_bytes=VMEM_MOST
        ),
        cost_estimate=pl.CostEstimate(flops=0, bytes_accessed=80_000_000, transcendentals=0),
        name="plane_scatter",
    )(*after, terms.reshape(8, rows, width))


def later_terms_kernel(normed, cotangent, swiglu, inner, out):
    both = swiglu.shape[1]
    out[:, :both] = once(normed[...], swiglu[...], TN).astype(LOW)
    out[:, both:] = once(cotangent[...], inner[...], TN).astype(LOW)


def later_terms(normed, cotangent, swiglu, inner):
    tokens, rows = normed.shape
    columns = swiglu.shape[1] + inner.shape[1]
    step = 256
    return pl.pallas_call(
        later_terms_kernel,
        grid=(rows // step,),
        in_specs=[pl.BlockSpec((tokens, step), lambda i: (0, i))] * 2
        + [whole_spec(swiglu.shape), whole_spec(inner.shape)],
        out_specs=rows_spec((step, columns)),
        out_shape=jax.ShapeDtypeStruct((rows, columns), LOW),
        compiler_params=pltpu.CompilerParams(vmem_limit_bytes=VMEM_MOST),
        cost_estimate=cost(2 * tokens * rows * columns, 2e7),
        name="later_terms",
    )(normed, cotangent, swiglu, inner)


def mixer_terms_kernel(gated, branch, normed, mixed, out, project):
    step = pl.program_id(0)
    layers, columns = pl.num_programs(0), mixed.shape[1]
    rows = normed.shape[1]
    few = project.shape[0] // layers

    @pl.when(step == 0)
    def _():
        project[...] = once(gated[...], branch[...], TN).astype(LOW)

    out[0, :rows, :] = once(normed[...], mixed[...], TN).astype(LOW)
    here = pl.ds(pl.multiple_of(step * few, few), few)
    for half in range(2):
        out[0, rows + half * few : rows + (half + 1) * few, :] = project[
            here, half * columns : (half + 1) * columns
        ]


def mixer_terms(gated, branch, normed, mixed, after=()):
    tokens, rows = normed.shape
    columns = mixed.shape[1]
    layers = lax.axis_size("z")
    few = gated.shape[1] // layers
    share = rows // layers + 2 * few
    return pl.pallas_call(
        behind(mixer_terms_kernel, len(after)),
        grid=(layers,),
        in_specs=[pl.BlockSpec(memory_space=pl.ANY)] * len(after)
        + [
            whole_spec(gated.shape),
            whole_spec(branch.shape),
            pl.BlockSpec((tokens, rows // layers), lambda i: (0, i)),
            whole_spec(mixed.shape),
        ],
        out_specs=pl.BlockSpec((1, share, columns), lambda i: (i, 0, 0)),
        out_shape=jax.ShapeDtypeStruct((layers, share, columns), LOW),
        scratch_shapes=[pltpu.VMEM((gated.shape[1], branch.shape[1]), LOW)],
        compiler_params=pltpu.CompilerParams(vmem_limit_bytes=VMEM_MOST),
        cost_estimate=cost(2 * tokens * rows * columns, 2e7),
        name="mixer_terms",
    )(*after, gated, branch, normed, mixed)


def chain_kernel(reverse, whole, term, out, arriving, leaving, sent, arrived):
    z, y, x, core = (lax.axis_index(name) for name in ALL)
    layers = lax.axis_size("z")
    at = layers - 1 - z if reverse else z
    nearer = jnp.clip(z + (1 if reverse else -1), 0, layers - 1)
    further = jnp.clip(z + (-1 if reverse else 1), 0, layers - 1)
    barrier = pltpu.get_barrier_semaphore()

    @pl.when(at > 0)
    def _():
        pl.semaphore_signal(barrier, inc=1, device_id=(nearer, y, x, core), device_id_type=MESH)

    copy = remote(leaving, arriving, sent, arrived, (further, y, x, core))
    size = out.shape[1]
    factor = whole.at[:, :size]
    if not reverse:
        term = whole.at[:, size:]

    @pl.when(at == 0)
    def _():
        out[...] = jnp.zeros_like(out)
        leaving[...] = term[...].astype(LOW)

    @pl.when(at > 0)
    def _():
        copy.wait_recv()
        out[...] = arriving[...].astype(WIDE)

    @pl.when((at > 0) & (at < layers - 1))
    def _():
        for h in range(2):
            rows = slice(h * 128, (h + 1) * 128)
            moved = thrice(factor[rows, :], out[rows, :], TN if reverse else NN)
            leaving[rows, :] = (moved + term[rows, :]).astype(LOW)

    @pl.when(at < layers - 1)
    def _():
        pl.semaphore_wait(barrier, 1)
        copy.start()
        copy.wait_send()


def chain(whole, term, reverse, place):
    shape = (whole.shape[0], whole.shape[1] // 2)
    return pl.pallas_call(
        partial(chain_kernel, reverse),
        out_shape=jax.ShapeDtypeStruct(shape, WIDE),
        in_specs=[pl.BlockSpec(memory_space=pltpu.VMEM)] * 2,
        out_specs=pl.BlockSpec(memory_space=pltpu.VMEM),
        scratch_shapes=[pltpu.VMEM(shape, LOW), pltpu.VMEM(shape, LOW), DMA, DMA],
        compiler_params=pltpu.CompilerParams(
            collective_id=place, has_side_effects=True, vmem_limit_bytes=VMEM_MOST
        ),
        cost_estimate=pl.CostEstimate(flops=0, bytes_accessed=40_000_000, transcendentals=0),
        name="chain",
    )(whole, term)


def later_back_steps(sums_a, sums_b, gate_up, down, own_sem, sent, arrived):
    z, y, x, core, over_x, over_y, sibling = neighbours()
    rows, hidden = down.shape
    per_chip = hidden // 4
    me = rank_of(y, x, core)
    flips = [(k >> 2, (k >> 1) & 1, k & 1) for k in range(8)]
    devices = [(z, turned(y, a), turned(x, b), turned(core, c)) for a, b, c in flips]
    ranks = [rank_of(*device[1:]) for device in devices]

    def parts(rank, t):
        chip = y * 2 + x
        here = pl.ds(pl.multiple_of(rank * rows, rows), rows)
        found = []
        for half, sums in enumerate((sums_a, sums_b)):
            begin, size, slot = units_of(hidden, t, half)
            first = pl.multiple_of(chip * per_chip + begin, 128)
            up = pl.multiple_of(hidden + first, 128)
            found += [
                (sums.at[here, pl.ds(0, size)], gate_up.at[:, pl.ds(first, size)]),
                (sums.at[here, pl.ds(slot, size)], gate_up.at[:, pl.ds(up, size)]),
                (sums.at[here, pl.ds(2 * slot, size)], down.at[:, pl.ds(first, size)]),
            ]
        return found

    def amount(t):
        return [
            down.at[:, pl.ds(0, 3 * units_of(hidden, t, half)[1])] for half in range(2)
        ]

    for t in range(2):

        @pl.when(core == t)
        def _():
            for k in (2, 4, 6, 3, 5, 7, 1):
                for i, (source, target) in enumerate(parts(ranks[k], t)):
                    remote(
                        source, target, sent.at[k, i // 3], arrived.at[k, i // 3], devices[k]
                    ).start()
            for i, (source, target) in enumerate(parts(me, t)):
                pltpu.make_async_copy(source, target, own_sem.at[i]).start()

    yield
    for t in range(2):

        @pl.when(core == t)
        def _():
            for i, (source, target) in enumerate(parts(me, t)):
                pltpu.make_async_copy(source, target, own_sem.at[i]).wait()

    for k in range(1, 8):
        for t in range(2):
            @pl.when(turned(core, k & 1) == t)
            def _():
                for half, place in enumerate(amount(t)):
                    remote(
                        place, place, sent.at[k, half], arrived.at[k, half], devices[k]
                    ).wait_recv()

            @pl.when(core == t)
            def _():
                for half, place in enumerate(amount(t)):
                    remote(
                        place, place, sent.at[k, half], arrived.at[k, half], devices[k]
                    ).wait_send()


def return_all_kernel(terms_a, terms_b, sums_a, sums_b, out_a, out_b, gate_up, down, *rest):
    z, y, x, core, over_x, over_y, sibling = neighbours()
    flips = [(k >> 2, (k >> 1) & 1, k & 1) for k in range(1, 8)]
    greet([(z, turned(y, a), turned(x, b), turned(core, c)) for a, b, c in flips])
    count = (len(rest) - 3) // 2
    running = [
        scatter_steps(terms_a, out_a, *rest[:count]),
        scatter_steps(terms_b, out_b, *rest[count : 2 * count]),
        later_back_steps(sums_a, sums_b, gate_up, down, *rest[2 * count :]),
    ]
    while running:
        for steps in list(running):
            if next(steps, running) is running:
                running.remove(steps)


def return_all(terms_a, terms_b, sums_a, sums_b, hidden, place, after=()):
    rows, width = terms_a.shape[0] // 8, terms_a.shape[1]
    owned = sums_a.shape[0] // 8
    any_, vmem = pl.BlockSpec(memory_space=pl.ANY), pl.BlockSpec(memory_space=pltpu.VMEM)
    like = jax.ShapeDtypeStruct
    return pl.pallas_call(
        behind(return_all_kernel, len(after)),
        out_shape=[
            like((rows, width), WIDE),
            like((rows, width), WIDE),
            like((owned, 2 * hidden), LOW),
            like((owned, hidden), LOW),
        ],
        in_specs=[any_] * len(after) + [vmem, vmem, any_, any_],
        out_specs=[vmem, vmem, any_, any_],
        scratch_shapes=scatter_scratch(rows, width) * 2 + [DMA((6,)), DMA((8, 2)), DMA((8, 2))],
        compiler_params=pltpu.CompilerParams(
            collective_id=place, has_side_effects=True, vmem_limit_bytes=VMEM_MOST
        ),
        cost_estimate=pl.CostEstimate(flops=0, bytes_accessed=200_000_000, transcendentals=0),
        name="return_all",
    )(
        *after, terms_a.reshape(8, rows, width), terms_b.reshape(8, rows, width), sums_a, sums_b
    )


def last_kernel(
    sums, grad_kernel, decays, head_gain, gain_mlp, gain_mixer, rate_terms,
    mixer, project, all_kernel, all_decays, all_head, all_mlp, all_mixer, all_rates,
    small, layers_in, gathered, z_sent, z_arrived, small_sent, small_arrived,
    own_sem, project_own, sent, arrived, far_sent, far_arrived
):
    z, y, x, core, over_x, over_y, sibling = neighbours()
    layers = layers_in.shape[0]
    rows, columns = mixer.shape
    wide, width = columns // 32, columns // 4
    me = rank_of(y, x, core)
    flips = [(k >> 2, (k >> 1) & 1, k & 1) for k in range(8)]
    devices = [(z, turned(y, a), turned(x, b), turned(core, c)) for a, b, c in flips]
    ranks = [rank_of(*device[1:]) for device in devices]
    others_z = [(lax.rem(z + k, layers), y, x, core) for k in range(1, layers)]
    owner = (me // 2, lax.rem(me, 2), z // 2, lax.rem(z, 2))
    holder_rank = 2 * z + y
    holder = (2 * x + core, holder_rank // 4, lax.rem(holder_rank // 2, 2), lax.rem(holder_rank, 2))
    local = (owner[0] == z) & (owner[1] == y) & (owner[2] == x) & (owner[3] == core)
    barrier = pltpu.get_barrier_semaphore()
    for other in devices[1:] + others_z:
        pl.semaphore_signal(barrier, inc=1, device_id=other, device_id_type=MESH)

    @pl.when(jnp.logical_not(local))
    def _():
        pl.semaphore_signal(barrier, inc=1, device_id=holder, device_id_type=MESH)

    high = 6 * 128
    small[...] = jnp.zeros_like(small)
    small[0:4, :high] = grad_kernel[0:4, :]
    small[0:1, high : high + 128] = decays[0:1, :]
    small[0:1, high + 128 :] = decays[1:2, :]
    small[1:2, high : high + 128] = head_gain[0:1, :]
    small[4:6, :] = gain_mlp[...]
    small[6:8, :] = gain_mixer[...]
    half = small.shape[1]
    small[8:12, :] = rate_terms[0:4, :half]
    small[12:16, :] = rate_terms[0:4, half:]
    pl.semaphore_wait(barrier, 7 + len(others_z) + jnp.where(local, 0, 1))
    to_layers = [
        remote(small, layers_in.at[z], z_sent.at[k], z_arrived.at[k], other)
        for k, other in enumerate(others_z)
    ]
    for copy in to_layers:
        copy.start()
    layers_in[z] = small[...]

    halves_ = [
        (
            sums.at[pl.ds(8 * rows + part * rows, rows)],
            project.at[:, pl.ds(part * 4 * wide, 4 * wide)],
        )
        for part in range(2)
    ]

    @pl.when(jnp.logical_not(local))
    def _():
        for source, target in halves_:
            remote(source, target, far_sent, far_arrived, owner).start()

    @pl.when(local)
    def _():
        for i, (source, target) in enumerate(halves_):
            pltpu.make_async_copy(source, target, project_own.at[i]).start()

    def parts(rank):
        here = pl.ds(pl.multiple_of(rank * rows, rows), rows)
        return [
            (
                sums.at[here, pl.ds(p * wide, wide)],
                mixer.at[:, pl.ds(pl.multiple_of(p * width + me * wide, 128), wide)],
            )
            for p in range(4)
        ]

    for k in (2, 4, 6, 3, 5, 7, 1):
        for source, target in parts(ranks[k]):
            remote(source, target, sent.at[k], arrived.at[k], devices[k]).start()
    owns = [
        pltpu.make_async_copy(source, target, own_sem.at[i])
        for i, (source, target) in enumerate(parts(me))
    ]
    for copy in owns:
        copy.start()
    for copy in to_layers:
        copy.wait_recv()
    total = layers_in[0]
    for k in range(1, layers):
        total = total + layers_in[k]
    gathered[me] = total
    spread = [
        remote(gathered.at[me], gathered.at[me], small_sent.at[k], small_arrived.at[k], devices[k])
        for k in range(1, 8)
    ]
    for copy in spread:
        copy.start()
    for k in range(1, 8):
        place = gathered.at[ranks[k]]
        remote(place, place, small_sent.at[k], small_arrived.at[k], devices[k]).wait_recv()
    whole = gathered[0]
    for r in range(8):
        for part in range(3):
            all_kernel[0:4, part * 8 * wide + r * wide : part * 8 * wide + (r + 1) * wide] = (
                gathered[r, 0:4, part * wide : (part + 1) * wide]
            )
        all_decays[r : r + 1, :] = gathered[r, 0:1, high:]
        all_rates[r] = gathered[r, 8:16, :]
        if r:
            whole = whole + gathered[r]
    all_head[...] = whole[1:2, high : high + 128]
    all_mlp[...] = whole[4:6, :]
    all_mixer[...] = whole[6:8, :]
    for copy in owns:
        copy.wait()
    place = mixer.at[:, pl.ds(0, 4 * wide)]
    for k in range(1, 8):
        remote(place, place, sent.at[k], arrived.at[k], devices[k]).wait()

    @pl.when(jnp.logical_not(local))
    def _():
        remote(project, project, far_sent, far_arrived, owner).wait()

    @pl.when(local)
    def _():
        for i, (source, target) in enumerate(halves_):
            pltpu.make_async_copy(source, target, project_own.at[i]).wait()

    for copy in to_layers + spread:
        copy.wait_send()


def last(sums, rows, smalls, place, after=()):
    columns = sums.shape[1]
    layers = lax.axis_size("z")
    any_, vmem = pl.BlockSpec(memory_space=pl.ANY), pl.BlockSpec(memory_space=pltpu.VMEM)
    like = jax.ShapeDtypeStruct
    small = (16, 1024)
    return pl.pallas_call(
        behind(last_kernel, len(after)),
        out_shape=[
            like((rows, 8 * columns), LOW),
            like((rows, 2 * columns), LOW),
            like((4, 6 * columns), WIDE),
            like((8, 256), WIDE),
            like((1, 128), WIDE),
            like((2, 1024), WIDE),
            like((2, 1024), WIDE),
            like((8, 8, 1024), WIDE),
        ],
        in_specs=[any_] * (len(after) + 1) + [vmem] * 6,
        out_specs=[any_, any_] + [vmem] * 6,
        scratch_shapes=[
            pltpu.VMEM(small, WIDE),
            pltpu.VMEM((layers,) + small, WIDE),
            pltpu.VMEM((8,) + small, WIDE),
            DMA((layers - 1,)),
            DMA((layers - 1,)),
            DMA((8,)),
            DMA((8,)),
            DMA((4,)),
            DMA((2,)),
            DMA((8,)),
            DMA((8,)),
            DMA,
            DMA,
        ],
        compiler_params=pltpu.CompilerParams(
            collective_id=place, has_side_effects=True, vmem_limit_bytes=VMEM_MOST
        ),
        cost_estimate=pl.CostEstimate(flops=0, bytes_accessed=80_000_000, transcendentals=0),
        name="last",
    )(*after, sums, *smalls)


def heads_on_plane(
    tokens,
    w_mixer,
    w_rates,
    w_project,
    w_gate_up,
    w_down,
    conv_kernel,
    decay_log,
    decay_bias,
    head_gain,
    gain_mixer,
    gain_mlp,
    cotangent,
):
    length, width = tokens.shape
    size = head_gain.shape[0]
    rows = w_mixer.shape[0]
    hidden = w_down.shape[1]
    layers = lax.axis_size("z")
    ranks = lax.axis_size(ALL) // layers
    own = decay_log.shape[0] // ranks
    layer, rank = lax.axis_index("z"), lax.axis_index(PLANE)
    low = jnp.bfloat16
    wide = own * size

    def over_layers(terms):
        return lax.psum_scatter(terms, "z", scatter_dimension=0, tiled=True)

    gather = plane_gather

    def scatter(terms, place, after=()):
        return plane_scatter(terms.astype(low), place, after)

    source = tokens.astype(jnp.float32)
    normed, norm_pull = jax.vjp(norm_scale, source, gain_mixer)
    mixer, later_a, later_b, project, normed_all, cotangent_all, tail, all_rates = front(
        w_mixer, w_gate_up, w_down, w_project, w_rates, normed.astype(low), cotangent, 1
    )
    total = length * ranks
    normed_all = normed_all.reshape(total, width)
    cotangent_all = cotangent_all.reshape(total, width)
    later_a = lax.all_gather(later_a, "z", axis=0, tiled=True)
    later_b = lax.all_gather(later_b, "z", axis=0, tiled=True)
    slot = later_a.shape[1] // 3
    all_rates = jnp.swapaxes(all_rates, 0, 1).reshape(width, 128)
    head_at = jnp.arange(2 * own) // own * (ranks * own) + jnp.arange(2 * own) % own + rank * own
    pick = jnp.pad(
        jax.nn.one_hot(head_at, 128, axis=0, dtype=low), ((0, 0), (0, 128 - 2 * own))
    )
    kernel = lax.dynamic_index_in_dim(
        conv_kernel.reshape(4, 3, ranks, wide), rank, 2, False
    ).reshape(4, 3 * wide)
    kernel = jnp.pad(kernel, ((0, 4), (0, 0)))
    log_rate = lax.dynamic_slice_in_dim(decay_log, rank * own, own)
    bias = lax.dynamic_slice_in_dim(decay_bias, rank * own, own)

    downward = [(z + 1, z) for z in range(layers - 1)]
    head_gains = jnp.broadcast_to(head_gain, (8, size))
    pads = ((0, 7), (2, 124))
    rates = jnp.pad(-jnp.exp(log_rate)[None], pads) + jnp.roll(jnp.pad(bias[None], pads), 1, 0)
    (
        mixed_low, gates, rate_in, ue, inverse, scores, steps, before, qk, columns, whole, rate_weight
    ) = prepare(normed_all, mixer, all_rates, pick, tail, kernel, rates)
    start = chain(whole, whole, False, 7)
    branch, gated_low, fresh, states, outputs = finish(
        start, before, ue, scores, qk, columns, gates, head_gains, project
    )
    hidden_state = source + scatter(branch, 2)
    normed_two, norm_two_pull = jax.vjp(norm_scale, hidden_state, gain_mlp)
    normed_two_all = gather(normed_two.astype(low), 3)
    inners, sums_of, back_terms = [], [], 0.0
    for weights in (later_a, later_b):
        gate_up_weight, down_weight = weights[:, : 2 * slot], weights[:, 2 * slot :]
        inner_act, inner_pull = jax.vjp(swiglu, dot_bf16(normed_two_all, gate_up_weight))
        inner_low = inner_act.astype(low)
        grad_inner = dot_bf16(cotangent_all, down_weight)
        grad_swiglu = inner_pull(grad_inner)[0].astype(low)
        sums_of.append(
            over_layers(later_terms(normed_two_all, cotangent_all, grad_swiglu, inner_low))
        )
        back_terms = back_terms + dot_nt(grad_swiglu, gate_up_weight)
        inners.append((inner_low, down_weight))
    later_sum_a, later_sum_b = sums_of
    grad_hidden_part, grad_gain_mlp = norm_two_pull(scatter(back_terms, 5))
    grad_hidden = cotangent.astype(jnp.float32) + grad_hidden_part
    grad_branch = gather(grad_hidden.astype(low), 6)
    grad_out, back_scores, returns, grad_gate, local, grad_head_gain = give_back(
        grad_branch, project, gates, head_gains, outputs, scores, ue, qk, columns, steps
    )
    end = chain(whole, local, True, 8)
    grad_mixed, grad_rates, grad_kernel, sums, first_rows, edge = gradients(
        end, returns, steps, grad_out, back_scores, fresh, states, inverse, scores, qk, columns,
        mixed_low, rate_in, grad_gate, kernel, rates, (later_sum_a,)
    )
    following = lax.ppermute(first_rows[:3].astype(low), "z", downward).astype(jnp.float32)
    late = [
        sum(kernel[j] * following[r - j] for j in range(r + 1)) for r in range(3)
    ]
    edge = jnp.concatenate([edge[:13], edge[13:] + jnp.stack(late)], 0).astype(low)
    grad_mixed = lax.dynamic_update_slice(grad_mixed, edge, (total - 16, 0))
    terms = mixer_terms(gated_low, grad_branch, normed_all, grad_mixed, (later_sum_b,))
    rate_terms = dot_tn(grad_rates, normed_all)
    mixer_sum = lax.psum_scatter(terms, "z", scatter_dimension=0)
    source_terms = dot_nt(grad_mixed, mixer) + dot_nt(grad_rates, rate_weight)
    out_terms = sum(dot_nt(*pair) for pair in inners)
    from_source, from_inner, grad_gate_up, grad_down = return_all(
        source_terms.astype(low), out_terms.astype(low), later_sum_a, later_sum_b, hidden, 10, (terms,)
    )
    grad_source, grad_gain_mixer = norm_pull(from_source)
    grad_tokens = (grad_hidden + grad_source).astype(low)
    result = (hidden_state + from_inner).astype(low)
    grad_gate_up, grad_down = grad_gate_up.astype(jnp.float32), grad_down.astype(jnp.float32)
    smalls = (
        grad_kernel,
        sums,
        grad_head_gain,
        grad_gain_mlp.reshape(2, -1),
        grad_gain_mixer.reshape(2, -1),
        rate_terms,
    )
    (
        grad_mixer, grad_project, grad_kernel, decays, grad_head_gain, grad_gain_mlp,
        grad_gain_mixer, rate_sums
    ) = last(mixer_sum, rows, smalls, 11, (grad_gate_up, grad_down, result, grad_tokens))
    rate_sums = jnp.swapaxes(rate_sums.reshape(ranks, 2, 2 * own, -1, rows), 1, 2)
    rate_sums = rate_sums.reshape(ranks, 2, own, -1, rows)
    grad_rates = lax.dynamic_index_in_dim(rate_sums, layer * ranks + rank, 3, False)
    grad_rates = jnp.transpose(grad_rates, (3, 1, 0, 2)).reshape(rows, -1)
    return (
        result,
        grad_tokens,
        grad_mixer.astype(jnp.float32),
        grad_rates,
        grad_project.astype(jnp.float32),
        grad_gate_up,
        grad_down,
        grad_kernel,
        decays[:, 128 + own : 128 + 2 * own].reshape(-1),
        decays[:, own : 2 * own].reshape(-1),
        grad_head_gain[0],
        grad_gain_mixer.reshape(-1),
        grad_gain_mlp.reshape(-1),
    )


def by_planes(mesh, members):
    seq, core = mesh.shape["seq"], mesh.shape["fsdp"]
    layers, ranks = seq // 4, 4 * core
    heads, size = members[7].shape[0], members[9].shape[0]
    return (
        core == 2
        and layers == 4
        and members[0].shape[0] == seq * core * size
        and heads % ranks == 0
        and members[5].shape[1] % (4 * 128) == 0
    )


def solution(mesh):
    rows, copied = P(("seq", "fsdp"), None), P()

    def run(*members):
        if by_planes(mesh, members):
            places = Mesh(mesh.devices.reshape(-1, 2, 2, 2), ALL)
            split, body = P(ALL, None), heads_on_plane
        else:
            places, split, body = mesh, rows, on_device
        return jax.shard_map(
            body,
            mesh=places,
            in_specs=(split,) * 6 + (copied,) * 6 + (split,),
            out_specs=(split,) * 7 + (copied,) * 6,
            check_vma=False,
        )(*members)

    return run
```

```python
from functools import partial

import jax
import jax.numpy as jnp
from jax import lax
from jax.experimental import pallas as pl
from jax.experimental.pallas import tpu as pltpu
from jax.sharding import Mesh
from jax.sharding import PartitionSpec as P

BLOCK = 64


highest = lax.Precision.HIGHEST


def shifted(value, axis, by):
    length = lax.axis_size(axis)
    pairs = [(i, i + by) for i in range(length) if 0 <= i + by < length]
    return lax.ppermute(value, axis, pairs)


def prefix_2(value, axis, join, neutral):
    place = lax.axis_index(axis)
    gathered = jax.tree.map(
        lambda a, kind: lax.all_gather(a.astype(kind), axis), value, (jnp.bfloat16, jnp.bfloat16)
    )
    state = jax.tree.map(lambda a, e: jnp.zeros_like(a) + jnp.asarray(e, a.dtype), value, neutral)

    def one(turn, state):
        return join(
            state,
            jax.tree.map(
                lambda a, own: lax.dynamic_index_in_dim(a, turn, 0, False).astype(own.dtype),
                gathered,
                value,
            ),
        )

    return lax.fori_loop(0, place, one, state)


def entering(value, axis, combine, identity):
    length, place = (lax.axis_size(axis), lax.axis_index(axis))
    everything = jax.tree.map(
        lambda part, kind: lax.all_gather(part.astype(kind), axis),
        value,
        jax.tree.map(lambda a: jnp.bfloat16 if a.dtype == jnp.float32 else a.dtype, value),
    )
    start = jax.tree.map(
        lambda part, zero: jnp.broadcast_to(jnp.asarray(zero, part.dtype), part.shape),
        value,
        identity,
    )

    def turn(k, before):
        at = length - 1 - k
        reached = at > place
        new = combine(
            before, jax.tree.map(lambda part, own: part[at].astype(own.dtype), everything, value)
        )
        return jax.tree.map(lambda a, b: jnp.where(reached, a, b), new, before)

    return lax.fori_loop(0, length, turn, start)


def round_trip(values_in):
    return lax.optimization_barrier(values_in.astype(jnp.bfloat16)).astype(jnp.float32)


def norm_scale(values_in, scales):
    return (
        values_in
        * lax.rsqrt(jnp.mean(values_in * values_in, axis=-1, keepdims=True) + 1e-06)
        * scales
    )


def features(extended, kernel, head_count):
    length = extended.shape[0] - 3
    summed = kernel[0] * extended[0:length]
    for offset in range(1, 4):
        summed = summed + kernel[offset] * extended[offset : offset + length]
    active = jax.nn.silu(summed)
    model_width = active.shape[1] // 3

    def unit_rows(member):
        shaped = member.reshape(length, head_count, -1)
        return shaped * lax.rsqrt(jnp.sum(shaped * shaped, axis=-1, keepdims=True) + 1e-06)

    queries = unit_rows(active[:, :model_width])
    queries = queries * queries.shape[-1] ** (-0.5)
    keys_all = unit_rows(active[:, model_width : 2 * model_width])
    values_all = active[:, 2 * model_width :].reshape(length, head_count, -1)
    return (queries, keys_all, values_all)


def rates_of(rate_inputs, decay_log, decay_bias):
    head_count = decay_log.shape[0]
    strength = jax.nn.sigmoid(rate_inputs[:, :head_count])
    decays = -jnp.exp(decay_log) * jax.nn.softplus(rate_inputs[:, head_count:] + decay_bias)
    return (strength, decays)


def head_output(outputs, gate_part, head_gain):
    normed_heads = (
        outputs * lax.rsqrt(jnp.mean(outputs * outputs, axis=-1, keepdims=True) + 1e-05) * head_gain
    )
    return normed_heads.reshape(outputs.shape[0], -1) * jax.nn.silu(gate_part)


def swiglu(gate_up):
    half_width = gate_up.shape[1] // 2
    return jax.nn.silu(gate_up[:, :half_width]) * gate_up[:, half_width:]


def to_blocks(member):
    block_count = member.shape[0] // BLOCK
    shaped = member.reshape((block_count, BLOCK) + member.shape[1:])
    return jnp.moveaxis(shaped, 2, 1)


def from_blocks(member):
    shaped = jnp.moveaxis(member, 1, 2)
    return shaped.reshape((-1,) + shaped.shape[2:])


def unit_pair(head_count, head_size):
    identity_matrix = jnp.eye(head_size, dtype=jnp.float32)
    return (
        jnp.broadcast_to(identity_matrix, (head_count, head_size, head_size)),
        jnp.zeros((head_count, head_size, head_size), jnp.float32),
    )


def combine(earlier, later):
    product = jnp.einsum("hab,hbc->hac", earlier[0], later[0], precision=highest)
    carried = jnp.einsum("hab,hbc->hac", earlier[1], later[0], precision=highest) + later[1]
    return (product, carried)


def block_terms(query_block, key_block, value_block, strength_block, decay_block):
    block_size = key_block.shape[1]
    lower_ones = jnp.tril(jnp.ones((block_size, block_size), jnp.float32))
    cumulative = jnp.einsum("hd,cd->hc", decay_block, lower_ones, precision=highest)
    positions = jnp.arange(block_size)
    causal = positions[:, None] >= positions[None, :]
    strict = positions[:, None] > positions[None, :]
    spread = cumulative[:, :, None] - cumulative[:, None, :]
    ratios = jnp.where(causal, jnp.exp(jnp.where(causal, spread, 0.0)), 0.0)
    key_products = jnp.einsum("hcd,hed->hce", key_block, key_block, precision=highest)
    lower_part = jnp.where(strict, strength_block[:, :, None] * ratios * key_products, 0.0)
    system = lower_part + jnp.eye(block_size, dtype=jnp.float32)
    gammas = jnp.exp(cumulative)
    updates = lax.linalg.triangular_solve(
        system,
        strength_block[:, :, None] * value_block,
        left_side=True,
        lower=True,
        unit_diagonal=True,
    )
    erasers = lax.linalg.triangular_solve(
        system,
        (strength_block * gammas)[:, :, None] * key_block,
        left_side=True,
        lower=True,
        unit_diagonal=True,
    )
    scores = jnp.einsum("hcd,hed->hce", query_block, key_block, precision=highest) * ratios
    tail_keys = jnp.exp(cumulative[:, -1:] - cumulative)[:, :, None] * key_block
    return (gammas, scores, updates, erasers, tail_keys)


def run_blocks(query_blocks, block_parts, start_state):

    def advance(carried, element):
        query_block, gammas, scores, updates, erasers, tail_keys = element
        fresh_values = updates - jnp.einsum("hcd,hvd->hcv", erasers, carried, precision=highest)
        produced = gammas[:, :, None] * jnp.einsum(
            "hcd,hvd->hcv", query_block, carried, precision=highest
        )
        produced = produced + jnp.einsum("hce,hev->hcv", scores, fresh_values, precision=highest)
        carried = gammas[:, -1][:, None, None] * carried + jnp.einsum(
            "hcv,hcd->hvd", fresh_values, tail_keys, precision=highest
        )
        return (carried, produced)

    end_state, produced = lax.scan(advance, start_state, (query_blocks,) + tuple(block_parts))
    return (produced, end_state)


def span(query_blocks, key_blocks, value_blocks, strength_blocks, decay_blocks, start_state):
    block_parts = jax.vmap(block_terms)(
        query_blocks, key_blocks, value_blocks, strength_blocks, decay_blocks
    )
    return run_blocks(query_blocks, block_parts, start_state)


def block_maps(block_parts, head_size):
    gammas, scores, updates, erasers, tail_keys = block_parts
    identity_matrix = jnp.eye(head_size, dtype=jnp.float32)
    transitions = gammas[:, :, -1][:, :, None, None] * identity_matrix - jnp.einsum(
        "nhcd,nhce->nhde", erasers, tail_keys, precision=highest
    )
    writes = jnp.einsum("nhcv,nhce->nhve", updates, tail_keys, precision=highest)

    def compose(carried, element):
        return (combine(carried, element), None)

    initial = unit_pair(transitions.shape[1], head_size)
    return lax.scan(compose, initial, (transitions, writes))[0]


def term_rows(left, right, precise):
    if precise:
        return jnp.einsum(
            "tr,tc->rc", left, right, precision=highest, preferred_element_type=jnp.float32
        )
    return jnp.einsum("tr,tc->rc", left, right, preferred_element_type=jnp.float32)


def on_device(
    tokens,
    w_mixer,
    w_rates,
    w_project,
    w_gate_up,
    w_down,
    conv_kernel,
    decay_log,
    decay_bias,
    head_gain,
    gain_mixer,
    gain_mlp,
    cotangent,
):
    length, model_width = tokens.shape
    head_count = decay_log.shape[0]
    head_size = head_gain.shape[0]
    conv_width = 3 * model_width
    full_mixer, full_rates, full_project, full_gate_up, full_down = (
        lax.all_gather(w_mixer, ("seq", "fsdp"), axis=0, tiled=True),
        lax.all_gather(w_rates, ("seq", "fsdp"), axis=0, tiled=True),
        lax.all_gather(w_project, ("seq", "fsdp"), axis=0, tiled=True),
        lax.all_gather(w_gate_up, ("seq", "fsdp"), axis=0, tiled=True),
        lax.all_gather(w_down, ("seq", "fsdp"), axis=0, tiled=True),
    )
    source = tokens.astype(jnp.float32)
    normed, norm_pull = jax.vjp(norm_scale, source, gain_mixer)
    normed_low = normed.astype(jnp.bfloat16)
    mixed_low = jnp.dot(normed_low, full_mixer, preferred_element_type=jnp.float32).astype(
        jnp.bfloat16
    )
    rate_inputs = jnp.dot(normed_low, full_rates, preferred_element_type=jnp.float32)
    previous = shifted(mixed_low[length - 3 :, :conv_width], ("seq", "fsdp"), 1)
    extended = jnp.concatenate([previous, mixed_low[:, :conv_width]], 0).astype(jnp.float32)
    triple, feature_pull = jax.vjp(partial(features, head_count=head_count), extended, conv_kernel)
    queries, keys_all, values_all = (round_trip(member) for member in triple)
    (strength, decays), rate_pull = jax.vjp(rates_of, rate_inputs, decay_log, decay_bias)
    blocks = tuple(
        (to_blocks(member) for member in (queries, keys_all, values_all, strength, decays))
    )
    block_parts = jax.vmap(block_terms)(*blocks)
    span_trans, span_writes = block_maps(block_parts, head_size)
    identity = unit_pair(head_count, head_size)
    prefix = prefix_2((span_trans, span_writes), ("seq", "fsdp"), combine, identity)
    start_state = prefix[1]
    output_blocks = run_blocks(blocks[0], block_parts, start_state)[0]
    outputs = from_blocks(output_blocks)
    gate_part = mixed_low[:, conv_width:].astype(jnp.float32)
    gated, head_pull = jax.vjp(head_output, outputs, gate_part, head_gain)
    gated_low = gated.astype(jnp.bfloat16)
    hidden_state = source + jnp.dot(gated_low, full_project, preferred_element_type=jnp.float32)
    normed_two, norm_two_pull = jax.vjp(norm_scale, hidden_state, gain_mlp)
    normed_two_low = normed_two.astype(jnp.bfloat16)
    gate_up = jnp.dot(normed_two_low, full_gate_up, preferred_element_type=jnp.float32)
    inner_act, inner_pull = jax.vjp(swiglu, gate_up)
    inner_low = inner_act.astype(jnp.bfloat16)
    result = hidden_state + jnp.einsum(
        "tf,df->td", inner_low, full_down, preferred_element_type=jnp.float32
    )
    upstream = cotangent.astype(jnp.float32)
    grad_inner = jnp.dot(cotangent, full_down, preferred_element_type=jnp.float32)
    grad_swiglu_low = inner_pull(grad_inner)[0].astype(jnp.bfloat16)
    grad_normed_two = jnp.einsum(
        "tc,dc->td", grad_swiglu_low, full_gate_up, preferred_element_type=jnp.float32
    )
    grad_hidden_part, grad_gain_mlp = norm_two_pull(grad_normed_two)
    grad_hidden = upstream + grad_hidden_part
    grad_hidden_low = grad_hidden.astype(jnp.bfloat16)
    grad_gated = jnp.einsum(
        "te,de->td", grad_hidden_low, full_project, preferred_element_type=jnp.float32
    )
    grad_outputs, grad_gate, grad_head_gain = head_pull(grad_gated)
    grad_out_blocks = to_blocks(grad_outputs)
    primal_pair, span_pull = jax.vjp(span, *blocks, start_state)
    local_grads = span_pull((grad_out_blocks, jnp.zeros_like(start_state)))
    suffix = entering(
        (jnp.swapaxes(span_trans, 1, 2), local_grads[5]), ("seq", "fsdp"), combine, identity
    )
    later_grads = span_pull((jnp.zeros_like(grad_out_blocks), suffix[1]))
    grad_blocks = [
        from_blocks(front_grad + back_grad)
        for front_grad, back_grad in zip(local_grads[:5], later_grads[:5])
    ]
    grad_triple = tuple((round_trip(member) for member in grad_blocks[:3]))
    grad_extended, grad_kernel = feature_pull(grad_triple)
    grad_inputs, grad_decay_log, grad_decay_bias = rate_pull((grad_blocks[3], grad_blocks[4]))
    following = shifted(grad_extended[:3].astype(jnp.bfloat16), ("seq", "fsdp"), -1).astype(
        jnp.float32
    )
    grad_conv = grad_extended[3:] + jnp.pad(following, ((length - 3, 0), (0, 0)))
    grad_mixed_low = jnp.concatenate([grad_conv, grad_gate], 1).astype(jnp.bfloat16)
    grad_normed = jnp.einsum(
        "tc,dc->td", grad_mixed_low, full_mixer, preferred_element_type=jnp.float32
    )
    grad_normed = grad_normed + jnp.dot(
        grad_inputs, full_rates.astype(jnp.float32).T, precision=highest
    )
    grad_source, grad_gain_mixer = norm_pull(grad_normed)
    grad_tokens = (grad_hidden + grad_source).astype(jnp.bfloat16)
    normed_wide = normed_low.astype(jnp.float32)
    grad_mixer = lax.psum_scatter(
        term_rows(normed_low, grad_mixed_low, False),
        ("seq", "fsdp"),
        scatter_dimension=0,
        tiled=True,
    )
    grad_rates = lax.psum_scatter(
        term_rows(normed_wide, grad_inputs, True), ("seq", "fsdp"), scatter_dimension=0, tiled=True
    )
    grad_project = lax.psum_scatter(
        term_rows(gated_low, grad_hidden_low, False),
        ("seq", "fsdp"),
        scatter_dimension=0,
        tiled=True,
    )
    grad_gate_up = lax.psum_scatter(
        term_rows(normed_two_low, grad_swiglu_low, False),
        ("seq", "fsdp"),
        scatter_dimension=0,
        tiled=True,
    )
    grad_down = lax.psum_scatter(
        term_rows(cotangent, inner_low, False), ("seq", "fsdp"), scatter_dimension=0, tiled=True
    )
    small_sums = lax.psum(
        (
            grad_kernel,
            grad_decay_log,
            grad_decay_bias,
            grad_head_gain,
            grad_gain_mixer,
            grad_gain_mlp,
        ),
        ("seq", "fsdp"),
    )
    return (
        result.astype(jnp.bfloat16),
        grad_tokens,
        grad_mixer,
        grad_rates,
        grad_project,
        grad_gate_up,
        grad_down,
        small_sums[0],
        small_sums[1],
        small_sums[2],
        small_sums[3],
        small_sums[4],
        small_sums[5],
    )


def dot_bf16(left, right):
    return jnp.dot(left, right, preferred_element_type=jnp.float32)


def dot_nt(left, right):
    return lax.dot_general(
        left, right, (((1,), (1,)), ((), ())), preferred_element_type=jnp.float32
    )


def dot_tn(left, right):
    return lax.dot_general(
        left, right, (((0,), (0,)), ((), ())), preferred_element_type=jnp.float32
    )


def exact(left, right, dims=((1,), (0,))):
    return lax.dot_general(
        left, right, (dims, ((), ())), precision=highest, preferred_element_type=jnp.float32
    )


NT = ((1,), (1,))
TN = ((0,), (0,))


PLANE = ("y", "x", "core")
ALL = ("z",) + PLANE


LOW, WIDE = jnp.bfloat16, jnp.float32
NN = ((1,), (0,))
VMEM_MOST = 56 << 20


def once(left, right, dims=NN):
    return lax.dot_general(
        left.astype(LOW), right.astype(LOW), (dims, ((), ())), preferred_element_type=WIDE
    )


def halves(value):
    high = value.astype(LOW)
    return high, (value - high.astype(WIDE)).astype(LOW)


def thrice(left, right, dims=NN):
    if not isinstance(left, tuple):
        left = halves(left)
    if not isinstance(right, tuple):
        right = halves(right)
    return (
        once(left[0], right[0], dims) + once(left[0], right[1], dims) + once(left[1], right[0], dims)
    )


def pair_rows(first, second):
    return jnp.concatenate([first, second], 0)


def pair_diagonal(first, second):
    zero = jnp.zeros_like(first)
    return pair_rows(
        jnp.concatenate([first, zero], 1), jnp.concatenate([zero, second], 1)
    )


def square_iotas(size):
    return (
        lax.broadcasted_iota(jnp.int32, (size, size), 0),
        lax.broadcasted_iota(jnp.int32, (size, size), 1),
    )


def decay_ratios(column, row, causal):
    return jnp.where(causal, jnp.exp(jnp.minimum(column - row, 0.0)), 0.0)


def inverses(lowers, differ):
    size = lowers[0].shape[0]
    results = [
        jnp.where(differ == 0, 1.0, 0.0) - jnp.where(differ == 1, lower, 0.0) for lower in lowers
    ]
    for level in range(1, 7):
        parts = [halves(result) for result in results]
        below = [jnp.where((differ >> level) == 1, lower, 0.0) for lower in lowers]
        inner = [thrice(b, p) for b, p in zip(below, parts)]
        results = [r - thrice(p, i) for r, p, i in zip(results, parts, inner)]
    return results


def silu_unit(summed):
    active = summed * jax.nn.sigmoid(summed)
    scale = lax.rsqrt(jnp.sum(active * active, axis=-1, keepdims=True) + 1e-06)
    return active, scale


def conv_of(ext, kernel, column, offset, count):
    at = pl.ds(column, 128)
    summed = kernel[0:1, at] * ext[pl.ds(offset, count), at]
    for j in range(1, 4):
        summed = summed + kernel[j : j + 1, at] * ext[pl.ds(offset + j, count), at]
    return summed


def softplus(value):
    return jnp.maximum(value, 0.0) + jnp.log1p(jnp.exp(-jnp.abs(value)))


def prepare_kernel(
    normed, mixer, all_rates, pick, tail, kernel, rates, mixed, gates, rate_in, ue, inverse, scores, steps, before,
    qk, columns, total, rate_weight, ext, carry
):
    step = pl.program_id(0)
    size = 128
    span = normed.shape[0]
    count = span // size
    conv = 6 * size

    @pl.when(step == 0)
    def _():
        rate_weight[...] = once(all_rates[...], pick[...]).astype(LOW)
        first = once(tail[...], mixer[...])
        low = first.astype(LOW)
        mixed[pl.ds(0, 16), :] = low[:, :conv]
        ext[pl.ds(0, 8), :] = low.astype(WIDE)[8:16, :conv]
        rows, cols = square_iotas(size)
        one = jnp.where(rows == cols, 1.0, 0.0)
        zero = jnp.zeros_like(one)
        carry[...] = pair_rows(
            jnp.concatenate([one, zero], 1), jnp.concatenate([one, zero], 1)
        )

    products = once(normed[...], mixer[...])
    low = products.astype(LOW)
    mixed[pl.ds(pl.multiple_of(16 + step * span, 16), span), :] = low[:, :conv]
    gates[...] = low[:, conv:]
    ext[pl.ds(8, span), :] = low[:, :conv].astype(WIDE)
    rate = once(normed[...], rate_weight[...])
    rate_in[...] = rate
    strength = jax.nn.sigmoid(rate)
    decay = rates[0:1, :] * softplus(rate + rates[1:2, :])
    unit = []
    for part in range(3):
        unit.append([])
        for head in range(2):
            summed = conv_of(ext, kernel, part * 256 + head * size, 5, span)
            active, scale = silu_unit(summed)
            if part == 0:
                active = active * scale * size**-0.5
            if part == 1:
                active = active * scale
            unit[part].append(active.astype(LOW))
    ext[pl.ds(0, 8), :] = ext[pl.ds(span, 8), :]
    small_rows, small_cols = square_iotas(size)
    causal = small_rows >= small_cols
    ones = jnp.where(causal, 1.0, 0.0)
    rows, cols = square_iotas(2 * size)
    differ = rows ^ cols
    lowers, keep = [], []
    for b in range(count):
        at = slice(b * size, (b + 1) * size)
        cumulative = lax.dot_general(
            ones, decay[at], (NN, ((), ())), precision=highest, preferred_element_type=WIDE
        )
        across = cumulative.T
        ratios = pair_diagonal(
            *(
                decay_ratios(cumulative[:, 2 + h : 3 + h], across[2 + h : 3 + h, :], causal)
                for h in range(2)
            )
        )
        query, key, value = (pair_rows(unit[p][0][at], unit[p][1][at]) for p in range(3))
        beta = pair_rows(strength[at, 0:1], strength[at, 1:2])
        column = pair_rows(cumulative[:, 2:3], cumulative[:, 3:4])
        lower = jnp.where(rows > cols, beta * ratios * once(key, key, NT), 0.0)
        lowers.append(lower)
        score = ratios * once(query, key, NT)
        scores[b] = score.astype(LOW)
        qk[b] = jnp.concatenate([query, key], 1)
        lanes = lax.broadcasted_iota(jnp.int32, (2 * size, 128), 1)
        columns[b] = jnp.where(lanes == 0, beta, jnp.where(lanes == 1, column, 0.0))
        keep.append((key.astype(WIDE), value.astype(WIDE), beta, column))
    for b, inv in enumerate(inverses(lowers, differ)):
        key, value, beta, column = keep[b]
        inverse[b] = inv.astype(LOW)
        gammas = jnp.exp(column)
        both = thrice(inv, jnp.concatenate([beta * value, (beta * gammas) * key], 1))
        ue[b] = both
        before[b] = carry[...]
        next_rows = []
        for h in range(2):
            at = slice(h * size, (h + 1) * size)
            last = column[(h + 1) * size - 1 : (h + 1) * size, :]
            tails = jnp.exp(last - column[at]) * key[at]
            made = thrice(tails, both[at], TN)
            advance = jnp.where(small_rows == small_cols, jnp.exp(last), 0.0) - made[:, size:]
            steps[b, at, :] = advance
            moved = thrice(advance, carry[at, :])
            next_rows.append(
                jnp.concatenate([moved[:, :size], moved[:, size:] + made[:, :size]], 1)
            )
        carry[...] = pair_rows(*next_rows)

    @pl.when(step == pl.num_programs(0) - 1)
    def _():
        total[...] = carry[...]


def output_kernel(
    start, before, ue, scores, qk, columns, mixed, gain, project, partial_out, gated_out,
    fresh_out, state_out, out_out
):
    size = 128
    count = ue.shape[0]
    for b in range(count):
        gated = []
        tokens = pl.ds(b * size, size)
        fresh_parts, queried = [], []
        for h in range(2):
            at = slice(h * size, (h + 1) * size)
            pre = before[b, at, :]
            state = thrice(pre[:, :size], start[at, :]) + pre[:, size:]
            state_out[b, at, :] = state
            seen = thrice(
                pair_rows(ue[b, at, size:], qk[b, at, :size].astype(WIDE)), state
            )
            fresh_parts.append(ue[b, at, :size] - seen[:size])
            queried.append(jnp.exp(columns[b, at, 1:2]) * seen[size:])
        fresh = pair_rows(*fresh_parts)
        fresh_out[b] = fresh.astype(LOW)
        outputs = pair_rows(*queried) + once(scores[b], fresh)
        out_out[b] = outputs
        for h in range(2):
            at = slice(h * size, (h + 1) * size)
            one = outputs[at]
            scale = lax.rsqrt(jnp.mean(one * one, axis=-1, keepdims=True) + 1e-05)
            gate = mixed[tokens, pl.ds(h * size, size)].astype(WIDE)
            gated.append((one * scale * gain[0:1, :] * (gate * jax.nn.sigmoid(gate))).astype(LOW))
        both = jnp.concatenate(gated, 1)
        gated_out[tokens, :] = both
        partial_out[tokens, :] = once(both, project[...]).astype(LOW)


def return_kernel(
    branch, project, mixed, gain, out, scores, ue, qk, columns, steps, grad_out, back_scores,
    returns, grad_gate, total, grad_gain, carry
):
    size = 128
    count = ue.shape[0]

    @pl.when(pl.program_id(0) == 0)
    def _():
        carry[...] = jnp.zeros_like(carry)
        grad_gain[...] = jnp.zeros_like(grad_gain)

    grad_gated = once(branch[...], project[...], NT)
    for b in reversed(range(count)):
        tokens = pl.ds(b * size, size)
        grads = []
        for h in range(2):
            at, wide = slice(h * size, (h + 1) * size), pl.ds(h * size, size)
            one = out[b, at, :]
            scale = lax.rsqrt(jnp.mean(one * one, axis=-1, keepdims=True) + 1e-05)
            gate = mixed[tokens, wide].astype(WIDE)
            open_ = jax.nn.sigmoid(gate)
            given = grad_gated[b * size : (b + 1) * size, at]
            normal = one * scale
            through = given * gate * open_
            grad_gain[0:1, :] += jnp.sum(through * normal, axis=0, keepdims=True)
            grad_gate[tokens, wide] = (
                given * normal * gain[0:1, :] * (open_ * (1.0 + gate * (1.0 - open_)))
            ).astype(LOW)
            f = through * gain[0:1, :]
            grads.append(
                scale * f
                - one * (scale * scale * scale) * jnp.mean(f * one, axis=-1, keepdims=True)
            )
        grad = pair_rows(*grads)
        grad_out[b] = grad
        back = once(scores[b], grad, TN)
        back_scores[b] = back
        for h in range(2):
            at = slice(h * size, (h + 1) * size)
            scaled = jnp.exp(columns[b, at, 1:2]) * qk[b, at, :size].astype(WIDE)
            given = once(
                pair_rows(scaled, -ue[b, at, size:]), pair_rows(grad[at], back[at]), TN
            )
            returns[b, at, :] = given
            carry[at, :] = thrice(steps[b, at, :], carry[at, :], TN) + given

    @pl.when(pl.program_id(0) == pl.num_programs(0) - 1)
    def _():
        total[...] = carry[...]


def gradient_kernel(
    end, returns, steps, grad_out, back_scores, fresh, states, inverse, scores, qk, columns,
    mixed, rate_in, grad_gate, kernel, rates, grad_mixed, grad_rates, grad_kernel, sums, front,
    edge, ext, gext, carry
):
    size = 128
    count = fresh.shape[0]
    span = count * size
    conv = 6 * size
    turn = pl.program_id(0)
    step = pl.num_programs(0) - 1 - turn

    @pl.when(turn == 0)
    def _():
        carry[...] = end[...]
        grad_kernel[...] = jnp.zeros_like(grad_kernel)
        sums[...] = jnp.zeros_like(sums)
        gext[pl.ds(span, 8), :] = jnp.zeros((8, conv), WIDE)

    ext[...] = mixed[pl.ds(pl.multiple_of(step * span, 16), span + 16), :].astype(WIDE)
    small_rows, small_cols = square_iotas(size)
    causal = small_rows >= small_cols
    upper = jnp.where(small_rows <= small_cols, 1.0, 0.0)
    rows, cols = square_iotas(2 * size)
    lanes = lax.broadcasted_iota(jnp.int32, (size, 128), 1)
    values = []
    for h in range(2):
        summed = conv_of(ext, kernel, 512 + h * size, 13, span)
        values.append(summed * jax.nn.sigmoid(summed))
    unit_grads = [[None] * count for _ in range(6)]
    for b in reversed(range(count)):
        tokens = slice(b * size, (b + 1) * size)
        grad_state = carry[...]
        after = [
            thrice(steps[b, h * size : (h + 1) * size, :], grad_state[h * size : (h + 1) * size], TN)
            for h in range(2)
        ]
        carry[...] = pair_rows(*after) + returns[b]
        beta, column = columns[b, :, 0:1], columns[b, :, 1:2]
        across = [columns[b, pl.ds(h * size, size), :].T[1:2, :] for h in range(2)]
        ratios = pair_diagonal(
            *(
                decay_ratios(column[h * size : (h + 1) * size], across[h], causal)
                for h in range(2)
            )
        )
        query, key = qk[b, :, :size].astype(WIDE), qk[b, :, size:].astype(WIDE)
        value = pair_rows(
            *(values[h][tokens].astype(LOW).astype(WIDE) for h in range(2))
        )
        gammas = jnp.exp(column)
        last = [column[(h + 1) * size - 1 : (h + 1) * size] for h in range(2)]
        tail_scale = pair_rows(
            *(jnp.exp(last[h] - column[h * size : (h + 1) * size]) for h in range(2))
        )
        tails = tail_scale * key
        grad = grad_out[b]
        from_tails = [
            once(tails[h * size : (h + 1) * size], grad_state[h * size : (h + 1) * size])
            for h in range(2)
        ]
        grad_fresh = back_scores[b] + pair_rows(*from_tails)
        solved = once(inverse[b], grad_fresh, TN)
        made = fresh[b].astype(WIDE)
        pairs = once(pair_rows(-solved, grad), made, NT)
        score = scores[b].astype(WIDE)
        lower_part = jnp.where(rows > cols, pairs[: 2 * size] * ratios, 0.0)
        score_part = pairs[2 * size :] * ratios
        products = once(key, key, NT)
        weighed = beta * lower_part
        grad_decayed, grad_erase, grad_tails = [], [], []
        for h in range(2):
            at = slice(h * size, (h + 1) * size)
            state = states[b, at, :]
            both = once(pair_rows(grad[at], -solved[at]), state, NT)
            grad_decayed.append(both[:size])
            grad_erase.append(both[size:])
            grad_tails.append(once(made[at], grad_state[at], NT))
        grad_decayed, grad_erase, grad_tails = (
            pair_rows(*m) for m in (grad_decayed, grad_erase, grad_tails)
        )
        stacked = pair_rows(score_part, weighed)
        with_key = once(stacked, key)
        turned = once(stacked, pair_rows(query, key), TN)
        grad_query = gammas * grad_decayed + with_key[: 2 * size]
        grad_key = (
            turned
            + with_key[2 * size :]
            + (beta * gammas) * grad_erase
            + tail_scale * grad_tails
        )
        grad_value = beta * solved
        erase_key = jnp.sum(grad_erase * key, axis=1, keepdims=True) * gammas
        lower_products = lower_part * products
        grad_beta = (
            jnp.sum(lower_products, axis=1, keepdims=True)
            + jnp.sum(solved * value, axis=1, keepdims=True)
            + erase_key
        )
        both = pairs[2 * size :] * score + beta * lower_products
        tail_sum = jnp.sum(grad_tails * tails, axis=1, keepdims=True)
        to_column = jnp.sum(both, axis=0, keepdims=True)
        grad_column = (
            jnp.sum(both, axis=1, keepdims=True)
            + gammas * jnp.sum(grad_decayed * query, axis=1, keepdims=True)
            + beta * erase_key
            - tail_sum
        )
        grad_rate = jnp.zeros((size, 128), WIDE)
        grad_step = jnp.zeros((size, 128), WIDE)
        for h in range(2):
            at = slice(h * size, (h + 1) * size)
            kept = jnp.sum(states[b, at, :] * grad_state[at]) * jnp.exp(last[h])
            finish = kept + jnp.sum(tail_sum[at], axis=0, keepdims=True)
            turned_row = jnp.broadcast_to(to_column[:, at], (size, size)).T
            cumulated = grad_column[at] - turned_row
            summed = lax.dot_general(
                upper, cumulated, (NN, ((), ())), precision=highest, preferred_element_type=WIDE
            )
            grad_step = jnp.where(lanes == 2 + h, summed + finish, grad_step)
            grad_rate = jnp.where(lanes == h, grad_beta[at], grad_rate)
        rate = rate_in[tokens, :]
        strength = jax.nn.sigmoid(rate)
        slope = jax.nn.sigmoid(rate + rates[1:2, :])
        grad_in = grad_rate * strength * (1.0 - strength) + grad_step * rates[0:1, :] * slope
        decay = rates[0:1, :] * softplus(rate + rates[1:2, :])
        sums[0:1, :] += jnp.sum(grad_in, axis=0, keepdims=True)
        sums[1:2, :] += jnp.sum(grad_step * decay, axis=0, keepdims=True)
        grad_rates[tokens, :] = grad_in.astype(LOW)
        grad_mixed[tokens, conv:] = grad_gate[tokens, :]
        for part, member in enumerate((grad_query, grad_key, grad_value)):
            rounded = member.astype(LOW).astype(WIDE)
            for h in range(2):
                unit_grads[2 * part + h][b] = rounded[h * size : (h + 1) * size]
    for part in range(3):
        for h in range(2):
            at = part * 256 + h * size
            wide = pl.ds(at, size)
            given = jnp.concatenate(unit_grads[2 * part + h], 0)
            summed = conv_of(ext, kernel, at, 13, span)
            open_ = jax.nn.sigmoid(summed)
            if part < 2:
                active, scale = silu_unit(summed)
                if part == 0:
                    given = given * size**-0.5
                inner = jnp.sum(active * given, axis=-1, keepdims=True)
                given = scale * given - (scale * scale * scale) * inner * active
            slope = open_ * (1.0 + summed * (1.0 - open_))
            grad_conv = given * slope
            gext[pl.ds(0, span), wide] = grad_conv
            for j in range(4):
                grad_kernel[j : j + 1, wide] += jnp.sum(
                    grad_conv * ext[pl.ds(13 + j, span), wide], axis=0, keepdims=True
                )
            moved = kernel[0:1, wide] * gext[pl.ds(3, span), wide]
            for j in range(1, 4):
                moved = moved + kernel[j : j + 1, wide] * gext[pl.ds(3 - j, span), wide]
            grad_mixed[:, wide] = moved.astype(LOW)

            @pl.when(turn == 0)
            def _():
                edge[:, wide] = moved[span - 16 :]

    gext[pl.ds(span, 8), :] = gext[pl.ds(0, 8), :]

    @pl.when(turn == pl.num_programs(0) - 1)
    def _():
        front[...] = gext[pl.ds(0, 8), :]


def whole_spec(shape):
    return pl.BlockSpec(shape, lambda i: (0,) * len(shape))


def rows_spec(shape, turn=None):
    zeros = (0,) * (len(shape) - 1)
    if turn is None:
        return pl.BlockSpec(shape, lambda i: (i,) + zeros)
    return pl.BlockSpec(shape, lambda i: (turn - 1 - i,) + zeros)


GROUP, PREPARED = 2, 4


def cost(flops, touched):
    return pl.CostEstimate(flops=int(flops), bytes_accessed=int(touched), transcendentals=0)


def prepare(normed, mixer, all_rates, pick, tail, kernel, rates):
    total, width = normed.shape
    blocks = total // 128
    steps = blocks // PREPARED
    span = PREPARED * 128
    like = jax.ShapeDtypeStruct
    return pl.pallas_call(
        prepare_kernel,
        grid=(steps,),
        in_specs=[
            rows_spec((span, width)),
            whole_spec(mixer.shape),
            whole_spec(all_rates.shape),
            whole_spec(pick.shape),
            whole_spec(tail.shape),
            whole_spec(kernel.shape),
            whole_spec(rates.shape),
        ],
        out_specs=[
            whole_spec((total + 16, 768)),
            rows_spec((span, 256)),
            rows_spec((span, 128)),
            rows_spec((PREPARED, 256, 256)),
            rows_spec((PREPARED, 256, 256)),
            rows_spec((PREPARED, 256, 256)),
            rows_spec((PREPARED, 256, 128)),
            rows_spec((PREPARED, 256, 256)),
            rows_spec((PREPARED, 256, 256)),
            rows_spec((PREPARED, 256, 128)),
            whole_spec((256, 256)),
            whole_spec(all_rates.shape),
        ],
        out_shape=[
            like((total + 16, 768), LOW),
            like((total, 256), LOW),
            like((total, 128), WIDE),
            like((blocks, 256, 256), WIDE),
            like((blocks, 256, 256), LOW),
            like((blocks, 256, 256), LOW),
            like((blocks, 256, 128), WIDE),
            like((blocks, 256, 256), WIDE),
            like((blocks, 256, 256), LOW),
            like((blocks, 256, 128), WIDE),
            like((256, 256), WIDE),
            like(all_rates.shape, LOW),
        ],
        scratch_shapes=[pltpu.VMEM((span + 8, 768), WIDE), pltpu.VMEM((256, 256), WIDE)],
        compiler_params=pltpu.CompilerParams(vmem_limit_bytes=VMEM_MOST),
        cost_estimate=cost(4e10, 2e7),
        name="prepare",
    )(normed, mixer, all_rates, pick, tail, kernel, rates)


def finish(start, before, ue, scores, qk, columns, gates, gain, project):
    blocks = ue.shape[0]
    total, width = blocks * 128, project.shape[1]
    span = GROUP * 128
    like = jax.ShapeDtypeStruct
    return pl.pallas_call(
        output_kernel,
        grid=(blocks // GROUP,),
        in_specs=[
            whole_spec(start.shape),
            rows_spec((GROUP, 256, 256)),
            rows_spec((GROUP, 256, 256)),
            rows_spec((GROUP, 256, 256)),
            rows_spec((GROUP, 256, 256)),
            rows_spec((GROUP, 256, 128)),
            rows_spec((span, 256)),
            whole_spec(gain.shape),
            whole_spec(project.shape),
        ],
        out_specs=[
            rows_spec((span, width)),
            rows_spec((span, 256)),
            rows_spec((GROUP, 256, 128)),
            rows_spec((GROUP, 256, 128)),
            rows_spec((GROUP, 256, 128)),
        ],
        out_shape=[
            like((total, width), LOW),
            like((total, 256), LOW),
            like((blocks, 256, 128), LOW),
            like((blocks, 256, 128), WIDE),
            like((blocks, 256, 128), WIDE),
        ],
        compiler_params=pltpu.CompilerParams(vmem_limit_bytes=VMEM_MOST),
        cost_estimate=cost(1e10, 1e7),
        name="finish",
    )(start, before, ue, scores, qk, columns, gates, gain, project)


def give_back(branch, project, gates, gain, out, scores, ue, qk, columns, steps):
    blocks = ue.shape[0]
    total, width = branch.shape
    turns = blocks // GROUP
    span = GROUP * 128
    like = jax.ShapeDtypeStruct
    block = lambda *shape: rows_spec((GROUP,) + shape, turns)
    return pl.pallas_call(
        return_kernel,
        grid=(turns,),
        in_specs=[
            rows_spec((span, width), turns),
            whole_spec(project.shape),
            rows_spec((span, 256), turns),
            whole_spec(gain.shape),
            block(256, 128),
            block(256, 256),
            block(256, 256),
            block(256, 256),
            block(256, 128),
            block(256, 128),
        ],
        out_specs=[
            block(256, 128),
            block(256, 128),
            block(256, 128),
            rows_spec((span, 256), turns),
            whole_spec((256, 128)),
            whole_spec((8, 128)),
        ],
        out_shape=[
            like((blocks, 256, 128), WIDE),
            like((blocks, 256, 128), WIDE),
            like((blocks, 256, 128), WIDE),
            like((total, 256), LOW),
            like((256, 128), WIDE),
            like((8, 128), WIDE),
        ],
        scratch_shapes=[pltpu.VMEM((256, 128), WIDE)],
        compiler_params=pltpu.CompilerParams(vmem_limit_bytes=VMEM_MOST),
        cost_estimate=cost(1e10, 1e7),
        name="give_back",
    )(branch, project, gates, gain, out, scores, ue, qk, columns, steps)


def gradients(
    end, returns, steps, grad_out, back_scores, fresh, states, inverse, scores, qk, columns,
    mixed, rate_in, grad_gate, kernel, rates, after=()
):
    blocks = fresh.shape[0]
    total = blocks * 128
    turns = blocks // GROUP
    span = GROUP * 128
    like = jax.ShapeDtypeStruct
    block = lambda *shape: rows_spec((GROUP,) + shape, turns)
    return pl.pallas_call(
        behind(gradient_kernel, len(after)),
        grid=(turns,),
        in_specs=[pl.BlockSpec(memory_space=pl.ANY)] * len(after)
        + [
            whole_spec(end.shape),
            block(256, 128),
            block(256, 128),
            block(256, 128),
            block(256, 128),
            block(256, 128),
            block(256, 128),
            block(256, 256),
            block(256, 256),
            block(256, 256),
            block(256, 128),
            whole_spec(mixed.shape),
            rows_spec((span, 128), turns),
            rows_spec((span, 256), turns),
            whole_spec(kernel.shape),
            whole_spec(rates.shape),
        ],
        out_specs=[
            rows_spec((span, 1024), turns),
            rows_spec((span, 128), turns),
            whole_spec((8, 768)),
            whole_spec((8, 128)),
            whole_spec((8, 768)),
            whole_spec((16, 768)),
        ],
        out_shape=[
            like((total, 1024), LOW),
            like((total, 128), LOW),
            like((8, 768), WIDE),
            like((8, 128), WIDE),
            like((8, 768), WIDE),
            like((16, 768), WIDE),
        ],
        scratch_shapes=[
            pltpu.VMEM((span + 16, 768), WIDE),
            pltpu.VMEM((span + 8, 768), WIDE),
            pltpu.VMEM((256, 128), WIDE),
        ],
        compiler_params=pltpu.CompilerParams(vmem_limit_bytes=VMEM_MOST),
        cost_estimate=cost(2e10, 1e7),
        name="gradients",
    )(
        *after, end, returns, steps, grad_out, back_scores, fresh, states, inverse, scores, qk, columns,
        mixed, rate_in, grad_gate, kernel, rates
    )


MESH = pl.DeviceIdType.MESH
DMA = pltpu.SemaphoreType.DMA


def neighbours():
    z, y, x, core = (lax.axis_index(name) for name in ALL)
    over_x, over_y, sibling = (z, y, 1 - x, core), (z, 1 - y, x, core), (z, y, x, 1 - core)
    return z, y, x, core, over_x, over_y, sibling


def rank_of(y, x, core):
    return (y * 2 + x) * 2 + core


def greet(others):
    barrier = pltpu.get_barrier_semaphore()
    for other in others:
        pl.semaphore_signal(barrier, inc=1, device_id=other, device_id_type=MESH)
    pl.semaphore_wait(barrier, len(others))


def remote(source, target, sent, arrived, device):
    return pltpu.make_async_remote_copy(
        source, target, sent, arrived, device_id=device, device_id_type=MESH
    )


class Gather:
    def __init__(
        self, mine, out, own_sem, sent, arrived, across_sent, across_arrived, core_sent, core_arrived
    ):
        z, y, x, core, over_x, over_y, sibling = neighbours()
        half = mine.shape[0] // 2
        me, other = rank_of(y, x, core), 1 - core
        piece = lambda slot, p: out.at[slot, pl.ds(p * half, half)]
        from_axis = [rank_of(y, 1 - x, core), rank_of(1 - y, x, core)]
        theirs = [rank_of(y, 1 - x, other), rank_of(1 - y, x, other)]
        over = [over_x, over_y]
        self.own = pltpu.make_async_copy(mine, out.at[me], own_sem)

        def to_core(slot, p, k):
            place = piece(slot, p)
            return remote(place, place, core_sent.at[k], core_arrived.at[k], sibling)

        self.first = [
            remote(
                mine.at[pl.ds(p * half, half)], piece(me, p), sent.at[axis, p],
                arrived.at[axis, p], over[axis]
            )
            for axis, p in ((0, 0), (1, 1), (0, 1), (1, 0))
        ]
        self.first_core = remote(mine, out.at[me], core_sent.at[6], core_arrived.at[6], sibling)
        self.onward = [
            remote(
                piece(from_axis[axis], axis), piece(from_axis[axis], axis),
                across_sent.at[axis], across_arrived.at[axis], over[1 - axis]
            )
            for axis in range(2)
        ]
        self.shared = [
            to_core(from_axis[axis], p, 2 * axis + p)
            for axis, p in ((0, 0), (1, 1), (0, 1), (1, 0))
        ]
        mine_across = rank_of(1 - y, 1 - x, core)
        self.across = [
            remote(
                piece(mine_across, p), piece(mine_across, p), across_sent.at[p],
                across_arrived.at[p], over_x
            )
            for p in range(2)
        ]
        self.shared_across = [to_core(mine_across, p, 4 + p) for p in range(2)]
        self.last = [to_core(theirs[axis], p, 2 * axis + p) for axis in range(2) for p in range(2)]
        self.last += [to_core(rank_of(1 - y, 1 - x, other), p, 4 + p) for p in range(2)]
        place = out.at[rank_of(y, x, other)]
        self.last.append(remote(place, place, core_sent.at[6], core_arrived.at[6], sibling))

    def start(self):
        self.own.start()
        for copy in self.first:
            copy.start()
        self.first_core.start()

    def forward(self):
        for i in range(4):
            self.first[i].wait_recv()
            if i < 2:
                self.onward[i].start()
            self.shared[i].start()

    def finish(self):
        for p in range(2):
            self.across[p].wait_recv()
            self.shared_across[p].start()
        for copy in self.last:
            copy.wait_recv()
        self.own.wait()
        for copy in self.first + [self.first_core] + self.onward + self.shared + self.shared_across:
            copy.wait_send()


def gather_kernel(mine, out, *semaphores):
    greet(neighbours()[4:])
    gather = Gather(mine, out, *semaphores)
    gather.start()
    gather.forward()
    gather.finish()


GATHER_SEMAPHORES = [DMA, DMA((2, 2)), DMA((2, 2)), DMA((2,)), DMA((2,)), DMA((7,)), DMA((7,))]


def plane_gather(rows_here, place):
    rows, width = rows_here.shape
    out = pl.pallas_call(
        gather_kernel,
        out_shape=jax.ShapeDtypeStruct((8, rows, width), rows_here.dtype),
        in_specs=[pl.BlockSpec(memory_space=pltpu.VMEM)],
        out_specs=pl.BlockSpec(memory_space=pltpu.VMEM),
        scratch_shapes=GATHER_SEMAPHORES,
        compiler_params=pltpu.CompilerParams(
            collective_id=place, has_side_effects=True, vmem_limit_bytes=VMEM_MOST
        ),
        cost_estimate=pl.CostEstimate(flops=0, bytes_accessed=70_000_000, transcendentals=0),
        name="plane_gather",
    )(rows_here)
    return out.reshape(8 * rows, width)

def turned(place, flip):
    return place + flip - 2 * place * flip


def units_of(hidden, core, half):
    tiles = hidden // 4 // 128
    most = -(-tiles // 2)
    first = -(-most // 2)
    begin = core * most + half * first
    end = min(begin + first, tiles if core else most)
    return begin * 128, (end - begin) * 128, first * 128


def front_kernel(
    w_mixer, w_gate_up, w_down, w_project, tokens, gain, cotangent, own_rates, mixer, later_a,
    later_b, project, normed_all, cotangent_all, tail, rates, normed, zeros, w_rates, project_own, project_sent,
    project_arrived, rates_own, rates_z_sent, rates_z, rates_sent,
    rates_arrived, mixer_own, mixer_sent, mixer_arrived, up_sent, down_sent, z_arrived,
    later_own, later_sent, later_arrived, zero_sem, tail_sent, tail_arrived, *gather_semaphores
):
    z, y, x, core, over_x, over_y, sibling = neighbours()
    layers = lax.axis_size("z")
    rows, width = w_mixer.shape[0], w_mixer.shape[1] // 4
    wide = width // 8
    hidden = w_down.shape[1]
    per_chip = hidden // 4
    laters = (later_a, later_b)
    block = 8 * rows
    me = rank_of(y, x, core)
    low_z, high_z = jnp.maximum(z - 1, 0), jnp.minimum(z + 1, layers - 1)
    below, above = (low_z, y, x, core), (high_z, y, x, core)
    last = (me == 7) & (z < layers - 1)
    flips = [(k >> 2, (k >> 1) & 1, k & 1) for k in range(8)]
    ranks = [rank_of(turned(y, a), turned(x, b), turned(core, c)) for a, b, c in flips]
    devices = [(z, turned(y, a), turned(x, b), turned(core, c)) for a, b, c in flips]

    barrier = pltpu.get_barrier_semaphore()
    for k in range(1, 8):
        pl.semaphore_signal(barrier, inc=1, device_id=devices[k], device_id_type=MESH)

    @pl.when(z > 0)
    def _():
        pl.semaphore_signal(barrier, inc=1, device_id=below, device_id_type=MESH)
        pl.semaphore_signal(barrier, inc=1, device_id=(low_z, 1, 1, 1), device_id_type=MESH)

    @pl.when(z < layers - 1)
    def _():
        pl.semaphore_signal(barrier, inc=1, device_id=above, device_id_type=MESH)

    others_z = [(lax.rem(z + k, layers), y, x, core) for k in range(1, layers)]
    for other in others_z:
        pl.semaphore_signal(barrier, inc=1, device_id=other, device_id_type=MESH)
    keeps = (y == z // 2) & (x == lax.rem(z, 2)) & (core == y)
    own_j = 2 * x + core
    for j in range(4):

        @pl.when(jnp.logical_not(keeps & (own_j == j)))
        def _():
            pl.semaphore_signal(
                barrier, inc=1, device_id=(2 * y + x, core, j // 2, j % 2), device_id_type=MESH
            )

    pl.semaphore_wait(
        barrier,
        10 + layers - jnp.where(keeps, 1, 0) + jnp.where(z > 0, 1, 0) + jnp.where(z < layers - 1, 1, 0) + jnp.where(last, 8, 0),
    )

    def columns(p, rank):
        return w_mixer.at[:, pl.ds(pl.multiple_of(p * width + rank * wide, 128), wide)]

    def mixer_rows(layer, rank):
        return mixer.at[pl.ds(pl.multiple_of(layer * block + rank * rows, rows), rows)]

    mine = mixer_rows(z, me)
    owns = [
        pltpu.make_async_copy(columns(p, me), mine.at[:, pl.ds(p * wide, wide)], mixer_own.at[p])
        for p in range(4)
    ]
    for copy in owns:
        copy.start()
    for k in (2, 4, 6, 1, 3, 5, 7):
        for p in range(4):
            remote(
                columns(p, ranks[k]), mine.at[:, pl.ds(p * wide, wide)], mixer_sent.at[k],
                mixer_arrived.at[k], devices[k]
            ).start()

    def along(layer, rank, upward):
        place = mixer_rows(layer, rank)
        return remote(
            place, place, (up_sent if upward else down_sent).at[layer, rank],
            z_arrived.at[layer, rank], above if upward else below
        )

    def spread(rank):
        @pl.when(z < layers - 1)
        def _():
            along(z, rank, True).start()

        @pl.when(z > 0)
        def _():
            along(z, rank, False).start()

    for r in range(0, tokens.shape[0], 32):
        source = tokens[r : r + 32, :].astype(WIDE)
        scale = lax.rsqrt(jnp.mean(source * source, axis=-1, keepdims=True) + 1e-06)
        normed[r : r + 32, :] = (source * scale * gain[...]).astype(LOW)
    w_rates[...] = jnp.zeros_like(w_rates)
    w_rates[:, : own_rates.shape[1]] = own_rates[...]
    zeros[...] = jnp.zeros_like(zeros)
    count = len(gather_semaphores) // 2
    gather_normed = Gather(normed, normed_all, *gather_semaphores[:count])
    gather_cotangent = Gather(cotangent, cotangent_all, *gather_semaphores[count:])
    for copy in owns:
        copy.wait()
    spread(me)
    gather_normed.start()
    rate_copies = [
        remote(w_rates, rates.at[me, z], rates_z_sent.at[k], rates_z.at[k], other)
        for k, other in enumerate(others_z)
    ]
    for copy in rate_copies:
        copy.start()
    rate_own = pltpu.make_async_copy(w_rates, rates.at[me, z], rates_own)
    rate_own.start()

    def tails(a, b, c):
        k = (a * 2 + b) * 2 + c
        return remote(
            normed.at[pl.ds(normed.shape[0] - 16, 16)], tail, tail_sent.at[k], tail_arrived,
            (high_z, a, b, c)
        )

    @pl.when(last)
    def _():
        for a, b, c in flips:
            tails(a, b, c).start()

    for k in (1, 2, 4, 3, 5, 6, 7):
        place = mixer_rows(z, ranks[k])
        remote(place, place, mixer_sent.at[k], mixer_arrived.at[k], devices[k]).wait_recv()
        spread(ranks[k])

    def pass_on(far):
        @pl.loop(0, 8)
        def _(rank):
            @pl.when(z - far >= 0)
            def _():
                copy = along(jnp.maximum(z - far, 0), rank, True)
                copy.wait_recv()

                @pl.when(z < layers - 1)
                def _():
                    copy.start()

            @pl.when(z + far <= layers - 1)
            def _():
                copy = along(jnp.minimum(z + far, layers - 1), rank, False)
                copy.wait_recv()

                @pl.when(z > 0)
                def _():
                    copy.start()

    here = pl.ds(pl.multiple_of(me * rows, rows), rows)

    def shares(chip, t):
        found = []
        for half, later in enumerate(laters):
            begin, size, slot = units_of(hidden, t, half)
            first = pl.multiple_of(chip * per_chip + begin, 128)
            up = pl.multiple_of(hidden + first, 128)
            found += [
                (w_gate_up.at[:, pl.ds(first, size)], later.at[here, pl.ds(0, size)]),
                (w_gate_up.at[:, pl.ds(up, size)], later.at[here, pl.ds(slot, size)]),
                (w_down.at[:, pl.ds(first, size)], later.at[here, pl.ds(2 * slot, size)]),
            ]
        return found

    def later_wait(t, semaphore, arrival):
        for half, later in enumerate(laters):
            place = later.at[pl.ds(0, rows), pl.ds(0, 3 * units_of(hidden, t, half)[1])]
            copy = remote(place, place, semaphore.at[half], semaphore.at[half], sibling)
            if arrival:
                copy.wait_recv()
            else:
                copy.wait_send()

    def send_later(f, t):
        a, b = f >> 1, f & 1
        for i, (source, target) in enumerate(shares(turned(y, a) * 2 + turned(x, b), t)):
            remote(
                source, target, later_sent.at[f, t, i // 3], later_arrived.at[f, core, i // 3],
                (z, turned(y, a), turned(x, b), t)
            ).start()

    for f in (1, 2, 3):
        for t in range(2):
            send_later(f, t)
    for t in range(2):

        @pl.when(core == t)
        def _():
            for i, (source, target) in enumerate(shares(y * 2 + x, t)):
                pltpu.make_async_copy(source, target, later_own.at[i]).start()

        @pl.when(core != t)
        def _():
            send_later(0, t)

    _, least, slot = units_of(hidden, 1, 1)
    pads = [
        pltpu.make_async_copy(
            zeros, later_b.at[:, pl.ds(i * slot + least, slot - least)], zero_sem.at[i]
        )
        for i in range(3)
    ]

    @pl.when(core == 1)
    def _():
        for copy in pads:
            copy.start()

    pass_on(1)
    rows_of = lambda j: project.at[pl.ds(pl.multiple_of(j * rows, rows), rows)]
    project_copies = [
        remote(
            w_project, rows_of(own_j), project_sent.at[k], project_arrived.at[own_j],
            (lax.rem(z + k, layers), z // 2, lax.rem(z, 2), y)
        )
        for k in range(4)
    ]
    project_kept = pltpu.make_async_copy(w_project, rows_of(own_j), project_own)

    @pl.when(keeps)
    def _():
        project_kept.start()

    @pl.when(jnp.logical_not(keeps))
    def _():
        project_copies[0].start()

    for copy in project_copies[1:]:
        copy.start()
    gather_normed.forward()
    gather_cotangent.start()
    pass_on(2)
    rate_own.wait()
    for copy in rate_copies:
        copy.wait_recv()
    for k in range(1, 8):
        place = rates.at[me]
        copy = remote(place, place, rates_sent.at[k], rates_arrived.at[k], devices[k])
        copy.start()
        rate_copies.append(copy)
    gather_normed.finish()
    gather_cotangent.forward()
    pass_on(3)
    gather_cotangent.finish()
    for j in range(4):

        @pl.when(jnp.logical_not(keeps & (own_j == j)))
        def _():
            remote(
                rows_of(j), rows_of(j), project_sent.at[0], project_arrived.at[j], sibling
            ).wait_recv()

    @pl.when(keeps)
    def _():
        project_kept.wait()

    @pl.when(jnp.logical_not(keeps))
    def _():
        project_copies[0].wait_send()

    for copy in project_copies[1:]:
        copy.wait_send()

    for t in range(2):

        @pl.when(core == t)
        def _():
            for f in range(4):
                for s in range(2):
                    if f or s != t:
                        later_wait(t, later_arrived.at[f, s], True)
            for i, (source, target) in enumerate(shares(y * 2 + x, t)):
                pltpu.make_async_copy(source, target, later_own.at[i]).wait()

    @pl.when(core == 1)
    def _():
        for copy in pads:
            copy.wait()

    for t in range(2):
        for f in range(1, 4):
            later_wait(t, later_sent.at[f, t], False)

        @pl.when(core != t)
        def _():
            later_wait(t, later_sent.at[0, t], False)

    for k in range(1, 8):
        remote(mine, mine, mixer_sent.at[k], mixer_arrived.at[k], devices[k]).wait_send()
        place = rates.at[ranks[k]]
        remote(place, place, rates_sent.at[k], rates_arrived.at[k], devices[k]).wait_recv()
    for copy in rate_copies:
        copy.wait_send()

    @pl.when(z == 0)
    def _():
        tail[...] = jnp.zeros_like(tail)

    @pl.when(z > 0)
    def _():
        tails(0, 0, 0).wait_recv()

    @pl.when(last)
    def _():
        for a, b, c in flips:
            tails(a, b, c).wait_send()

    for layer in range(4):

        @pl.loop(0, 8)
        def _(rank):
            @pl.when((z < layers - 1) & (layer <= z))
            def _():
                along(layer, rank, True).wait_send()

            @pl.when((z > 0) & (layer >= z))
            def _():
                along(layer, rank, False).wait_send()


def front(w_mixer, w_gate_up, w_down, w_project, w_rates, tokens, gain, cotangent, place):
    rows, columns = w_mixer.shape
    layers = lax.axis_size("z")
    hidden = w_down.shape[1]
    _, least, slot = units_of(hidden, 1, 1)
    length, width = tokens.shape
    like = jax.ShapeDtypeStruct
    any_, vmem = pl.BlockSpec(memory_space=pl.ANY), pl.BlockSpec(memory_space=pltpu.VMEM)
    return pl.pallas_call(
        front_kernel,
        out_shape=[
            like((8 * layers * rows, columns // 8), LOW),
            like((8 * rows, 3 * slot), LOW),
            like((8 * rows, 3 * slot), LOW),
            like((4 * rows, w_project.shape[1]), LOW),
            like((8, length, width), LOW),
            like((8, length, width), LOW),
            like((16, width), LOW),
            like((8, layers, rows, 128), LOW),
        ],
        in_specs=[any_, any_, any_, any_, vmem, vmem, vmem, vmem],
        out_specs=[any_, any_, any_, any_, vmem, vmem, vmem, vmem],
        scratch_shapes=[
            pltpu.VMEM((length, width), LOW),
            pltpu.VMEM((8 * rows, slot - least), LOW),
            pltpu.VMEM((rows, 128), LOW),
            DMA, DMA((4,)), DMA((4,)), DMA, DMA((layers - 1,)), DMA((layers - 1,)), DMA((8,)), DMA((8,)),
            DMA((4,)), DMA((8,)), DMA((8,)), DMA((4, 8)), DMA((4, 8)), DMA((4, 8)),
            DMA((6,)), DMA((4, 2, 2)), DMA((4, 2, 2)), DMA((3,)), DMA((8,)), DMA,
        ]
        + GATHER_SEMAPHORES * 2,
        compiler_params=pltpu.CompilerParams(
            collective_id=place, has_side_effects=True, vmem_limit_bytes=VMEM_MOST
        ),
        cost_estimate=pl.CostEstimate(flops=0, bytes_accessed=250_000_000, transcendentals=0),
        name="front",
    )(
        w_mixer, w_gate_up, w_down, w_project, tokens, gain[None], cotangent, w_rates
    )


def scatter_steps(
    terms, out, held, from_core, over_a, over_b, side_x, side_y, core_sent, core_arrived,
    across_sent, across_arrived, sent, arrived
):
    z, y, x, core, over_x, over_y, sibling = neighbours()
    rows = terms.shape[1]
    half, step = rows // 2, 16
    chunks = lambda c: [
        rank_of(1 - y, 1 - x, c), rank_of(y, 1 - x, c), rank_of(1 - y, x, c), rank_of(y, x, c)
    ]
    mine, theirs = chunks(core), chunks(1 - core)
    to_core = [
        remote(terms.at[theirs[i]], from_core.at[i], core_sent.at[i], core_arrived.at[i], sibling)
        for i in range(4)
    ]
    for copy in to_core:
        copy.start()
    yield

    def add(target, at, count, more=None):
        @pl.loop(0, count, step=step)
        def _(r):
            here = pl.ds(pl.multiple_of(at + r, step), step)
            total = terms[mine[target], here, :].astype(WIDE) + from_core[target, here, :].astype(WIDE)
            if more is not None:
                total = total + more[pl.ds(pl.multiple_of(r, step), step), :].astype(WIDE)
            held[target, here, :] = total.astype(LOW)

    top, bottom = pl.ds(0, half), pl.ds(half, half)
    to_core[0].wait_recv()
    add(0, 0, rows)
    top_y = remote(held.at[0, top], over_a, across_sent.at[0], across_arrived.at[0], over_y)
    bottom_x = remote(held.at[0, bottom], over_b, across_sent.at[1], across_arrived.at[1], over_x)
    top_y.start()
    bottom_x.start()
    yield
    to_core[1].wait_recv()
    add(1, half, half)
    x_bottom = remote(held.at[1, bottom], side_x.at[bottom], sent.at[0, 1], arrived.at[0, 1], over_x)
    x_bottom.start()
    to_core[2].wait_recv()
    add(2, 0, half)
    y_top = remote(held.at[2, top], side_y.at[top], sent.at[1, 0], arrived.at[1, 0], over_y)
    y_top.start()
    yield
    top_y.wait_recv()
    add(1, 0, half, over_a)
    x_top = remote(held.at[1, top], side_x.at[top], sent.at[0, 0], arrived.at[0, 0], over_x)
    x_top.start()
    bottom_x.wait_recv()
    add(2, half, half, over_b)
    y_bottom = remote(held.at[2, bottom], side_y.at[bottom], sent.at[1, 1], arrived.at[1, 1], over_y)
    y_bottom.start()
    yield
    to_core[3].wait_recv()
    for copy in (x_bottom, y_top, x_top, y_bottom):
        copy.wait_recv()

    @pl.loop(0, rows, step=step)
    def _(r):
        here = pl.ds(pl.multiple_of(r, step), step)
        out[here, :] = (
            terms[mine[3], here, :].astype(WIDE)
            + from_core[3, here, :].astype(WIDE)
            + (side_x[here, :].astype(WIDE) + side_y[here, :].astype(WIDE))
        )

    for copy in to_core + [top_y, bottom_x, x_bottom, y_top, x_top, y_bottom]:
        copy.wait_send()


def scatter_kernel(*refs):
    greet(neighbours()[4:])
    for _ in scatter_steps(*refs):
        pass


def scatter_scratch(rows, width):
    block = lambda *shape: pltpu.VMEM(shape, LOW)
    return [
        block(3, rows, width),
        block(4, rows, width),
        block(rows // 2, width),
        block(rows // 2, width),
        block(rows, width),
        block(rows, width),
        DMA((4,)),
        DMA((4,)),
        DMA((2,)),
        DMA((2,)),
        DMA((2, 2)),
        DMA((2, 2)),
    ]


def behind(kernel, count):
    return lambda *refs: kernel(*refs[count:])


def plane_scatter(terms, place, after=()):
    rows, width = terms.shape[0] // 8, terms.shape[1]
    return pl.pallas_call(
        behind(scatter_kernel, len(after)),
        out_shape=jax.ShapeDtypeStruct((rows, width), WIDE),
        in_specs=[pl.BlockSpec(memory_space=pl.ANY)] * len(after)
        + [pl.BlockSpec(memory_space=pltpu.VMEM)],
        out_specs=pl.BlockSpec(memory_space=pltpu.VMEM),
        scratch_shapes=scatter_scratch(rows, width),
        compiler_params=pltpu.CompilerParams(
            collective_id=place, has_side_effects=True, vmem_limit_bytes=VMEM_MOST
        ),
        cost_estimate=pl.CostEstimate(flops=0, bytes_accessed=80_000_000, transcendentals=0),
        name="plane_scatter",
    )(*after, terms.reshape(8, rows, width))


def later_terms_kernel(normed, cotangent, swiglu, inner, out):
    both = swiglu.shape[1]
    out[:, :both] = once(normed[...], swiglu[...], TN).astype(LOW)
    out[:, both:] = once(cotangent[...], inner[...], TN).astype(LOW)


def later_terms(normed, cotangent, swiglu, inner):
    tokens, rows = normed.shape
    columns = swiglu.shape[1] + inner.shape[1]
    step = 256
    return pl.pallas_call(
        later_terms_kernel,
        grid=(rows // step,),
        in_specs=[pl.BlockSpec((tokens, step), lambda i: (0, i))] * 2
        + [whole_spec(swiglu.shape), whole_spec(inner.shape)],
        out_specs=rows_spec((step, columns)),
        out_shape=jax.ShapeDtypeStruct((rows, columns), LOW),
        compiler_params=pltpu.CompilerParams(vmem_limit_bytes=VMEM_MOST),
        cost_estimate=cost(2 * tokens * rows * columns, 2e7),
        name="later_terms",
    )(normed, cotangent, swiglu, inner)


def mixer_terms_kernel(gated, branch, normed, mixed, out, project):
    step = pl.program_id(0)
    layers, columns = pl.num_programs(0), mixed.shape[1]
    rows = normed.shape[1]
    few = project.shape[0] // layers

    @pl.when(step == 0)
    def _():
        project[...] = once(gated[...], branch[...], TN).astype(LOW)

    out[0, :rows, :] = once(normed[...], mixed[...], TN).astype(LOW)
    here = pl.ds(pl.multiple_of(step * few, few), few)
    for half in range(2):
        out[0, rows + half * few : rows + (half + 1) * few, :] = project[
            here, half * columns : (half + 1) * columns
        ]


def mixer_terms(gated, branch, normed, mixed, after=()):
    tokens, rows = normed.shape
    columns = mixed.shape[1]
    layers = lax.axis_size("z")
    few = gated.shape[1] // layers
    share = rows // layers + 2 * few
    return pl.pallas_call(
        behind(mixer_terms_kernel, len(after)),
        grid=(layers,),
        in_specs=[pl.BlockSpec(memory_space=pl.ANY)] * len(after)
        + [
            whole_spec(gated.shape),
            whole_spec(branch.shape),
            pl.BlockSpec((tokens, rows // layers), lambda i: (0, i)),
            whole_spec(mixed.shape),
        ],
        out_specs=pl.BlockSpec((1, share, columns), lambda i: (i, 0, 0)),
        out_shape=jax.ShapeDtypeStruct((layers, share, columns), LOW),
        scratch_shapes=[pltpu.VMEM((gated.shape[1], branch.shape[1]), LOW)],
        compiler_params=pltpu.CompilerParams(vmem_limit_bytes=VMEM_MOST),
        cost_estimate=cost(2 * tokens * rows * columns, 2e7),
        name="mixer_terms",
    )(*after, gated, branch, normed, mixed)


def chain_kernel(reverse, whole, term, out, arriving, leaving, sent, arrived):
    z, y, x, core = (lax.axis_index(name) for name in ALL)
    layers = lax.axis_size("z")
    at = layers - 1 - z if reverse else z
    nearer = jnp.clip(z + (1 if reverse else -1), 0, layers - 1)
    further = jnp.clip(z + (-1 if reverse else 1), 0, layers - 1)
    barrier = pltpu.get_barrier_semaphore()

    @pl.when(at > 0)
    def _():
        pl.semaphore_signal(barrier, inc=1, device_id=(nearer, y, x, core), device_id_type=MESH)

    copy = remote(leaving, arriving, sent, arrived, (further, y, x, core))
    size = out.shape[1]
    factor = whole.at[:, :size]
    if not reverse:
        term = whole.at[:, size:]

    @pl.when(at == 0)
    def _():
        out[...] = jnp.zeros_like(out)
        leaving[...] = term[...].astype(LOW)

    @pl.when(at > 0)
    def _():
        copy.wait_recv()
        out[...] = arriving[...].astype(WIDE)

    @pl.when((at > 0) & (at < layers - 1))
    def _():
        for h in range(2):
            rows = slice(h * 128, (h + 1) * 128)
            moved = thrice(factor[rows, :], out[rows, :], TN if reverse else NN)
            leaving[rows, :] = (moved + term[rows, :]).astype(LOW)

    @pl.when(at < layers - 1)
    def _():
        pl.semaphore_wait(barrier, 1)
        copy.start()
        copy.wait_send()


def chain(whole, term, reverse, place):
    shape = (whole.shape[0], whole.shape[1] // 2)
    return pl.pallas_call(
        partial(chain_kernel, reverse),
        out_shape=jax.ShapeDtypeStruct(shape, WIDE),
        in_specs=[pl.BlockSpec(memory_space=pltpu.VMEM)] * 2,
        out_specs=pl.BlockSpec(memory_space=pltpu.VMEM),
        scratch_shapes=[pltpu.VMEM(shape, LOW), pltpu.VMEM(shape, LOW), DMA, DMA],
        compiler_params=pltpu.CompilerParams(
            collective_id=place, has_side_effects=True, vmem_limit_bytes=VMEM_MOST
        ),
        cost_estimate=pl.CostEstimate(flops=0, bytes_accessed=40_000_000, transcendentals=0),
        name="chain",
    )(whole, term)


def later_back_steps(sums_a, sums_b, gate_up, down, own_sem, sent, arrived):
    z, y, x, core, over_x, over_y, sibling = neighbours()
    rows, hidden = down.shape
    per_chip = hidden // 4
    me = rank_of(y, x, core)
    flips = [(k >> 2, (k >> 1) & 1, k & 1) for k in range(8)]
    devices = [(z, turned(y, a), turned(x, b), turned(core, c)) for a, b, c in flips]
    ranks = [rank_of(*device[1:]) for device in devices]

    def parts(rank, t):
        chip = y * 2 + x
        here = pl.ds(pl.multiple_of(rank * rows, rows), rows)
        found = []
        for half, sums in enumerate((sums_a, sums_b)):
            begin, size, slot = units_of(hidden, t, half)
            first = pl.multiple_of(chip * per_chip + begin, 128)
            up = pl.multiple_of(hidden + first, 128)
            found += [
                (sums.at[here, pl.ds(0, size)], gate_up.at[:, pl.ds(first, size)]),
                (sums.at[here, pl.ds(slot, size)], gate_up.at[:, pl.ds(up, size)]),
                (sums.at[here, pl.ds(2 * slot, size)], down.at[:, pl.ds(first, size)]),
            ]
        return found

    def amount(t):
        return [
            down.at[:, pl.ds(0, 3 * units_of(hidden, t, half)[1])] for half in range(2)
        ]

    for t in range(2):

        @pl.when(core == t)
        def _():
            for k in (2, 4, 6, 3, 5, 7, 1):
                for i, (source, target) in enumerate(parts(ranks[k], t)):
                    remote(
                        source, target, sent.at[k, i // 3], arrived.at[k, i // 3], devices[k]
                    ).start()
            for i, (source, target) in enumerate(parts(me, t)):
                pltpu.make_async_copy(source, target, own_sem.at[i]).start()

    yield
    for t in range(2):

        @pl.when(core == t)
        def _():
            for i, (source, target) in enumerate(parts(me, t)):
                pltpu.make_async_copy(source, target, own_sem.at[i]).wait()

    for k in range(1, 8):
        for t in range(2):
            @pl.when(turned(core, k & 1) == t)
            def _():
                for half, place in enumerate(amount(t)):
                    remote(
                        place, place, sent.at[k, half], arrived.at[k, half], devices[k]
                    ).wait_recv()

            @pl.when(core == t)
            def _():
                for half, place in enumerate(amount(t)):
                    remote(
                        place, place, sent.at[k, half], arrived.at[k, half], devices[k]
                    ).wait_send()


def project_steps(sums, out, own_sem, sent, arrived):
    z, y, x, core, over_x, over_y, sibling = neighbours()
    rows, width = out.shape
    me = rank_of(y, x, core)
    owner = (me // 2, lax.rem(me, 2), z // 2, lax.rem(z, 2))
    keeps = (me == 2 * z + y) & (z == 2 * x + core)
    halves_ = [
        (
            sums.at[pl.ds((8 + part) * rows, rows)],
            out.at[:, pl.ds(part * width // 2, width // 2)],
        )
        for part in range(2)
    ]

    @pl.when(jnp.logical_not(keeps))
    def _():
        for source, target in halves_:
            remote(source, target, sent, arrived, owner).start()

    @pl.when(keeps)
    def _():
        for i, (source, target) in enumerate(halves_):
            pltpu.make_async_copy(source, target, own_sem.at[i]).start()

    yield
    yield

    @pl.when(jnp.logical_not(keeps))
    def _():
        remote(out, out, sent, arrived, owner).wait()

    @pl.when(keeps)
    def _():
        for i, (source, target) in enumerate(halves_):
            pltpu.make_async_copy(source, target, own_sem.at[i]).wait()


def small_steps(small, layers_in, gathered, z_sent, z_arrived, sent, arrived):
    z, y, x, core, over_x, over_y, sibling = neighbours()
    layers = layers_in.shape[0]
    me = rank_of(y, x, core)
    flips = [(k >> 2, (k >> 1) & 1, k & 1) for k in range(8)]
    devices = [(z, turned(y, a), turned(x, b), turned(core, c)) for a, b, c in flips]
    ranks = [rank_of(*device[1:]) for device in devices]
    to_layers = [
        remote(
            small, layers_in.at[z], z_sent.at[k], z_arrived.at[k], (lax.rem(z + k, layers), y, x, core)
        )
        for k in range(1, layers)
    ]
    for copy in to_layers:
        copy.start()
    layers_in[z] = small[...]
    yield
    for copy in to_layers:
        copy.wait_recv()
    total = layers_in[0]
    for k in range(1, layers):
        total = total + layers_in[k]
    gathered[me] = total
    spread = [
        remote(gathered.at[me], gathered.at[me], sent.at[k], arrived.at[k], devices[k])
        for k in range(1, 8)
    ]
    for copy in spread:
        copy.start()
    yield
    for k in range(1, 8):
        place = gathered.at[ranks[k]]
        remote(place, place, sent.at[k], arrived.at[k], devices[k]).wait_recv()
    for copy in to_layers + spread:
        copy.wait_send()


def small_scratch(shape, layers):
    return [
        pltpu.VMEM(shape, WIDE),
        pltpu.VMEM((layers,) + shape, WIDE),
        pltpu.VMEM((8,) + shape, WIDE),
        DMA((layers,)),
        DMA((layers,)),
        DMA((8,)),
        DMA((8,)),
    ]


def together(running):
    while running:
        for steps in list(running):
            if next(steps, running) is running:
                running.remove(steps)


def others_of(z, y, x, core):
    flips = [(k >> 2, (k >> 1) & 1, k & 1) for k in range(1, 8)]
    layers = lax.axis_size("z")
    return [(z, turned(y, a), turned(x, b), turned(core, c)) for a, b, c in flips] + [
        (lax.rem(z + k, layers), y, x, core) for k in range(1, layers)
    ]


def return_all_kernel(
    terms_a, terms_b, sums_a, sums_b, grad_kernel, decays, head_gain, gain_mlp, rate_terms,
    out_a, out_b, gate_up, down, all_kernel, all_decays, all_head, all_mlp, all_rates, *rest
):
    z, y, x, core, over_x, over_y, sibling = neighbours()
    barrier = pltpu.get_barrier_semaphore()
    others = others_of(z, y, x, core)
    for other in others:
        pl.semaphore_signal(barrier, inc=1, device_id=other, device_id_type=MESH)
    small, gathered = rest[0], rest[2]
    high = 6 * 128
    wide = 256
    small[...] = jnp.zeros_like(small)
    small[0:4, :high] = grad_kernel[0:4, :]
    small[0:1, high : high + 128] = decays[0:1, :]
    small[0:1, high + 128 :] = decays[1:2, :]
    small[1:2, high : high + 128] = head_gain[0:1, :]
    small[4:6, :] = gain_mlp[...]
    half = small.shape[1]
    small[8:12, :] = rate_terms[0:4, :half]
    small[12:16, :] = rate_terms[0:4, half:]
    pl.semaphore_wait(barrier, len(others))
    scratch = rest[7:]
    count = (len(scratch) - 3) // 2
    together([
        scatter_steps(terms_a, out_a, *scratch[:count]),
        scatter_steps(terms_b, out_b, *scratch[count : 2 * count]),
        later_back_steps(sums_a, sums_b, gate_up, down, *scratch[2 * count :]),
        small_steps(*rest[:7]),
    ])
    whole = gathered[0]
    for r in range(8):
        for part in range(3):
            all_kernel[0:4, part * 8 * wide + r * wide : part * 8 * wide + (r + 1) * wide] = (
                gathered[r, 0:4, part * wide : (part + 1) * wide]
            )
        all_decays[r : r + 1, :] = gathered[r, 0:1, high:]
        all_rates[r] = gathered[r, 8:16, :]
        if r:
            whole = whole + gathered[r]
    all_head[...] = whole[1:2, high : high + 128]
    all_mlp[...] = whole[4:6, :]


def return_all(terms_a, terms_b, sums_a, sums_b, smalls, hidden, place, after=()):
    rows, width = terms_a.shape[0] // 8, terms_a.shape[1]
    owned = sums_a.shape[0] // 8
    layers = lax.axis_size("z")
    any_, vmem = pl.BlockSpec(memory_space=pl.ANY), pl.BlockSpec(memory_space=pltpu.VMEM)
    like = jax.ShapeDtypeStruct
    return pl.pallas_call(
        behind(return_all_kernel, len(after)),
        out_shape=[
            like((rows, width), WIDE),
            like((rows, width), WIDE),
            like((owned, 2 * hidden), LOW),
            like((owned, hidden), LOW),
            like((4, 6 * 1024), WIDE),
            like((8, 256), WIDE),
            like((1, 128), WIDE),
            like((2, 1024), WIDE),
            like((8, 8, 1024), WIDE),
        ],
        in_specs=[any_] * len(after) + [vmem, vmem, any_, any_] + [vmem] * 5,
        out_specs=[vmem, vmem, any_, any_] + [vmem] * 5,
        scratch_shapes=small_scratch((16, 1024), layers)
        + scatter_scratch(rows, width) * 2
        + [DMA((6,)), DMA((8, 2)), DMA((8, 2))],
        compiler_params=pltpu.CompilerParams(
            collective_id=place, has_side_effects=True, vmem_limit_bytes=VMEM_MOST
        ),
        cost_estimate=pl.CostEstimate(flops=0, bytes_accessed=200_000_000, transcendentals=0),
        name="return_all",
    )(
        *after, terms_a.reshape(8, rows, width), terms_b.reshape(8, rows, width), sums_a, sums_b,
        *smalls
    )


def mixer_back_steps(sums, mixer, own_sem, sent, arrived):
    z, y, x, core, over_x, over_y, sibling = neighbours()
    rows, columns = mixer.shape
    wide, width = columns // 32, columns // 4
    me = rank_of(y, x, core)
    flips = [(k >> 2, (k >> 1) & 1, k & 1) for k in range(8)]
    devices = [(z, turned(y, a), turned(x, b), turned(core, c)) for a, b, c in flips]
    ranks = [rank_of(*device[1:]) for device in devices]

    def parts(rank):
        here = pl.ds(pl.multiple_of(rank * rows, rows), rows)
        return [
            (
                sums.at[here, pl.ds(p * wide, wide)],
                mixer.at[:, pl.ds(pl.multiple_of(p * width + me * wide, 128), wide)],
            )
            for p in range(4)
        ]

    for k in (2, 4, 6, 3, 5, 7, 1):
        for source, target in parts(ranks[k]):
            remote(source, target, sent.at[k], arrived.at[k], devices[k]).start()
    owns = [
        pltpu.make_async_copy(source, target, own_sem.at[i])
        for i, (source, target) in enumerate(parts(me))
    ]
    for copy in owns:
        copy.start()
    yield
    yield
    for copy in owns:
        copy.wait()
    place = mixer.at[:, pl.ds(0, 4 * wide)]
    for k in range(1, 8):
        remote(place, place, sent.at[k], arrived.at[k], devices[k]).wait()


def last_kernel(sums, gain_mixer, mixer, project, all_mixer, *rest):
    z, y, x, core, over_x, over_y, sibling = neighbours()
    small, gathered = rest[0], rest[2]
    barrier = pltpu.get_barrier_semaphore()
    others = others_of(z, y, x, core)
    for other in others:
        pl.semaphore_signal(barrier, inc=1, device_id=other, device_id_type=MESH)
    me, source = rank_of(y, x, core), 2 * z + y
    keeps = (me == source) & (z == 2 * x + core)
    holder = (2 * x + core, source // 4, lax.rem(source // 2, 2), lax.rem(source, 2))

    @pl.when(jnp.logical_not(keeps))
    def _():
        pl.semaphore_signal(barrier, inc=1, device_id=holder, device_id_type=MESH)

    small[...] = gain_mixer[...]
    pl.semaphore_wait(barrier, len(others) + jnp.where(keeps, 0, 1))
    together([
        project_steps(sums, project, *rest[7:10]),
        small_steps(*rest[:7]),
        mixer_back_steps(sums, mixer, *rest[10:]),
    ])
    total = gathered[0]
    for r in range(1, 8):
        total = total + gathered[r]
    all_mixer[...] = total


def last(sums, rows, gain_mixer, place, after=()):
    columns = sums.shape[1]
    layers = lax.axis_size("z")
    any_, vmem = pl.BlockSpec(memory_space=pl.ANY), pl.BlockSpec(memory_space=pltpu.VMEM)
    like = jax.ShapeDtypeStruct
    return pl.pallas_call(
        behind(last_kernel, len(after)),
        out_shape=[
            like((rows, 8 * columns), LOW),
            like((rows, 2 * columns), LOW),
            like(gain_mixer.shape, WIDE),
        ],
        in_specs=[any_] * (len(after) + 1) + [vmem],
        out_specs=[any_, any_, vmem],
        scratch_shapes=small_scratch(gain_mixer.shape, layers)
        + [DMA((2,)), DMA, DMA, DMA((4,)), DMA((8,)), DMA((8,))],
        compiler_params=pltpu.CompilerParams(
            collective_id=place, has_side_effects=True, vmem_limit_bytes=VMEM_MOST
        ),
        cost_estimate=pl.CostEstimate(flops=0, bytes_accessed=60_000_000, transcendentals=0),
        name="last",
    )(*after, sums, gain_mixer)


def heads_on_plane(
    tokens,
    w_mixer,
    w_rates,
    w_project,
    w_gate_up,
    w_down,
    conv_kernel,
    decay_log,
    decay_bias,
    head_gain,
    gain_mixer,
    gain_mlp,
    cotangent,
):
    length, width = tokens.shape
    size = head_gain.shape[0]
    rows = w_mixer.shape[0]
    hidden = w_down.shape[1]
    layers = lax.axis_size("z")
    ranks = lax.axis_size(ALL) // layers
    own = decay_log.shape[0] // ranks
    layer, rank = lax.axis_index("z"), lax.axis_index(PLANE)
    low = jnp.bfloat16
    wide = own * size

    def over_layers(terms):
        return lax.psum_scatter(terms, "z", scatter_dimension=0, tiled=True)

    gather = plane_gather

    def scatter(terms, place, after=()):
        return plane_scatter(terms.astype(low), place, after)

    source = tokens.astype(jnp.float32)
    norm_pull = jax.vjp(norm_scale, source, gain_mixer)[1]
    mixer, later_a, later_b, project, normed_all, cotangent_all, tail, all_rates = front(
        w_mixer, w_gate_up, w_down, w_project, w_rates, tokens, gain_mixer, cotangent, 1
    )
    total = length * ranks
    normed_all = normed_all.reshape(total, width)
    cotangent_all = cotangent_all.reshape(total, width)
    later_a = lax.all_gather(later_a, "z", axis=0, tiled=True)
    later_b = lax.all_gather(later_b, "z", axis=0, tiled=True)
    slot = later_a.shape[1] // 3
    all_rates = jnp.swapaxes(all_rates, 0, 1).reshape(width, 128)
    head_at = jnp.arange(2 * own) // own * (ranks * own) + jnp.arange(2 * own) % own + rank * own
    pick = jnp.pad(
        jax.nn.one_hot(head_at, 128, axis=0, dtype=low), ((0, 0), (0, 128 - 2 * own))
    )
    kernel = lax.dynamic_index_in_dim(
        conv_kernel.reshape(4, 3, ranks, wide), rank, 2, False
    ).reshape(4, 3 * wide)
    kernel = jnp.pad(kernel, ((0, 4), (0, 0)))
    log_rate = lax.dynamic_slice_in_dim(decay_log, rank * own, own)
    bias = lax.dynamic_slice_in_dim(decay_bias, rank * own, own)

    downward = [(z + 1, z) for z in range(layers - 1)]
    head_gains = jnp.broadcast_to(head_gain, (8, size))
    pads = ((0, 7), (2, 124))
    rates = jnp.pad(-jnp.exp(log_rate)[None], pads) + jnp.roll(jnp.pad(bias[None], pads), 1, 0)
    (
        mixed_low, gates, rate_in, ue, inverse, scores, steps, before, qk, columns, whole, rate_weight
    ) = prepare(normed_all, mixer, all_rates, pick, tail, kernel, rates)
    start = chain(whole, whole, False, 7)
    branch, gated_low, fresh, states, outputs = finish(
        start, before, ue, scores, qk, columns, gates, head_gains, project
    )
    hidden_state = source + scatter(branch, 2)
    normed_two, norm_two_pull = jax.vjp(norm_scale, hidden_state, gain_mlp)
    normed_two_all = gather(normed_two.astype(low), 3)
    inners, sums_of, back_terms = [], [], 0.0
    for weights in (later_a, later_b):
        gate_up_weight, down_weight = weights[:, : 2 * slot], weights[:, 2 * slot :]
        inner_act, inner_pull = jax.vjp(swiglu, dot_bf16(normed_two_all, gate_up_weight))
        inner_low = inner_act.astype(low)
        grad_inner = dot_bf16(cotangent_all, down_weight)
        grad_swiglu = inner_pull(grad_inner)[0].astype(low)
        sums_of.append(
            over_layers(later_terms(normed_two_all, cotangent_all, grad_swiglu, inner_low))
        )
        back_terms = back_terms + dot_nt(grad_swiglu, gate_up_weight)
        inners.append((inner_low, down_weight))
    later_sum_a, later_sum_b = sums_of
    grad_hidden_part, grad_gain_mlp = norm_two_pull(scatter(back_terms, 5))
    grad_hidden = cotangent.astype(jnp.float32) + grad_hidden_part
    grad_branch = gather(grad_hidden.astype(low), 6)
    grad_out, back_scores, returns, grad_gate, local, grad_head_gain = give_back(
        grad_branch, project, gates, head_gains, outputs, scores, ue, qk, columns, steps
    )
    end = chain(whole, local, True, 8)
    grad_mixed, grad_rates, grad_kernel, sums, first_rows, edge = gradients(
        end, returns, steps, grad_out, back_scores, fresh, states, inverse, scores, qk, columns,
        mixed_low, rate_in, grad_gate, kernel, rates, (later_sum_a,)
    )
    following = lax.ppermute(first_rows[:3].astype(low), "z", downward).astype(jnp.float32)
    late = [
        sum(kernel[j] * following[r - j] for j in range(r + 1)) for r in range(3)
    ]
    edge = jnp.concatenate([edge[:13], edge[13:] + jnp.stack(late)], 0).astype(low)
    grad_mixed = lax.dynamic_update_slice(grad_mixed, edge, (total - 16, 0))
    terms = mixer_terms(gated_low, grad_branch, normed_all, grad_mixed)
    rate_terms = dot_tn(grad_rates, normed_all)
    mixer_sum = lax.psum_scatter(terms, "z", scatter_dimension=0)
    source_terms = dot_nt(grad_mixed, mixer) + dot_nt(grad_rates, rate_weight)
    out_terms = sum(dot_nt(*pair) for pair in inners)
    smalls = (grad_kernel, sums, grad_head_gain, grad_gain_mlp.reshape(2, -1), rate_terms)
    (
        from_source, from_inner, grad_gate_up, grad_down, grad_kernel, decays,
        grad_head_gain, grad_gain_mlp, rate_sums
    ) = return_all(
        source_terms.astype(low), out_terms.astype(low), later_sum_a, later_sum_b, smalls, hidden,
        10, (terms,)
    )
    grad_source, grad_gain_mixer = norm_pull(from_source)
    grad_tokens = (grad_hidden + grad_source).astype(low)
    result = (hidden_state + from_inner).astype(low)
    grad_gate_up, grad_down = grad_gate_up.astype(jnp.float32), grad_down.astype(jnp.float32)
    rate_sums = jnp.swapaxes(rate_sums.reshape(ranks, 2, 2 * own, -1, rows), 1, 2)
    rate_sums = rate_sums.reshape(ranks, 2, own, -1, rows)
    grad_rates = lax.dynamic_index_in_dim(rate_sums, layer * ranks + rank, 3, False)
    grad_rates = jnp.transpose(grad_rates, (3, 1, 0, 2)).reshape(rows, -1)
    grad_mixer, grad_project, grad_gain_mixer = last(
        mixer_sum, rows, grad_gain_mixer.reshape(8, -1), 11,
        (grad_gate_up, grad_down, result, grad_tokens, grad_rates),
    )
    return (
        result,
        grad_tokens,
        grad_mixer.astype(jnp.float32),
        grad_rates,
        grad_project.astype(jnp.float32),
        grad_gate_up,
        grad_down,
        grad_kernel,
        decays[:, 128 + own : 128 + 2 * own].reshape(-1),
        decays[:, own : 2 * own].reshape(-1),
        grad_head_gain[0],
        grad_gain_mixer.reshape(-1),
        grad_gain_mlp.reshape(-1),
    )


def by_planes(mesh, members):
    seq, core = mesh.shape["seq"], mesh.shape["fsdp"]
    layers, ranks = seq // 4, 4 * core
    heads, size = members[7].shape[0], members[9].shape[0]
    return (
        core == 2
        and layers == 4
        and members[0].shape[0] == seq * core * size
        and heads % ranks == 0
        and members[5].shape[1] % (4 * 128) == 0
    )


def solution(mesh):
    rows, copied = P(("seq", "fsdp"), None), P()

    def run(*members):
        if by_planes(mesh, members):
            places = Mesh(mesh.devices.reshape(-1, 2, 2, 2), ALL)
            split, body = P(ALL, None), heads_on_plane
        else:
            places, split, body = mesh, rows, on_device
        return jax.shard_map(
            body,
            mesh=places,
            in_specs=(split,) * 6 + (copied,) * 6 + (split,),
            out_specs=(split,) * 7 + (copied,) * 6,
            check_vma=False,
        )(*members)

    return run
```

```python
from functools import partial

import jax
import jax.numpy as jnp
from jax import lax
from jax.experimental import pallas as pl
from jax.experimental.pallas import tpu as pltpu
from jax.sharding import Mesh
from jax.sharding import PartitionSpec as P

BLOCK = 64


highest = lax.Precision.HIGHEST


def shifted(value, axis, by):
    length = lax.axis_size(axis)
    pairs = [(i, i + by) for i in range(length) if 0 <= i + by < length]
    return lax.ppermute(value, axis, pairs)


def prefix_2(value, axis, join, neutral):
    place = lax.axis_index(axis)
    gathered = jax.tree.map(
        lambda a, kind: lax.all_gather(a.astype(kind), axis), value, (jnp.bfloat16, jnp.bfloat16)
    )
    state = jax.tree.map(lambda a, e: jnp.zeros_like(a) + jnp.asarray(e, a.dtype), value, neutral)

    def one(turn, state):
        return join(
            state,
            jax.tree.map(
                lambda a, own: lax.dynamic_index_in_dim(a, turn, 0, False).astype(own.dtype),
                gathered,
                value,
            ),
        )

    return lax.fori_loop(0, place, one, state)


def entering(value, axis, combine, identity):
    length, place = (lax.axis_size(axis), lax.axis_index(axis))
    everything = jax.tree.map(
        lambda part, kind: lax.all_gather(part.astype(kind), axis),
        value,
        jax.tree.map(lambda a: jnp.bfloat16 if a.dtype == jnp.float32 else a.dtype, value),
    )
    start = jax.tree.map(
        lambda part, zero: jnp.broadcast_to(jnp.asarray(zero, part.dtype), part.shape),
        value,
        identity,
    )

    def turn(k, before):
        at = length - 1 - k
        reached = at > place
        new = combine(
            before, jax.tree.map(lambda part, own: part[at].astype(own.dtype), everything, value)
        )
        return jax.tree.map(lambda a, b: jnp.where(reached, a, b), new, before)

    return lax.fori_loop(0, length, turn, start)


def round_trip(values_in):
    return lax.optimization_barrier(values_in.astype(jnp.bfloat16)).astype(jnp.float32)


def norm_scale(values_in, scales):
    return (
        values_in
        * lax.rsqrt(jnp.mean(values_in * values_in, axis=-1, keepdims=True) + 1e-06)
        * scales
    )


def features(extended, kernel, head_count):
    length = extended.shape[0] - 3
    summed = kernel[0] * extended[0:length]
    for offset in range(1, 4):
        summed = summed + kernel[offset] * extended[offset : offset + length]
    active = jax.nn.silu(summed)
    model_width = active.shape[1] // 3

    def unit_rows(member):
        shaped = member.reshape(length, head_count, -1)
        return shaped * lax.rsqrt(jnp.sum(shaped * shaped, axis=-1, keepdims=True) + 1e-06)

    queries = unit_rows(active[:, :model_width])
    queries = queries * queries.shape[-1] ** (-0.5)
    keys_all = unit_rows(active[:, model_width : 2 * model_width])
    values_all = active[:, 2 * model_width :].reshape(length, head_count, -1)
    return (queries, keys_all, values_all)


def rates_of(rate_inputs, decay_log, decay_bias):
    head_count = decay_log.shape[0]
    strength = jax.nn.sigmoid(rate_inputs[:, :head_count])
    decays = -jnp.exp(decay_log) * jax.nn.softplus(rate_inputs[:, head_count:] + decay_bias)
    return (strength, decays)


def head_output(outputs, gate_part, head_gain):
    normed_heads = (
        outputs * lax.rsqrt(jnp.mean(outputs * outputs, axis=-1, keepdims=True) + 1e-05) * head_gain
    )
    return normed_heads.reshape(outputs.shape[0], -1) * jax.nn.silu(gate_part)


def swiglu(gate_up):
    half_width = gate_up.shape[1] // 2
    return jax.nn.silu(gate_up[:, :half_width]) * gate_up[:, half_width:]


def to_blocks(member):
    block_count = member.shape[0] // BLOCK
    shaped = member.reshape((block_count, BLOCK) + member.shape[1:])
    return jnp.moveaxis(shaped, 2, 1)


def from_blocks(member):
    shaped = jnp.moveaxis(member, 1, 2)
    return shaped.reshape((-1,) + shaped.shape[2:])


def unit_pair(head_count, head_size):
    identity_matrix = jnp.eye(head_size, dtype=jnp.float32)
    return (
        jnp.broadcast_to(identity_matrix, (head_count, head_size, head_size)),
        jnp.zeros((head_count, head_size, head_size), jnp.float32),
    )


def combine(earlier, later):
    product = jnp.einsum("hab,hbc->hac", earlier[0], later[0], precision=highest)
    carried = jnp.einsum("hab,hbc->hac", earlier[1], later[0], precision=highest) + later[1]
    return (product, carried)


def block_terms(query_block, key_block, value_block, strength_block, decay_block):
    block_size = key_block.shape[1]
    lower_ones = jnp.tril(jnp.ones((block_size, block_size), jnp.float32))
    cumulative = jnp.einsum("hd,cd->hc", decay_block, lower_ones, precision=highest)
    positions = jnp.arange(block_size)
    causal = positions[:, None] >= positions[None, :]
    strict = positions[:, None] > positions[None, :]
    spread = cumulative[:, :, None] - cumulative[:, None, :]
    ratios = jnp.where(causal, jnp.exp(jnp.where(causal, spread, 0.0)), 0.0)
    key_products = jnp.einsum("hcd,hed->hce", key_block, key_block, precision=highest)
    lower_part = jnp.where(strict, strength_block[:, :, None] * ratios * key_products, 0.0)
    system = lower_part + jnp.eye(block_size, dtype=jnp.float32)
    gammas = jnp.exp(cumulative)
    updates = lax.linalg.triangular_solve(
        system,
        strength_block[:, :, None] * value_block,
        left_side=True,
        lower=True,
        unit_diagonal=True,
    )
    erasers = lax.linalg.triangular_solve(
        system,
        (strength_block * gammas)[:, :, None] * key_block,
        left_side=True,
        lower=True,
        unit_diagonal=True,
    )
    scores = jnp.einsum("hcd,hed->hce", query_block, key_block, precision=highest) * ratios
    tail_keys = jnp.exp(cumulative[:, -1:] - cumulative)[:, :, None] * key_block
    return (gammas, scores, updates, erasers, tail_keys)


def run_blocks(query_blocks, block_parts, start_state):

    def advance(carried, element):
        query_block, gammas, scores, updates, erasers, tail_keys = element
        fresh_values = updates - jnp.einsum("hcd,hvd->hcv", erasers, carried, precision=highest)
        produced = gammas[:, :, None] * jnp.einsum(
            "hcd,hvd->hcv", query_block, carried, precision=highest
        )
        produced = produced + jnp.einsum("hce,hev->hcv", scores, fresh_values, precision=highest)
        carried = gammas[:, -1][:, None, None] * carried + jnp.einsum(
            "hcv,hcd->hvd", fresh_values, tail_keys, precision=highest
        )
        return (carried, produced)

    end_state, produced = lax.scan(advance, start_state, (query_blocks,) + tuple(block_parts))
    return (produced, end_state)


def span(query_blocks, key_blocks, value_blocks, strength_blocks, decay_blocks, start_state):
    block_parts = jax.vmap(block_terms)(
        query_blocks, key_blocks, value_blocks, strength_blocks, decay_blocks
    )
    return run_blocks(query_blocks, block_parts, start_state)


def block_maps(block_parts, head_size):
    gammas, scores, updates, erasers, tail_keys = block_parts
    identity_matrix = jnp.eye(head_size, dtype=jnp.float32)
    transitions = gammas[:, :, -1][:, :, None, None] * identity_matrix - jnp.einsum(
        "nhcd,nhce->nhde", erasers, tail_keys, precision=highest
    )
    writes = jnp.einsum("nhcv,nhce->nhve", updates, tail_keys, precision=highest)

    def compose(carried, element):
        return (combine(carried, element), None)

    initial = unit_pair(transitions.shape[1], head_size)
    return lax.scan(compose, initial, (transitions, writes))[0]


def term_rows(left, right, precise):
    if precise:
        return jnp.einsum(
            "tr,tc->rc", left, right, precision=highest, preferred_element_type=jnp.float32
        )
    return jnp.einsum("tr,tc->rc", left, right, preferred_element_type=jnp.float32)


def on_device(
    tokens,
    w_mixer,
    w_rates,
    w_project,
    w_gate_up,
    w_down,
    conv_kernel,
    decay_log,
    decay_bias,
    head_gain,
    gain_mixer,
    gain_mlp,
    cotangent,
):
    length, model_width = tokens.shape
    head_count = decay_log.shape[0]
    head_size = head_gain.shape[0]
    conv_width = 3 * model_width
    full_mixer, full_rates, full_project, full_gate_up, full_down = (
        lax.all_gather(w_mixer, ("seq", "fsdp"), axis=0, tiled=True),
        lax.all_gather(w_rates, ("seq", "fsdp"), axis=0, tiled=True),
        lax.all_gather(w_project, ("seq", "fsdp"), axis=0, tiled=True),
        lax.all_gather(w_gate_up, ("seq", "fsdp"), axis=0, tiled=True),
        lax.all_gather(w_down, ("seq", "fsdp"), axis=0, tiled=True),
    )
    source = tokens.astype(jnp.float32)
    normed, norm_pull = jax.vjp(norm_scale, source, gain_mixer)
    normed_low = normed.astype(jnp.bfloat16)
    mixed_low = jnp.dot(normed_low, full_mixer, preferred_element_type=jnp.float32).astype(
        jnp.bfloat16
    )
    rate_inputs = jnp.dot(normed_low, full_rates, preferred_element_type=jnp.float32)
    previous = shifted(mixed_low[length - 3 :, :conv_width], ("seq", "fsdp"), 1)
    extended = jnp.concatenate([previous, mixed_low[:, :conv_width]], 0).astype(jnp.float32)
    triple, feature_pull = jax.vjp(partial(features, head_count=head_count), extended, conv_kernel)
    queries, keys_all, values_all = (round_trip(member) for member in triple)
    (strength, decays), rate_pull = jax.vjp(rates_of, rate_inputs, decay_log, decay_bias)
    blocks = tuple(
        (to_blocks(member) for member in (queries, keys_all, values_all, strength, decays))
    )
    block_parts = jax.vmap(block_terms)(*blocks)
    span_trans, span_writes = block_maps(block_parts, head_size)
    identity = unit_pair(head_count, head_size)
    prefix = prefix_2((span_trans, span_writes), ("seq", "fsdp"), combine, identity)
    start_state = prefix[1]
    output_blocks = run_blocks(blocks[0], block_parts, start_state)[0]
    outputs = from_blocks(output_blocks)
    gate_part = mixed_low[:, conv_width:].astype(jnp.float32)
    gated, head_pull = jax.vjp(head_output, outputs, gate_part, head_gain)
    gated_low = gated.astype(jnp.bfloat16)
    hidden_state = source + jnp.dot(gated_low, full_project, preferred_element_type=jnp.float32)
    normed_two, norm_two_pull = jax.vjp(norm_scale, hidden_state, gain_mlp)
    normed_two_low = normed_two.astype(jnp.bfloat16)
    gate_up = jnp.dot(normed_two_low, full_gate_up, preferred_element_type=jnp.float32)
    inner_act, inner_pull = jax.vjp(swiglu, gate_up)
    inner_low = inner_act.astype(jnp.bfloat16)
    result = hidden_state + jnp.einsum(
        "tf,df->td", inner_low, full_down, preferred_element_type=jnp.float32
    )
    upstream = cotangent.astype(jnp.float32)
    grad_inner = jnp.dot(cotangent, full_down, preferred_element_type=jnp.float32)
    grad_swiglu_low = inner_pull(grad_inner)[0].astype(jnp.bfloat16)
    grad_normed_two = jnp.einsum(
        "tc,dc->td", grad_swiglu_low, full_gate_up, preferred_element_type=jnp.float32
    )
    grad_hidden_part, grad_gain_mlp = norm_two_pull(grad_normed_two)
    grad_hidden = upstream + grad_hidden_part
    grad_hidden_low = grad_hidden.astype(jnp.bfloat16)
    grad_gated = jnp.einsum(
        "te,de->td", grad_hidden_low, full_project, preferred_element_type=jnp.float32
    )
    grad_outputs, grad_gate, grad_head_gain = head_pull(grad_gated)
    grad_out_blocks = to_blocks(grad_outputs)
    primal_pair, span_pull = jax.vjp(span, *blocks, start_state)
    local_grads = span_pull((grad_out_blocks, jnp.zeros_like(start_state)))
    suffix = entering(
        (jnp.swapaxes(span_trans, 1, 2), local_grads[5]), ("seq", "fsdp"), combine, identity
    )
    later_grads = span_pull((jnp.zeros_like(grad_out_blocks), suffix[1]))
    grad_blocks = [
        from_blocks(front_grad + back_grad)
        for front_grad, back_grad in zip(local_grads[:5], later_grads[:5])
    ]
    grad_triple = tuple((round_trip(member) for member in grad_blocks[:3]))
    grad_extended, grad_kernel = feature_pull(grad_triple)
    grad_inputs, grad_decay_log, grad_decay_bias = rate_pull((grad_blocks[3], grad_blocks[4]))
    following = shifted(grad_extended[:3].astype(jnp.bfloat16), ("seq", "fsdp"), -1).astype(
        jnp.float32
    )
    grad_conv = grad_extended[3:] + jnp.pad(following, ((length - 3, 0), (0, 0)))
    grad_mixed_low = jnp.concatenate([grad_conv, grad_gate], 1).astype(jnp.bfloat16)
    grad_normed = jnp.einsum(
        "tc,dc->td", grad_mixed_low, full_mixer, preferred_element_type=jnp.float32
    )
    grad_normed = grad_normed + jnp.dot(
        grad_inputs, full_rates.astype(jnp.float32).T, precision=highest
    )
    grad_source, grad_gain_mixer = norm_pull(grad_normed)
    grad_tokens = (grad_hidden + grad_source).astype(jnp.bfloat16)
    normed_wide = normed_low.astype(jnp.float32)
    grad_mixer = lax.psum_scatter(
        term_rows(normed_low, grad_mixed_low, False),
        ("seq", "fsdp"),
        scatter_dimension=0,
        tiled=True,
    )
    grad_rates = lax.psum_scatter(
        term_rows(normed_wide, grad_inputs, True), ("seq", "fsdp"), scatter_dimension=0, tiled=True
    )
    grad_project = lax.psum_scatter(
        term_rows(gated_low, grad_hidden_low, False),
        ("seq", "fsdp"),
        scatter_dimension=0,
        tiled=True,
    )
    grad_gate_up = lax.psum_scatter(
        term_rows(normed_two_low, grad_swiglu_low, False),
        ("seq", "fsdp"),
        scatter_dimension=0,
        tiled=True,
    )
    grad_down = lax.psum_scatter(
        term_rows(cotangent, inner_low, False), ("seq", "fsdp"), scatter_dimension=0, tiled=True
    )
    small_sums = lax.psum(
        (
            grad_kernel,
            grad_decay_log,
            grad_decay_bias,
            grad_head_gain,
            grad_gain_mixer,
            grad_gain_mlp,
        ),
        ("seq", "fsdp"),
    )
    return (
        result.astype(jnp.bfloat16),
        grad_tokens,
        grad_mixer,
        grad_rates,
        grad_project,
        grad_gate_up,
        grad_down,
        small_sums[0],
        small_sums[1],
        small_sums[2],
        small_sums[3],
        small_sums[4],
        small_sums[5],
    )


def dot_bf16(left, right):
    return jnp.dot(left, right, preferred_element_type=jnp.float32)


def dot_nt(left, right):
    return lax.dot_general(
        left, right, (((1,), (1,)), ((), ())), preferred_element_type=jnp.float32
    )


def dot_tn(left, right):
    return lax.dot_general(
        left, right, (((0,), (0,)), ((), ())), preferred_element_type=jnp.float32
    )


def exact(left, right, dims=((1,), (0,))):
    return lax.dot_general(
        left, right, (dims, ((), ())), precision=highest, preferred_element_type=jnp.float32
    )


NT = ((1,), (1,))
TN = ((0,), (0,))


PLANE = ("y", "x", "core")
ALL = ("z",) + PLANE


LOW, WIDE = jnp.bfloat16, jnp.float32
NN = ((1,), (0,))
VMEM_MOST = 56 << 20


def once(left, right, dims=NN):
    return lax.dot_general(
        left.astype(LOW), right.astype(LOW), (dims, ((), ())), preferred_element_type=WIDE
    )


def halves(value):
    high = value.astype(LOW)
    return high, (value - high.astype(WIDE)).astype(LOW)


def thrice(left, right, dims=NN):
    if not isinstance(left, tuple):
        left = halves(left)
    if not isinstance(right, tuple):
        right = halves(right)
    return (
        once(left[0], right[0], dims) + once(left[0], right[1], dims) + once(left[1], right[0], dims)
    )


def pair_rows(first, second):
    return jnp.concatenate([first, second], 0)


def pair_diagonal(first, second):
    zero = jnp.zeros_like(first)
    return pair_rows(
        jnp.concatenate([first, zero], 1), jnp.concatenate([zero, second], 1)
    )


def square_iotas(size):
    return (
        lax.broadcasted_iota(jnp.int32, (size, size), 0),
        lax.broadcasted_iota(jnp.int32, (size, size), 1),
    )


def decay_ratios(column, row, causal):
    return jnp.where(causal, jnp.exp(jnp.minimum(column - row, 0.0)), 0.0)


def inverses(lowers, differ):
    size = lowers[0].shape[0]
    results = [
        jnp.where(differ == 0, 1.0, 0.0) - jnp.where(differ == 1, lower, 0.0) for lower in lowers
    ]
    for level in range(1, 7):
        parts = [halves(result) for result in results]
        below = [jnp.where((differ >> level) == 1, lower, 0.0) for lower in lowers]
        inner = [thrice(b, p) for b, p in zip(below, parts)]
        results = [r - thrice(p, i) for r, p, i in zip(results, parts, inner)]
    return results


def silu_unit(summed):
    active = summed * jax.nn.sigmoid(summed)
    scale = lax.rsqrt(jnp.sum(active * active, axis=-1, keepdims=True) + 1e-06)
    return active, scale


def conv_of(ext, kernel, column, offset, count):
    at = pl.ds(column, 128)
    summed = kernel[0:1, at] * ext[pl.ds(offset, count), at]
    for j in range(1, 4):
        summed = summed + kernel[j : j + 1, at] * ext[pl.ds(offset + j, count), at]
    return summed


def softplus(value):
    return jnp.maximum(value, 0.0) + jnp.log1p(jnp.exp(-jnp.abs(value)))


def prepare_kernel(
    normed, mixer, all_rates, pick, tail, kernel, rates, mixed, gates, rate_in, ue, inverse, scores, steps, before,
    qk, columns, total, rate_weight, ext, carry
):
    step = pl.program_id(0)
    size = 128
    span = normed.shape[0]
    count = span // size
    conv = 6 * size

    @pl.when(step == 0)
    def _():
        rate_weight[...] = once(all_rates[...], pick[...]).astype(LOW)
        first = once(tail[...], mixer[...])
        low = first.astype(LOW)
        mixed[pl.ds(0, 16), :] = low[:, :conv]
        ext[pl.ds(0, 8), :] = low.astype(WIDE)[8:16, :conv]
        rows, cols = square_iotas(size)
        one = jnp.where(rows == cols, 1.0, 0.0)
        zero = jnp.zeros_like(one)
        carry[...] = pair_rows(
            jnp.concatenate([one, zero], 1), jnp.concatenate([one, zero], 1)
        )

    products = once(normed[...], mixer[...])
    low = products.astype(LOW)
    mixed[pl.ds(pl.multiple_of(16 + step * span, 16), span), :] = low[:, :conv]
    gates[...] = low[:, conv:]
    ext[pl.ds(8, span), :] = low[:, :conv].astype(WIDE)
    rate = once(normed[...], rate_weight[...])
    rate_in[...] = rate
    strength = jax.nn.sigmoid(rate)
    decay = rates[0:1, :] * softplus(rate + rates[1:2, :])
    unit = []
    for part in range(3):
        unit.append([])
        for head in range(2):
            summed = conv_of(ext, kernel, part * 256 + head * size, 5, span)
            active, scale = silu_unit(summed)
            if part == 0:
                active = active * scale * size**-0.5
            if part == 1:
                active = active * scale
            unit[part].append(active.astype(LOW))
    ext[pl.ds(0, 8), :] = ext[pl.ds(span, 8), :]
    small_rows, small_cols = square_iotas(size)
    causal = small_rows >= small_cols
    ones = jnp.where(causal, 1.0, 0.0)
    rows, cols = square_iotas(2 * size)
    differ = rows ^ cols
    lowers, keep = [], []
    for b in range(count):
        at = slice(b * size, (b + 1) * size)
        cumulative = lax.dot_general(
            ones, decay[at], (NN, ((), ())), precision=highest, preferred_element_type=WIDE
        )
        across = cumulative.T
        ratios = pair_diagonal(
            *(
                decay_ratios(cumulative[:, 2 + h : 3 + h], across[2 + h : 3 + h, :], causal)
                for h in range(2)
            )
        )
        query, key, value = (pair_rows(unit[p][0][at], unit[p][1][at]) for p in range(3))
        beta = pair_rows(strength[at, 0:1], strength[at, 1:2])
        column = pair_rows(cumulative[:, 2:3], cumulative[:, 3:4])
        lower = jnp.where(rows > cols, beta * ratios * once(key, key, NT), 0.0)
        lowers.append(lower)
        score = ratios * once(query, key, NT)
        scores[b] = score.astype(LOW)
        qk[b] = jnp.concatenate([query, key], 1)
        lanes = lax.broadcasted_iota(jnp.int32, (2 * size, 128), 1)
        columns[b] = jnp.where(lanes == 0, beta, jnp.where(lanes == 1, column, 0.0))
        keep.append((key.astype(WIDE), value.astype(WIDE), beta, column))
    for b, inv in enumerate(inverses(lowers, differ)):
        key, value, beta, column = keep[b]
        inverse[b] = inv.astype(LOW)
        gammas = jnp.exp(column)
        both = thrice(inv, jnp.concatenate([beta * value, (beta * gammas) * key], 1))
        ue[b] = both
        before[b] = carry[...]
        next_rows = []
        for h in range(2):
            at = slice(h * size, (h + 1) * size)
            last = column[(h + 1) * size - 1 : (h + 1) * size, :]
            tails = jnp.exp(last - column[at]) * key[at]
            made = thrice(tails, both[at], TN)
            advance = jnp.where(small_rows == small_cols, jnp.exp(last), 0.0) - made[:, size:]
            steps[b, at, :] = advance
            moved = thrice(advance, carry[at, :])
            next_rows.append(
                jnp.concatenate([moved[:, :size], moved[:, size:] + made[:, :size]], 1)
            )
        carry[...] = pair_rows(*next_rows)

    @pl.when(step == pl.num_programs(0) - 1)
    def _():
        total[...] = carry[...]


def output_kernel(
    start, before, ue, scores, qk, columns, mixed, gain, project, partial_out, gated_out,
    fresh_out, state_out, out_out
):
    size = 128
    count = ue.shape[0]
    for b in range(count):
        gated = []
        tokens = pl.ds(b * size, size)
        fresh_parts, queried = [], []
        for h in range(2):
            at = slice(h * size, (h + 1) * size)
            pre = before[b, at, :]
            state = thrice(pre[:, :size], start[at, :]) + pre[:, size:]
            state_out[b, at, :] = state
            seen = thrice(
                pair_rows(ue[b, at, size:], qk[b, at, :size].astype(WIDE)), state
            )
            fresh_parts.append(ue[b, at, :size] - seen[:size])
            queried.append(jnp.exp(columns[b, at, 1:2]) * seen[size:])
        fresh = pair_rows(*fresh_parts)
        fresh_out[b] = fresh.astype(LOW)
        outputs = pair_rows(*queried) + once(scores[b], fresh)
        out_out[b] = outputs
        for h in range(2):
            at = slice(h * size, (h + 1) * size)
            one = outputs[at]
            scale = lax.rsqrt(jnp.mean(one * one, axis=-1, keepdims=True) + 1e-05)
            gate = mixed[tokens, pl.ds(h * size, size)].astype(WIDE)
            gated.append((one * scale * gain[0:1, :] * (gate * jax.nn.sigmoid(gate))).astype(LOW))
        both = jnp.concatenate(gated, 1)
        gated_out[tokens, :] = both
        partial_out[tokens, :] = once(both, project[...]).astype(LOW)


def return_kernel(
    branch, project, mixed, gain, out, scores, ue, qk, columns, steps, grad_out, back_scores,
    returns, grad_gate, total, grad_gain, carry
):
    size = 128
    count = ue.shape[0]

    @pl.when(pl.program_id(0) == 0)
    def _():
        carry[...] = jnp.zeros_like(carry)
        grad_gain[...] = jnp.zeros_like(grad_gain)

    grad_gated = once(branch[...], project[...], NT)
    for b in reversed(range(count)):
        tokens = pl.ds(b * size, size)
        grads = []
        for h in range(2):
            at, wide = slice(h * size, (h + 1) * size), pl.ds(h * size, size)
            one = out[b, at, :]
            scale = lax.rsqrt(jnp.mean(one * one, axis=-1, keepdims=True) + 1e-05)
            gate = mixed[tokens, wide].astype(WIDE)
            open_ = jax.nn.sigmoid(gate)
            given = grad_gated[b * size : (b + 1) * size, at]
            normal = one * scale
            through = given * gate * open_
            grad_gain[0:1, :] += jnp.sum(through * normal, axis=0, keepdims=True)
            grad_gate[tokens, wide] = (
                given * normal * gain[0:1, :] * (open_ * (1.0 + gate * (1.0 - open_)))
            ).astype(LOW)
            f = through * gain[0:1, :]
            grads.append(
                scale * f
                - one * (scale * scale * scale) * jnp.mean(f * one, axis=-1, keepdims=True)
            )
        grad = pair_rows(*grads)
        grad_out[b] = grad
        back = once(scores[b], grad, TN)
        back_scores[b] = back
        for h in range(2):
            at = slice(h * size, (h + 1) * size)
            scaled = jnp.exp(columns[b, at, 1:2]) * qk[b, at, :size].astype(WIDE)
            given = once(
                pair_rows(scaled, -ue[b, at, size:]), pair_rows(grad[at], back[at]), TN
            )
            returns[b, at, :] = given
            carry[at, :] = thrice(steps[b, at, :], carry[at, :], TN) + given

    @pl.when(pl.program_id(0) == pl.num_programs(0) - 1)
    def _():
        total[...] = carry[...]


def gradient_kernel(
    end, returns, steps, grad_out, back_scores, fresh, states, inverse, scores, qk, columns,
    mixed, rate_in, grad_gate, kernel, rates, grad_mixed, grad_rates, grad_kernel, sums, front,
    edge, ext, gext, carry
):
    size = 128
    count = fresh.shape[0]
    span = count * size
    conv = 6 * size
    turn = pl.program_id(0)
    step = pl.num_programs(0) - 1 - turn

    @pl.when(turn == 0)
    def _():
        carry[...] = end[...]
        grad_kernel[...] = jnp.zeros_like(grad_kernel)
        sums[...] = jnp.zeros_like(sums)
        gext[pl.ds(span, 8), :] = jnp.zeros((8, conv), WIDE)

    ext[...] = mixed[pl.ds(pl.multiple_of(step * span, 16), span + 16), :].astype(WIDE)
    small_rows, small_cols = square_iotas(size)
    causal = small_rows >= small_cols
    upper = jnp.where(small_rows <= small_cols, 1.0, 0.0)
    rows, cols = square_iotas(2 * size)
    lanes = lax.broadcasted_iota(jnp.int32, (size, 128), 1)
    values = []
    for h in range(2):
        summed = conv_of(ext, kernel, 512 + h * size, 13, span)
        values.append(summed * jax.nn.sigmoid(summed))
    unit_grads = [[None] * count for _ in range(6)]
    for b in reversed(range(count)):
        tokens = slice(b * size, (b + 1) * size)
        grad_state = carry[...]
        after = [
            thrice(steps[b, h * size : (h + 1) * size, :], grad_state[h * size : (h + 1) * size], TN)
            for h in range(2)
        ]
        carry[...] = pair_rows(*after) + returns[b]
        beta, column = columns[b, :, 0:1], columns[b, :, 1:2]
        across = [columns[b, pl.ds(h * size, size), :].T[1:2, :] for h in range(2)]
        ratios = pair_diagonal(
            *(
                decay_ratios(column[h * size : (h + 1) * size], across[h], causal)
                for h in range(2)
            )
        )
        query, key = qk[b, :, :size].astype(WIDE), qk[b, :, size:].astype(WIDE)
        value = pair_rows(
            *(values[h][tokens].astype(LOW).astype(WIDE) for h in range(2))
        )
        gammas = jnp.exp(column)
        last = [column[(h + 1) * size - 1 : (h + 1) * size] for h in range(2)]
        tail_scale = pair_rows(
            *(jnp.exp(last[h] - column[h * size : (h + 1) * size]) for h in range(2))
        )
        tails = tail_scale * key
        grad = grad_out[b]
        from_tails = [
            once(tails[h * size : (h + 1) * size], grad_state[h * size : (h + 1) * size])
            for h in range(2)
        ]
        grad_fresh = back_scores[b] + pair_rows(*from_tails)
        solved = once(inverse[b], grad_fresh, TN)
        made = fresh[b].astype(WIDE)
        pairs = once(pair_rows(-solved, grad), made, NT)
        score = scores[b].astype(WIDE)
        lower_part = jnp.where(rows > cols, pairs[: 2 * size] * ratios, 0.0)
        score_part = pairs[2 * size :] * ratios
        products = once(key, key, NT)
        weighed = beta * lower_part
        grad_decayed, grad_erase, grad_tails = [], [], []
        for h in range(2):
            at = slice(h * size, (h + 1) * size)
            state = states[b, at, :]
            both = once(pair_rows(grad[at], -solved[at]), state, NT)
            grad_decayed.append(both[:size])
            grad_erase.append(both[size:])
            grad_tails.append(once(made[at], grad_state[at], NT))
        grad_decayed, grad_erase, grad_tails = (
            pair_rows(*m) for m in (grad_decayed, grad_erase, grad_tails)
        )
        stacked = pair_rows(score_part, weighed)
        with_key = once(stacked, key)
        turned = once(stacked, pair_rows(query, key), TN)
        grad_query = gammas * grad_decayed + with_key[: 2 * size]
        grad_key = (
            turned
            + with_key[2 * size :]
            + (beta * gammas) * grad_erase
            + tail_scale * grad_tails
        )
        grad_value = beta * solved
        erase_key = jnp.sum(grad_erase * key, axis=1, keepdims=True) * gammas
        lower_products = lower_part * products
        grad_beta = (
            jnp.sum(lower_products, axis=1, keepdims=True)
            + jnp.sum(solved * value, axis=1, keepdims=True)
            + erase_key
        )
        both = pairs[2 * size :] * score + beta * lower_products
        tail_sum = jnp.sum(grad_tails * tails, axis=1, keepdims=True)
        to_column = jnp.sum(both, axis=0, keepdims=True)
        grad_column = (
            jnp.sum(both, axis=1, keepdims=True)
            + gammas * jnp.sum(grad_decayed * query, axis=1, keepdims=True)
            + beta * erase_key
            - tail_sum
        )
        grad_rate = jnp.zeros((size, 128), WIDE)
        grad_step = jnp.zeros((size, 128), WIDE)
        for h in range(2):
            at = slice(h * size, (h + 1) * size)
            kept = jnp.sum(states[b, at, :] * grad_state[at]) * jnp.exp(last[h])
            finish = kept + jnp.sum(tail_sum[at], axis=0, keepdims=True)
            turned_row = jnp.broadcast_to(to_column[:, at], (size, size)).T
            cumulated = grad_column[at] - turned_row
            summed = lax.dot_general(
                upper, cumulated, (NN, ((), ())), precision=highest, preferred_element_type=WIDE
            )
            grad_step = jnp.where(lanes == 2 + h, summed + finish, grad_step)
            grad_rate = jnp.where(lanes == h, grad_beta[at], grad_rate)
        rate = rate_in[tokens, :]
        strength = jax.nn.sigmoid(rate)
        slope = jax.nn.sigmoid(rate + rates[1:2, :])
        grad_in = grad_rate * strength * (1.0 - strength) + grad_step * rates[0:1, :] * slope
        decay = rates[0:1, :] * softplus(rate + rates[1:2, :])
        sums[0:1, :] += jnp.sum(grad_in, axis=0, keepdims=True)
        sums[1:2, :] += jnp.sum(grad_step * decay, axis=0, keepdims=True)
        grad_rates[tokens, :] = grad_in.astype(LOW)
        grad_mixed[tokens, conv:] = grad_gate[tokens, :]
        for part, member in enumerate((grad_query, grad_key, grad_value)):
            rounded = member.astype(LOW).astype(WIDE)
            for h in range(2):
                unit_grads[2 * part + h][b] = rounded[h * size : (h + 1) * size]
    for part in range(3):
        for h in range(2):
            at = part * 256 + h * size
            wide = pl.ds(at, size)
            given = jnp.concatenate(unit_grads[2 * part + h], 0)
            summed = conv_of(ext, kernel, at, 13, span)
            open_ = jax.nn.sigmoid(summed)
            if part < 2:
                active, scale = silu_unit(summed)
                if part == 0:
                    given = given * size**-0.5
                inner = jnp.sum(active * given, axis=-1, keepdims=True)
                given = scale * given - (scale * scale * scale) * inner * active
            slope = open_ * (1.0 + summed * (1.0 - open_))
            grad_conv = given * slope
            gext[pl.ds(0, span), wide] = grad_conv
            for j in range(4):
                grad_kernel[j : j + 1, wide] += jnp.sum(
                    grad_conv * ext[pl.ds(13 + j, span), wide], axis=0, keepdims=True
                )
            moved = kernel[0:1, wide] * gext[pl.ds(3, span), wide]
            for j in range(1, 4):
                moved = moved + kernel[j : j + 1, wide] * gext[pl.ds(3 - j, span), wide]
            grad_mixed[:, wide] = moved.astype(LOW)

            @pl.when(turn == 0)
            def _():
                edge[:, wide] = moved[span - 16 :]

    gext[pl.ds(span, 8), :] = gext[pl.ds(0, 8), :]

    @pl.when(turn == pl.num_programs(0) - 1)
    def _():
        front[...] = gext[pl.ds(0, 8), :]


def whole_spec(shape):
    return pl.BlockSpec(shape, lambda i: (0,) * len(shape))


def rows_spec(shape, turn=None):
    zeros = (0,) * (len(shape) - 1)
    if turn is None:
        return pl.BlockSpec(shape, lambda i: (i,) + zeros)
    return pl.BlockSpec(shape, lambda i: (turn - 1 - i,) + zeros)


GROUP, PREPARED = 2, 4


def cost(flops, touched):
    return pl.CostEstimate(flops=int(flops), bytes_accessed=int(touched), transcendentals=0)


def prepare(normed, mixer, all_rates, pick, tail, kernel, rates):
    total, width = normed.shape
    blocks = total // 128
    steps = blocks // PREPARED
    span = PREPARED * 128
    like = jax.ShapeDtypeStruct
    return pl.pallas_call(
        prepare_kernel,
        grid=(steps,),
        in_specs=[
            rows_spec((span, width)),
            whole_spec(mixer.shape),
            whole_spec(all_rates.shape),
            whole_spec(pick.shape),
            whole_spec(tail.shape),
            whole_spec(kernel.shape),
            whole_spec(rates.shape),
        ],
        out_specs=[
            whole_spec((total + 16, 768)),
            rows_spec((span, 256)),
            rows_spec((span, 128)),
            rows_spec((PREPARED, 256, 256)),
            rows_spec((PREPARED, 256, 256)),
            rows_spec((PREPARED, 256, 256)),
            rows_spec((PREPARED, 256, 128)),
            rows_spec((PREPARED, 256, 256)),
            rows_spec((PREPARED, 256, 256)),
            rows_spec((PREPARED, 256, 128)),
            whole_spec((256, 256)),
            whole_spec(all_rates.shape),
        ],
        out_shape=[
            like((total + 16, 768), LOW),
            like((total, 256), LOW),
            like((total, 128), WIDE),
            like((blocks, 256, 256), WIDE),
            like((blocks, 256, 256), LOW),
            like((blocks, 256, 256), LOW),
            like((blocks, 256, 128), WIDE),
            like((blocks, 256, 256), WIDE),
            like((blocks, 256, 256), LOW),
            like((blocks, 256, 128), WIDE),
            like((256, 256), WIDE),
            like(all_rates.shape, LOW),
        ],
        scratch_shapes=[pltpu.VMEM((span + 8, 768), WIDE), pltpu.VMEM((256, 256), WIDE)],
        compiler_params=pltpu.CompilerParams(vmem_limit_bytes=VMEM_MOST),
        cost_estimate=cost(4e10, 2e7),
        name="prepare",
    )(normed, mixer, all_rates, pick, tail, kernel, rates)


def finish(start, before, ue, scores, qk, columns, gates, gain, project):
    blocks = ue.shape[0]
    total, width = blocks * 128, project.shape[1]
    span = GROUP * 128
    like = jax.ShapeDtypeStruct
    return pl.pallas_call(
        output_kernel,
        grid=(blocks // GROUP,),
        in_specs=[
            whole_spec(start.shape),
            rows_spec((GROUP, 256, 256)),
            rows_spec((GROUP, 256, 256)),
            rows_spec((GROUP, 256, 256)),
            rows_spec((GROUP, 256, 256)),
            rows_spec((GROUP, 256, 128)),
            rows_spec((span, 256)),
            whole_spec(gain.shape),
            whole_spec(project.shape),
        ],
        out_specs=[
            rows_spec((span, width)),
            rows_spec((span, 256)),
            rows_spec((GROUP, 256, 128)),
            rows_spec((GROUP, 256, 128)),
            rows_spec((GROUP, 256, 128)),
        ],
        out_shape=[
            like((total, width), LOW),
            like((total, 256), LOW),
            like((blocks, 256, 128), LOW),
            like((blocks, 256, 128), WIDE),
            like((blocks, 256, 128), WIDE),
        ],
        compiler_params=pltpu.CompilerParams(vmem_limit_bytes=VMEM_MOST),
        cost_estimate=cost(1e10, 1e7),
        name="finish",
    )(start, before, ue, scores, qk, columns, gates, gain, project)


def give_back(branch, project, gates, gain, out, scores, ue, qk, columns, steps):
    blocks = ue.shape[0]
    total, width = branch.shape
    turns = blocks // GROUP
    span = GROUP * 128
    like = jax.ShapeDtypeStruct
    block = lambda *shape: rows_spec((GROUP,) + shape, turns)
    return pl.pallas_call(
        return_kernel,
        grid=(turns,),
        in_specs=[
            rows_spec((span, width), turns),
            whole_spec(project.shape),
            rows_spec((span, 256), turns),
            whole_spec(gain.shape),
            block(256, 128),
            block(256, 256),
            block(256, 256),
            block(256, 256),
            block(256, 128),
            block(256, 128),
        ],
        out_specs=[
            block(256, 128),
            block(256, 128),
            block(256, 128),
            rows_spec((span, 256), turns),
            whole_spec((256, 128)),
            whole_spec((8, 128)),
        ],
        out_shape=[
            like((blocks, 256, 128), WIDE),
            like((blocks, 256, 128), WIDE),
            like((blocks, 256, 128), WIDE),
            like((total, 256), LOW),
            like((256, 128), WIDE),
            like((8, 128), WIDE),
        ],
        scratch_shapes=[pltpu.VMEM((256, 128), WIDE)],
        compiler_params=pltpu.CompilerParams(vmem_limit_bytes=VMEM_MOST),
        cost_estimate=cost(1e10, 1e7),
        name="give_back",
    )(branch, project, gates, gain, out, scores, ue, qk, columns, steps)


def gradients(
    end, returns, steps, grad_out, back_scores, fresh, states, inverse, scores, qk, columns,
    mixed, rate_in, grad_gate, kernel, rates, after=()
):
    blocks = fresh.shape[0]
    total = blocks * 128
    turns = blocks // GROUP
    span = GROUP * 128
    like = jax.ShapeDtypeStruct
    block = lambda *shape: rows_spec((GROUP,) + shape, turns)
    return pl.pallas_call(
        behind(gradient_kernel, len(after)),
        grid=(turns,),
        in_specs=[pl.BlockSpec(memory_space=pl.ANY)] * len(after)
        + [
            whole_spec(end.shape),
            block(256, 128),
            block(256, 128),
            block(256, 128),
            block(256, 128),
            block(256, 128),
            block(256, 128),
            block(256, 256),
            block(256, 256),
            block(256, 256),
            block(256, 128),
            whole_spec(mixed.shape),
            rows_spec((span, 128), turns),
            rows_spec((span, 256), turns),
            whole_spec(kernel.shape),
            whole_spec(rates.shape),
        ],
        out_specs=[
            rows_spec((span, 1024), turns),
            rows_spec((span, 128), turns),
            whole_spec((8, 768)),
            whole_spec((8, 128)),
            whole_spec((8, 768)),
            whole_spec((16, 768)),
        ],
        out_shape=[
            like((total, 1024), LOW),
            like((total, 128), LOW),
            like((8, 768), WIDE),
            like((8, 128), WIDE),
            like((8, 768), WIDE),
            like((16, 768), WIDE),
        ],
        scratch_shapes=[
            pltpu.VMEM((span + 16, 768), WIDE),
            pltpu.VMEM((span + 8, 768), WIDE),
            pltpu.VMEM((256, 128), WIDE),
        ],
        compiler_params=pltpu.CompilerParams(vmem_limit_bytes=VMEM_MOST),
        cost_estimate=cost(2e10, 1e7),
        name="gradients",
    )(
        *after, end, returns, steps, grad_out, back_scores, fresh, states, inverse, scores, qk, columns,
        mixed, rate_in, grad_gate, kernel, rates
    )


MESH = pl.DeviceIdType.MESH
DMA = pltpu.SemaphoreType.DMA


def neighbours():
    z, y, x, core = (lax.axis_index(name) for name in ALL)
    over_x, over_y, sibling = (z, y, 1 - x, core), (z, 1 - y, x, core), (z, y, x, 1 - core)
    return z, y, x, core, over_x, over_y, sibling


def rank_of(y, x, core):
    return (y * 2 + x) * 2 + core


def greet(others):
    barrier = pltpu.get_barrier_semaphore()
    for other in others:
        pl.semaphore_signal(barrier, inc=1, device_id=other, device_id_type=MESH)
    pl.semaphore_wait(barrier, len(others))


def remote(source, target, sent, arrived, device):
    return pltpu.make_async_remote_copy(
        source, target, sent, arrived, device_id=device, device_id_type=MESH
    )


class Gather:
    def __init__(
        self, mine, out, own_sem, sent, arrived, across_sent, across_arrived, core_sent, core_arrived
    ):
        z, y, x, core, over_x, over_y, sibling = neighbours()
        half = mine.shape[0] // 2
        me, other = rank_of(y, x, core), 1 - core
        piece = lambda slot, p: out.at[slot, pl.ds(p * half, half)]
        from_axis = [rank_of(y, 1 - x, core), rank_of(1 - y, x, core)]
        theirs = [rank_of(y, 1 - x, other), rank_of(1 - y, x, other)]
        over = [over_x, over_y]
        self.own = pltpu.make_async_copy(mine, out.at[me], own_sem)

        def to_core(slot, p, k):
            place = piece(slot, p)
            return remote(place, place, core_sent.at[k], core_arrived.at[k], sibling)

        self.first = [
            remote(
                mine.at[pl.ds(p * half, half)], piece(me, p), sent.at[axis, p],
                arrived.at[axis, p], over[axis]
            )
            for axis, p in ((0, 0), (1, 1), (0, 1), (1, 0))
        ]
        self.first_core = remote(mine, out.at[me], core_sent.at[6], core_arrived.at[6], sibling)
        self.onward = [
            remote(
                piece(from_axis[axis], axis), piece(from_axis[axis], axis),
                across_sent.at[axis], across_arrived.at[axis], over[1 - axis]
            )
            for axis in range(2)
        ]
        self.shared = [
            to_core(from_axis[axis], p, 2 * axis + p)
            for axis, p in ((0, 0), (1, 1), (0, 1), (1, 0))
        ]
        mine_across = rank_of(1 - y, 1 - x, core)
        self.across = [
            remote(
                piece(mine_across, p), piece(mine_across, p), across_sent.at[p],
                across_arrived.at[p], over_x
            )
            for p in range(2)
        ]
        self.shared_across = [to_core(mine_across, p, 4 + p) for p in range(2)]
        self.last = [to_core(theirs[axis], p, 2 * axis + p) for axis in range(2) for p in range(2)]
        self.last += [to_core(rank_of(1 - y, 1 - x, other), p, 4 + p) for p in range(2)]
        place = out.at[rank_of(y, x, other)]
        self.last.append(remote(place, place, core_sent.at[6], core_arrived.at[6], sibling))

    def start(self):
        self.own.start()
        for copy in self.first:
            copy.start()
        self.first_core.start()

    def forward(self):
        for i in range(4):
            self.first[i].wait_recv()
            if i < 2:
                self.onward[i].start()
            self.shared[i].start()

    def finish(self):
        for p in range(2):
            self.across[p].wait_recv()
            self.shared_across[p].start()
        for copy in self.last:
            copy.wait_recv()
        self.own.wait()
        for copy in self.first + [self.first_core] + self.onward + self.shared + self.shared_across:
            copy.wait_send()


def gather_kernel(mine, out, *semaphores):
    greet(neighbours()[4:])
    gather = Gather(mine, out, *semaphores)
    gather.start()
    gather.forward()
    gather.finish()


GATHER_SEMAPHORES = [DMA, DMA((2, 2)), DMA((2, 2)), DMA((2,)), DMA((2,)), DMA((7,)), DMA((7,))]


def plane_gather(rows_here, place):
    rows, width = rows_here.shape
    out = pl.pallas_call(
        gather_kernel,
        out_shape=jax.ShapeDtypeStruct((8, rows, width), rows_here.dtype),
        in_specs=[pl.BlockSpec(memory_space=pltpu.VMEM)],
        out_specs=pl.BlockSpec(memory_space=pltpu.VMEM),
        scratch_shapes=GATHER_SEMAPHORES,
        compiler_params=pltpu.CompilerParams(
            collective_id=place, has_side_effects=True, vmem_limit_bytes=VMEM_MOST
        ),
        cost_estimate=pl.CostEstimate(flops=0, bytes_accessed=70_000_000, transcendentals=0),
        name="plane_gather",
    )(rows_here)
    return out.reshape(8 * rows, width)

def turned(place, flip):
    return place + flip - 2 * place * flip


def units_of(hidden, core, half):
    tiles = hidden // 4 // 128
    most = -(-tiles // 2)
    first = -(-most // 2)
    begin = core * most + half * first
    end = min(begin + first, tiles if core else most)
    return begin * 128, (end - begin) * 128, first * 128


def front_kernel(
    w_mixer, w_gate_up, w_down, w_project, tokens, gain, cotangent, own_rates, mixer, later_a,
    later_b, project, normed_all, cotangent_all, tail, rates, normed, zeros, w_rates, shelf, project_own,
    project_sent, shelf_arrived, project_arrived, rates_own, rates_z_sent, rates_z, rates_sent,
    rates_arrived, mixer_own, mixer_sent, mixer_arrived, up_sent, down_sent, z_arrived,
    later_own, later_sent, later_arrived, zero_sem, tail_sent, tail_arrived, *gather_semaphores
):
    z, y, x, core, over_x, over_y, sibling = neighbours()
    layers = lax.axis_size("z")
    rows, width = w_mixer.shape[0], w_mixer.shape[1] // 4
    wide = width // 8
    hidden = w_down.shape[1]
    per_chip = hidden // 4
    laters = (later_a, later_b)
    block = 8 * rows
    me = rank_of(y, x, core)
    low_z, high_z = jnp.maximum(z - 1, 0), jnp.minimum(z + 1, layers - 1)
    below, above = (low_z, y, x, core), (high_z, y, x, core)
    last = (me == 7) & (z < layers - 1)
    flips = [(k >> 2, (k >> 1) & 1, k & 1) for k in range(8)]
    ranks = [rank_of(turned(y, a), turned(x, b), turned(core, c)) for a, b, c in flips]
    devices = [(z, turned(y, a), turned(x, b), turned(core, c)) for a, b, c in flips]

    barrier = pltpu.get_barrier_semaphore()
    for k in range(1, 8):
        pl.semaphore_signal(barrier, inc=1, device_id=devices[k], device_id_type=MESH)

    @pl.when(z > 0)
    def _():
        pl.semaphore_signal(barrier, inc=1, device_id=below, device_id_type=MESH)
        pl.semaphore_signal(barrier, inc=1, device_id=(low_z, 1, 1, 1), device_id_type=MESH)

    @pl.when(z < layers - 1)
    def _():
        pl.semaphore_signal(barrier, inc=1, device_id=above, device_id_type=MESH)

    others_z = [(lax.rem(z + k, layers), y, x, core) for k in range(1, layers)]
    for other in others_z:
        pl.semaphore_signal(barrier, inc=1, device_id=other, device_id_type=MESH)
    pl.semaphore_wait(
        barrier,
        6 + layers + jnp.where(z > 0, 1, 0) + jnp.where(z < layers - 1, 1, 0) + jnp.where(last, 8, 0),
    )

    def columns(p, rank):
        return w_mixer.at[:, pl.ds(pl.multiple_of(p * width + rank * wide, 128), wide)]

    def mixer_rows(layer, rank):
        return mixer.at[pl.ds(pl.multiple_of(layer * block + rank * rows, rows), rows)]

    mine = mixer_rows(z, me)
    owns = [
        pltpu.make_async_copy(columns(p, me), mine.at[:, pl.ds(p * wide, wide)], mixer_own.at[p])
        for p in range(4)
    ]
    for copy in owns:
        copy.start()
    for k in (2, 4, 6, 1, 3, 5, 7):
        for p in range(4):
            remote(
                columns(p, ranks[k]), mine.at[:, pl.ds(p * wide, wide)], mixer_sent.at[k],
                mixer_arrived.at[k], devices[k]
            ).start()

    def along(layer, rank, upward):
        place = mixer_rows(layer, rank)
        return remote(
            place, place, (up_sent if upward else down_sent).at[layer, rank],
            z_arrived.at[layer, rank], above if upward else below
        )

    def spread(rank):
        @pl.when(z < layers - 1)
        def _():
            along(z, rank, True).start()

        @pl.when(z > 0)
        def _():
            along(z, rank, False).start()

    for r in range(0, tokens.shape[0], 32):
        source = tokens[r : r + 32, :].astype(WIDE)
        scale = lax.rsqrt(jnp.mean(source * source, axis=-1, keepdims=True) + 1e-06)
        normed[r : r + 32, :] = (source * scale * gain[...]).astype(LOW)
    w_rates[...] = jnp.zeros_like(w_rates)
    w_rates[:, : own_rates.shape[1]] = own_rates[...]
    zeros[...] = jnp.zeros_like(zeros)
    count = len(gather_semaphores) // 2
    gather_normed = Gather(normed, normed_all, *gather_semaphores[:count])
    gather_cotangent = Gather(cotangent, cotangent_all, *gather_semaphores[count:])
    for copy in owns:
        copy.wait()
    spread(me)
    gather_normed.start()
    rate_copies = [
        remote(w_rates, rates.at[me, z], rates_z_sent.at[k], rates_z.at[k], other)
        for k, other in enumerate(others_z)
    ]
    for copy in rate_copies:
        copy.start()
    rate_own = pltpu.make_async_copy(w_rates, rates.at[me, z], rates_own)
    rate_own.start()

    def tails(a, b, c):
        k = (a * 2 + b) * 2 + c
        return remote(
            normed.at[pl.ds(normed.shape[0] - 16, 16)], tail, tail_sent.at[k], tail_arrived,
            (high_z, a, b, c)
        )

    @pl.when(last)
    def _():
        for a, b, c in flips:
            tails(a, b, c).start()

    for k in (1, 2, 4, 3, 5, 6, 7):
        place = mixer_rows(z, ranks[k])
        remote(place, place, mixer_sent.at[k], mixer_arrived.at[k], devices[k]).wait_recv()
        spread(ranks[k])

    def pass_on(far):
        @pl.loop(0, 8)
        def _(rank):
            @pl.when(z - far >= 0)
            def _():
                copy = along(jnp.maximum(z - far, 0), rank, True)
                copy.wait_recv()

                @pl.when(z < layers - 1)
                def _():
                    copy.start()

            @pl.when(z + far <= layers - 1)
            def _():
                copy = along(jnp.minimum(z + far, layers - 1), rank, False)
                copy.wait_recv()

                @pl.when(z > 0)
                def _():
                    copy.start()

    here = pl.ds(pl.multiple_of(me * rows, rows), rows)

    def shares(chip, t):
        found = []
        for half, later in enumerate(laters):
            begin, size, slot = units_of(hidden, t, half)
            first = pl.multiple_of(chip * per_chip + begin, 128)
            up = pl.multiple_of(hidden + first, 128)
            found += [
                (w_gate_up.at[:, pl.ds(first, size)], later.at[here, pl.ds(0, size)]),
                (w_gate_up.at[:, pl.ds(up, size)], later.at[here, pl.ds(slot, size)]),
                (w_down.at[:, pl.ds(first, size)], later.at[here, pl.ds(2 * slot, size)]),
            ]
        return found

    def later_wait(t, semaphore, arrival):
        for half, later in enumerate(laters):
            place = later.at[pl.ds(0, rows), pl.ds(0, 3 * units_of(hidden, t, half)[1])]
            copy = remote(place, place, semaphore.at[half], semaphore.at[half], sibling)
            if arrival:
                copy.wait_recv()
            else:
                copy.wait_send()

    def send_later(f, t):
        a, b = f >> 1, f & 1
        for i, (source, target) in enumerate(shares(turned(y, a) * 2 + turned(x, b), t)):
            remote(
                source, target, later_sent.at[f, t, i // 3], later_arrived.at[f, core, i // 3],
                (z, turned(y, a), turned(x, b), t)
            ).start()

    for f in (1, 2, 3):
        for t in range(2):
            send_later(f, t)
    for t in range(2):

        @pl.when(core == t)
        def _():
            for i, (source, target) in enumerate(shares(y * 2 + x, t)):
                pltpu.make_async_copy(source, target, later_own.at[i]).start()

        @pl.when(core != t)
        def _():
            send_later(0, t)

    _, least, slot = units_of(hidden, 1, 1)
    pads = [
        pltpu.make_async_copy(
            zeros, later_b.at[:, pl.ds(i * slot + least, slot - least)], zero_sem.at[i]
        )
        for i in range(3)
    ]

    @pl.when(core == 1)
    def _():
        for copy in pads:
            copy.start()

    pass_on(1)
    project_copies = [
        remote(w_project, shelf.at[z], project_sent.at[k], shelf_arrived.at[z], other)
        for k, other in enumerate(others_z)
    ]
    project_kept = pltpu.make_async_copy(w_project, shelf.at[z], project_own.at[0])
    project_kept.start()
    for copy in project_copies:
        copy.start()
    gather_normed.forward()
    gather_cotangent.start()
    pass_on(2)
    rate_own.wait()
    for copy in rate_copies:
        copy.wait_recv()
    for k in range(1, 8):
        place = rates.at[me]
        copy = remote(place, place, rates_sent.at[k], rates_arrived.at[k], devices[k])
        copy.start()
        rate_copies.append(copy)
    gather_normed.finish()
    gather_cotangent.forward()
    own_j, keeps = 2 * x + core, core == y
    rows_of = lambda j: project.at[pl.ds(pl.multiple_of(j * rows, rows), rows)]

    def hand_on(l):
        return remote(
            shelf.at[l], rows_of(own_j), project_sent.at[layers - 1 + l], project_arrived.at[own_j],
            (z, l // 2, l % 2, y)
        )

    kept_here = pltpu.make_async_copy(shelf.at[2 * y + x], rows_of(own_j), project_own.at[1])
    project_kept.wait()
    for l in range(layers):
        is_own = keeps & (l == 2 * y + x)

        @pl.when(z != l)
        def _():
            remote(
                shelf.at[l], shelf.at[l], project_sent.at[0], shelf_arrived.at[l], sibling
            ).wait_recv()

        @pl.when(is_own)
        def _():
            kept_here.start()

        @pl.when(jnp.logical_not(is_own))
        def _():
            hand_on(l).start()

    pass_on(3)
    gather_cotangent.finish()
    for j in range(4):

        @pl.when(jnp.logical_not(keeps & (own_j == j)))
        def _():
            remote(
                rows_of(j), rows_of(j), project_sent.at[0], project_arrived.at[j], sibling
            ).wait_recv()

    @pl.when(keeps)
    def _():
        kept_here.wait()

    for copy in project_copies:
        copy.wait_send()
    for l in range(layers):

        @pl.when(jnp.logical_not(keeps & (l == 2 * y + x)))
        def _():
            hand_on(l).wait_send()

    for t in range(2):

        @pl.when(core == t)
        def _():
            for f in range(4):
                for s in range(2):
                    if f or s != t:
                        later_wait(t, later_arrived.at[f, s], True)
            for i, (source, target) in enumerate(shares(y * 2 + x, t)):
                pltpu.make_async_copy(source, target, later_own.at[i]).wait()

    @pl.when(core == 1)
    def _():
        for copy in pads:
            copy.wait()

    for t in range(2):
        for f in range(1, 4):
            later_wait(t, later_sent.at[f, t], False)

        @pl.when(core != t)
        def _():
            later_wait(t, later_sent.at[0, t], False)

    for k in range(1, 8):
        remote(mine, mine, mixer_sent.at[k], mixer_arrived.at[k], devices[k]).wait_send()
        place = rates.at[ranks[k]]
        remote(place, place, rates_sent.at[k], rates_arrived.at[k], devices[k]).wait_recv()
    for copy in rate_copies:
        copy.wait_send()

    @pl.when(z == 0)
    def _():
        tail[...] = jnp.zeros_like(tail)

    @pl.when(z > 0)
    def _():
        tails(0, 0, 0).wait_recv()

    @pl.when(last)
    def _():
        for a, b, c in flips:
            tails(a, b, c).wait_send()

    for layer in range(4):

        @pl.loop(0, 8)
        def _(rank):
            @pl.when((z < layers - 1) & (layer <= z))
            def _():
                along(layer, rank, True).wait_send()

            @pl.when((z > 0) & (layer >= z))
            def _():
                along(layer, rank, False).wait_send()


def front(w_mixer, w_gate_up, w_down, w_project, w_rates, tokens, gain, cotangent, place):
    rows, columns = w_mixer.shape
    layers = lax.axis_size("z")
    hidden = w_down.shape[1]
    _, least, slot = units_of(hidden, 1, 1)
    length, width = tokens.shape
    like = jax.ShapeDtypeStruct
    any_, vmem = pl.BlockSpec(memory_space=pl.ANY), pl.BlockSpec(memory_space=pltpu.VMEM)
    return pl.pallas_call(
        front_kernel,
        out_shape=[
            like((8 * layers * rows, columns // 8), LOW),
            like((8 * rows, 3 * slot), LOW),
            like((8 * rows, 3 * slot), LOW),
            like((4 * rows, w_project.shape[1]), LOW),
            like((8, length, width), LOW),
            like((8, length, width), LOW),
            like((16, width), LOW),
            like((8, layers, rows, 128), LOW),
        ],
        in_specs=[any_, any_, any_, any_, vmem, vmem, vmem, vmem],
        out_specs=[any_, any_, any_, any_, vmem, vmem, vmem, vmem],
        scratch_shapes=[
            pltpu.VMEM((length, width), LOW),
            pltpu.VMEM((8 * rows, slot - least), LOW),
            pltpu.VMEM((rows, 128), LOW),
            pltpu.VMEM((layers, rows, width), LOW),
            DMA((2,)), DMA((2 * layers - 1,)), DMA((layers,)), DMA((4,)),
            DMA, DMA((layers - 1,)), DMA((layers - 1,)), DMA((8,)), DMA((8,)),
            DMA((4,)), DMA((8,)), DMA((8,)), DMA((4, 8)), DMA((4, 8)), DMA((4, 8)),
            DMA((6,)), DMA((4, 2, 2)), DMA((4, 2, 2)), DMA((3,)), DMA((8,)), DMA,
        ]
        + GATHER_SEMAPHORES * 2,
        compiler_params=pltpu.CompilerParams(
            collective_id=place, has_side_effects=True, vmem_limit_bytes=VMEM_MOST
        ),
        cost_estimate=pl.CostEstimate(flops=0, bytes_accessed=250_000_000, transcendentals=0),
        name="front",
    )(
        w_mixer, w_gate_up, w_down, w_project, tokens, gain[None], cotangent, w_rates
    )


def scatter_steps(
    terms, out, held, from_core, over_a, over_b, side_x, side_y, core_sent, core_arrived,
    across_sent, across_arrived, sent, arrived
):
    z, y, x, core, over_x, over_y, sibling = neighbours()
    rows = terms.shape[1]
    half, step = rows // 2, 16
    chunks = lambda c: [
        rank_of(1 - y, 1 - x, c), rank_of(y, 1 - x, c), rank_of(1 - y, x, c), rank_of(y, x, c)
    ]
    mine, theirs = chunks(core), chunks(1 - core)
    to_core = [
        remote(terms.at[theirs[i]], from_core.at[i], core_sent.at[i], core_arrived.at[i], sibling)
        for i in range(4)
    ]
    for copy in to_core:
        copy.start()
    yield

    def add(target, at, count, more=None):
        @pl.loop(0, count, step=step)
        def _(r):
            here = pl.ds(pl.multiple_of(at + r, step), step)
            total = terms[mine[target], here, :].astype(WIDE) + from_core[target, here, :].astype(WIDE)
            if more is not None:
                total = total + more[pl.ds(pl.multiple_of(r, step), step), :].astype(WIDE)
            held[target, here, :] = total.astype(LOW)

    top, bottom = pl.ds(0, half), pl.ds(half, half)
    to_core[0].wait_recv()
    add(0, 0, rows)
    top_y = remote(held.at[0, top], over_a, across_sent.at[0], across_arrived.at[0], over_y)
    bottom_x = remote(held.at[0, bottom], over_b, across_sent.at[1], across_arrived.at[1], over_x)
    top_y.start()
    bottom_x.start()
    yield
    to_core[1].wait_recv()
    add(1, half, half)
    x_bottom = remote(held.at[1, bottom], side_x.at[bottom], sent.at[0, 1], arrived.at[0, 1], over_x)
    x_bottom.start()
    to_core[2].wait_recv()
    add(2, 0, half)
    y_top = remote(held.at[2, top], side_y.at[top], sent.at[1, 0], arrived.at[1, 0], over_y)
    y_top.start()
    yield
    top_y.wait_recv()
    add(1, 0, half, over_a)
    x_top = remote(held.at[1, top], side_x.at[top], sent.at[0, 0], arrived.at[0, 0], over_x)
    x_top.start()
    bottom_x.wait_recv()
    add(2, half, half, over_b)
    y_bottom = remote(held.at[2, bottom], side_y.at[bottom], sent.at[1, 1], arrived.at[1, 1], over_y)
    y_bottom.start()
    yield
    to_core[3].wait_recv()
    for copy in (x_bottom, y_top, x_top, y_bottom):
        copy.wait_recv()

    @pl.loop(0, rows, step=step)
    def _(r):
        here = pl.ds(pl.multiple_of(r, step), step)
        out[here, :] = (
            terms[mine[3], here, :].astype(WIDE)
            + from_core[3, here, :].astype(WIDE)
            + (side_x[here, :].astype(WIDE) + side_y[here, :].astype(WIDE))
        )

    for copy in to_core + [top_y, bottom_x, x_bottom, y_top, x_top, y_bottom]:
        copy.wait_send()


def scatter_kernel(*refs):
    greet(neighbours()[4:])
    for _ in scatter_steps(*refs):
        pass


def scatter_scratch(rows, width):
    block = lambda *shape: pltpu.VMEM(shape, LOW)
    return [
        block(3, rows, width),
        block(4, rows, width),
        block(rows // 2, width),
        block(rows // 2, width),
        block(rows, width),
        block(rows, width),
        DMA((4,)),
        DMA((4,)),
        DMA((2,)),
        DMA((2,)),
        DMA((2, 2)),
        DMA((2, 2)),
    ]


def behind(kernel, count):
    return lambda *refs: kernel(*refs[count:])


def plane_scatter(terms, place, after=()):
    rows, width = terms.shape[0] // 8, terms.shape[1]
    return pl.pallas_call(
        behind(scatter_kernel, len(after)),
        out_shape=jax.ShapeDtypeStruct((rows, width), WIDE),
        in_specs=[pl.BlockSpec(memory_space=pl.ANY)] * len(after)
        + [pl.BlockSpec(memory_space=pltpu.VMEM)],
        out_specs=pl.BlockSpec(memory_space=pltpu.VMEM),
        scratch_shapes=scatter_scratch(rows, width),
        compiler_params=pltpu.CompilerParams(
            collective_id=place, has_side_effects=True, vmem_limit_bytes=VMEM_MOST
        ),
        cost_estimate=pl.CostEstimate(flops=0, bytes_accessed=80_000_000, transcendentals=0),
        name="plane_scatter",
    )(*after, terms.reshape(8, rows, width))


def feed_forward_kernel(normed, cotangent, weights, *rest):
    before, (inner, grad_swiglu, back, out) = rest[:-4], rest[-4:]
    slot = inner.shape[1]
    gate_up, down = weights.at[:, : 2 * slot], weights.at[:, 2 * slot :]
    both = once(normed[...], gate_up[...])
    given = once(cotangent[...], down[...])
    a, b = both[:, :slot], both[:, slot:]
    open_ = jax.nn.sigmoid(a)
    active = a * open_
    inner_low = (active * b).astype(LOW)
    swiglu = jnp.concatenate(
        [given * b * open_ * (1.0 + a * (1.0 - open_)), given * active], 1
    ).astype(LOW)
    inner[...] = inner_low
    grad_swiglu[...] = swiglu
    terms = [once(swiglu, gate_up[...], NT), once(inner_low, down[...], NT)]
    for i, target in enumerate((back, out)):
        term = terms[i] + before[i][...] if before else terms[i]
        target[...] = term.astype(target.dtype)


def feed_forward(normed, cotangent, weights, before=()):
    tokens, width = normed.shape
    slot = weights.shape[1] // 3
    step = 256
    like = jax.ShapeDtypeStruct
    kind = LOW if before else WIDE
    return pl.pallas_call(
        feed_forward_kernel,
        grid=(tokens // step,),
        in_specs=[rows_spec((step, width)), rows_spec((step, width)), whole_spec(weights.shape)]
        + [rows_spec((step, width))] * len(before),
        out_specs=[
            rows_spec((step, slot)),
            rows_spec((step, 2 * slot)),
            rows_spec((step, width)),
            rows_spec((step, width)),
        ],
        out_shape=[
            like((tokens, slot), LOW),
            like((tokens, 2 * slot), LOW),
            like((tokens, width), kind),
            like((tokens, width), kind),
        ],
        compiler_params=pltpu.CompilerParams(vmem_limit_bytes=VMEM_MOST),
        cost_estimate=cost(2 * tokens * width * 6 * slot, 3e7),
        name="feed_forward",
    )(normed, cotangent, weights, *before)


def later_terms_kernel(normed, cotangent, swiglu, inner, out):
    both = swiglu.shape[1]
    out[:, :both] = once(normed[...], swiglu[...], TN).astype(LOW)
    out[:, both:] = once(cotangent[...], inner[...], TN).astype(LOW)


def later_terms(normed, cotangent, swiglu, inner):
    tokens, rows = normed.shape
    columns = swiglu.shape[1] + inner.shape[1]
    step = 256
    return pl.pallas_call(
        later_terms_kernel,
        grid=(rows // step,),
        in_specs=[pl.BlockSpec((tokens, step), lambda i: (0, i))] * 2
        + [whole_spec(swiglu.shape), whole_spec(inner.shape)],
        out_specs=rows_spec((step, columns)),
        out_shape=jax.ShapeDtypeStruct((rows, columns), LOW),
        compiler_params=pltpu.CompilerParams(vmem_limit_bytes=VMEM_MOST),
        cost_estimate=cost(2 * tokens * rows * columns, 2e7),
        name="later_terms",
    )(normed, cotangent, swiglu, inner)


def mixer_terms_kernel(slots, normed, mixed, out):
    rows, columns = normed.shape[1], mixed.shape[1]
    few = slots.shape[1]
    out[0, :rows, :] = once(normed[...], mixed[...], TN).astype(LOW)
    for half in range(2):
        out[0, rows + half * few : rows + (half + 1) * few, :] = slots[
            0, :, half * columns : (half + 1) * columns
        ]


def mixer_terms(slots, normed, mixed):
    tokens, rows = normed.shape
    columns = mixed.shape[1]
    layers, few, width = slots.shape
    share = rows // layers + 2 * few
    return pl.pallas_call(
        mixer_terms_kernel,
        grid=(layers,),
        in_specs=[
            rows_spec((1, few, width)),
            pl.BlockSpec((tokens, rows // layers), lambda i: (0, i)),
            whole_spec(mixed.shape),
        ],
        out_specs=rows_spec((1, share, columns)),
        out_shape=jax.ShapeDtypeStruct((layers, share, columns), LOW),
        compiler_params=pltpu.CompilerParams(vmem_limit_bytes=VMEM_MOST),
        cost_estimate=cost(2 * tokens * rows * columns, 2e7),
        name="mixer_terms",
    )(slots, normed, mixed)


def chain_kernel(reverse, whole, term, out, arriving, leaving, sent, arrived):
    z, y, x, core = (lax.axis_index(name) for name in ALL)
    layers = lax.axis_size("z")
    at = layers - 1 - z if reverse else z
    nearer = jnp.clip(z + (1 if reverse else -1), 0, layers - 1)
    further = jnp.clip(z + (-1 if reverse else 1), 0, layers - 1)
    barrier = pltpu.get_barrier_semaphore()

    @pl.when(at > 0)
    def _():
        pl.semaphore_signal(barrier, inc=1, device_id=(nearer, y, x, core), device_id_type=MESH)

    copy = remote(leaving, arriving, sent, arrived, (further, y, x, core))
    size = out.shape[1]
    factor = whole.at[:, :size]
    if not reverse:
        term = whole.at[:, size:]

    @pl.when(at == 0)
    def _():
        out[...] = jnp.zeros_like(out)
        leaving[...] = term[...].astype(LOW)

    @pl.when(at > 0)
    def _():
        copy.wait_recv()
        out[...] = arriving[...].astype(WIDE)

    @pl.when((at > 0) & (at < layers - 1))
    def _():
        for h in range(2):
            rows = slice(h * 128, (h + 1) * 128)
            moved = thrice(factor[rows, :], out[rows, :], TN if reverse else NN)
            leaving[rows, :] = (moved + term[rows, :]).astype(LOW)

    @pl.when(at < layers - 1)
    def _():
        pl.semaphore_wait(barrier, 1)
        copy.start()
        copy.wait_send()


def back_chain_kernel(
    whole, term, terms, out, slots, arriving, leaving, sent, arrived, kept, slot_sent, slot_arrived
):
    z, y, x, core, over_x, over_y, sibling = neighbours()
    layers = lax.axis_size("z")
    rows = slots.shape[1]
    at = layers - 1 - z
    nearer = (jnp.minimum(z + 1, layers - 1), y, x, core)
    further = (jnp.maximum(z - 1, 0), y, x, core)
    own_j, keeps = 2 * x + core, core == y
    barrier = pltpu.get_barrier_semaphore()

    @pl.when(at > 0)
    def _():
        pl.semaphore_signal(barrier, inc=1, device_id=nearer, device_id_type=MESH)

    for l in range(layers):

        @pl.when(jnp.logical_not(keeps & (l == 2 * y + x)))
        def _():
            pl.semaphore_signal(
                barrier, inc=1, device_id=(z, l // 2, l % 2, y), device_id_type=MESH
            )

    pl.semaphore_wait(
        barrier, layers - jnp.where(keeps, 1, 0) + jnp.where(at < layers - 1, 1, 0)
    )
    chain_copy = remote(leaving, arriving, sent, arrived, further)
    mine = slots.at[2 * y + x]

    def pass_terms(j):
        return remote(
            terms.at[pl.ds(j * rows, rows)], mine, slot_sent.at[j], slot_arrived.at[2 * y + x],
            (z, core, j // 2, j % 2)
        )

    kept_copy = pltpu.make_async_copy(
        terms.at[pl.ds(pl.multiple_of(own_j * rows, rows), rows)], mine, kept
    )

    @pl.when(at == 0)
    def _():
        out[...] = jnp.zeros_like(out)
        leaving[...] = term[...].astype(LOW)
        chain_copy.start()

    for j in range(4):

        @pl.when(jnp.logical_not(keeps & (own_j == j)))
        def _():
            pass_terms(j).start()

    @pl.when(keeps)
    def _():
        kept_copy.start()

    @pl.when(at > 0)
    def _():
        chain_copy.wait_recv()
        out[...] = arriving[...].astype(WIDE)

    @pl.when((at > 0) & (at < layers - 1))
    def _():
        size = out.shape[1]
        for h in range(2):
            here = slice(h * 128, (h + 1) * 128)
            moved = thrice(whole[here, :size], out[here, :], TN)
            leaving[here, :] = (moved + term[here, :]).astype(LOW)
        chain_copy.start()

    for l in range(layers):

        @pl.when(jnp.logical_not(keeps & (l == 2 * y + x)))
        def _():
            remote(
                slots.at[l], slots.at[l], slot_sent.at[0], slot_arrived.at[l], sibling
            ).wait_recv()

    @pl.when(keeps)
    def _():
        kept_copy.wait()

    for j in range(4):

        @pl.when(jnp.logical_not(keeps & (own_j == j)))
        def _():
            pass_terms(j).wait_send()

    @pl.when(at < layers - 1)
    def _():
        chain_copy.wait_send()


def back_chain(whole, term, terms, place):
    shape = (whole.shape[0], whole.shape[1] // 2)
    layers = lax.axis_size("z")
    rows, width = terms.shape[0] // 4, terms.shape[1]
    like = jax.ShapeDtypeStruct
    return pl.pallas_call(
        back_chain_kernel,
        out_shape=[like(shape, WIDE), like((layers, rows, width), LOW)],
        in_specs=[pl.BlockSpec(memory_space=pltpu.VMEM)] * 3,
        out_specs=[pl.BlockSpec(memory_space=pltpu.VMEM)] * 2,
        scratch_shapes=[
            pltpu.VMEM(shape, LOW), pltpu.VMEM(shape, LOW), DMA, DMA, DMA, DMA((4,)), DMA((layers,)),
        ],
        compiler_params=pltpu.CompilerParams(
            collective_id=place, has_side_effects=True, vmem_limit_bytes=VMEM_MOST
        ),
        cost_estimate=pl.CostEstimate(flops=0, bytes_accessed=50_000_000, transcendentals=0),
        name="back_chain",
    )(whole, term, terms)


def chain(whole, term, reverse, place):
    shape = (whole.shape[0], whole.shape[1] // 2)
    return pl.pallas_call(
        partial(chain_kernel, reverse),
        out_shape=jax.ShapeDtypeStruct(shape, WIDE),
        in_specs=[pl.BlockSpec(memory_space=pltpu.VMEM)] * 2,
        out_specs=pl.BlockSpec(memory_space=pltpu.VMEM),
        scratch_shapes=[pltpu.VMEM(shape, LOW), pltpu.VMEM(shape, LOW), DMA, DMA],
        compiler_params=pltpu.CompilerParams(
            collective_id=place, has_side_effects=True, vmem_limit_bytes=VMEM_MOST
        ),
        cost_estimate=pl.CostEstimate(flops=0, bytes_accessed=40_000_000, transcendentals=0),
        name="chain",
    )(whole, term)


def later_back_steps(sums_a, sums_b, gate_up, down, own_sem, sent, arrived):
    z, y, x, core, over_x, over_y, sibling = neighbours()
    rows, hidden = down.shape
    per_chip = hidden // 4
    me = rank_of(y, x, core)
    flips = [(k >> 2, (k >> 1) & 1, k & 1) for k in range(8)]
    devices = [(z, turned(y, a), turned(x, b), turned(core, c)) for a, b, c in flips]
    ranks = [rank_of(*device[1:]) for device in devices]

    def parts(rank, t):
        chip = y * 2 + x
        here = pl.ds(pl.multiple_of(rank * rows, rows), rows)
        found = []
        for half, sums in enumerate((sums_a, sums_b)):
            begin, size, slot = units_of(hidden, t, half)
            first = pl.multiple_of(chip * per_chip + begin, 128)
            up = pl.multiple_of(hidden + first, 128)
            found += [
                (sums.at[here, pl.ds(0, size)], gate_up.at[:, pl.ds(first, size)]),
                (sums.at[here, pl.ds(slot, size)], gate_up.at[:, pl.ds(up, size)]),
                (sums.at[here, pl.ds(2 * slot, size)], down.at[:, pl.ds(first, size)]),
            ]
        return found

    def amount(t):
        return [
            down.at[:, pl.ds(0, 3 * units_of(hidden, t, half)[1])] for half in range(2)
        ]

    for t in range(2):

        @pl.when(core == t)
        def _():
            for k in (2, 4, 6, 3, 5, 7, 1):
                for i, (source, target) in enumerate(parts(ranks[k], t)):
                    remote(
                        source, target, sent.at[k, i // 3], arrived.at[k, i // 3], devices[k]
                    ).start()
            for i, (source, target) in enumerate(parts(me, t)):
                pltpu.make_async_copy(source, target, own_sem.at[i]).start()

    for _ in range(5):
        yield
    for t in range(2):

        @pl.when(core == t)
        def _():
            for i, (source, target) in enumerate(parts(me, t)):
                pltpu.make_async_copy(source, target, own_sem.at[i]).wait()

    for k in range(1, 8):
        for t in range(2):
            @pl.when(turned(core, k & 1) == t)
            def _():
                for half, place in enumerate(amount(t)):
                    remote(
                        place, place, sent.at[k, half], arrived.at[k, half], devices[k]
                    ).wait_recv()

            @pl.when(core == t)
            def _():
                for half, place in enumerate(amount(t)):
                    remote(
                        place, place, sent.at[k, half], arrived.at[k, half], devices[k]
                    ).wait_send()


def small_steps(small, layers_in, gathered, z_sent, z_arrived, sent, arrived, patience=2):
    z, y, x, core, over_x, over_y, sibling = neighbours()
    layers = layers_in.shape[0]
    me = rank_of(y, x, core)
    flips = [(k >> 2, (k >> 1) & 1, k & 1) for k in range(8)]
    devices = [(z, turned(y, a), turned(x, b), turned(core, c)) for a, b, c in flips]
    ranks = [rank_of(*device[1:]) for device in devices]
    to_layers = [
        remote(
            small, layers_in.at[z], z_sent.at[k], z_arrived.at[k], (lax.rem(z + k, layers), y, x, core)
        )
        for k in range(1, layers)
    ]
    for copy in to_layers:
        copy.start()
    layers_in[z] = small[...]
    for _ in range(patience):
        yield
    for copy in to_layers:
        copy.wait_recv()
    total = layers_in[0]
    for k in range(1, layers):
        total = total + layers_in[k]
    gathered[me] = total
    spread = [
        remote(gathered.at[me], gathered.at[me], sent.at[k], arrived.at[k], devices[k])
        for k in range(1, 8)
    ]
    for copy in spread:
        copy.start()
    for _ in range(patience):
        yield
    for k in range(1, 8):
        place = gathered.at[ranks[k]]
        remote(place, place, sent.at[k], arrived.at[k], devices[k]).wait_recv()
    for copy in to_layers + spread:
        copy.wait_send()


def small_scratch(shape, layers):
    return [
        pltpu.VMEM(shape, WIDE),
        pltpu.VMEM((layers,) + shape, WIDE),
        pltpu.VMEM((8,) + shape, WIDE),
        DMA((layers,)),
        DMA((layers,)),
        DMA((8,)),
        DMA((8,)),
    ]


def together(running):
    while running:
        for steps in list(running):
            if next(steps, running) is running:
                running.remove(steps)


def others_of(z, y, x, core):
    flips = [(k >> 2, (k >> 1) & 1, k & 1) for k in range(1, 8)]
    layers = lax.axis_size("z")
    return [(z, turned(y, a), turned(x, b), turned(core, c)) for a, b, c in flips] + [
        (lax.rem(z + k, layers), y, x, core) for k in range(1, layers)
    ]


def source_steps(terms, out, tokens, small, scatter_parts, small_parts):
    yield from scatter_steps(terms, out, *scatter_parts)
    total = jnp.zeros((1, out.shape[1]), WIDE)
    for first in range(0, out.shape[0], 32):
        source = tokens[first : first + 32, :].astype(WIDE)
        scale = lax.rsqrt(jnp.mean(source * source, axis=-1, keepdims=True) + 1e-06)
        total = total + jnp.sum(
            out[first : first + 32, :] * source * scale, axis=0, keepdims=True
        )
    step = small.shape[1]
    for row in range(small.shape[0]):
        small[row : row + 1, :] = total[:, row * step : (row + 1) * step]
    yield from small_steps(small, *small_parts, patience=1)


def return_all_kernel(
    terms_a, terms_b, sums_a, sums_b, tokens, grad_kernel, decays, head_gain, gain_mlp, rate_terms,
    out_a, out_b, gate_up, down, all_kernel, all_decays, all_head, all_mlp, all_rates, all_mixer,
    *rest
):
    z, y, x, core, over_x, over_y, sibling = neighbours()
    barrier = pltpu.get_barrier_semaphore()
    others = others_of(z, y, x, core)
    for other in others:
        pl.semaphore_signal(barrier, inc=1, device_id=other, device_id_type=MESH)
    small, gathered = rest[0], rest[2]
    high = 6 * 128
    wide = 256
    small[...] = jnp.zeros_like(small)
    small[0:4, :high] = grad_kernel[0:4, :]
    small[0:1, high : high + 128] = decays[0:1, :]
    small[0:1, high + 128 :] = decays[1:2, :]
    small[1:2, high : high + 128] = head_gain[0:1, :]
    small[4:6, :] = gain_mlp[...]
    half = small.shape[1]
    small[8:12, :] = rate_terms[0:4, :half]
    small[12:16, :] = rate_terms[0:4, half:]
    pl.semaphore_wait(barrier, len(others))
    gain_parts, scratch = rest[7:14], rest[14:]
    count = (len(scratch) - 3) // 2
    together([
        source_steps(
            terms_a, out_a, tokens, gain_parts[0], scratch[:count], gain_parts[1:]
        ),
        scatter_steps(terms_b, out_b, *scratch[count : 2 * count]),
        later_back_steps(sums_a, sums_b, gate_up, down, *scratch[2 * count :]),
        small_steps(*rest[:7]),
    ])
    gains = gain_parts[2]
    whole = gains[0]
    for r in range(1, 8):
        whole = whole + gains[r]
    all_mixer[...] = whole
    whole = gathered[0]
    for r in range(8):
        for part in range(3):
            all_kernel[0:4, part * 8 * wide + r * wide : part * 8 * wide + (r + 1) * wide] = (
                gathered[r, 0:4, part * wide : (part + 1) * wide]
            )
        all_decays[r : r + 1, :] = gathered[r, 0:1, high:]
        all_rates[r] = gathered[r, 8:16, :]
        if r:
            whole = whole + gathered[r]
    all_head[...] = whole[1:2, high : high + 128]
    all_mlp[...] = whole[4:6, :]


def return_all(terms_a, terms_b, sums_a, sums_b, tokens, smalls, hidden, place, after=()):
    rows, width = terms_a.shape[0] // 8, terms_a.shape[1]
    owned = sums_a.shape[0] // 8
    layers = lax.axis_size("z")
    any_, vmem = pl.BlockSpec(memory_space=pl.ANY), pl.BlockSpec(memory_space=pltpu.VMEM)
    like = jax.ShapeDtypeStruct
    return pl.pallas_call(
        behind(return_all_kernel, len(after)),
        out_shape=[
            like((rows, width), WIDE),
            like((rows, width), WIDE),
            like((owned, 2 * hidden), LOW),
            like((owned, hidden), LOW),
            like((4, 6 * 1024), WIDE),
            like((8, 256), WIDE),
            like((1, 128), WIDE),
            like((2, 1024), WIDE),
            like((8, 8, 1024), WIDE),
            like((8, 256), WIDE),
        ],
        in_specs=[any_] * len(after) + [vmem, vmem, any_, any_] + [vmem] * 6,
        out_specs=[vmem, vmem, any_, any_] + [vmem] * 6,
        scratch_shapes=small_scratch((16, 1024), layers)
        + small_scratch((8, 256), layers)
        + scatter_scratch(rows, width) * 2
        + [DMA((6,)), DMA((8, 2)), DMA((8, 2))],
        compiler_params=pltpu.CompilerParams(
            collective_id=place, has_side_effects=True, vmem_limit_bytes=VMEM_MOST
        ),
        cost_estimate=pl.CostEstimate(flops=0, bytes_accessed=200_000_000, transcendentals=0),
        name="return_all",
    )(
        *after, terms_a.reshape(8, rows, width), terms_b.reshape(8, rows, width), sums_a, sums_b,
        tokens, *smalls
    )


def mixer_back_steps(sums, mixer, own_sem, sent, arrived):
    z, y, x, core, over_x, over_y, sibling = neighbours()
    rows, columns = mixer.shape
    wide, width = columns // 32, columns // 4
    me = rank_of(y, x, core)
    flips = [(k >> 2, (k >> 1) & 1, k & 1) for k in range(8)]
    devices = [(z, turned(y, a), turned(x, b), turned(core, c)) for a, b, c in flips]
    ranks = [rank_of(*device[1:]) for device in devices]

    def parts(rank):
        here = pl.ds(pl.multiple_of(rank * rows, rows), rows)
        return [
            (
                sums.at[here, pl.ds(p * wide, wide)],
                mixer.at[:, pl.ds(pl.multiple_of(p * width + me * wide, 128), wide)],
            )
            for p in range(4)
        ]

    for k in (2, 4, 6, 3, 5, 7, 1):
        for source, target in parts(ranks[k]):
            remote(source, target, sent.at[k], arrived.at[k], devices[k]).start()
    owns = [
        pltpu.make_async_copy(source, target, own_sem.at[i])
        for i, (source, target) in enumerate(parts(me))
    ]
    for copy in owns:
        copy.start()
    yield
    yield
    for copy in owns:
        copy.wait()
    place = mixer.at[:, pl.ds(0, 4 * wide)]
    for k in range(1, 8):
        remote(place, place, sent.at[k], arrived.at[k], devices[k]).wait()


def last_kernel(sums, mixer, *rest):
    z, y, x, core, over_x, over_y, sibling = neighbours()
    greet(others_of(z, y, x, core)[:7])
    together([mixer_back_steps(sums, mixer, *rest)])


def last(sums, rows, place, after=()):
    columns = sums.shape[1]
    any_ = pl.BlockSpec(memory_space=pl.ANY)
    return pl.pallas_call(
        behind(last_kernel, len(after)),
        out_shape=jax.ShapeDtypeStruct((rows, 8 * columns), LOW),
        in_specs=[any_] * (len(after) + 1),
        out_specs=any_,
        scratch_shapes=[DMA((4,)), DMA((8,)), DMA((8,))],
        compiler_params=pltpu.CompilerParams(
            collective_id=place, has_side_effects=True, vmem_limit_bytes=VMEM_MOST
        ),
        cost_estimate=pl.CostEstimate(flops=0, bytes_accessed=60_000_000, transcendentals=0),
        name="last",
    )(*after, sums)


def heads_on_plane(
    tokens,
    w_mixer,
    w_rates,
    w_project,
    w_gate_up,
    w_down,
    conv_kernel,
    decay_log,
    decay_bias,
    head_gain,
    gain_mixer,
    gain_mlp,
    cotangent,
):
    length, width = tokens.shape
    size = head_gain.shape[0]
    rows = w_mixer.shape[0]
    hidden = w_down.shape[1]
    layers = lax.axis_size("z")
    ranks = lax.axis_size(ALL) // layers
    own = decay_log.shape[0] // ranks
    layer, rank = lax.axis_index("z"), lax.axis_index(PLANE)
    low = jnp.bfloat16
    wide = own * size

    def over_layers(terms):
        return lax.psum_scatter(terms, "z", scatter_dimension=0, tiled=True)

    gather = plane_gather

    def scatter(terms, place, after=()):
        return plane_scatter(terms.astype(low), place, after)

    source = tokens.astype(jnp.float32)
    norm_pull = jax.vjp(norm_scale, source, gain_mixer)[1]
    mixer, later_a, later_b, project, normed_all, cotangent_all, tail, all_rates = front(
        w_mixer, w_gate_up, w_down, w_project, w_rates, tokens, gain_mixer, cotangent, 1
    )
    total = length * ranks
    normed_all = normed_all.reshape(total, width)
    cotangent_all = cotangent_all.reshape(total, width)
    later_a = lax.all_gather(later_a, "z", axis=0, tiled=True)
    later_b = lax.all_gather(later_b, "z", axis=0, tiled=True)
    slot = later_a.shape[1] // 3
    all_rates = jnp.swapaxes(all_rates, 0, 1).reshape(width, 128)
    head_at = jnp.arange(2 * own) // own * (ranks * own) + jnp.arange(2 * own) % own + rank * own
    pick = jnp.pad(
        jax.nn.one_hot(head_at, 128, axis=0, dtype=low), ((0, 0), (0, 128 - 2 * own))
    )
    kernel = lax.dynamic_index_in_dim(
        conv_kernel.reshape(4, 3, ranks, wide), rank, 2, False
    ).reshape(4, 3 * wide)
    kernel = jnp.pad(kernel, ((0, 4), (0, 0)))
    log_rate = lax.dynamic_slice_in_dim(decay_log, rank * own, own)
    bias = lax.dynamic_slice_in_dim(decay_bias, rank * own, own)

    downward = [(z + 1, z) for z in range(layers - 1)]
    head_gains = jnp.broadcast_to(head_gain, (8, size))
    pads = ((0, 7), (2, 124))
    rates = jnp.pad(-jnp.exp(log_rate)[None], pads) + jnp.roll(jnp.pad(bias[None], pads), 1, 0)
    (
        mixed_low, gates, rate_in, ue, inverse, scores, steps, before, qk, columns, whole, rate_weight
    ) = prepare(normed_all, mixer, all_rates, pick, tail, kernel, rates)
    start = chain(whole, whole, False, 7)
    branch, gated_low, fresh, states, outputs = finish(
        start, before, ue, scores, qk, columns, gates, head_gains, project
    )
    hidden_state = source + scatter(branch, 2)
    normed_two, norm_two_pull = jax.vjp(norm_scale, hidden_state, gain_mlp)
    normed_two_all = gather(normed_two.astype(low), 3)
    sums_of, terms_so_far = [], ()
    for weights in (later_a, later_b):
        inner, grad_swiglu, *terms_so_far = feed_forward(
            normed_two_all, cotangent_all, weights, terms_so_far
        )
        sums_of.append(
            over_layers(later_terms(normed_two_all, cotangent_all, grad_swiglu, inner))
        )
    back_terms, out_terms = terms_so_far
    later_sum_a, later_sum_b = sums_of
    grad_hidden_part, grad_gain_mlp = norm_two_pull(scatter(back_terms, 5))
    grad_hidden = cotangent.astype(jnp.float32) + grad_hidden_part
    grad_branch = gather(grad_hidden.astype(low), 6)
    grad_out, back_scores, returns, grad_gate, local, grad_head_gain = give_back(
        grad_branch, project, gates, head_gains, outputs, scores, ue, qk, columns, steps
    )
    project_terms = dot_tn(gated_low, grad_branch).astype(low)
    later_state, slots = back_chain(whole, local, project_terms, 8)
    grad_mixed, grad_rates, grad_kernel, sums, first_rows, edge = gradients(
        later_state, returns, steps, grad_out, back_scores, fresh, states, inverse, scores, qk, columns,
        mixed_low, rate_in, grad_gate, kernel, rates, (later_sum_a,)
    )
    following = lax.ppermute(first_rows[:3].astype(low), "z", downward).astype(jnp.float32)
    late = [
        sum(kernel[j] * following[r - j] for j in range(r + 1)) for r in range(3)
    ]
    edge = jnp.concatenate([edge[:13], edge[13:] + jnp.stack(late)], 0).astype(low)
    grad_mixed = lax.dynamic_update_slice(grad_mixed, edge, (total - 16, 0))
    terms = mixer_terms(slots, normed_all, grad_mixed)
    rate_terms = dot_tn(grad_rates, normed_all)
    mixer_sum = lax.psum_scatter(terms, "z", scatter_dimension=0)
    source_terms = dot_nt(grad_mixed, mixer) + dot_nt(grad_rates, rate_weight)
    smalls = (grad_kernel, sums, grad_head_gain, grad_gain_mlp.reshape(2, -1), rate_terms)
    (
        from_source, from_inner, grad_gate_up, grad_down, grad_kernel, decays, grad_head_gain,
        grad_gain_mlp, rate_sums, grad_gain_mixer
    ) = return_all(
        source_terms.astype(low), out_terms, later_sum_a, later_sum_b, tokens, smalls, hidden, 10,
        (terms,)
    )
    grad_source = norm_pull(from_source)[0]
    grad_tokens = (grad_hidden + grad_source).astype(low)
    result = (hidden_state + from_inner).astype(low)
    grad_gate_up, grad_down = grad_gate_up.astype(jnp.float32), grad_down.astype(jnp.float32)
    rate_sums = jnp.swapaxes(rate_sums.reshape(ranks, 2, 2 * own, -1, rows), 1, 2)
    rate_sums = rate_sums.reshape(ranks, 2, own, -1, rows)
    grad_rates = lax.dynamic_index_in_dim(rate_sums, layer * ranks + rank, 3, False)
    grad_rates = jnp.transpose(grad_rates, (3, 1, 0, 2)).reshape(rows, -1)
    few = (ranks + 1) * rows
    grad_project = jnp.concatenate(
        [mixer_sum[ranks * rows : few], mixer_sum[few:]], 1
    ).astype(jnp.float32)
    grad_mixer = last(
        mixer_sum, rows, 11,
        (grad_gate_up, grad_down, result, grad_tokens, grad_rates, grad_gain_mixer),
    )
    return (
        result,
        grad_tokens,
        grad_mixer.astype(jnp.float32),
        grad_rates,
        grad_project,
        grad_gate_up,
        grad_down,
        grad_kernel,
        decays[:, 128 + own : 128 + 2 * own].reshape(-1),
        decays[:, own : 2 * own].reshape(-1),
        grad_head_gain[0],
        grad_gain_mixer.reshape(-1),
        grad_gain_mlp.reshape(-1),
    )


def by_planes(mesh, members):
    seq, core = mesh.shape["seq"], mesh.shape["fsdp"]
    layers, ranks = seq // 4, 4 * core
    heads, size = members[7].shape[0], members[9].shape[0]
    return (
        core == 2
        and layers == 4
        and members[0].shape[0] == seq * core * size
        and heads % ranks == 0
        and members[5].shape[1] % (4 * 128) == 0
    )


def solution(mesh):
    rows, copied = P(("seq", "fsdp"), None), P()

    def run(*members):
        if by_planes(mesh, members):
            places = Mesh(mesh.devices.reshape(-1, 2, 2, 2), ALL)
            split, body = P(ALL, None), heads_on_plane
        else:
            places, split, body = mesh, rows, on_device
        return jax.shard_map(
            body,
            mesh=places,
            in_specs=(split,) * 6 + (copied,) * 6 + (split,),
            out_specs=(split,) * 7 + (copied,) * 6,
            check_vma=False,
        )(*members)

    return run
```

```python
from functools import partial

import jax
import jax.numpy as jnp
from jax import lax
from jax.experimental import pallas as pl
from jax.experimental.pallas import tpu as pltpu
from jax.sharding import Mesh
from jax.sharding import PartitionSpec as P

BLOCK = 64


highest = lax.Precision.HIGHEST


def shifted(value, axis, by):
    length = lax.axis_size(axis)
    pairs = [(i, i + by) for i in range(length) if 0 <= i + by < length]
    return lax.ppermute(value, axis, pairs)


def prefix_2(value, axis, join, neutral):
    place = lax.axis_index(axis)
    gathered = jax.tree.map(
        lambda a, kind: lax.all_gather(a.astype(kind), axis), value, (jnp.bfloat16, jnp.bfloat16)
    )
    state = jax.tree.map(lambda a, e: jnp.zeros_like(a) + jnp.asarray(e, a.dtype), value, neutral)

    def one(turn, state):
        return join(
            state,
            jax.tree.map(
                lambda a, own: lax.dynamic_index_in_dim(a, turn, 0, False).astype(own.dtype),
                gathered,
                value,
            ),
        )

    return lax.fori_loop(0, place, one, state)


def entering(value, axis, combine, identity):
    length, place = (lax.axis_size(axis), lax.axis_index(axis))
    everything = jax.tree.map(
        lambda part, kind: lax.all_gather(part.astype(kind), axis),
        value,
        jax.tree.map(lambda a: jnp.bfloat16 if a.dtype == jnp.float32 else a.dtype, value),
    )
    start = jax.tree.map(
        lambda part, zero: jnp.broadcast_to(jnp.asarray(zero, part.dtype), part.shape),
        value,
        identity,
    )

    def turn(k, before):
        at = length - 1 - k
        reached = at > place
        new = combine(
            before, jax.tree.map(lambda part, own: part[at].astype(own.dtype), everything, value)
        )
        return jax.tree.map(lambda a, b: jnp.where(reached, a, b), new, before)

    return lax.fori_loop(0, length, turn, start)


def round_trip(values_in):
    return lax.optimization_barrier(values_in.astype(jnp.bfloat16)).astype(jnp.float32)


def norm_scale(values_in, scales):
    return (
        values_in
        * lax.rsqrt(jnp.mean(values_in * values_in, axis=-1, keepdims=True) + 1e-06)
        * scales
    )


def features(extended, kernel, head_count):
    length = extended.shape[0] - 3
    summed = kernel[0] * extended[0:length]
    for offset in range(1, 4):
        summed = summed + kernel[offset] * extended[offset : offset + length]
    active = jax.nn.silu(summed)
    model_width = active.shape[1] // 3

    def unit_rows(member):
        shaped = member.reshape(length, head_count, -1)
        return shaped * lax.rsqrt(jnp.sum(shaped * shaped, axis=-1, keepdims=True) + 1e-06)

    queries = unit_rows(active[:, :model_width])
    queries = queries * queries.shape[-1] ** (-0.5)
    keys_all = unit_rows(active[:, model_width : 2 * model_width])
    values_all = active[:, 2 * model_width :].reshape(length, head_count, -1)
    return (queries, keys_all, values_all)


def rates_of(rate_inputs, decay_log, decay_bias):
    head_count = decay_log.shape[0]
    strength = jax.nn.sigmoid(rate_inputs[:, :head_count])
    decays = -jnp.exp(decay_log) * jax.nn.softplus(rate_inputs[:, head_count:] + decay_bias)
    return (strength, decays)


def head_output(outputs, gate_part, head_gain):
    normed_heads = (
        outputs * lax.rsqrt(jnp.mean(outputs * outputs, axis=-1, keepdims=True) + 1e-05) * head_gain
    )
    return normed_heads.reshape(outputs.shape[0], -1) * jax.nn.silu(gate_part)


def swiglu(gate_up):
    half_width = gate_up.shape[1] // 2
    return jax.nn.silu(gate_up[:, :half_width]) * gate_up[:, half_width:]


def to_blocks(member):
    block_count = member.shape[0] // BLOCK
    shaped = member.reshape((block_count, BLOCK) + member.shape[1:])
    return jnp.moveaxis(shaped, 2, 1)


def from_blocks(member):
    shaped = jnp.moveaxis(member, 1, 2)
    return shaped.reshape((-1,) + shaped.shape[2:])


def unit_pair(head_count, head_size):
    identity_matrix = jnp.eye(head_size, dtype=jnp.float32)
    return (
        jnp.broadcast_to(identity_matrix, (head_count, head_size, head_size)),
        jnp.zeros((head_count, head_size, head_size), jnp.float32),
    )


def combine(earlier, later):
    product = jnp.einsum("hab,hbc->hac", earlier[0], later[0], precision=highest)
    carried = jnp.einsum("hab,hbc->hac", earlier[1], later[0], precision=highest) + later[1]
    return (product, carried)


def block_terms(query_block, key_block, value_block, strength_block, decay_block):
    block_size = key_block.shape[1]
    lower_ones = jnp.tril(jnp.ones((block_size, block_size), jnp.float32))
    cumulative = jnp.einsum("hd,cd->hc", decay_block, lower_ones, precision=highest)
    positions = jnp.arange(block_size)
    causal = positions[:, None] >= positions[None, :]
    strict = positions[:, None] > positions[None, :]
    spread = cumulative[:, :, None] - cumulative[:, None, :]
    ratios = jnp.where(causal, jnp.exp(jnp.where(causal, spread, 0.0)), 0.0)
    key_products = jnp.einsum("hcd,hed->hce", key_block, key_block, precision=highest)
    lower_part = jnp.where(strict, strength_block[:, :, None] * ratios * key_products, 0.0)
    system = lower_part + jnp.eye(block_size, dtype=jnp.float32)
    gammas = jnp.exp(cumulative)
    updates = lax.linalg.triangular_solve(
        system,
        strength_block[:, :, None] * value_block,
        left_side=True,
        lower=True,
        unit_diagonal=True,
    )
    erasers = lax.linalg.triangular_solve(
        system,
        (strength_block * gammas)[:, :, None] * key_block,
        left_side=True,
        lower=True,
        unit_diagonal=True,
    )
    scores = jnp.einsum("hcd,hed->hce", query_block, key_block, precision=highest) * ratios
    tail_keys = jnp.exp(cumulative[:, -1:] - cumulative)[:, :, None] * key_block
    return (gammas, scores, updates, erasers, tail_keys)


def run_blocks(query_blocks, block_parts, start_state):

    def advance(carried, element):
        query_block, gammas, scores, updates, erasers, tail_keys = element
        fresh_values = updates - jnp.einsum("hcd,hvd->hcv", erasers, carried, precision=highest)
        produced = gammas[:, :, None] * jnp.einsum(
            "hcd,hvd->hcv", query_block, carried, precision=highest
        )
        produced = produced + jnp.einsum("hce,hev->hcv", scores, fresh_values, precision=highest)
        carried = gammas[:, -1][:, None, None] * carried + jnp.einsum(
            "hcv,hcd->hvd", fresh_values, tail_keys, precision=highest
        )
        return (carried, produced)

    end_state, produced = lax.scan(advance, start_state, (query_blocks,) + tuple(block_parts))
    return (produced, end_state)


def span(query_blocks, key_blocks, value_blocks, strength_blocks, decay_blocks, start_state):
    block_parts = jax.vmap(block_terms)(
        query_blocks, key_blocks, value_blocks, strength_blocks, decay_blocks
    )
    return run_blocks(query_blocks, block_parts, start_state)


def block_maps(block_parts, head_size):
    gammas, scores, updates, erasers, tail_keys = block_parts
    identity_matrix = jnp.eye(head_size, dtype=jnp.float32)
    transitions = gammas[:, :, -1][:, :, None, None] * identity_matrix - jnp.einsum(
        "nhcd,nhce->nhde", erasers, tail_keys, precision=highest
    )
    writes = jnp.einsum("nhcv,nhce->nhve", updates, tail_keys, precision=highest)

    def compose(carried, element):
        return (combine(carried, element), None)

    initial = unit_pair(transitions.shape[1], head_size)
    return lax.scan(compose, initial, (transitions, writes))[0]


def term_rows(left, right, precise):
    if precise:
        return jnp.einsum(
            "tr,tc->rc", left, right, precision=highest, preferred_element_type=jnp.float32
        )
    return jnp.einsum("tr,tc->rc", left, right, preferred_element_type=jnp.float32)


def on_device(
    tokens,
    w_mixer,
    w_rates,
    w_project,
    w_gate_up,
    w_down,
    conv_kernel,
    decay_log,
    decay_bias,
    head_gain,
    gain_mixer,
    gain_mlp,
    cotangent,
):
    length, model_width = tokens.shape
    head_count = decay_log.shape[0]
    head_size = head_gain.shape[0]
    conv_width = 3 * model_width
    full_mixer, full_rates, full_project, full_gate_up, full_down = (
        lax.all_gather(w_mixer, ("seq", "fsdp"), axis=0, tiled=True),
        lax.all_gather(w_rates, ("seq", "fsdp"), axis=0, tiled=True),
        lax.all_gather(w_project, ("seq", "fsdp"), axis=0, tiled=True),
        lax.all_gather(w_gate_up, ("seq", "fsdp"), axis=0, tiled=True),
        lax.all_gather(w_down, ("seq", "fsdp"), axis=0, tiled=True),
    )
    source = tokens.astype(jnp.float32)
    normed, norm_pull = jax.vjp(norm_scale, source, gain_mixer)
    normed_low = normed.astype(jnp.bfloat16)
    mixed_low = jnp.dot(normed_low, full_mixer, preferred_element_type=jnp.float32).astype(
        jnp.bfloat16
    )
    rate_inputs = jnp.dot(normed_low, full_rates, preferred_element_type=jnp.float32)
    previous = shifted(mixed_low[length - 3 :, :conv_width], ("seq", "fsdp"), 1)
    extended = jnp.concatenate([previous, mixed_low[:, :conv_width]], 0).astype(jnp.float32)
    triple, feature_pull = jax.vjp(partial(features, head_count=head_count), extended, conv_kernel)
    queries, keys_all, values_all = (round_trip(member) for member in triple)
    (strength, decays), rate_pull = jax.vjp(rates_of, rate_inputs, decay_log, decay_bias)
    blocks = tuple(
        (to_blocks(member) for member in (queries, keys_all, values_all, strength, decays))
    )
    block_parts = jax.vmap(block_terms)(*blocks)
    span_trans, span_writes = block_maps(block_parts, head_size)
    identity = unit_pair(head_count, head_size)
    prefix = prefix_2((span_trans, span_writes), ("seq", "fsdp"), combine, identity)
    start_state = prefix[1]
    output_blocks = run_blocks(blocks[0], block_parts, start_state)[0]
    outputs = from_blocks(output_blocks)
    gate_part = mixed_low[:, conv_width:].astype(jnp.float32)
    gated, head_pull = jax.vjp(head_output, outputs, gate_part, head_gain)
    gated_low = gated.astype(jnp.bfloat16)
    hidden_state = source + jnp.dot(gated_low, full_project, preferred_element_type=jnp.float32)
    normed_two, norm_two_pull = jax.vjp(norm_scale, hidden_state, gain_mlp)
    normed_two_low = normed_two.astype(jnp.bfloat16)
    gate_up = jnp.dot(normed_two_low, full_gate_up, preferred_element_type=jnp.float32)
    inner_act, inner_pull = jax.vjp(swiglu, gate_up)
    inner_low = inner_act.astype(jnp.bfloat16)
    result = hidden_state + jnp.einsum(
        "tf,df->td", inner_low, full_down, preferred_element_type=jnp.float32
    )
    upstream = cotangent.astype(jnp.float32)
    grad_inner = jnp.dot(cotangent, full_down, preferred_element_type=jnp.float32)
    grad_swiglu_low = inner_pull(grad_inner)[0].astype(jnp.bfloat16)
    grad_normed_two = jnp.einsum(
        "tc,dc->td", grad_swiglu_low, full_gate_up, preferred_element_type=jnp.float32
    )
    grad_hidden_part, grad_gain_mlp = norm_two_pull(grad_normed_two)
    grad_hidden = upstream + grad_hidden_part
    grad_hidden_low = grad_hidden.astype(jnp.bfloat16)
    grad_gated = jnp.einsum(
        "te,de->td", grad_hidden_low, full_project, preferred_element_type=jnp.float32
    )
    grad_outputs, grad_gate, grad_head_gain = head_pull(grad_gated)
    grad_out_blocks = to_blocks(grad_outputs)
    primal_pair, span_pull = jax.vjp(span, *blocks, start_state)
    local_grads = span_pull((grad_out_blocks, jnp.zeros_like(start_state)))
    suffix = entering(
        (jnp.swapaxes(span_trans, 1, 2), local_grads[5]), ("seq", "fsdp"), combine, identity
    )
    later_grads = span_pull((jnp.zeros_like(grad_out_blocks), suffix[1]))
    grad_blocks = [
        from_blocks(front_grad + back_grad)
        for front_grad, back_grad in zip(local_grads[:5], later_grads[:5])
    ]
    grad_triple = tuple((round_trip(member) for member in grad_blocks[:3]))
    grad_extended, grad_kernel = feature_pull(grad_triple)
    grad_inputs, grad_decay_log, grad_decay_bias = rate_pull((grad_blocks[3], grad_blocks[4]))
    following = shifted(grad_extended[:3].astype(jnp.bfloat16), ("seq", "fsdp"), -1).astype(
        jnp.float32
    )
    grad_conv = grad_extended[3:] + jnp.pad(following, ((length - 3, 0), (0, 0)))
    grad_mixed_low = jnp.concatenate([grad_conv, grad_gate], 1).astype(jnp.bfloat16)
    grad_normed = jnp.einsum(
        "tc,dc->td", grad_mixed_low, full_mixer, preferred_element_type=jnp.float32
    )
    grad_normed = grad_normed + jnp.dot(
        grad_inputs, full_rates.astype(jnp.float32).T, precision=highest
    )
    grad_source, grad_gain_mixer = norm_pull(grad_normed)
    grad_tokens = (grad_hidden + grad_source).astype(jnp.bfloat16)
    normed_wide = normed_low.astype(jnp.float32)
    grad_mixer = lax.psum_scatter(
        term_rows(normed_low, grad_mixed_low, False),
        ("seq", "fsdp"),
        scatter_dimension=0,
        tiled=True,
    )
    grad_rates = lax.psum_scatter(
        term_rows(normed_wide, grad_inputs, True), ("seq", "fsdp"), scatter_dimension=0, tiled=True
    )
    grad_project = lax.psum_scatter(
        term_rows(gated_low, grad_hidden_low, False),
        ("seq", "fsdp"),
        scatter_dimension=0,
        tiled=True,
    )
    grad_gate_up = lax.psum_scatter(
        term_rows(normed_two_low, grad_swiglu_low, False),
        ("seq", "fsdp"),
        scatter_dimension=0,
        tiled=True,
    )
    grad_down = lax.psum_scatter(
        term_rows(cotangent, inner_low, False), ("seq", "fsdp"), scatter_dimension=0, tiled=True
    )
    small_sums = lax.psum(
        (
            grad_kernel,
            grad_decay_log,
            grad_decay_bias,
            grad_head_gain,
            grad_gain_mixer,
            grad_gain_mlp,
        ),
        ("seq", "fsdp"),
    )
    return (
        result.astype(jnp.bfloat16),
        grad_tokens,
        grad_mixer,
        grad_rates,
        grad_project,
        grad_gate_up,
        grad_down,
        small_sums[0],
        small_sums[1],
        small_sums[2],
        small_sums[3],
        small_sums[4],
        small_sums[5],
    )


def dot_bf16(left, right):
    return jnp.dot(left, right, preferred_element_type=jnp.float32)


def dot_nt(left, right):
    return lax.dot_general(
        left, right, (((1,), (1,)), ((), ())), preferred_element_type=jnp.float32
    )


def dot_tn(left, right):
    return lax.dot_general(
        left, right, (((0,), (0,)), ((), ())), preferred_element_type=jnp.float32
    )


def exact(left, right, dims=((1,), (0,))):
    return lax.dot_general(
        left, right, (dims, ((), ())), precision=highest, preferred_element_type=jnp.float32
    )


NT = ((1,), (1,))
TN = ((0,), (0,))


PLANE = ("y", "x", "core")
ALL = ("z",) + PLANE


LOW, WIDE = jnp.bfloat16, jnp.float32
NN = ((1,), (0,))
VMEM_MOST = 56 << 20


def once(left, right, dims=NN):
    return lax.dot_general(
        left.astype(LOW), right.astype(LOW), (dims, ((), ())), preferred_element_type=WIDE
    )


def halves(value):
    high = value.astype(LOW)
    return high, (value - high.astype(WIDE)).astype(LOW)


def thrice(left, right, dims=NN):
    if not isinstance(left, tuple):
        left = halves(left)
    if not isinstance(right, tuple):
        right = halves(right)
    return (
        once(left[0], right[0], dims) + once(left[0], right[1], dims) + once(left[1], right[0], dims)
    )


def pair_rows(first, second):
    return jnp.concatenate([first, second], 0)


def pair_diagonal(first, second):
    zero = jnp.zeros_like(first)
    return pair_rows(
        jnp.concatenate([first, zero], 1), jnp.concatenate([zero, second], 1)
    )


def square_iotas(size):
    return (
        lax.broadcasted_iota(jnp.int32, (size, size), 0),
        lax.broadcasted_iota(jnp.int32, (size, size), 1),
    )


def decay_ratios(column, row, causal):
    return jnp.where(causal, jnp.exp(jnp.minimum(column - row, 0.0)), 0.0)


def inverses(lowers, differ):
    size = lowers[0].shape[0]
    results = [
        jnp.where(differ == 0, 1.0, 0.0) - jnp.where(differ == 1, lower, 0.0) for lower in lowers
    ]
    for level in range(1, 7):
        parts = [halves(result) for result in results]
        below = [jnp.where((differ >> level) == 1, lower, 0.0) for lower in lowers]
        inner = [thrice(b, p) for b, p in zip(below, parts)]
        results = [r - thrice(p, i) for r, p, i in zip(results, parts, inner)]
    return results


def silu_unit(summed):
    active = summed * jax.nn.sigmoid(summed)
    scale = lax.rsqrt(jnp.sum(active * active, axis=-1, keepdims=True) + 1e-06)
    return active, scale


def conv_of(ext, kernel, column, offset, count):
    at = pl.ds(column, 128)
    summed = kernel[0:1, at] * ext[pl.ds(offset, count), at]
    for j in range(1, 4):
        summed = summed + kernel[j : j + 1, at] * ext[pl.ds(offset + j, count), at]
    return summed


def softplus(value):
    return jnp.maximum(value, 0.0) + jnp.log1p(jnp.exp(-jnp.abs(value)))


def prepare_kernel(
    normed, mixer, all_rates, pick, tail, kernel, rates, mixed, gates, rate_in, ue, inverse, scores, steps, before,
    qk, columns, total, rate_weight, ext, carry
):
    step = pl.program_id(0)
    size = 128
    span = normed.shape[0]
    count = span // size
    conv = 6 * size

    @pl.when(step == 0)
    def _():
        rate_weight[...] = once(all_rates[...], pick[...]).astype(LOW)
        first = once(tail[...], mixer[...])
        low = first.astype(LOW)
        mixed[pl.ds(0, 16), :] = low[:, :conv]
        ext[pl.ds(0, 8), :] = low.astype(WIDE)[8:16, :conv]
        rows, cols = square_iotas(size)
        one = jnp.where(rows == cols, 1.0, 0.0)
        zero = jnp.zeros_like(one)
        carry[...] = pair_rows(
            jnp.concatenate([one, zero], 1), jnp.concatenate([one, zero], 1)
        )

    products = once(normed[...], mixer[...])
    low = products.astype(LOW)
    mixed[pl.ds(pl.multiple_of(16 + step * span, 16), span), :] = low[:, :conv]
    gates[...] = low[:, conv:]
    ext[pl.ds(8, span), :] = low[:, :conv].astype(WIDE)
    rate = once(normed[...], rate_weight[...])
    rate_in[...] = rate
    strength = jax.nn.sigmoid(rate)
    decay = rates[0:1, :] * softplus(rate + rates[1:2, :])
    unit = []
    for part in range(3):
        unit.append([])
        for head in range(2):
            summed = conv_of(ext, kernel, part * 256 + head * size, 5, span)
            active, scale = silu_unit(summed)
            if part == 0:
                active = active * scale * size**-0.5
            if part == 1:
                active = active * scale
            unit[part].append(active.astype(LOW))
    ext[pl.ds(0, 8), :] = ext[pl.ds(span, 8), :]
    small_rows, small_cols = square_iotas(size)
    causal = small_rows >= small_cols
    ones = jnp.where(causal, 1.0, 0.0)
    rows, cols = square_iotas(2 * size)
    differ = rows ^ cols
    lowers, keep = [], []
    for b in range(count):
        at = slice(b * size, (b + 1) * size)
        cumulative = lax.dot_general(
            ones, decay[at], (NN, ((), ())), precision=highest, preferred_element_type=WIDE
        )
        across = cumulative.T
        ratios = pair_diagonal(
            *(
                decay_ratios(cumulative[:, 2 + h : 3 + h], across[2 + h : 3 + h, :], causal)
                for h in range(2)
            )
        )
        query, key, value = (pair_rows(unit[p][0][at], unit[p][1][at]) for p in range(3))
        beta = pair_rows(strength[at, 0:1], strength[at, 1:2])
        column = pair_rows(cumulative[:, 2:3], cumulative[:, 3:4])
        lower = jnp.where(rows > cols, beta * ratios * once(key, key, NT), 0.0)
        lowers.append(lower)
        score = ratios * once(query, key, NT)
        scores[b] = score.astype(LOW)
        qk[b] = jnp.concatenate([query, key], 1)
        lanes = lax.broadcasted_iota(jnp.int32, (2 * size, 128), 1)
        columns[b] = jnp.where(lanes == 0, beta, jnp.where(lanes == 1, column, 0.0))
        keep.append((key.astype(WIDE), value.astype(WIDE), beta, column))
    for b, inv in enumerate(inverses(lowers, differ)):
        key, value, beta, column = keep[b]
        inverse[b] = inv.astype(LOW)
        gammas = jnp.exp(column)
        both = thrice(inv, jnp.concatenate([beta * value, (beta * gammas) * key], 1))
        ue[b] = both
        before[b] = carry[...]
        next_rows = []
        for h in range(2):
            at = slice(h * size, (h + 1) * size)
            last = column[(h + 1) * size - 1 : (h + 1) * size, :]
            tails = jnp.exp(last - column[at]) * key[at]
            made = thrice(tails, both[at], TN)
            advance = jnp.where(small_rows == small_cols, jnp.exp(last), 0.0) - made[:, size:]
            steps[b, at, :] = advance
            moved = thrice(advance, carry[at, :])
            next_rows.append(
                jnp.concatenate([moved[:, :size], moved[:, size:] + made[:, :size]], 1)
            )
        carry[...] = pair_rows(*next_rows)

    @pl.when(step == pl.num_programs(0) - 1)
    def _():
        total[...] = carry[...]


def output_kernel(
    start, before, ue, scores, qk, columns, mixed, gain, project, partial_out, gated_out,
    fresh_out, state_out, out_out
):
    size = 128
    count = ue.shape[0]
    for b in range(count):
        gated = []
        tokens = pl.ds(b * size, size)
        fresh_parts, queried = [], []
        for h in range(2):
            at = slice(h * size, (h + 1) * size)
            pre = before[b, at, :]
            state = thrice(pre[:, :size], start[at, :]) + pre[:, size:]
            state_out[b, at, :] = state
            seen = thrice(
                pair_rows(ue[b, at, size:], qk[b, at, :size].astype(WIDE)), state
            )
            fresh_parts.append(ue[b, at, :size] - seen[:size])
            queried.append(jnp.exp(columns[b, at, 1:2]) * seen[size:])
        fresh = pair_rows(*fresh_parts)
        fresh_out[b] = fresh.astype(LOW)
        outputs = pair_rows(*queried) + once(scores[b], fresh)
        out_out[b] = outputs
        for h in range(2):
            at = slice(h * size, (h + 1) * size)
            one = outputs[at]
            scale = lax.rsqrt(jnp.mean(one * one, axis=-1, keepdims=True) + 1e-05)
            gate = mixed[tokens, pl.ds(h * size, size)].astype(WIDE)
            gated.append((one * scale * gain[0:1, :] * (gate * jax.nn.sigmoid(gate))).astype(LOW))
        both = jnp.concatenate(gated, 1)
        gated_out[tokens, :] = both
        partial_out[tokens, :] = once(both, project[...]).astype(LOW)


def return_kernel(
    branch, project, mixed, gain, out, scores, ue, qk, columns, steps, grad_out, back_scores,
    returns, grad_gate, total, grad_gain, carry
):
    size = 128
    count = ue.shape[0]

    @pl.when(pl.program_id(0) == 0)
    def _():
        carry[...] = jnp.zeros_like(carry)
        grad_gain[...] = jnp.zeros_like(grad_gain)

    grad_gated = once(branch[...], project[...], NT)
    for b in reversed(range(count)):
        tokens = pl.ds(b * size, size)
        grads = []
        for h in range(2):
            at, wide = slice(h * size, (h + 1) * size), pl.ds(h * size, size)
            one = out[b, at, :]
            scale = lax.rsqrt(jnp.mean(one * one, axis=-1, keepdims=True) + 1e-05)
            gate = mixed[tokens, wide].astype(WIDE)
            open_ = jax.nn.sigmoid(gate)
            given = grad_gated[b * size : (b + 1) * size, at]
            normal = one * scale
            through = given * gate * open_
            grad_gain[0:1, :] += jnp.sum(through * normal, axis=0, keepdims=True)
            grad_gate[tokens, wide] = (
                given * normal * gain[0:1, :] * (open_ * (1.0 + gate * (1.0 - open_)))
            ).astype(LOW)
            f = through * gain[0:1, :]
            grads.append(
                scale * f
                - one * (scale * scale * scale) * jnp.mean(f * one, axis=-1, keepdims=True)
            )
        grad = pair_rows(*grads)
        grad_out[b] = grad
        back = once(scores[b], grad, TN)
        back_scores[b] = back
        for h in range(2):
            at = slice(h * size, (h + 1) * size)
            scaled = jnp.exp(columns[b, at, 1:2]) * qk[b, at, :size].astype(WIDE)
            given = once(
                pair_rows(scaled, -ue[b, at, size:]), pair_rows(grad[at], back[at]), TN
            )
            returns[b, at, :] = given
            carry[at, :] = thrice(steps[b, at, :], carry[at, :], TN) + given

    @pl.when(pl.program_id(0) == pl.num_programs(0) - 1)
    def _():
        total[...] = carry[...]


def gradient_kernel(
    end, returns, steps, grad_out, back_scores, fresh, states, inverse, scores, qk, columns,
    mixed, rate_in, grad_gate, kernel, rates, grad_mixed, grad_rates, grad_kernel, sums, front,
    edge, ext, gext, carry
):
    size = 128
    count = fresh.shape[0]
    span = count * size
    conv = 6 * size
    turn = pl.program_id(0)
    step = pl.num_programs(0) - 1 - turn

    @pl.when(turn == 0)
    def _():
        carry[...] = end[...]
        grad_kernel[...] = jnp.zeros_like(grad_kernel)
        sums[...] = jnp.zeros_like(sums)
        gext[pl.ds(span, 8), :] = jnp.zeros((8, conv), WIDE)

    ext[...] = mixed[pl.ds(pl.multiple_of(step * span, 16), span + 16), :].astype(WIDE)
    small_rows, small_cols = square_iotas(size)
    causal = small_rows >= small_cols
    upper = jnp.where(small_rows <= small_cols, 1.0, 0.0)
    rows, cols = square_iotas(2 * size)
    lanes = lax.broadcasted_iota(jnp.int32, (size, 128), 1)
    values = []
    for h in range(2):
        summed = conv_of(ext, kernel, 512 + h * size, 13, span)
        values.append(summed * jax.nn.sigmoid(summed))
    unit_grads = [[None] * count for _ in range(6)]
    for b in reversed(range(count)):
        tokens = slice(b * size, (b + 1) * size)
        grad_state = carry[...]
        after = [
            thrice(steps[b, h * size : (h + 1) * size, :], grad_state[h * size : (h + 1) * size], TN)
            for h in range(2)
        ]
        carry[...] = pair_rows(*after) + returns[b]
        beta, column = columns[b, :, 0:1], columns[b, :, 1:2]
        across = [columns[b, pl.ds(h * size, size), :].T[1:2, :] for h in range(2)]
        ratios = pair_diagonal(
            *(
                decay_ratios(column[h * size : (h + 1) * size], across[h], causal)
                for h in range(2)
            )
        )
        query, key = qk[b, :, :size].astype(WIDE), qk[b, :, size:].astype(WIDE)
        value = pair_rows(
            *(values[h][tokens].astype(LOW).astype(WIDE) for h in range(2))
        )
        gammas = jnp.exp(column)
        last = [column[(h + 1) * size - 1 : (h + 1) * size] for h in range(2)]
        tail_scale = pair_rows(
            *(jnp.exp(last[h] - column[h * size : (h + 1) * size]) for h in range(2))
        )
        tails = tail_scale * key
        grad = grad_out[b]
        from_tails = [
            once(tails[h * size : (h + 1) * size], grad_state[h * size : (h + 1) * size])
            for h in range(2)
        ]
        grad_fresh = back_scores[b] + pair_rows(*from_tails)
        solved = once(inverse[b], grad_fresh, TN)
        made = fresh[b].astype(WIDE)
        pairs = once(pair_rows(-solved, grad), made, NT)
        score = scores[b].astype(WIDE)
        lower_part = jnp.where(rows > cols, pairs[: 2 * size] * ratios, 0.0)
        score_part = pairs[2 * size :] * ratios
        products = once(key, key, NT)
        weighed = beta * lower_part
        grad_decayed, grad_erase, grad_tails = [], [], []
        for h in range(2):
            at = slice(h * size, (h + 1) * size)
            state = states[b, at, :]
            both = once(pair_rows(grad[at], -solved[at]), state, NT)
            grad_decayed.append(both[:size])
            grad_erase.append(both[size:])
            grad_tails.append(once(made[at], grad_state[at], NT))
        grad_decayed, grad_erase, grad_tails = (
            pair_rows(*m) for m in (grad_decayed, grad_erase, grad_tails)
        )
        stacked = pair_rows(score_part, weighed)
        with_key = once(stacked, key)
        turned = once(stacked, pair_rows(query, key), TN)
        grad_query = gammas * grad_decayed + with_key[: 2 * size]
        grad_key = (
            turned
            + with_key[2 * size :]
            + (beta * gammas) * grad_erase
            + tail_scale * grad_tails
        )
        grad_value = beta * solved
        erase_key = jnp.sum(grad_erase * key, axis=1, keepdims=True) * gammas
        lower_products = lower_part * products
        grad_beta = (
            jnp.sum(lower_products, axis=1, keepdims=True)
            + jnp.sum(solved * value, axis=1, keepdims=True)
            + erase_key
        )
        both = pairs[2 * size :] * score + beta * lower_products
        tail_sum = jnp.sum(grad_tails * tails, axis=1, keepdims=True)
        to_column = jnp.sum(both, axis=0, keepdims=True)
        grad_column = (
            jnp.sum(both, axis=1, keepdims=True)
            + gammas * jnp.sum(grad_decayed * query, axis=1, keepdims=True)
            + beta * erase_key
            - tail_sum
        )
        grad_rate = jnp.zeros((size, 128), WIDE)
        grad_step = jnp.zeros((size, 128), WIDE)
        for h in range(2):
            at = slice(h * size, (h + 1) * size)
            kept = jnp.sum(states[b, at, :] * grad_state[at]) * jnp.exp(last[h])
            finish = kept + jnp.sum(tail_sum[at], axis=0, keepdims=True)
            turned_row = jnp.broadcast_to(to_column[:, at], (size, size)).T
            cumulated = grad_column[at] - turned_row
            summed = lax.dot_general(
                upper, cumulated, (NN, ((), ())), precision=highest, preferred_element_type=WIDE
            )
            grad_step = jnp.where(lanes == 2 + h, summed + finish, grad_step)
            grad_rate = jnp.where(lanes == h, grad_beta[at], grad_rate)
        rate = rate_in[tokens, :]
        strength = jax.nn.sigmoid(rate)
        slope = jax.nn.sigmoid(rate + rates[1:2, :])
        grad_in = grad_rate * strength * (1.0 - strength) + grad_step * rates[0:1, :] * slope
        decay = rates[0:1, :] * softplus(rate + rates[1:2, :])
        sums[0:1, :] += jnp.sum(grad_in, axis=0, keepdims=True)
        sums[1:2, :] += jnp.sum(grad_step * decay, axis=0, keepdims=True)
        grad_rates[tokens, :] = grad_in.astype(LOW)
        grad_mixed[tokens, conv:] = grad_gate[tokens, :]
        for part, member in enumerate((grad_query, grad_key, grad_value)):
            rounded = member.astype(LOW).astype(WIDE)
            for h in range(2):
                unit_grads[2 * part + h][b] = rounded[h * size : (h + 1) * size]
    for part in range(3):
        for h in range(2):
            at = part * 256 + h * size
            wide = pl.ds(at, size)
            given = jnp.concatenate(unit_grads[2 * part + h], 0)
            summed = conv_of(ext, kernel, at, 13, span)
            open_ = jax.nn.sigmoid(summed)
            if part < 2:
                active, scale = silu_unit(summed)
                if part == 0:
                    given = given * size**-0.5
                inner = jnp.sum(active * given, axis=-1, keepdims=True)
                given = scale * given - (scale * scale * scale) * inner * active
            slope = open_ * (1.0 + summed * (1.0 - open_))
            grad_conv = given * slope
            gext[pl.ds(0, span), wide] = grad_conv
            for j in range(4):
                grad_kernel[j : j + 1, wide] += jnp.sum(
                    grad_conv * ext[pl.ds(13 + j, span), wide], axis=0, keepdims=True
                )
            moved = kernel[0:1, wide] * gext[pl.ds(3, span), wide]
            for j in range(1, 4):
                moved = moved + kernel[j : j + 1, wide] * gext[pl.ds(3 - j, span), wide]
            grad_mixed[:, wide] = moved.astype(LOW)

            @pl.when(turn == 0)
            def _():
                edge[:, wide] = moved[span - 16 :]

    gext[pl.ds(span, 8), :] = gext[pl.ds(0, 8), :]

    @pl.when(turn == pl.num_programs(0) - 1)
    def _():
        front[...] = gext[pl.ds(0, 8), :]


def whole_spec(shape):
    return pl.BlockSpec(shape, lambda i: (0,) * len(shape))


def rows_spec(shape, turn=None):
    zeros = (0,) * (len(shape) - 1)
    if turn is None:
        return pl.BlockSpec(shape, lambda i: (i,) + zeros)
    return pl.BlockSpec(shape, lambda i: (turn - 1 - i,) + zeros)


GROUP, PREPARED = 2, 4


def cost(flops, touched):
    return pl.CostEstimate(flops=int(flops), bytes_accessed=int(touched), transcendentals=0)


def prepare(normed, mixer, all_rates, pick, tail, kernel, rates):
    total, width = normed.shape
    blocks = total // 128
    steps = blocks // PREPARED
    span = PREPARED * 128
    like = jax.ShapeDtypeStruct
    return pl.pallas_call(
        prepare_kernel,
        grid=(steps,),
        in_specs=[
            rows_spec((span, width)),
            whole_spec(mixer.shape),
            whole_spec(all_rates.shape),
            whole_spec(pick.shape),
            whole_spec(tail.shape),
            whole_spec(kernel.shape),
            whole_spec(rates.shape),
        ],
        out_specs=[
            whole_spec((total + 16, 768)),
            rows_spec((span, 256)),
            rows_spec((span, 128)),
            rows_spec((PREPARED, 256, 256)),
            rows_spec((PREPARED, 256, 256)),
            rows_spec((PREPARED, 256, 256)),
            rows_spec((PREPARED, 256, 128)),
            rows_spec((PREPARED, 256, 256)),
            rows_spec((PREPARED, 256, 256)),
            rows_spec((PREPARED, 256, 128)),
            whole_spec((256, 256)),
            whole_spec(all_rates.shape),
        ],
        out_shape=[
            like((total + 16, 768), LOW),
            like((total, 256), LOW),
            like((total, 128), WIDE),
            like((blocks, 256, 256), WIDE),
            like((blocks, 256, 256), LOW),
            like((blocks, 256, 256), LOW),
            like((blocks, 256, 128), WIDE),
            like((blocks, 256, 256), WIDE),
            like((blocks, 256, 256), LOW),
            like((blocks, 256, 128), WIDE),
            like((256, 256), WIDE),
            like(all_rates.shape, LOW),
        ],
        scratch_shapes=[pltpu.VMEM((span + 8, 768), WIDE), pltpu.VMEM((256, 256), WIDE)],
        compiler_params=pltpu.CompilerParams(vmem_limit_bytes=VMEM_MOST),
        cost_estimate=cost(4e10, 2e7),
        name="prepare",
    )(normed, mixer, all_rates, pick, tail, kernel, rates)


def finish(start, before, ue, scores, qk, columns, gates, gain, project):
    blocks = ue.shape[0]
    total, width = blocks * 128, project.shape[1]
    span = GROUP * 128
    like = jax.ShapeDtypeStruct
    return pl.pallas_call(
        output_kernel,
        grid=(blocks // GROUP,),
        in_specs=[
            whole_spec(start.shape),
            rows_spec((GROUP, 256, 256)),
            rows_spec((GROUP, 256, 256)),
            rows_spec((GROUP, 256, 256)),
            rows_spec((GROUP, 256, 256)),
            rows_spec((GROUP, 256, 128)),
            rows_spec((span, 256)),
            whole_spec(gain.shape),
            whole_spec(project.shape),
        ],
        out_specs=[
            rows_spec((span, width)),
            rows_spec((span, 256)),
            rows_spec((GROUP, 256, 128)),
            rows_spec((GROUP, 256, 128)),
            rows_spec((GROUP, 256, 128)),
        ],
        out_shape=[
            like((total, width), LOW),
            like((total, 256), LOW),
            like((blocks, 256, 128), LOW),
            like((blocks, 256, 128), WIDE),
            like((blocks, 256, 128), WIDE),
        ],
        compiler_params=pltpu.CompilerParams(vmem_limit_bytes=VMEM_MOST),
        cost_estimate=cost(1e10, 1e7),
        name="finish",
    )(start, before, ue, scores, qk, columns, gates, gain, project)


def give_back(branch, project, gates, gain, out, scores, ue, qk, columns, steps):
    blocks = ue.shape[0]
    total, width = branch.shape
    turns = blocks // GROUP
    span = GROUP * 128
    like = jax.ShapeDtypeStruct
    block = lambda *shape: rows_spec((GROUP,) + shape, turns)
    return pl.pallas_call(
        return_kernel,
        grid=(turns,),
        in_specs=[
            rows_spec((span, width), turns),
            whole_spec(project.shape),
            rows_spec((span, 256), turns),
            whole_spec(gain.shape),
            block(256, 128),
            block(256, 256),
            block(256, 256),
            block(256, 256),
            block(256, 128),
            block(256, 128),
        ],
        out_specs=[
            block(256, 128),
            block(256, 128),
            block(256, 128),
            rows_spec((span, 256), turns),
            whole_spec((256, 128)),
            whole_spec((8, 128)),
        ],
        out_shape=[
            like((blocks, 256, 128), WIDE),
            like((blocks, 256, 128), WIDE),
            like((blocks, 256, 128), WIDE),
            like((total, 256), LOW),
            like((256, 128), WIDE),
            like((8, 128), WIDE),
        ],
        scratch_shapes=[pltpu.VMEM((256, 128), WIDE)],
        compiler_params=pltpu.CompilerParams(vmem_limit_bytes=VMEM_MOST),
        cost_estimate=cost(1e10, 1e7),
        name="give_back",
    )(branch, project, gates, gain, out, scores, ue, qk, columns, steps)


def gradients(
    end, returns, steps, grad_out, back_scores, fresh, states, inverse, scores, qk, columns,
    mixed, rate_in, grad_gate, kernel, rates, after=()
):
    blocks = fresh.shape[0]
    total = blocks * 128
    turns = blocks // GROUP
    span = GROUP * 128
    like = jax.ShapeDtypeStruct
    block = lambda *shape: rows_spec((GROUP,) + shape, turns)
    return pl.pallas_call(
        behind(gradient_kernel, len(after)),
        grid=(turns,),
        in_specs=[pl.BlockSpec(memory_space=pl.ANY)] * len(after)
        + [
            whole_spec(end.shape),
            block(256, 128),
            block(256, 128),
            block(256, 128),
            block(256, 128),
            block(256, 128),
            block(256, 128),
            block(256, 256),
            block(256, 256),
            block(256, 256),
            block(256, 128),
            whole_spec(mixed.shape),
            rows_spec((span, 128), turns),
            rows_spec((span, 256), turns),
            whole_spec(kernel.shape),
            whole_spec(rates.shape),
        ],
        out_specs=[
            rows_spec((span, 1024), turns),
            rows_spec((span, 128), turns),
            whole_spec((8, 768)),
            whole_spec((8, 128)),
            whole_spec((8, 768)),
            whole_spec((16, 768)),
        ],
        out_shape=[
            like((total, 1024), LOW),
            like((total, 128), LOW),
            like((8, 768), WIDE),
            like((8, 128), WIDE),
            like((8, 768), WIDE),
            like((16, 768), WIDE),
        ],
        scratch_shapes=[
            pltpu.VMEM((span + 16, 768), WIDE),
            pltpu.VMEM((span + 8, 768), WIDE),
            pltpu.VMEM((256, 128), WIDE),
        ],
        compiler_params=pltpu.CompilerParams(vmem_limit_bytes=VMEM_MOST),
        cost_estimate=cost(2e10, 1e7),
        name="gradients",
    )(
        *after, end, returns, steps, grad_out, back_scores, fresh, states, inverse, scores, qk, columns,
        mixed, rate_in, grad_gate, kernel, rates
    )


MESH = pl.DeviceIdType.MESH
DMA = pltpu.SemaphoreType.DMA


def neighbours():
    z, y, x, core = (lax.axis_index(name) for name in ALL)
    over_x, over_y, sibling = (z, y, 1 - x, core), (z, 1 - y, x, core), (z, y, x, 1 - core)
    return z, y, x, core, over_x, over_y, sibling


def rank_of(y, x, core):
    return (y * 2 + x) * 2 + core


def greet(others):
    barrier = pltpu.get_barrier_semaphore()
    for other in others:
        pl.semaphore_signal(barrier, inc=1, device_id=other, device_id_type=MESH)
    pl.semaphore_wait(barrier, len(others))


def remote(source, target, sent, arrived, device):
    return pltpu.make_async_remote_copy(
        source, target, sent, arrived, device_id=device, device_id_type=MESH
    )


class Gather:
    def __init__(
        self, mine, out, own_sem, sent, arrived, across_sent, across_arrived, core_sent, core_arrived
    ):
        z, y, x, core, over_x, over_y, sibling = neighbours()
        half = mine.shape[0] // 2
        me, other = rank_of(y, x, core), 1 - core
        piece = lambda slot, p: out.at[slot, pl.ds(p * half, half)]
        from_axis = [rank_of(y, 1 - x, core), rank_of(1 - y, x, core)]
        theirs = [rank_of(y, 1 - x, other), rank_of(1 - y, x, other)]
        over = [over_x, over_y]
        self.own = pltpu.make_async_copy(mine, out.at[me], own_sem)

        def to_core(slot, p, k):
            place = piece(slot, p)
            return remote(place, place, core_sent.at[k], core_arrived.at[k], sibling)

        self.first = [
            remote(
                mine.at[pl.ds(p * half, half)], piece(me, p), sent.at[axis, p],
                arrived.at[axis, p], over[axis]
            )
            for axis, p in ((0, 0), (1, 1), (0, 1), (1, 0))
        ]
        self.first_core = remote(mine, out.at[me], core_sent.at[6], core_arrived.at[6], sibling)
        self.onward = [
            remote(
                piece(from_axis[axis], axis), piece(from_axis[axis], axis),
                across_sent.at[axis], across_arrived.at[axis], over[1 - axis]
            )
            for axis in range(2)
        ]
        self.shared = [
            to_core(from_axis[axis], p, 2 * axis + p)
            for axis, p in ((0, 0), (1, 1), (0, 1), (1, 0))
        ]
        mine_across = rank_of(1 - y, 1 - x, core)
        self.across = [
            remote(
                piece(mine_across, p), piece(mine_across, p), across_sent.at[p],
                across_arrived.at[p], over_x
            )
            for p in range(2)
        ]
        self.shared_across = [to_core(mine_across, p, 4 + p) for p in range(2)]
        self.last = [to_core(theirs[axis], p, 2 * axis + p) for axis in range(2) for p in range(2)]
        self.last += [to_core(rank_of(1 - y, 1 - x, other), p, 4 + p) for p in range(2)]
        place = out.at[rank_of(y, x, other)]
        self.last.append(remote(place, place, core_sent.at[6], core_arrived.at[6], sibling))

    def start(self):
        self.own.start()
        for copy in self.first:
            copy.start()
        self.first_core.start()

    def forward(self):
        for i in range(4):
            self.first[i].wait_recv()
            if i < 2:
                self.onward[i].start()
            self.shared[i].start()

    def finish(self):
        for p in range(2):
            self.across[p].wait_recv()
            self.shared_across[p].start()
        for copy in self.last:
            copy.wait_recv()
        self.own.wait()
        for copy in self.first + [self.first_core] + self.onward + self.shared + self.shared_across:
            copy.wait_send()


def gather_kernel(mine, out, *semaphores):
    greet(neighbours()[4:])
    gather = Gather(mine, out, *semaphores)
    gather.start()
    gather.forward()
    gather.finish()


GATHER_SEMAPHORES = [DMA, DMA((2, 2)), DMA((2, 2)), DMA((2,)), DMA((2,)), DMA((7,)), DMA((7,))]


def plane_gather(rows_here, place, after=()):
    rows, width = rows_here.shape
    out = pl.pallas_call(
        behind(gather_kernel, len(after)),
        out_shape=jax.ShapeDtypeStruct((8, rows, width), rows_here.dtype),
        in_specs=[pl.BlockSpec(memory_space=pl.ANY)] * len(after)
        + [pl.BlockSpec(memory_space=pltpu.VMEM)],
        out_specs=pl.BlockSpec(memory_space=pltpu.VMEM),
        scratch_shapes=GATHER_SEMAPHORES,
        compiler_params=pltpu.CompilerParams(
            collective_id=place, has_side_effects=True, vmem_limit_bytes=VMEM_MOST
        ),
        cost_estimate=pl.CostEstimate(flops=0, bytes_accessed=70_000_000, transcendentals=0),
        name="plane_gather",
    )(*after, rows_here)
    return out.reshape(8 * rows, width)

def turned(place, flip):
    return place + flip - 2 * place * flip


def units_of(hidden, core, half):
    tiles = hidden // 4 // 128
    most = -(-tiles // 2)
    first = -(-most // 2)
    begin = core * most + half * first
    end = min(begin + first, tiles if core else most)
    return begin * 128, (end - begin) * 128, first * 128


def front_kernel(
    w_mixer, w_gate_up, w_down, w_project, tokens, gain, own_rates, mixer, later_a,
    later_b, project, normed_all, tail, rates, normed, zeros, w_rates, shelf, project_own,
    project_sent, shelf_arrived, project_arrived, rates_own, rates_z_sent, rates_z, rates_sent,
    rates_arrived, mixer_own, mixer_sent, mixer_arrived, up_sent, down_sent, z_arrived,
    later_own, later_sent, later_arrived, zero_sem, tail_sent, tail_arrived, *gather_semaphores
):
    z, y, x, core, over_x, over_y, sibling = neighbours()
    layers = lax.axis_size("z")
    rows, width = w_mixer.shape[0], w_mixer.shape[1] // 4
    wide = width // 8
    hidden = w_down.shape[1]
    per_chip = hidden // 4
    laters = (later_a, later_b)
    block = 8 * rows
    me = rank_of(y, x, core)
    low_z, high_z = jnp.maximum(z - 1, 0), jnp.minimum(z + 1, layers - 1)
    below, above = (low_z, y, x, core), (high_z, y, x, core)
    last = (me == 7) & (z < layers - 1)
    flips = [(k >> 2, (k >> 1) & 1, k & 1) for k in range(8)]
    ranks = [rank_of(turned(y, a), turned(x, b), turned(core, c)) for a, b, c in flips]
    devices = [(z, turned(y, a), turned(x, b), turned(core, c)) for a, b, c in flips]

    barrier = pltpu.get_barrier_semaphore()
    for k in range(1, 8):
        pl.semaphore_signal(barrier, inc=1, device_id=devices[k], device_id_type=MESH)

    @pl.when(z > 0)
    def _():
        pl.semaphore_signal(barrier, inc=1, device_id=below, device_id_type=MESH)
        pl.semaphore_signal(barrier, inc=1, device_id=(low_z, 1, 1, 1), device_id_type=MESH)

    @pl.when(z < layers - 1)
    def _():
        pl.semaphore_signal(barrier, inc=1, device_id=above, device_id_type=MESH)

    others_z = [(lax.rem(z + k, layers), y, x, core) for k in range(1, layers)]
    for other in others_z:
        pl.semaphore_signal(barrier, inc=1, device_id=other, device_id_type=MESH)
    pl.semaphore_wait(
        barrier,
        6 + layers + jnp.where(z > 0, 1, 0) + jnp.where(z < layers - 1, 1, 0) + jnp.where(last, 8, 0),
    )

    def columns(p, rank):
        return w_mixer.at[:, pl.ds(pl.multiple_of(p * width + rank * wide, 128), wide)]

    def mixer_rows(layer, rank):
        return mixer.at[pl.ds(pl.multiple_of(layer * block + rank * rows, rows), rows)]

    mine = mixer_rows(z, me)
    owns = [
        pltpu.make_async_copy(columns(p, me), mine.at[:, pl.ds(p * wide, wide)], mixer_own.at[p])
        for p in range(4)
    ]
    for copy in owns:
        copy.start()
    for k in (2, 4, 6, 1, 3, 5, 7):
        for p in range(4):
            remote(
                columns(p, ranks[k]), mine.at[:, pl.ds(p * wide, wide)], mixer_sent.at[k],
                mixer_arrived.at[k], devices[k]
            ).start()

    def along(layer, rank, upward):
        place = mixer_rows(layer, rank)
        return remote(
            place, place, (up_sent if upward else down_sent).at[layer, rank],
            z_arrived.at[layer, rank], above if upward else below
        )

    def spread(rank):
        @pl.when(z < layers - 1)
        def _():
            along(z, rank, True).start()

        @pl.when(z > 0)
        def _():
            along(z, rank, False).start()

    for r in range(0, tokens.shape[0], 32):
        source = tokens[r : r + 32, :].astype(WIDE)
        scale = lax.rsqrt(jnp.mean(source * source, axis=-1, keepdims=True) + 1e-06)
        normed[r : r + 32, :] = (source * scale * gain[...]).astype(LOW)
    w_rates[...] = jnp.zeros_like(w_rates)
    w_rates[:, : own_rates.shape[1]] = own_rates[...]
    zeros[...] = jnp.zeros_like(zeros)
    gather_normed = Gather(normed, normed_all, *gather_semaphores)
    for copy in owns:
        copy.wait()
    spread(me)
    gather_normed.start()
    rate_copies = [
        remote(w_rates, rates.at[me, z], rates_z_sent.at[k], rates_z.at[k], other)
        for k, other in enumerate(others_z)
    ]
    for copy in rate_copies:
        copy.start()
    rate_own = pltpu.make_async_copy(w_rates, rates.at[me, z], rates_own)
    rate_own.start()

    def tails(a, b, c):
        k = (a * 2 + b) * 2 + c
        return remote(
            normed.at[pl.ds(normed.shape[0] - 16, 16)], tail, tail_sent.at[k], tail_arrived,
            (high_z, a, b, c)
        )

    @pl.when(last)
    def _():
        for a, b, c in flips:
            tails(a, b, c).start()

    for k in (1, 2, 4, 3, 5, 6, 7):
        place = mixer_rows(z, ranks[k])
        remote(place, place, mixer_sent.at[k], mixer_arrived.at[k], devices[k]).wait_recv()
        spread(ranks[k])

    def pass_on(far):
        @pl.loop(0, 8)
        def _(rank):
            @pl.when(z - far >= 0)
            def _():
                copy = along(jnp.maximum(z - far, 0), rank, True)
                copy.wait_recv()

                @pl.when(z < layers - 1)
                def _():
                    copy.start()

            @pl.when(z + far <= layers - 1)
            def _():
                copy = along(jnp.minimum(z + far, layers - 1), rank, False)
                copy.wait_recv()

                @pl.when(z > 0)
                def _():
                    copy.start()

    here = pl.ds(pl.multiple_of(me * rows, rows), rows)

    def shares(chip, t):
        found = []
        for half, later in enumerate(laters):
            begin, size, slot = units_of(hidden, t, half)
            first = pl.multiple_of(chip * per_chip + begin, 128)
            up = pl.multiple_of(hidden + first, 128)
            found += [
                (w_gate_up.at[:, pl.ds(first, size)], later.at[here, pl.ds(0, size)]),
                (w_gate_up.at[:, pl.ds(up, size)], later.at[here, pl.ds(slot, size)]),
                (w_down.at[:, pl.ds(first, size)], later.at[here, pl.ds(2 * slot, size)]),
            ]
        return found

    def later_wait(t, semaphore, arrival):
        for half, later in enumerate(laters):
            place = later.at[pl.ds(0, rows), pl.ds(0, 3 * units_of(hidden, t, half)[1])]
            copy = remote(place, place, semaphore.at[half], semaphore.at[half], sibling)
            if arrival:
                copy.wait_recv()
            else:
                copy.wait_send()

    def send_later(f, t):
        a, b = f >> 1, f & 1
        for i, (source, target) in enumerate(shares(turned(y, a) * 2 + turned(x, b), t)):
            remote(
                source, target, later_sent.at[f, t, i // 3], later_arrived.at[f, core, i // 3],
                (z, turned(y, a), turned(x, b), t)
            ).start()

    for f in (1, 2, 3):
        for t in range(2):
            send_later(f, t)
    for t in range(2):

        @pl.when(core == t)
        def _():
            for i, (source, target) in enumerate(shares(y * 2 + x, t)):
                pltpu.make_async_copy(source, target, later_own.at[i]).start()

        @pl.when(core != t)
        def _():
            send_later(0, t)

    _, least, slot = units_of(hidden, 1, 1)
    pads = [
        pltpu.make_async_copy(
            zeros, later_b.at[:, pl.ds(i * slot + least, slot - least)], zero_sem.at[i]
        )
        for i in range(3)
    ]

    @pl.when(core == 1)
    def _():
        for copy in pads:
            copy.start()

    pass_on(1)
    project_copies = [
        remote(w_project, shelf.at[z], project_sent.at[k], shelf_arrived.at[z], other)
        for k, other in enumerate(others_z)
    ]
    project_kept = pltpu.make_async_copy(w_project, shelf.at[z], project_own.at[0])
    project_kept.start()
    for copy in project_copies:
        copy.start()
    gather_normed.forward()
    pass_on(2)
    rate_own.wait()
    for copy in rate_copies:
        copy.wait_recv()
    for k in range(1, 8):
        place = rates.at[me]
        copy = remote(place, place, rates_sent.at[k], rates_arrived.at[k], devices[k])
        copy.start()
        rate_copies.append(copy)
    gather_normed.finish()
    own_j, keeps = 2 * x + core, core == y
    rows_of = lambda j: project.at[pl.ds(pl.multiple_of(j * rows, rows), rows)]

    def hand_on(l):
        return remote(
            shelf.at[l], rows_of(own_j), project_sent.at[layers - 1 + l], project_arrived.at[own_j],
            (z, l // 2, l % 2, y)
        )

    kept_here = pltpu.make_async_copy(shelf.at[2 * y + x], rows_of(own_j), project_own.at[1])
    project_kept.wait()
    for l in range(layers):
        is_own = keeps & (l == 2 * y + x)

        @pl.when(z != l)
        def _():
            remote(
                shelf.at[l], shelf.at[l], project_sent.at[0], shelf_arrived.at[l], sibling
            ).wait_recv()

        @pl.when(is_own)
        def _():
            kept_here.start()

        @pl.when(jnp.logical_not(is_own))
        def _():
            hand_on(l).start()

    pass_on(3)
    for j in range(4):

        @pl.when(jnp.logical_not(keeps & (own_j == j)))
        def _():
            remote(
                rows_of(j), rows_of(j), project_sent.at[0], project_arrived.at[j], sibling
            ).wait_recv()

    @pl.when(keeps)
    def _():
        kept_here.wait()

    for copy in project_copies:
        copy.wait_send()
    for l in range(layers):

        @pl.when(jnp.logical_not(keeps & (l == 2 * y + x)))
        def _():
            hand_on(l).wait_send()

    for t in range(2):

        @pl.when(core == t)
        def _():
            for f in range(4):
                for s in range(2):
                    if f or s != t:
                        later_wait(t, later_arrived.at[f, s], True)
            for i, (source, target) in enumerate(shares(y * 2 + x, t)):
                pltpu.make_async_copy(source, target, later_own.at[i]).wait()

    @pl.when(core == 1)
    def _():
        for copy in pads:
            copy.wait()

    for t in range(2):
        for f in range(1, 4):
            later_wait(t, later_sent.at[f, t], False)

        @pl.when(core != t)
        def _():
            later_wait(t, later_sent.at[0, t], False)

    for k in range(1, 8):
        remote(mine, mine, mixer_sent.at[k], mixer_arrived.at[k], devices[k]).wait_send()
        place = rates.at[ranks[k]]
        remote(place, place, rates_sent.at[k], rates_arrived.at[k], devices[k]).wait_recv()
    for copy in rate_copies:
        copy.wait_send()

    @pl.when(z == 0)
    def _():
        tail[...] = jnp.zeros_like(tail)

    @pl.when(z > 0)
    def _():
        tails(0, 0, 0).wait_recv()

    @pl.when(last)
    def _():
        for a, b, c in flips:
            tails(a, b, c).wait_send()

    for layer in range(4):

        @pl.loop(0, 8)
        def _(rank):
            @pl.when((z < layers - 1) & (layer <= z))
            def _():
                along(layer, rank, True).wait_send()

            @pl.when((z > 0) & (layer >= z))
            def _():
                along(layer, rank, False).wait_send()


def front(w_mixer, w_gate_up, w_down, w_project, w_rates, tokens, gain, place):
    rows, columns = w_mixer.shape
    layers = lax.axis_size("z")
    hidden = w_down.shape[1]
    _, least, slot = units_of(hidden, 1, 1)
    length, width = tokens.shape
    like = jax.ShapeDtypeStruct
    any_, vmem = pl.BlockSpec(memory_space=pl.ANY), pl.BlockSpec(memory_space=pltpu.VMEM)
    return pl.pallas_call(
        front_kernel,
        out_shape=[
            like((8 * layers * rows, columns // 8), LOW),
            like((8 * rows, 3 * slot), LOW),
            like((8 * rows, 3 * slot), LOW),
            like((4 * rows, w_project.shape[1]), LOW),
            like((8, length, width), LOW),
            like((16, width), LOW),
            like((8, layers, rows, 128), LOW),
        ],
        in_specs=[any_, any_, any_, any_, vmem, vmem, vmem],
        out_specs=[any_, any_, any_, any_, vmem, vmem, vmem],
        scratch_shapes=[
            pltpu.VMEM((length, width), LOW),
            pltpu.VMEM((8 * rows, slot - least), LOW),
            pltpu.VMEM((rows, 128), LOW),
            pltpu.VMEM((layers, rows, width), LOW),
            DMA((2,)), DMA((2 * layers - 1,)), DMA((layers,)), DMA((4,)),
            DMA, DMA((layers - 1,)), DMA((layers - 1,)), DMA((8,)), DMA((8,)),
            DMA((4,)), DMA((8,)), DMA((8,)), DMA((4, 8)), DMA((4, 8)), DMA((4, 8)),
            DMA((6,)), DMA((4, 2, 2)), DMA((4, 2, 2)), DMA((3,)), DMA((8,)), DMA,
        ]
        + GATHER_SEMAPHORES,
        compiler_params=pltpu.CompilerParams(
            collective_id=place, has_side_effects=True, vmem_limit_bytes=VMEM_MOST
        ),
        cost_estimate=pl.CostEstimate(flops=0, bytes_accessed=250_000_000, transcendentals=0),
        name="front",
    )(
        w_mixer, w_gate_up, w_down, w_project, tokens, gain[None], w_rates
    )


def scatter_steps(
    terms, out, held, from_core, over_a, over_b, side_x, side_y, core_sent, core_arrived,
    across_sent, across_arrived, sent, arrived
):
    z, y, x, core, over_x, over_y, sibling = neighbours()
    rows = terms.shape[1]
    half, step = rows // 2, 16
    chunks = lambda c: [
        rank_of(1 - y, 1 - x, c), rank_of(y, 1 - x, c), rank_of(1 - y, x, c), rank_of(y, x, c)
    ]
    mine, theirs = chunks(core), chunks(1 - core)
    to_core = [
        remote(terms.at[theirs[i]], from_core.at[i], core_sent.at[i], core_arrived.at[i], sibling)
        for i in range(4)
    ]
    for copy in to_core:
        copy.start()
    yield

    def add(target, at, count, more=None):
        @pl.loop(0, count, step=step)
        def _(r):
            here = pl.ds(pl.multiple_of(at + r, step), step)
            total = terms[mine[target], here, :].astype(WIDE) + from_core[target, here, :].astype(WIDE)
            if more is not None:
                total = total + more[pl.ds(pl.multiple_of(r, step), step), :].astype(WIDE)
            held[target, here, :] = total.astype(LOW)

    top, bottom = pl.ds(0, half), pl.ds(half, half)
    to_core[0].wait_recv()
    add(0, 0, rows)
    top_y = remote(held.at[0, top], over_a, across_sent.at[0], across_arrived.at[0], over_y)
    bottom_x = remote(held.at[0, bottom], over_b, across_sent.at[1], across_arrived.at[1], over_x)
    top_y.start()
    bottom_x.start()
    yield
    to_core[1].wait_recv()
    add(1, half, half)
    x_bottom = remote(held.at[1, bottom], side_x.at[bottom], sent.at[0, 1], arrived.at[0, 1], over_x)
    x_bottom.start()
    to_core[2].wait_recv()
    add(2, 0, half)
    y_top = remote(held.at[2, top], side_y.at[top], sent.at[1, 0], arrived.at[1, 0], over_y)
    y_top.start()
    yield
    top_y.wait_recv()
    add(1, 0, half, over_a)
    x_top = remote(held.at[1, top], side_x.at[top], sent.at[0, 0], arrived.at[0, 0], over_x)
    x_top.start()
    bottom_x.wait_recv()
    add(2, half, half, over_b)
    y_bottom = remote(held.at[2, bottom], side_y.at[bottom], sent.at[1, 1], arrived.at[1, 1], over_y)
    y_bottom.start()
    yield
    to_core[3].wait_recv()
    for copy in (x_bottom, y_top, x_top, y_bottom):
        copy.wait_recv()

    @pl.loop(0, rows, step=step)
    def _(r):
        here = pl.ds(pl.multiple_of(r, step), step)
        out[here, :] = (
            terms[mine[3], here, :].astype(WIDE)
            + from_core[3, here, :].astype(WIDE)
            + (side_x[here, :].astype(WIDE) + side_y[here, :].astype(WIDE))
        )

    for copy in to_core + [top_y, bottom_x, x_bottom, y_top, x_top, y_bottom]:
        copy.wait_send()


def scatter_kernel(*refs):
    greet(neighbours()[4:])
    for _ in scatter_steps(*refs):
        pass


def scatter_scratch(rows, width):
    block = lambda *shape: pltpu.VMEM(shape, LOW)
    return [
        block(3, rows, width),
        block(4, rows, width),
        block(rows // 2, width),
        block(rows // 2, width),
        block(rows, width),
        block(rows, width),
        DMA((4,)),
        DMA((4,)),
        DMA((2,)),
        DMA((2,)),
        DMA((2, 2)),
        DMA((2, 2)),
    ]


def behind(kernel, count):
    return lambda *refs: kernel(*refs[count:])


def plane_scatter(terms, place, after=()):
    rows, width = terms.shape[0] // 8, terms.shape[1]
    return pl.pallas_call(
        behind(scatter_kernel, len(after)),
        out_shape=jax.ShapeDtypeStruct((rows, width), WIDE),
        in_specs=[pl.BlockSpec(memory_space=pl.ANY)] * len(after)
        + [pl.BlockSpec(memory_space=pltpu.VMEM)],
        out_specs=pl.BlockSpec(memory_space=pltpu.VMEM),
        scratch_shapes=scatter_scratch(rows, width),
        compiler_params=pltpu.CompilerParams(
            collective_id=place, has_side_effects=True, vmem_limit_bytes=VMEM_MOST
        ),
        cost_estimate=pl.CostEstimate(flops=0, bytes_accessed=80_000_000, transcendentals=0),
        name="plane_scatter",
    )(*after, terms.reshape(8, rows, width))


def feed_forward_kernel(normed, cotangent, weights, *rest):
    before, (inner, grad_swiglu, back, out) = rest[:-4], rest[-4:]
    slot = inner.shape[1]
    gate_up, down = weights.at[:, : 2 * slot], weights.at[:, 2 * slot :]
    both = once(normed[...], gate_up[...])
    given = once(cotangent[...], down[...])
    a, b = both[:, :slot], both[:, slot:]
    open_ = jax.nn.sigmoid(a)
    active = a * open_
    inner_low = (active * b).astype(LOW)
    swiglu = jnp.concatenate(
        [given * b * open_ * (1.0 + a * (1.0 - open_)), given * active], 1
    ).astype(LOW)
    inner[...] = inner_low
    grad_swiglu[...] = swiglu
    terms = [once(swiglu, gate_up[...], NT), once(inner_low, down[...], NT)]
    for i, target in enumerate((back, out)):
        term = terms[i] + before[i][...] if before else terms[i]
        target[...] = term.astype(target.dtype)


def feed_forward(normed, cotangent, weights, before=()):
    tokens, width = normed.shape
    slot = weights.shape[1] // 3
    step = 256
    like = jax.ShapeDtypeStruct
    kind = LOW if before else WIDE
    return pl.pallas_call(
        feed_forward_kernel,
        grid=(tokens // step,),
        in_specs=[rows_spec((step, width)), rows_spec((step, width)), whole_spec(weights.shape)]
        + [rows_spec((step, width))] * len(before),
        out_specs=[
            rows_spec((step, slot)),
            rows_spec((step, 2 * slot)),
            rows_spec((step, width)),
            rows_spec((step, width)),
        ],
        out_shape=[
            like((tokens, slot), LOW),
            like((tokens, 2 * slot), LOW),
            like((tokens, width), kind),
            like((tokens, width), kind),
        ],
        compiler_params=pltpu.CompilerParams(vmem_limit_bytes=VMEM_MOST),
        cost_estimate=cost(2 * tokens * width * 6 * slot, 3e7),
        name="feed_forward",
    )(normed, cotangent, weights, *before)


def later_terms_kernel(normed, cotangent, swiglu, inner, out):
    both = swiglu.shape[1]
    out[:, :both] = once(normed[...], swiglu[...], TN).astype(LOW)
    out[:, both:] = once(cotangent[...], inner[...], TN).astype(LOW)


def later_terms(normed, cotangent, swiglu, inner):
    tokens, rows = normed.shape
    columns = swiglu.shape[1] + inner.shape[1]
    step = 256
    return pl.pallas_call(
        later_terms_kernel,
        grid=(rows // step,),
        in_specs=[pl.BlockSpec((tokens, step), lambda i: (0, i))] * 2
        + [whole_spec(swiglu.shape), whole_spec(inner.shape)],
        out_specs=rows_spec((step, columns)),
        out_shape=jax.ShapeDtypeStruct((rows, columns), LOW),
        compiler_params=pltpu.CompilerParams(vmem_limit_bytes=VMEM_MOST),
        cost_estimate=cost(2 * tokens * rows * columns, 2e7),
        name="later_terms",
    )(normed, cotangent, swiglu, inner)


def mixer_terms_kernel(slots, normed, mixed, out):
    rows, columns = normed.shape[1], mixed.shape[1]
    few = slots.shape[1]
    out[0, :rows, :] = once(normed[...], mixed[...], TN).astype(LOW)
    for half in range(2):
        out[0, rows + half * few : rows + (half + 1) * few, :] = slots[
            0, :, half * columns : (half + 1) * columns
        ]


def mixer_terms(slots, normed, mixed):
    tokens, rows = normed.shape
    columns = mixed.shape[1]
    layers, few, width = slots.shape
    share = rows // layers + 2 * few
    return pl.pallas_call(
        mixer_terms_kernel,
        grid=(layers,),
        in_specs=[
            rows_spec((1, few, width)),
            pl.BlockSpec((tokens, rows // layers), lambda i: (0, i)),
            whole_spec(mixed.shape),
        ],
        out_specs=rows_spec((1, share, columns)),
        out_shape=jax.ShapeDtypeStruct((layers, share, columns), LOW),
        compiler_params=pltpu.CompilerParams(vmem_limit_bytes=VMEM_MOST),
        cost_estimate=cost(2 * tokens * rows * columns, 2e7),
        name="mixer_terms",
    )(slots, normed, mixed)


def chain_kernel(reverse, whole, term, out, arriving, leaving, sent, arrived):
    z, y, x, core = (lax.axis_index(name) for name in ALL)
    layers = lax.axis_size("z")
    at = layers - 1 - z if reverse else z
    nearer = jnp.clip(z + (1 if reverse else -1), 0, layers - 1)
    further = jnp.clip(z + (-1 if reverse else 1), 0, layers - 1)
    barrier = pltpu.get_barrier_semaphore()

    @pl.when(at > 0)
    def _():
        pl.semaphore_signal(barrier, inc=1, device_id=(nearer, y, x, core), device_id_type=MESH)

    copy = remote(leaving, arriving, sent, arrived, (further, y, x, core))
    size = out.shape[1]
    factor = whole.at[:, :size]
    if not reverse:
        term = whole.at[:, size:]

    @pl.when(at == 0)
    def _():
        out[...] = jnp.zeros_like(out)
        leaving[...] = term[...].astype(LOW)

    @pl.when(at > 0)
    def _():
        copy.wait_recv()
        out[...] = arriving[...].astype(WIDE)

    @pl.when((at > 0) & (at < layers - 1))
    def _():
        for h in range(2):
            rows = slice(h * 128, (h + 1) * 128)
            moved = thrice(factor[rows, :], out[rows, :], TN if reverse else NN)
            leaving[rows, :] = (moved + term[rows, :]).astype(LOW)

    @pl.when(at < layers - 1)
    def _():
        pl.semaphore_wait(barrier, 1)
        copy.start()
        copy.wait_send()


def back_chain_kernel(
    whole, term, terms, out, slots, arriving, leaving, sent, arrived, kept, slot_sent, slot_arrived
):
    z, y, x, core, over_x, over_y, sibling = neighbours()
    layers = lax.axis_size("z")
    rows = slots.shape[1]
    at = layers - 1 - z
    nearer = (jnp.minimum(z + 1, layers - 1), y, x, core)
    further = (jnp.maximum(z - 1, 0), y, x, core)
    own_j, keeps = 2 * x + core, core == y
    barrier = pltpu.get_barrier_semaphore()

    @pl.when(at > 0)
    def _():
        pl.semaphore_signal(barrier, inc=1, device_id=nearer, device_id_type=MESH)

    for l in range(layers):

        @pl.when(jnp.logical_not(keeps & (l == 2 * y + x)))
        def _():
            pl.semaphore_signal(
                barrier, inc=1, device_id=(z, l // 2, l % 2, y), device_id_type=MESH
            )

    pl.semaphore_wait(
        barrier, layers - jnp.where(keeps, 1, 0) + jnp.where(at < layers - 1, 1, 0)
    )
    chain_copy = remote(leaving, arriving, sent, arrived, further)
    mine = slots.at[2 * y + x]

    def pass_terms(j):
        return remote(
            terms.at[pl.ds(j * rows, rows)], mine, slot_sent.at[j], slot_arrived.at[2 * y + x],
            (z, core, j // 2, j % 2)
        )

    kept_copy = pltpu.make_async_copy(
        terms.at[pl.ds(pl.multiple_of(own_j * rows, rows), rows)], mine, kept
    )

    @pl.when(at == 0)
    def _():
        out[...] = jnp.zeros_like(out)
        leaving[...] = term[...].astype(LOW)
        chain_copy.start()

    for j in range(4):

        @pl.when(jnp.logical_not(keeps & (own_j == j)))
        def _():
            pass_terms(j).start()

    @pl.when(keeps)
    def _():
        kept_copy.start()

    @pl.when(at > 0)
    def _():
        chain_copy.wait_recv()
        out[...] = arriving[...].astype(WIDE)

    @pl.when((at > 0) & (at < layers - 1))
    def _():
        size = out.shape[1]
        for h in range(2):
            here = slice(h * 128, (h + 1) * 128)
            moved = thrice(whole[here, :size], out[here, :], TN)
            leaving[here, :] = (moved + term[here, :]).astype(LOW)
        chain_copy.start()

    for l in range(layers):

        @pl.when(jnp.logical_not(keeps & (l == 2 * y + x)))
        def _():
            remote(
                slots.at[l], slots.at[l], slot_sent.at[0], slot_arrived.at[l], sibling
            ).wait_recv()

    @pl.when(keeps)
    def _():
        kept_copy.wait()

    for j in range(4):

        @pl.when(jnp.logical_not(keeps & (own_j == j)))
        def _():
            pass_terms(j).wait_send()

    @pl.when(at < layers - 1)
    def _():
        chain_copy.wait_send()


def back_chain(whole, term, terms, place):
    shape = (whole.shape[0], whole.shape[1] // 2)
    layers = lax.axis_size("z")
    rows, width = terms.shape[0] // 4, terms.shape[1]
    like = jax.ShapeDtypeStruct
    return pl.pallas_call(
        back_chain_kernel,
        out_shape=[like(shape, WIDE), like((layers, rows, width), LOW)],
        in_specs=[pl.BlockSpec(memory_space=pltpu.VMEM)] * 3,
        out_specs=[pl.BlockSpec(memory_space=pltpu.VMEM)] * 2,
        scratch_shapes=[
            pltpu.VMEM(shape, LOW), pltpu.VMEM(shape, LOW), DMA, DMA, DMA, DMA((4,)), DMA((layers,)),
        ],
        compiler_params=pltpu.CompilerParams(
            collective_id=place, has_side_effects=True, vmem_limit_bytes=VMEM_MOST
        ),
        cost_estimate=pl.CostEstimate(flops=0, bytes_accessed=50_000_000, transcendentals=0),
        name="back_chain",
    )(whole, term, terms)


def chain(whole, term, reverse, place):
    shape = (whole.shape[0], whole.shape[1] // 2)
    return pl.pallas_call(
        partial(chain_kernel, reverse),
        out_shape=jax.ShapeDtypeStruct(shape, WIDE),
        in_specs=[pl.BlockSpec(memory_space=pltpu.VMEM)] * 2,
        out_specs=pl.BlockSpec(memory_space=pltpu.VMEM),
        scratch_shapes=[pltpu.VMEM(shape, LOW), pltpu.VMEM(shape, LOW), DMA, DMA],
        compiler_params=pltpu.CompilerParams(
            collective_id=place, has_side_effects=True, vmem_limit_bytes=VMEM_MOST
        ),
        cost_estimate=pl.CostEstimate(flops=0, bytes_accessed=40_000_000, transcendentals=0),
        name="chain",
    )(whole, term)


def later_back_steps(sums_a, sums_b, gate_up, down, own_sem, sent, arrived):
    z, y, x, core, over_x, over_y, sibling = neighbours()
    rows, hidden = down.shape
    per_chip = hidden // 4
    me = rank_of(y, x, core)
    flips = [(k >> 2, (k >> 1) & 1, k & 1) for k in range(8)]
    devices = [(z, turned(y, a), turned(x, b), turned(core, c)) for a, b, c in flips]
    ranks = [rank_of(*device[1:]) for device in devices]

    def parts(rank, t):
        chip = y * 2 + x
        here = pl.ds(pl.multiple_of(rank * rows, rows), rows)
        found = []
        for half, sums in enumerate((sums_a, sums_b)):
            begin, size, slot = units_of(hidden, t, half)
            first = pl.multiple_of(chip * per_chip + begin, 128)
            up = pl.multiple_of(hidden + first, 128)
            found += [
                (sums.at[here, pl.ds(0, size)], gate_up.at[:, pl.ds(first, size)]),
                (sums.at[here, pl.ds(slot, size)], gate_up.at[:, pl.ds(up, size)]),
                (sums.at[here, pl.ds(2 * slot, size)], down.at[:, pl.ds(first, size)]),
            ]
        return found

    def amount(t):
        return [
            down.at[:, pl.ds(0, 3 * units_of(hidden, t, half)[1])] for half in range(2)
        ]

    for t in range(2):

        @pl.when(core == t)
        def _():
            for k in (2, 4, 6, 3, 5, 7, 1):
                for i, (source, target) in enumerate(parts(ranks[k], t)):
                    remote(
                        source, target, sent.at[k, i // 3], arrived.at[k, i // 3], devices[k]
                    ).start()
            for i, (source, target) in enumerate(parts(me, t)):
                pltpu.make_async_copy(source, target, own_sem.at[i]).start()

    for _ in range(5):
        yield
    for t in range(2):

        @pl.when(core == t)
        def _():
            for i, (source, target) in enumerate(parts(me, t)):
                pltpu.make_async_copy(source, target, own_sem.at[i]).wait()

    for k in range(1, 8):
        for t in range(2):
            @pl.when(turned(core, k & 1) == t)
            def _():
                for half, place in enumerate(amount(t)):
                    remote(
                        place, place, sent.at[k, half], arrived.at[k, half], devices[k]
                    ).wait_recv()

            @pl.when(core == t)
            def _():
                for half, place in enumerate(amount(t)):
                    remote(
                        place, place, sent.at[k, half], arrived.at[k, half], devices[k]
                    ).wait_send()


def small_steps(small, layers_in, gathered, z_sent, z_arrived, sent, arrived, patience=2):
    z, y, x, core, over_x, over_y, sibling = neighbours()
    layers = layers_in.shape[0]
    me = rank_of(y, x, core)
    flips = [(k >> 2, (k >> 1) & 1, k & 1) for k in range(8)]
    devices = [(z, turned(y, a), turned(x, b), turned(core, c)) for a, b, c in flips]
    ranks = [rank_of(*device[1:]) for device in devices]
    to_layers = [
        remote(
            small, layers_in.at[z], z_sent.at[k], z_arrived.at[k], (lax.rem(z + k, layers), y, x, core)
        )
        for k in range(1, layers)
    ]
    for copy in to_layers:
        copy.start()
    layers_in[z] = small[...]
    for _ in range(patience):
        yield
    for copy in to_layers:
        copy.wait_recv()
    total = layers_in[0]
    for k in range(1, layers):
        total = total + layers_in[k]
    gathered[me] = total
    spread = [
        remote(gathered.at[me], gathered.at[me], sent.at[k], arrived.at[k], devices[k])
        for k in range(1, 8)
    ]
    for copy in spread:
        copy.start()
    for _ in range(patience):
        yield
    for k in range(1, 8):
        place = gathered.at[ranks[k]]
        remote(place, place, sent.at[k], arrived.at[k], devices[k]).wait_recv()
    for copy in to_layers + spread:
        copy.wait_send()


def small_scratch(shape, layers):
    return [
        pltpu.VMEM(shape, WIDE),
        pltpu.VMEM((layers,) + shape, WIDE),
        pltpu.VMEM((8,) + shape, WIDE),
        DMA((layers,)),
        DMA((layers,)),
        DMA((8,)),
        DMA((8,)),
    ]


def together(running):
    while running:
        for steps in list(running):
            if next(steps, running) is running:
                running.remove(steps)


def others_of(z, y, x, core):
    flips = [(k >> 2, (k >> 1) & 1, k & 1) for k in range(1, 8)]
    layers = lax.axis_size("z")
    return [(z, turned(y, a), turned(x, b), turned(core, c)) for a, b, c in flips] + [
        (lax.rem(z + k, layers), y, x, core) for k in range(1, layers)
    ]


def source_steps(terms, out, tokens, small, scatter_parts, small_parts):
    yield from scatter_steps(terms, out, *scatter_parts)
    total = jnp.zeros((1, out.shape[1]), WIDE)
    for first in range(0, out.shape[0], 32):
        source = tokens[first : first + 32, :].astype(WIDE)
        scale = lax.rsqrt(jnp.mean(source * source, axis=-1, keepdims=True) + 1e-06)
        total = total + jnp.sum(
            out[first : first + 32, :] * source * scale, axis=0, keepdims=True
        )
    step = small.shape[1]
    for row in range(small.shape[0]):
        small[row : row + 1, :] = total[:, row * step : (row + 1) * step]
    yield from small_steps(small, *small_parts, patience=1)


def return_all_kernel(
    terms_a, terms_b, sums_a, sums_b, tokens, grad_kernel, decays, head_gain, gain_mlp, rate_terms,
    out_a, out_b, gate_up, down, all_kernel, all_decays, all_head, all_mlp, all_rates, all_mixer,
    *rest
):
    z, y, x, core, over_x, over_y, sibling = neighbours()
    barrier = pltpu.get_barrier_semaphore()
    others = others_of(z, y, x, core)
    for other in others:
        pl.semaphore_signal(barrier, inc=1, device_id=other, device_id_type=MESH)
    small, gathered = rest[0], rest[2]
    high = 6 * 128
    wide = 256
    small[...] = jnp.zeros_like(small)
    small[0:4, :high] = grad_kernel[0:4, :]
    small[0:1, high : high + 128] = decays[0:1, :]
    small[0:1, high + 128 :] = decays[1:2, :]
    small[1:2, high : high + 128] = head_gain[0:1, :]
    small[4:6, :] = gain_mlp[...]
    half = small.shape[1]
    small[8:12, :] = rate_terms[0:4, :half]
    small[12:16, :] = rate_terms[0:4, half:]
    pl.semaphore_wait(barrier, len(others))
    gain_parts, scratch = rest[7:14], rest[14:]
    count = (len(scratch) - 3) // 2
    together([
        source_steps(
            terms_a, out_a, tokens, gain_parts[0], scratch[:count], gain_parts[1:]
        ),
        scatter_steps(terms_b, out_b, *scratch[count : 2 * count]),
        later_back_steps(sums_a, sums_b, gate_up, down, *scratch[2 * count :]),
        small_steps(*rest[:7]),
    ])
    gains = gain_parts[2]
    whole = gains[0]
    for r in range(1, 8):
        whole = whole + gains[r]
    all_mixer[...] = whole
    whole = gathered[0]
    for r in range(8):
        for part in range(3):
            all_kernel[0:4, part * 8 * wide + r * wide : part * 8 * wide + (r + 1) * wide] = (
                gathered[r, 0:4, part * wide : (part + 1) * wide]
            )
        all_decays[r : r + 1, :] = gathered[r, 0:1, high:]
        all_rates[r] = gathered[r, 8:16, :]
        if r:
            whole = whole + gathered[r]
    all_head[...] = whole[1:2, high : high + 128]
    all_mlp[...] = whole[4:6, :]


def return_all(terms_a, terms_b, sums_a, sums_b, tokens, smalls, hidden, place, after=()):
    rows, width = terms_a.shape[0] // 8, terms_a.shape[1]
    owned = sums_a.shape[0] // 8
    layers = lax.axis_size("z")
    any_, vmem = pl.BlockSpec(memory_space=pl.ANY), pl.BlockSpec(memory_space=pltpu.VMEM)
    like = jax.ShapeDtypeStruct
    return pl.pallas_call(
        behind(return_all_kernel, len(after)),
        out_shape=[
            like((rows, width), WIDE),
            like((rows, width), WIDE),
            like((owned, 2 * hidden), LOW),
            like((owned, hidden), LOW),
            like((4, 6 * 1024), WIDE),
            like((8, 256), WIDE),
            like((1, 128), WIDE),
            like((2, 1024), WIDE),
            like((8, 8, 1024), WIDE),
            like((8, 256), WIDE),
        ],
        in_specs=[any_] * len(after) + [vmem, vmem, any_, any_] + [vmem] * 6,
        out_specs=[vmem, vmem, any_, any_] + [vmem] * 6,
        scratch_shapes=small_scratch((16, 1024), layers)
        + small_scratch((8, 256), layers)
        + scatter_scratch(rows, width) * 2
        + [DMA((6,)), DMA((8, 2)), DMA((8, 2))],
        compiler_params=pltpu.CompilerParams(
            collective_id=place, has_side_effects=True, vmem_limit_bytes=VMEM_MOST
        ),
        cost_estimate=pl.CostEstimate(flops=0, bytes_accessed=200_000_000, transcendentals=0),
        name="return_all",
    )(
        *after, terms_a.reshape(8, rows, width), terms_b.reshape(8, rows, width), sums_a, sums_b,
        tokens, *smalls
    )


def mixer_back_steps(sums, mixer, own_sem, sent, arrived):
    z, y, x, core, over_x, over_y, sibling = neighbours()
    rows, columns = mixer.shape
    wide, width = columns // 32, columns // 4
    me = rank_of(y, x, core)
    flips = [(k >> 2, (k >> 1) & 1, k & 1) for k in range(8)]
    devices = [(z, turned(y, a), turned(x, b), turned(core, c)) for a, b, c in flips]
    ranks = [rank_of(*device[1:]) for device in devices]

    def parts(rank):
        here = pl.ds(pl.multiple_of(rank * rows, rows), rows)
        return [
            (
                sums.at[here, pl.ds(p * wide, wide)],
                mixer.at[:, pl.ds(pl.multiple_of(p * width + me * wide, 128), wide)],
            )
            for p in range(4)
        ]

    for k in (2, 4, 6, 3, 5, 7, 1):
        for source, target in parts(ranks[k]):
            remote(source, target, sent.at[k], arrived.at[k], devices[k]).start()
    owns = [
        pltpu.make_async_copy(source, target, own_sem.at[i])
        for i, (source, target) in enumerate(parts(me))
    ]
    for copy in owns:
        copy.start()
    yield
    yield
    for copy in owns:
        copy.wait()
    place = mixer.at[:, pl.ds(0, 4 * wide)]
    for k in range(1, 8):
        remote(place, place, sent.at[k], arrived.at[k], devices[k]).wait()


def last_kernel(sums, mixer, *rest):
    z, y, x, core, over_x, over_y, sibling = neighbours()
    greet(others_of(z, y, x, core)[:7])
    together([mixer_back_steps(sums, mixer, *rest)])


def last(sums, rows, place, after=()):
    columns = sums.shape[1]
    any_ = pl.BlockSpec(memory_space=pl.ANY)
    return pl.pallas_call(
        behind(last_kernel, len(after)),
        out_shape=jax.ShapeDtypeStruct((rows, 8 * columns), LOW),
        in_specs=[any_] * (len(after) + 1),
        out_specs=any_,
        scratch_shapes=[DMA((4,)), DMA((8,)), DMA((8,))],
        compiler_params=pltpu.CompilerParams(
            collective_id=place, has_side_effects=True, vmem_limit_bytes=VMEM_MOST
        ),
        cost_estimate=pl.CostEstimate(flops=0, bytes_accessed=60_000_000, transcendentals=0),
        name="last",
    )(*after, sums)


def heads_on_plane(
    tokens,
    w_mixer,
    w_rates,
    w_project,
    w_gate_up,
    w_down,
    conv_kernel,
    decay_log,
    decay_bias,
    head_gain,
    gain_mixer,
    gain_mlp,
    cotangent,
):
    length, width = tokens.shape
    size = head_gain.shape[0]
    rows = w_mixer.shape[0]
    hidden = w_down.shape[1]
    layers = lax.axis_size("z")
    ranks = lax.axis_size(ALL) // layers
    own = decay_log.shape[0] // ranks
    layer, rank = lax.axis_index("z"), lax.axis_index(PLANE)
    low = jnp.bfloat16
    wide = own * size

    def over_layers(terms):
        return lax.psum_scatter(terms, "z", scatter_dimension=0, tiled=True)

    gather = plane_gather

    def scatter(terms, place, after=()):
        return plane_scatter(terms.astype(low), place, after)

    source = tokens.astype(jnp.float32)
    norm_pull = jax.vjp(norm_scale, source, gain_mixer)[1]
    mixer, later_a, later_b, project, normed_all, tail, all_rates = front(
        w_mixer, w_gate_up, w_down, w_project, w_rates, tokens, gain_mixer, 1
    )
    total = length * ranks
    normed_all = normed_all.reshape(total, width)
    later_a = lax.all_gather(later_a, "z", axis=0, tiled=True)
    later_b = lax.all_gather(later_b, "z", axis=0, tiled=True)
    slot = later_a.shape[1] // 3
    all_rates = jnp.swapaxes(all_rates, 0, 1).reshape(width, 128)
    head_at = jnp.arange(2 * own) // own * (ranks * own) + jnp.arange(2 * own) % own + rank * own
    pick = jnp.pad(
        jax.nn.one_hot(head_at, 128, axis=0, dtype=low), ((0, 0), (0, 128 - 2 * own))
    )
    kernel = lax.dynamic_index_in_dim(
        conv_kernel.reshape(4, 3, ranks, wide), rank, 2, False
    ).reshape(4, 3 * wide)
    kernel = jnp.pad(kernel, ((0, 4), (0, 0)))
    log_rate = lax.dynamic_slice_in_dim(decay_log, rank * own, own)
    bias = lax.dynamic_slice_in_dim(decay_bias, rank * own, own)

    downward = [(z + 1, z) for z in range(layers - 1)]
    head_gains = jnp.broadcast_to(head_gain, (8, size))
    pads = ((0, 7), (2, 124))
    rates = jnp.pad(-jnp.exp(log_rate)[None], pads) + jnp.roll(jnp.pad(bias[None], pads), 1, 0)
    (
        mixed_low, gates, rate_in, ue, inverse, scores, steps, before, qk, columns, whole, rate_weight
    ) = prepare(normed_all, mixer, all_rates, pick, tail, kernel, rates)
    start = chain(whole, whole, False, 7)
    branch, gated_low, fresh, states, outputs = finish(
        start, before, ue, scores, qk, columns, gates, head_gains, project
    )
    hidden_state = source + scatter(branch, 2)
    normed_two, norm_two_pull = jax.vjp(norm_scale, hidden_state, gain_mlp)
    normed_two_all = gather(normed_two.astype(low), 3)
    cotangent_all = gather(cotangent, 4, (normed_two_all,))
    sums_of, terms_so_far = [], ()
    for weights in (later_a, later_b):
        inner, grad_swiglu, *terms_so_far = feed_forward(
            normed_two_all, cotangent_all, weights, terms_so_far
        )
        sums_of.append(
            over_layers(later_terms(normed_two_all, cotangent_all, grad_swiglu, inner))
        )
    back_terms, out_terms = terms_so_far
    later_sum_a, later_sum_b = sums_of
    grad_hidden_part, grad_gain_mlp = norm_two_pull(scatter(back_terms, 5))
    grad_hidden = cotangent.astype(jnp.float32) + grad_hidden_part
    grad_branch = gather(grad_hidden.astype(low), 6)
    grad_out, back_scores, returns, grad_gate, local, grad_head_gain = give_back(
        grad_branch, project, gates, head_gains, outputs, scores, ue, qk, columns, steps
    )
    project_terms = dot_tn(gated_low, grad_branch).astype(low)
    later_state, slots = back_chain(whole, local, project_terms, 8)
    grad_mixed, grad_rates, grad_kernel, sums, first_rows, edge = gradients(
        later_state, returns, steps, grad_out, back_scores, fresh, states, inverse, scores, qk, columns,
        mixed_low, rate_in, grad_gate, kernel, rates, (later_sum_a,)
    )
    following = lax.ppermute(first_rows[:3].astype(low), "z", downward).astype(jnp.float32)
    late = [
        sum(kernel[j] * following[r - j] for j in range(r + 1)) for r in range(3)
    ]
    edge = jnp.concatenate([edge[:13], edge[13:] + jnp.stack(late)], 0).astype(low)
    grad_mixed = lax.dynamic_update_slice(grad_mixed, edge, (total - 16, 0))
    terms = mixer_terms(slots, normed_all, grad_mixed)
    rate_terms = dot_tn(grad_rates, normed_all)
    mixer_sum = lax.psum_scatter(terms, "z", scatter_dimension=0)
    source_terms = dot_nt(grad_mixed, mixer) + dot_nt(grad_rates, rate_weight)
    smalls = (grad_kernel, sums, grad_head_gain, grad_gain_mlp.reshape(2, -1), rate_terms)
    (
        from_source, from_inner, grad_gate_up, grad_down, grad_kernel, decays, grad_head_gain,
        grad_gain_mlp, rate_sums, grad_gain_mixer
    ) = return_all(
        source_terms.astype(low), out_terms, later_sum_a, later_sum_b, tokens, smalls, hidden, 10,
        (terms,)
    )
    grad_source = norm_pull(from_source)[0]
    grad_tokens = (grad_hidden + grad_source).astype(low)
    result = (hidden_state + from_inner).astype(low)
    grad_gate_up, grad_down = grad_gate_up.astype(jnp.float32), grad_down.astype(jnp.float32)
    rate_sums = jnp.swapaxes(rate_sums.reshape(ranks, 2, 2 * own, -1, rows), 1, 2)
    rate_sums = rate_sums.reshape(ranks, 2, own, -1, rows)
    grad_rates = lax.dynamic_index_in_dim(rate_sums, layer * ranks + rank, 3, False)
    grad_rates = jnp.transpose(grad_rates, (3, 1, 0, 2)).reshape(rows, -1)
    few = (ranks + 1) * rows
    grad_project = jnp.concatenate(
        [mixer_sum[ranks * rows : few], mixer_sum[few:]], 1
    ).astype(jnp.float32)
    grad_mixer = last(
        mixer_sum, rows, 11,
        (grad_gate_up, grad_down, result, grad_tokens, grad_rates, grad_gain_mixer),
    )
    return (
        result,
        grad_tokens,
        grad_mixer.astype(jnp.float32),
        grad_rates,
        grad_project,
        grad_gate_up,
        grad_down,
        grad_kernel,
        decays[:, 128 + own : 128 + 2 * own].reshape(-1),
        decays[:, own : 2 * own].reshape(-1),
        grad_head_gain[0],
        grad_gain_mixer.reshape(-1),
        grad_gain_mlp.reshape(-1),
    )


def by_planes(mesh, members):
    seq, core = mesh.shape["seq"], mesh.shape["fsdp"]
    layers, ranks = seq // 4, 4 * core
    heads, size = members[7].shape[0], members[9].shape[0]
    return (
        core == 2
        and layers == 4
        and members[0].shape[0] == seq * core * size
        and heads % ranks == 0
        and members[5].shape[1] % (4 * 128) == 0
    )


def solution(mesh):
    rows, copied = P(("seq", "fsdp"), None), P()

    def run(*members):
        if by_planes(mesh, members):
            places = Mesh(mesh.devices.reshape(-1, 2, 2, 2), ALL)
            split, body = P(ALL, None), heads_on_plane
        else:
            places, split, body = mesh, rows, on_device
        return jax.shard_map(
            body,
            mesh=places,
            in_specs=(split,) * 6 + (copied,) * 6 + (split,),
            out_specs=(split,) * 7 + (copied,) * 6,
            check_vma=False,
        )(*members)

    return run
```

```python
from functools import partial

import jax
import jax.numpy as jnp
from jax import lax
from jax.experimental import pallas as pl
from jax.experimental.pallas import tpu as pltpu
from jax.sharding import Mesh
from jax.sharding import PartitionSpec as P

BLOCK = 64


highest = lax.Precision.HIGHEST


def shifted(value, axis, by):
    length = lax.axis_size(axis)
    pairs = [(i, i + by) for i in range(length) if 0 <= i + by < length]
    return lax.ppermute(value, axis, pairs)


def prefix_2(value, axis, join, neutral):
    place = lax.axis_index(axis)
    gathered = jax.tree.map(
        lambda a, kind: lax.all_gather(a.astype(kind), axis), value, (jnp.bfloat16, jnp.bfloat16)
    )
    state = jax.tree.map(lambda a, e: jnp.zeros_like(a) + jnp.asarray(e, a.dtype), value, neutral)

    def one(turn, state):
        return join(
            state,
            jax.tree.map(
                lambda a, own: lax.dynamic_index_in_dim(a, turn, 0, False).astype(own.dtype),
                gathered,
                value,
            ),
        )

    return lax.fori_loop(0, place, one, state)


def entering(value, axis, combine, identity):
    length, place = (lax.axis_size(axis), lax.axis_index(axis))
    everything = jax.tree.map(
        lambda part, kind: lax.all_gather(part.astype(kind), axis),
        value,
        jax.tree.map(lambda a: jnp.bfloat16 if a.dtype == jnp.float32 else a.dtype, value),
    )
    start = jax.tree.map(
        lambda part, zero: jnp.broadcast_to(jnp.asarray(zero, part.dtype), part.shape),
        value,
        identity,
    )

    def turn(k, before):
        at = length - 1 - k
        reached = at > place
        new = combine(
            before, jax.tree.map(lambda part, own: part[at].astype(own.dtype), everything, value)
        )
        return jax.tree.map(lambda a, b: jnp.where(reached, a, b), new, before)

    return lax.fori_loop(0, length, turn, start)


def round_trip(values_in):
    return lax.optimization_barrier(values_in.astype(jnp.bfloat16)).astype(jnp.float32)


def norm_scale(values_in, scales):
    return (
        values_in
        * lax.rsqrt(jnp.mean(values_in * values_in, axis=-1, keepdims=True) + 1e-06)
        * scales
    )


def features(extended, kernel, head_count):
    length = extended.shape[0] - 3
    summed = kernel[0] * extended[0:length]
    for offset in range(1, 4):
        summed = summed + kernel[offset] * extended[offset : offset + length]
    active = jax.nn.silu(summed)
    model_width = active.shape[1] // 3

    def unit_rows(member):
        shaped = member.reshape(length, head_count, -1)
        return shaped * lax.rsqrt(jnp.sum(shaped * shaped, axis=-1, keepdims=True) + 1e-06)

    queries = unit_rows(active[:, :model_width])
    queries = queries * queries.shape[-1] ** (-0.5)
    keys_all = unit_rows(active[:, model_width : 2 * model_width])
    values_all = active[:, 2 * model_width :].reshape(length, head_count, -1)
    return (queries, keys_all, values_all)


def rates_of(rate_inputs, decay_log, decay_bias):
    head_count = decay_log.shape[0]
    strength = jax.nn.sigmoid(rate_inputs[:, :head_count])
    decays = -jnp.exp(decay_log) * jax.nn.softplus(rate_inputs[:, head_count:] + decay_bias)
    return (strength, decays)


def head_output(outputs, gate_part, head_gain):
    normed_heads = (
        outputs * lax.rsqrt(jnp.mean(outputs * outputs, axis=-1, keepdims=True) + 1e-05) * head_gain
    )
    return normed_heads.reshape(outputs.shape[0], -1) * jax.nn.silu(gate_part)


def swiglu(gate_up):
    half_width = gate_up.shape[1] // 2
    return jax.nn.silu(gate_up[:, :half_width]) * gate_up[:, half_width:]


def to_blocks(member):
    block_count = member.shape[0] // BLOCK
    shaped = member.reshape((block_count, BLOCK) + member.shape[1:])
    return jnp.moveaxis(shaped, 2, 1)


def from_blocks(member):
    shaped = jnp.moveaxis(member, 1, 2)
    return shaped.reshape((-1,) + shaped.shape[2:])


def unit_pair(head_count, head_size):
    identity_matrix = jnp.eye(head_size, dtype=jnp.float32)
    return (
        jnp.broadcast_to(identity_matrix, (head_count, head_size, head_size)),
        jnp.zeros((head_count, head_size, head_size), jnp.float32),
    )


def combine(earlier, later):
    product = jnp.einsum("hab,hbc->hac", earlier[0], later[0], precision=highest)
    carried = jnp.einsum("hab,hbc->hac", earlier[1], later[0], precision=highest) + later[1]
    return (product, carried)


def block_terms(query_block, key_block, value_block, strength_block, decay_block):
    block_size = key_block.shape[1]
    lower_ones = jnp.tril(jnp.ones((block_size, block_size), jnp.float32))
    cumulative = jnp.einsum("hd,cd->hc", decay_block, lower_ones, precision=highest)
    positions = jnp.arange(block_size)
    causal = positions[:, None] >= positions[None, :]
    strict = positions[:, None] > positions[None, :]
    spread = cumulative[:, :, None] - cumulative[:, None, :]
    ratios = jnp.where(causal, jnp.exp(jnp.where(causal, spread, 0.0)), 0.0)
    key_products = jnp.einsum("hcd,hed->hce", key_block, key_block, precision=highest)
    lower_part = jnp.where(strict, strength_block[:, :, None] * ratios * key_products, 0.0)
    system = lower_part + jnp.eye(block_size, dtype=jnp.float32)
    gammas = jnp.exp(cumulative)
    updates = lax.linalg.triangular_solve(
        system,
        strength_block[:, :, None] * value_block,
        left_side=True,
        lower=True,
        unit_diagonal=True,
    )
    erasers = lax.linalg.triangular_solve(
        system,
        (strength_block * gammas)[:, :, None] * key_block,
        left_side=True,
        lower=True,
        unit_diagonal=True,
    )
    scores = jnp.einsum("hcd,hed->hce", query_block, key_block, precision=highest) * ratios
    tail_keys = jnp.exp(cumulative[:, -1:] - cumulative)[:, :, None] * key_block
    return (gammas, scores, updates, erasers, tail_keys)


def run_blocks(query_blocks, block_parts, start_state):

    def advance(carried, element):
        query_block, gammas, scores, updates, erasers, tail_keys = element
        fresh_values = updates - jnp.einsum("hcd,hvd->hcv", erasers, carried, precision=highest)
        produced = gammas[:, :, None] * jnp.einsum(
            "hcd,hvd->hcv", query_block, carried, precision=highest
        )
        produced = produced + jnp.einsum("hce,hev->hcv", scores, fresh_values, precision=highest)
        carried = gammas[:, -1][:, None, None] * carried + jnp.einsum(
            "hcv,hcd->hvd", fresh_values, tail_keys, precision=highest
        )
        return (carried, produced)

    end_state, produced = lax.scan(advance, start_state, (query_blocks,) + tuple(block_parts))
    return (produced, end_state)


def span(query_blocks, key_blocks, value_blocks, strength_blocks, decay_blocks, start_state):
    block_parts = jax.vmap(block_terms)(
        query_blocks, key_blocks, value_blocks, strength_blocks, decay_blocks
    )
    return run_blocks(query_blocks, block_parts, start_state)


def block_maps(block_parts, head_size):
    gammas, scores, updates, erasers, tail_keys = block_parts
    identity_matrix = jnp.eye(head_size, dtype=jnp.float32)
    transitions = gammas[:, :, -1][:, :, None, None] * identity_matrix - jnp.einsum(
        "nhcd,nhce->nhde", erasers, tail_keys, precision=highest
    )
    writes = jnp.einsum("nhcv,nhce->nhve", updates, tail_keys, precision=highest)

    def compose(carried, element):
        return (combine(carried, element), None)

    initial = unit_pair(transitions.shape[1], head_size)
    return lax.scan(compose, initial, (transitions, writes))[0]


def term_rows(left, right, precise):
    if precise:
        return jnp.einsum(
            "tr,tc->rc", left, right, precision=highest, preferred_element_type=jnp.float32
        )
    return jnp.einsum("tr,tc->rc", left, right, preferred_element_type=jnp.float32)


def on_device(
    tokens,
    w_mixer,
    w_rates,
    w_project,
    w_gate_up,
    w_down,
    conv_kernel,
    decay_log,
    decay_bias,
    head_gain,
    gain_mixer,
    gain_mlp,
    cotangent,
):
    length, model_width = tokens.shape
    head_count = decay_log.shape[0]
    head_size = head_gain.shape[0]
    conv_width = 3 * model_width
    full_mixer, full_rates, full_project, full_gate_up, full_down = (
        lax.all_gather(w_mixer, ("seq", "fsdp"), axis=0, tiled=True),
        lax.all_gather(w_rates, ("seq", "fsdp"), axis=0, tiled=True),
        lax.all_gather(w_project, ("seq", "fsdp"), axis=0, tiled=True),
        lax.all_gather(w_gate_up, ("seq", "fsdp"), axis=0, tiled=True),
        lax.all_gather(w_down, ("seq", "fsdp"), axis=0, tiled=True),
    )
    source = tokens.astype(jnp.float32)
    normed, norm_pull = jax.vjp(norm_scale, source, gain_mixer)
    normed_low = normed.astype(jnp.bfloat16)
    mixed_low = jnp.dot(normed_low, full_mixer, preferred_element_type=jnp.float32).astype(
        jnp.bfloat16
    )
    rate_inputs = jnp.dot(normed_low, full_rates, preferred_element_type=jnp.float32)
    previous = shifted(mixed_low[length - 3 :, :conv_width], ("seq", "fsdp"), 1)
    extended = jnp.concatenate([previous, mixed_low[:, :conv_width]], 0).astype(jnp.float32)
    triple, feature_pull = jax.vjp(partial(features, head_count=head_count), extended, conv_kernel)
    queries, keys_all, values_all = (round_trip(member) for member in triple)
    (strength, decays), rate_pull = jax.vjp(rates_of, rate_inputs, decay_log, decay_bias)
    blocks = tuple(
        (to_blocks(member) for member in (queries, keys_all, values_all, strength, decays))
    )
    block_parts = jax.vmap(block_terms)(*blocks)
    span_trans, span_writes = block_maps(block_parts, head_size)
    identity = unit_pair(head_count, head_size)
    prefix = prefix_2((span_trans, span_writes), ("seq", "fsdp"), combine, identity)
    start_state = prefix[1]
    output_blocks = run_blocks(blocks[0], block_parts, start_state)[0]
    outputs = from_blocks(output_blocks)
    gate_part = mixed_low[:, conv_width:].astype(jnp.float32)
    gated, head_pull = jax.vjp(head_output, outputs, gate_part, head_gain)
    gated_low = gated.astype(jnp.bfloat16)
    hidden_state = source + jnp.dot(gated_low, full_project, preferred_element_type=jnp.float32)
    normed_two, norm_two_pull = jax.vjp(norm_scale, hidden_state, gain_mlp)
    normed_two_low = normed_two.astype(jnp.bfloat16)
    gate_up = jnp.dot(normed_two_low, full_gate_up, preferred_element_type=jnp.float32)
    inner_act, inner_pull = jax.vjp(swiglu, gate_up)
    inner_low = inner_act.astype(jnp.bfloat16)
    result = hidden_state + jnp.einsum(
        "tf,df->td", inner_low, full_down, preferred_element_type=jnp.float32
    )
    upstream = cotangent.astype(jnp.float32)
    grad_inner = jnp.dot(cotangent, full_down, preferred_element_type=jnp.float32)
    grad_swiglu_low = inner_pull(grad_inner)[0].astype(jnp.bfloat16)
    grad_normed_two = jnp.einsum(
        "tc,dc->td", grad_swiglu_low, full_gate_up, preferred_element_type=jnp.float32
    )
    grad_hidden_part, grad_gain_mlp = norm_two_pull(grad_normed_two)
    grad_hidden = upstream + grad_hidden_part
    grad_hidden_low = grad_hidden.astype(jnp.bfloat16)
    grad_gated = jnp.einsum(
        "te,de->td", grad_hidden_low, full_project, preferred_element_type=jnp.float32
    )
    grad_outputs, grad_gate, grad_head_gain = head_pull(grad_gated)
    grad_out_blocks = to_blocks(grad_outputs)
    primal_pair, span_pull = jax.vjp(span, *blocks, start_state)
    local_grads = span_pull((grad_out_blocks, jnp.zeros_like(start_state)))
    suffix = entering(
        (jnp.swapaxes(span_trans, 1, 2), local_grads[5]), ("seq", "fsdp"), combine, identity
    )
    later_grads = span_pull((jnp.zeros_like(grad_out_blocks), suffix[1]))
    grad_blocks = [
        from_blocks(front_grad + back_grad)
        for front_grad, back_grad in zip(local_grads[:5], later_grads[:5])
    ]
    grad_triple = tuple((round_trip(member) for member in grad_blocks[:3]))
    grad_extended, grad_kernel = feature_pull(grad_triple)
    grad_inputs, grad_decay_log, grad_decay_bias = rate_pull((grad_blocks[3], grad_blocks[4]))
    following = shifted(grad_extended[:3].astype(jnp.bfloat16), ("seq", "fsdp"), -1).astype(
        jnp.float32
    )
    grad_conv = grad_extended[3:] + jnp.pad(following, ((length - 3, 0), (0, 0)))
    grad_mixed_low = jnp.concatenate([grad_conv, grad_gate], 1).astype(jnp.bfloat16)
    grad_normed = jnp.einsum(
        "tc,dc->td", grad_mixed_low, full_mixer, preferred_element_type=jnp.float32
    )
    grad_normed = grad_normed + jnp.dot(
        grad_inputs, full_rates.astype(jnp.float32).T, precision=highest
    )
    grad_source, grad_gain_mixer = norm_pull(grad_normed)
    grad_tokens = (grad_hidden + grad_source).astype(jnp.bfloat16)
    normed_wide = normed_low.astype(jnp.float32)
    grad_mixer = lax.psum_scatter(
        term_rows(normed_low, grad_mixed_low, False),
        ("seq", "fsdp"),
        scatter_dimension=0,
        tiled=True,
    )
    grad_rates = lax.psum_scatter(
        term_rows(normed_wide, grad_inputs, True), ("seq", "fsdp"), scatter_dimension=0, tiled=True
    )
    grad_project = lax.psum_scatter(
        term_rows(gated_low, grad_hidden_low, False),
        ("seq", "fsdp"),
        scatter_dimension=0,
        tiled=True,
    )
    grad_gate_up = lax.psum_scatter(
        term_rows(normed_two_low, grad_swiglu_low, False),
        ("seq", "fsdp"),
        scatter_dimension=0,
        tiled=True,
    )
    grad_down = lax.psum_scatter(
        term_rows(cotangent, inner_low, False), ("seq", "fsdp"), scatter_dimension=0, tiled=True
    )
    small_sums = lax.psum(
        (
            grad_kernel,
            grad_decay_log,
            grad_decay_bias,
            grad_head_gain,
            grad_gain_mixer,
            grad_gain_mlp,
        ),
        ("seq", "fsdp"),
    )
    return (
        result.astype(jnp.bfloat16),
        grad_tokens,
        grad_mixer,
        grad_rates,
        grad_project,
        grad_gate_up,
        grad_down,
        small_sums[0],
        small_sums[1],
        small_sums[2],
        small_sums[3],
        small_sums[4],
        small_sums[5],
    )


def dot_bf16(left, right):
    return jnp.dot(left, right, preferred_element_type=jnp.float32)


def dot_nt(left, right):
    return lax.dot_general(
        left, right, (((1,), (1,)), ((), ())), preferred_element_type=jnp.float32
    )


def dot_tn(left, right):
    return lax.dot_general(
        left, right, (((0,), (0,)), ((), ())), preferred_element_type=jnp.float32
    )


def exact(left, right, dims=((1,), (0,))):
    return lax.dot_general(
        left, right, (dims, ((), ())), precision=highest, preferred_element_type=jnp.float32
    )


NT = ((1,), (1,))
TN = ((0,), (0,))


PLANE = ("y", "x", "core")
ALL = ("z",) + PLANE


LOW, WIDE = jnp.bfloat16, jnp.float32
NN = ((1,), (0,))
VMEM_MOST = 56 << 20


def once(left, right, dims=NN):
    return lax.dot_general(
        left.astype(LOW), right.astype(LOW), (dims, ((), ())), preferred_element_type=WIDE
    )


def halves(value):
    high = value.astype(LOW)
    return high, (value - high.astype(WIDE)).astype(LOW)


def thrice(left, right, dims=NN):
    if not isinstance(left, tuple):
        left = halves(left)
    if not isinstance(right, tuple):
        right = halves(right)
    return (
        once(left[0], right[0], dims) + once(left[0], right[1], dims) + once(left[1], right[0], dims)
    )


def pair_rows(first, second):
    return jnp.concatenate([first, second], 0)


def pair_diagonal(first, second):
    zero = jnp.zeros_like(first)
    return pair_rows(
        jnp.concatenate([first, zero], 1), jnp.concatenate([zero, second], 1)
    )


def square_iotas(size):
    return (
        lax.broadcasted_iota(jnp.int32, (size, size), 0),
        lax.broadcasted_iota(jnp.int32, (size, size), 1),
    )


def decay_ratios(column, row, causal):
    return jnp.where(causal, jnp.exp(jnp.minimum(column - row, 0.0)), 0.0)


def inverses(lowers, differ):
    size = lowers[0].shape[0]
    results = [
        jnp.where(differ == 0, 1.0, 0.0) - jnp.where(differ == 1, lower, 0.0) for lower in lowers
    ]
    for level in range(1, 7):
        parts = [halves(result) for result in results]
        below = [jnp.where((differ >> level) == 1, lower, 0.0) for lower in lowers]
        inner = [thrice(b, p) for b, p in zip(below, parts)]
        results = [r - thrice(p, i) for r, p, i in zip(results, parts, inner)]
    return results


def silu_unit(summed):
    active = summed * jax.nn.sigmoid(summed)
    scale = lax.rsqrt(jnp.sum(active * active, axis=-1, keepdims=True) + 1e-06)
    return active, scale


def conv_of(ext, kernel, column, offset, count):
    at = pl.ds(column, 128)
    summed = kernel[0:1, at] * ext[pl.ds(offset, count), at]
    for j in range(1, 4):
        summed = summed + kernel[j : j + 1, at] * ext[pl.ds(offset + j, count), at]
    return summed


def softplus(value):
    return jnp.maximum(value, 0.0) + jnp.log1p(jnp.exp(-jnp.abs(value)))


def prepare_kernel(
    normed, mixer, all_rates, pick, tail, kernel, rates, mixed, gates, rate_in, ue, inverse, scores, steps, before,
    qk, columns, total, rate_weight, ext, carry
):
    step = pl.program_id(0)
    size = 128
    span = normed.shape[0]
    count = span // size
    conv = 6 * size

    @pl.when(step == 0)
    def _():
        rate_weight[...] = once(all_rates[...], pick[...]).astype(LOW)
        first = once(tail[...], mixer[...])
        low = first.astype(LOW)
        mixed[pl.ds(0, 16), :] = low[:, :conv]
        ext[pl.ds(0, 8), :] = low.astype(WIDE)[8:16, :conv]
        rows, cols = square_iotas(size)
        one = jnp.where(rows == cols, 1.0, 0.0)
        zero = jnp.zeros_like(one)
        carry[...] = pair_rows(
            jnp.concatenate([one, zero], 1), jnp.concatenate([one, zero], 1)
        )

    products = once(normed[...], mixer[...])
    low = products.astype(LOW)
    mixed[pl.ds(pl.multiple_of(16 + step * span, 16), span), :] = low[:, :conv]
    gates[...] = low[:, conv:]
    ext[pl.ds(8, span), :] = low[:, :conv].astype(WIDE)
    rate = once(normed[...], rate_weight[...])
    rate_in[...] = rate
    strength = jax.nn.sigmoid(rate)
    decay = rates[0:1, :] * softplus(rate + rates[1:2, :])
    unit = []
    for part in range(3):
        unit.append([])
        for head in range(2):
            summed = conv_of(ext, kernel, part * 256 + head * size, 5, span)
            active, scale = silu_unit(summed)
            if part == 0:
                active = active * scale * size**-0.5
            if part == 1:
                active = active * scale
            unit[part].append(active.astype(LOW))
    ext[pl.ds(0, 8), :] = ext[pl.ds(span, 8), :]
    small_rows, small_cols = square_iotas(size)
    causal = small_rows >= small_cols
    ones = jnp.where(causal, 1.0, 0.0)
    rows, cols = square_iotas(2 * size)
    differ = rows ^ cols
    lowers, keep = [], []
    for b in range(count):
        at = slice(b * size, (b + 1) * size)
        cumulative = lax.dot_general(
            ones, decay[at], (NN, ((), ())), precision=highest, preferred_element_type=WIDE
        )
        across = cumulative.T
        ratios = pair_diagonal(
            *(
                decay_ratios(cumulative[:, 2 + h : 3 + h], across[2 + h : 3 + h, :], causal)
                for h in range(2)
            )
        )
        query, key, value = (pair_rows(unit[p][0][at], unit[p][1][at]) for p in range(3))
        beta = pair_rows(strength[at, 0:1], strength[at, 1:2])
        column = pair_rows(cumulative[:, 2:3], cumulative[:, 3:4])
        lower = jnp.where(rows > cols, beta * ratios * once(key, key, NT), 0.0)
        lowers.append(lower)
        score = ratios * once(query, key, NT)
        scores[b] = score.astype(LOW)
        qk[b] = jnp.concatenate([query, key], 1)
        lanes = lax.broadcasted_iota(jnp.int32, (2 * size, 128), 1)
        columns[b] = jnp.where(lanes == 0, beta, jnp.where(lanes == 1, column, 0.0))
        keep.append((key.astype(WIDE), value.astype(WIDE), beta, column))
    for b, inv in enumerate(inverses(lowers, differ)):
        key, value, beta, column = keep[b]
        inverse[b] = inv.astype(LOW)
        gammas = jnp.exp(column)
        both = thrice(inv, jnp.concatenate([beta * value, (beta * gammas) * key], 1))
        ue[b] = both
        before[b] = carry[...]
        next_rows = []
        for h in range(2):
            at = slice(h * size, (h + 1) * size)
            last = column[(h + 1) * size - 1 : (h + 1) * size, :]
            tails = jnp.exp(last - column[at]) * key[at]
            made = thrice(tails, both[at], TN)
            advance = jnp.where(small_rows == small_cols, jnp.exp(last), 0.0) - made[:, size:]
            steps[b, at, :] = advance
            moved = thrice(advance, carry[at, :])
            next_rows.append(
                jnp.concatenate([moved[:, :size], moved[:, size:] + made[:, :size]], 1)
            )
        carry[...] = pair_rows(*next_rows)

    @pl.when(step == pl.num_programs(0) - 1)
    def _():
        total[...] = carry[...]


def output_kernel(
    start, before, ue, scores, qk, columns, mixed, gain, project, partial_out, gated_out,
    fresh_out, state_out, out_out
):
    size = 128
    count = ue.shape[0]
    for b in range(count):
        gated = []
        tokens = pl.ds(b * size, size)
        fresh_parts, queried = [], []
        for h in range(2):
            at = slice(h * size, (h + 1) * size)
            pre = before[b, at, :]
            state = thrice(pre[:, :size], start[at, :]) + pre[:, size:]
            state_out[b, at, :] = state
            seen = thrice(
                pair_rows(ue[b, at, size:], qk[b, at, :size].astype(WIDE)), state
            )
            fresh_parts.append(ue[b, at, :size] - seen[:size])
            queried.append(jnp.exp(columns[b, at, 1:2]) * seen[size:])
        fresh = pair_rows(*fresh_parts)
        fresh_out[b] = fresh.astype(LOW)
        outputs = pair_rows(*queried) + once(scores[b], fresh)
        out_out[b] = outputs
        for h in range(2):
            at = slice(h * size, (h + 1) * size)
            one = outputs[at]
            scale = lax.rsqrt(jnp.mean(one * one, axis=-1, keepdims=True) + 1e-05)
            gate = mixed[tokens, pl.ds(h * size, size)].astype(WIDE)
            gated.append((one * scale * gain[0:1, :] * (gate * jax.nn.sigmoid(gate))).astype(LOW))
        both = jnp.concatenate(gated, 1)
        gated_out[tokens, :] = both
        partial_out[tokens, :] = once(both, project[...]).astype(LOW)


def return_kernel(
    branch, project, mixed, gain, out, scores, ue, qk, columns, steps, grad_out, back_scores,
    returns, grad_gate, total, grad_gain, carry
):
    size = 128
    count = ue.shape[0]

    @pl.when(pl.program_id(0) == 0)
    def _():
        carry[...] = jnp.zeros_like(carry)
        grad_gain[...] = jnp.zeros_like(grad_gain)

    grad_gated = once(branch[...], project[...], NT)
    for b in reversed(range(count)):
        tokens = pl.ds(b * size, size)
        grads = []
        for h in range(2):
            at, wide = slice(h * size, (h + 1) * size), pl.ds(h * size, size)
            one = out[b, at, :]
            scale = lax.rsqrt(jnp.mean(one * one, axis=-1, keepdims=True) + 1e-05)
            gate = mixed[tokens, wide].astype(WIDE)
            open_ = jax.nn.sigmoid(gate)
            given = grad_gated[b * size : (b + 1) * size, at]
            normal = one * scale
            through = given * gate * open_
            grad_gain[0:1, :] += jnp.sum(through * normal, axis=0, keepdims=True)
            grad_gate[tokens, wide] = (
                given * normal * gain[0:1, :] * (open_ * (1.0 + gate * (1.0 - open_)))
            ).astype(LOW)
            f = through * gain[0:1, :]
            grads.append(
                scale * f
                - one * (scale * scale * scale) * jnp.mean(f * one, axis=-1, keepdims=True)
            )
        grad = pair_rows(*grads)
        grad_out[b] = grad
        back = once(scores[b], grad, TN)
        back_scores[b] = back
        for h in range(2):
            at = slice(h * size, (h + 1) * size)
            scaled = jnp.exp(columns[b, at, 1:2]) * qk[b, at, :size].astype(WIDE)
            given = once(
                pair_rows(scaled, -ue[b, at, size:]), pair_rows(grad[at], back[at]), TN
            )
            returns[b, at, :] = given
            carry[at, :] = thrice(steps[b, at, :], carry[at, :], TN) + given

    @pl.when(pl.program_id(0) == pl.num_programs(0) - 1)
    def _():
        total[...] = carry[...]


def gradient_kernel(
    end, returns, steps, grad_out, back_scores, fresh, states, inverse, scores, qk, columns,
    mixed, rate_in, grad_gate, kernel, rates, grad_mixed, grad_rates, grad_kernel, sums, front,
    edge, ext, gext, carry
):
    size = 128
    count = fresh.shape[0]
    span = count * size
    conv = 6 * size
    turn = pl.program_id(0)
    step = pl.num_programs(0) - 1 - turn

    @pl.when(turn == 0)
    def _():
        carry[...] = end[...]
        grad_kernel[...] = jnp.zeros_like(grad_kernel)
        sums[...] = jnp.zeros_like(sums)
        gext[pl.ds(span, 8), :] = jnp.zeros((8, conv), WIDE)

    ext[...] = mixed[pl.ds(pl.multiple_of(step * span, 16), span + 16), :].astype(WIDE)
    small_rows, small_cols = square_iotas(size)
    causal = small_rows >= small_cols
    upper = jnp.where(small_rows <= small_cols, 1.0, 0.0)
    rows, cols = square_iotas(2 * size)
    lanes = lax.broadcasted_iota(jnp.int32, (size, 128), 1)
    values = []
    for h in range(2):
        summed = conv_of(ext, kernel, 512 + h * size, 13, span)
        values.append(summed * jax.nn.sigmoid(summed))
    unit_grads = [[None] * count for _ in range(6)]
    for b in reversed(range(count)):
        tokens = slice(b * size, (b + 1) * size)
        grad_state = carry[...]
        after = [
            thrice(steps[b, h * size : (h + 1) * size, :], grad_state[h * size : (h + 1) * size], TN)
            for h in range(2)
        ]
        carry[...] = pair_rows(*after) + returns[b]
        beta, column = columns[b, :, 0:1], columns[b, :, 1:2]
        across = [columns[b, pl.ds(h * size, size), :].T[1:2, :] for h in range(2)]
        ratios = pair_diagonal(
            *(
                decay_ratios(column[h * size : (h + 1) * size], across[h], causal)
                for h in range(2)
            )
        )
        query, key = qk[b, :, :size].astype(WIDE), qk[b, :, size:].astype(WIDE)
        value = pair_rows(
            *(values[h][tokens].astype(LOW).astype(WIDE) for h in range(2))
        )
        gammas = jnp.exp(column)
        last = [column[(h + 1) * size - 1 : (h + 1) * size] for h in range(2)]
        tail_scale = pair_rows(
            *(jnp.exp(last[h] - column[h * size : (h + 1) * size]) for h in range(2))
        )
        tails = tail_scale * key
        grad = grad_out[b]
        from_tails = [
            once(tails[h * size : (h + 1) * size], grad_state[h * size : (h + 1) * size])
            for h in range(2)
        ]
        grad_fresh = back_scores[b] + pair_rows(*from_tails)
        solved = once(inverse[b], grad_fresh, TN)
        made = fresh[b].astype(WIDE)
        pairs = once(pair_rows(-solved, grad), made, NT)
        score = scores[b].astype(WIDE)
        lower_part = jnp.where(rows > cols, pairs[: 2 * size] * ratios, 0.0)
        score_part = pairs[2 * size :] * ratios
        products = once(key, key, NT)
        weighed = beta * lower_part
        grad_decayed, grad_erase, grad_tails = [], [], []
        for h in range(2):
            at = slice(h * size, (h + 1) * size)
            state = states[b, at, :]
            both = once(pair_rows(grad[at], -solved[at]), state, NT)
            grad_decayed.append(both[:size])
            grad_erase.append(both[size:])
            grad_tails.append(once(made[at], grad_state[at], NT))
        grad_decayed, grad_erase, grad_tails = (
            pair_rows(*m) for m in (grad_decayed, grad_erase, grad_tails)
        )
        stacked = pair_rows(score_part, weighed)
        with_key = once(stacked, key)
        turned = once(stacked, pair_rows(query, key), TN)
        grad_query = gammas * grad_decayed + with_key[: 2 * size]
        grad_key = (
            turned
            + with_key[2 * size :]
            + (beta * gammas) * grad_erase
            + tail_scale * grad_tails
        )
        grad_value = beta * solved
        erase_key = jnp.sum(grad_erase * key, axis=1, keepdims=True) * gammas
        lower_products = lower_part * products
        grad_beta = (
            jnp.sum(lower_products, axis=1, keepdims=True)
            + jnp.sum(solved * value, axis=1, keepdims=True)
            + erase_key
        )
        both = pairs[2 * size :] * score + beta * lower_products
        tail_sum = jnp.sum(grad_tails * tails, axis=1, keepdims=True)
        to_column = jnp.sum(both, axis=0, keepdims=True)
        grad_column = (
            jnp.sum(both, axis=1, keepdims=True)
            + gammas * jnp.sum(grad_decayed * query, axis=1, keepdims=True)
            + beta * erase_key
            - tail_sum
        )
        grad_rate = jnp.zeros((size, 128), WIDE)
        grad_step = jnp.zeros((size, 128), WIDE)
        for h in range(2):
            at = slice(h * size, (h + 1) * size)
            kept = jnp.sum(states[b, at, :] * grad_state[at]) * jnp.exp(last[h])
            finish = kept + jnp.sum(tail_sum[at], axis=0, keepdims=True)
            turned_row = jnp.broadcast_to(to_column[:, at], (size, size)).T
            cumulated = grad_column[at] - turned_row
            summed = lax.dot_general(
                upper, cumulated, (NN, ((), ())), precision=highest, preferred_element_type=WIDE
            )
            grad_step = jnp.where(lanes == 2 + h, summed + finish, grad_step)
            grad_rate = jnp.where(lanes == h, grad_beta[at], grad_rate)
        rate = rate_in[tokens, :]
        strength = jax.nn.sigmoid(rate)
        slope = jax.nn.sigmoid(rate + rates[1:2, :])
        grad_in = grad_rate * strength * (1.0 - strength) + grad_step * rates[0:1, :] * slope
        decay = rates[0:1, :] * softplus(rate + rates[1:2, :])
        sums[0:1, :] += jnp.sum(grad_in, axis=0, keepdims=True)
        sums[1:2, :] += jnp.sum(grad_step * decay, axis=0, keepdims=True)
        grad_rates[tokens, :] = grad_in.astype(LOW)
        grad_mixed[tokens, conv:] = grad_gate[tokens, :]
        for part, member in enumerate((grad_query, grad_key, grad_value)):
            rounded = member.astype(LOW).astype(WIDE)
            for h in range(2):
                unit_grads[2 * part + h][b] = rounded[h * size : (h + 1) * size]
    for part in range(3):
        for h in range(2):
            at = part * 256 + h * size
            wide = pl.ds(at, size)
            given = jnp.concatenate(unit_grads[2 * part + h], 0)
            summed = conv_of(ext, kernel, at, 13, span)
            open_ = jax.nn.sigmoid(summed)
            if part < 2:
                active, scale = silu_unit(summed)
                if part == 0:
                    given = given * size**-0.5
                inner = jnp.sum(active * given, axis=-1, keepdims=True)
                given = scale * given - (scale * scale * scale) * inner * active
            slope = open_ * (1.0 + summed * (1.0 - open_))
            grad_conv = given * slope
            gext[pl.ds(0, span), wide] = grad_conv
            for j in range(4):
                grad_kernel[j : j + 1, wide] += jnp.sum(
                    grad_conv * ext[pl.ds(13 + j, span), wide], axis=0, keepdims=True
                )
            moved = kernel[0:1, wide] * gext[pl.ds(3, span), wide]
            for j in range(1, 4):
                moved = moved + kernel[j : j + 1, wide] * gext[pl.ds(3 - j, span), wide]
            grad_mixed[:, wide] = moved.astype(LOW)

            @pl.when(turn == 0)
            def _():
                edge[:, wide] = moved[span - 16 :]

    gext[pl.ds(span, 8), :] = gext[pl.ds(0, 8), :]

    @pl.when(turn == pl.num_programs(0) - 1)
    def _():
        front[...] = gext[pl.ds(0, 8), :]


def whole_spec(shape):
    return pl.BlockSpec(shape, lambda i: (0,) * len(shape))


def rows_spec(shape, turn=None):
    zeros = (0,) * (len(shape) - 1)
    if turn is None:
        return pl.BlockSpec(shape, lambda i: (i,) + zeros)
    return pl.BlockSpec(shape, lambda i: (turn - 1 - i,) + zeros)


GROUP, PREPARED = 2, 4


def cost(flops, touched):
    return pl.CostEstimate(flops=int(flops), bytes_accessed=int(touched), transcendentals=0)


def prepare(normed, mixer, all_rates, pick, tail, kernel, rates):
    total, width = normed.shape
    blocks = total // 128
    steps = blocks // PREPARED
    span = PREPARED * 128
    like = jax.ShapeDtypeStruct
    return pl.pallas_call(
        prepare_kernel,
        grid=(steps,),
        in_specs=[
            rows_spec((span, width)),
            whole_spec(mixer.shape),
            whole_spec(all_rates.shape),
            whole_spec(pick.shape),
            whole_spec(tail.shape),
            whole_spec(kernel.shape),
            whole_spec(rates.shape),
        ],
        out_specs=[
            whole_spec((total + 16, 768)),
            rows_spec((span, 256)),
            rows_spec((span, 128)),
            rows_spec((PREPARED, 256, 256)),
            rows_spec((PREPARED, 256, 256)),
            rows_spec((PREPARED, 256, 256)),
            rows_spec((PREPARED, 256, 128)),
            rows_spec((PREPARED, 256, 256)),
            rows_spec((PREPARED, 256, 256)),
            rows_spec((PREPARED, 256, 128)),
            whole_spec((256, 256)),
            whole_spec(all_rates.shape),
        ],
        out_shape=[
            like((total + 16, 768), LOW),
            like((total, 256), LOW),
            like((total, 128), WIDE),
            like((blocks, 256, 256), WIDE),
            like((blocks, 256, 256), LOW),
            like((blocks, 256, 256), LOW),
            like((blocks, 256, 128), WIDE),
            like((blocks, 256, 256), WIDE),
            like((blocks, 256, 256), LOW),
            like((blocks, 256, 128), WIDE),
            like((256, 256), WIDE),
            like(all_rates.shape, LOW),
        ],
        scratch_shapes=[pltpu.VMEM((span + 8, 768), WIDE), pltpu.VMEM((256, 256), WIDE)],
        compiler_params=pltpu.CompilerParams(vmem_limit_bytes=VMEM_MOST),
        cost_estimate=cost(4e10, 2e7),
        name="prepare",
    )(normed, mixer, all_rates, pick, tail, kernel, rates)


def finish(start, before, ue, scores, qk, columns, gates, gain, project):
    blocks = ue.shape[0]
    total, width = blocks * 128, project.shape[1]
    span = GROUP * 128
    like = jax.ShapeDtypeStruct
    return pl.pallas_call(
        output_kernel,
        grid=(blocks // GROUP,),
        in_specs=[
            whole_spec(start.shape),
            rows_spec((GROUP, 256, 256)),
            rows_spec((GROUP, 256, 256)),
            rows_spec((GROUP, 256, 256)),
            rows_spec((GROUP, 256, 256)),
            rows_spec((GROUP, 256, 128)),
            rows_spec((span, 256)),
            whole_spec(gain.shape),
            whole_spec(project.shape),
        ],
        out_specs=[
            rows_spec((span, width)),
            rows_spec((span, 256)),
            rows_spec((GROUP, 256, 128)),
            rows_spec((GROUP, 256, 128)),
            rows_spec((GROUP, 256, 128)),
        ],
        out_shape=[
            like((total, width), LOW),
            like((total, 256), LOW),
            like((blocks, 256, 128), LOW),
            like((blocks, 256, 128), WIDE),
            like((blocks, 256, 128), WIDE),
        ],
        compiler_params=pltpu.CompilerParams(vmem_limit_bytes=VMEM_MOST),
        cost_estimate=cost(1e10, 1e7),
        name="finish",
    )(start, before, ue, scores, qk, columns, gates, gain, project)


def give_back(branch, project, gates, gain, out, scores, ue, qk, columns, steps):
    blocks = ue.shape[0]
    total, width = branch.shape
    turns = blocks // GROUP
    span = GROUP * 128
    like = jax.ShapeDtypeStruct
    block = lambda *shape: rows_spec((GROUP,) + shape, turns)
    return pl.pallas_call(
        return_kernel,
        grid=(turns,),
        in_specs=[
            rows_spec((span, width), turns),
            whole_spec(project.shape),
            rows_spec((span, 256), turns),
            whole_spec(gain.shape),
            block(256, 128),
            block(256, 256),
            block(256, 256),
            block(256, 256),
            block(256, 128),
            block(256, 128),
        ],
        out_specs=[
            block(256, 128),
            block(256, 128),
            block(256, 128),
            rows_spec((span, 256), turns),
            whole_spec((256, 128)),
            whole_spec((8, 128)),
        ],
        out_shape=[
            like((blocks, 256, 128), WIDE),
            like((blocks, 256, 128), WIDE),
            like((blocks, 256, 128), WIDE),
            like((total, 256), LOW),
            like((256, 128), WIDE),
            like((8, 128), WIDE),
        ],
        scratch_shapes=[pltpu.VMEM((256, 128), WIDE)],
        compiler_params=pltpu.CompilerParams(vmem_limit_bytes=VMEM_MOST),
        cost_estimate=cost(1e10, 1e7),
        name="give_back",
    )(branch, project, gates, gain, out, scores, ue, qk, columns, steps)


def gradients(
    end, returns, steps, grad_out, back_scores, fresh, states, inverse, scores, qk, columns,
    mixed, rate_in, grad_gate, kernel, rates, after=()
):
    blocks = fresh.shape[0]
    total = blocks * 128
    turns = blocks // GROUP
    span = GROUP * 128
    like = jax.ShapeDtypeStruct
    block = lambda *shape: rows_spec((GROUP,) + shape, turns)
    return pl.pallas_call(
        behind(gradient_kernel, len(after)),
        grid=(turns,),
        in_specs=[pl.BlockSpec(memory_space=pl.ANY)] * len(after)
        + [
            whole_spec(end.shape),
            block(256, 128),
            block(256, 128),
            block(256, 128),
            block(256, 128),
            block(256, 128),
            block(256, 128),
            block(256, 256),
            block(256, 256),
            block(256, 256),
            block(256, 128),
            whole_spec(mixed.shape),
            rows_spec((span, 128), turns),
            rows_spec((span, 256), turns),
            whole_spec(kernel.shape),
            whole_spec(rates.shape),
        ],
        out_specs=[
            rows_spec((span, 1024), turns),
            rows_spec((span, 128), turns),
            whole_spec((8, 768)),
            whole_spec((8, 128)),
            whole_spec((8, 768)),
            whole_spec((16, 768)),
        ],
        out_shape=[
            like((total, 1024), LOW),
            like((total, 128), LOW),
            like((8, 768), WIDE),
            like((8, 128), WIDE),
            like((8, 768), WIDE),
            like((16, 768), WIDE),
        ],
        scratch_shapes=[
            pltpu.VMEM((span + 16, 768), WIDE),
            pltpu.VMEM((span + 8, 768), WIDE),
            pltpu.VMEM((256, 128), WIDE),
        ],
        compiler_params=pltpu.CompilerParams(vmem_limit_bytes=VMEM_MOST),
        cost_estimate=cost(2e10, 1e7),
        name="gradients",
    )(
        *after, end, returns, steps, grad_out, back_scores, fresh, states, inverse, scores, qk, columns,
        mixed, rate_in, grad_gate, kernel, rates
    )


MESH = pl.DeviceIdType.MESH
DMA = pltpu.SemaphoreType.DMA


def neighbours():
    z, y, x, core = (lax.axis_index(name) for name in ALL)
    over_x, over_y, sibling = (z, y, 1 - x, core), (z, 1 - y, x, core), (z, y, x, 1 - core)
    return z, y, x, core, over_x, over_y, sibling


def rank_of(y, x, core):
    return (y * 2 + x) * 2 + core


def greet(others):
    barrier = pltpu.get_barrier_semaphore()
    for other in others:
        pl.semaphore_signal(barrier, inc=1, device_id=other, device_id_type=MESH)
    pl.semaphore_wait(barrier, len(others))


def remote(source, target, sent, arrived, device):
    return pltpu.make_async_remote_copy(
        source, target, sent, arrived, device_id=device, device_id_type=MESH
    )


class Gather:
    def __init__(
        self, mine, out, own_sem, sent, arrived, across_sent, across_arrived, core_sent, core_arrived
    ):
        z, y, x, core, over_x, over_y, sibling = neighbours()
        half = mine.shape[0] // 2
        me, other = rank_of(y, x, core), 1 - core
        piece = lambda slot, p: out.at[slot, pl.ds(p * half, half)]
        from_axis = [rank_of(y, 1 - x, core), rank_of(1 - y, x, core)]
        theirs = [rank_of(y, 1 - x, other), rank_of(1 - y, x, other)]
        over = [over_x, over_y]
        self.own = pltpu.make_async_copy(mine, out.at[me], own_sem)

        def to_core(slot, p, k):
            place = piece(slot, p)
            return remote(place, place, core_sent.at[k], core_arrived.at[k], sibling)

        self.first = [
            remote(
                mine.at[pl.ds(p * half, half)], piece(me, p), sent.at[axis, p],
                arrived.at[axis, p], over[axis]
            )
            for axis, p in ((0, 0), (1, 1), (0, 1), (1, 0))
        ]
        self.first_core = remote(mine, out.at[me], core_sent.at[6], core_arrived.at[6], sibling)
        self.onward = [
            remote(
                piece(from_axis[axis], axis), piece(from_axis[axis], axis),
                across_sent.at[axis], across_arrived.at[axis], over[1 - axis]
            )
            for axis in range(2)
        ]
        self.shared = [
            to_core(from_axis[axis], p, 2 * axis + p)
            for axis, p in ((0, 0), (1, 1), (0, 1), (1, 0))
        ]
        mine_across = rank_of(1 - y, 1 - x, core)
        self.across = [
            remote(
                piece(mine_across, p), piece(mine_across, p), across_sent.at[p],
                across_arrived.at[p], over_x
            )
            for p in range(2)
        ]
        self.shared_across = [to_core(mine_across, p, 4 + p) for p in range(2)]
        self.last = [to_core(theirs[axis], p, 2 * axis + p) for axis in range(2) for p in range(2)]
        self.last += [to_core(rank_of(1 - y, 1 - x, other), p, 4 + p) for p in range(2)]
        place = out.at[rank_of(y, x, other)]
        self.last.append(remote(place, place, core_sent.at[6], core_arrived.at[6], sibling))

    def start(self):
        self.own.start()
        for copy in self.first:
            copy.start()
        self.first_core.start()

    def forward(self):
        for i in range(4):
            self.first[i].wait_recv()
            if i < 2:
                self.onward[i].start()
            self.shared[i].start()

    def finish(self):
        for p in range(2):
            self.across[p].wait_recv()
            self.shared_across[p].start()
        for copy in self.last:
            copy.wait_recv()
        self.own.wait()
        for copy in self.first + [self.first_core] + self.onward + self.shared + self.shared_across:
            copy.wait_send()


def gather_kernel(mine, out, *semaphores):
    greet(neighbours()[4:])
    gather = Gather(mine, out, *semaphores)
    gather.start()
    gather.forward()
    gather.finish()


GATHER_SEMAPHORES = [DMA, DMA((2, 2)), DMA((2, 2)), DMA((2,)), DMA((2,)), DMA((7,)), DMA((7,))]


def plane_gather(rows_here, place, after=()):
    rows, width = rows_here.shape
    out = pl.pallas_call(
        behind(gather_kernel, len(after)),
        out_shape=jax.ShapeDtypeStruct((8, rows, width), rows_here.dtype),
        in_specs=[pl.BlockSpec(memory_space=pl.ANY)] * len(after)
        + [pl.BlockSpec(memory_space=pltpu.VMEM)],
        out_specs=pl.BlockSpec(memory_space=pltpu.VMEM),
        scratch_shapes=GATHER_SEMAPHORES,
        compiler_params=pltpu.CompilerParams(
            collective_id=place, has_side_effects=True, vmem_limit_bytes=VMEM_MOST
        ),
        cost_estimate=pl.CostEstimate(flops=0, bytes_accessed=70_000_000, transcendentals=0),
        name="plane_gather",
    )(*after, rows_here)
    return out.reshape(8 * rows, width)

def turned(place, flip):
    return place + flip - 2 * place * flip


def units_of(hidden, core, half):
    tiles = hidden // 4 // 128
    most = -(-tiles // 2)
    first = -(-most // 2)
    begin = core * most + half * first
    end = min(begin + first, tiles if core else most)
    return begin * 128, (end - begin) * 128, first * 128


def front_kernel(
    w_mixer, w_gate_up, w_down, w_project, tokens, gain, own_rates, mixer, later_a,
    later_b, project, normed_all, tail, rates, normed, zeros, w_rates, shelf, project_own,
    project_sent, shelf_arrived, project_arrived, rates_own, rates_z_sent, rates_z, rates_sent,
    rates_arrived, mixer_own, mixer_sent, mixer_arrived, up_sent, down_sent, z_arrived,
    later_own, later_sent, later_arrived, zero_sem, tail_sent, tail_arrived, *gather_semaphores
):
    z, y, x, core, over_x, over_y, sibling = neighbours()
    layers = lax.axis_size("z")
    rows, width = w_mixer.shape[0], w_mixer.shape[1] // 4
    wide = width // 8
    hidden = w_down.shape[1]
    per_chip = hidden // 4
    laters = (later_a, later_b)
    block = 8 * rows
    me = rank_of(y, x, core)
    low_z, high_z = jnp.maximum(z - 1, 0), jnp.minimum(z + 1, layers - 1)
    below, above = (low_z, y, x, core), (high_z, y, x, core)
    last = (me == 7) & (z < layers - 1)
    flips = [(k >> 2, (k >> 1) & 1, k & 1) for k in range(8)]
    ranks = [rank_of(turned(y, a), turned(x, b), turned(core, c)) for a, b, c in flips]
    devices = [(z, turned(y, a), turned(x, b), turned(core, c)) for a, b, c in flips]

    barrier = pltpu.get_barrier_semaphore()
    for k in range(1, 8):
        pl.semaphore_signal(barrier, inc=1, device_id=devices[k], device_id_type=MESH)

    @pl.when(z > 0)
    def _():
        pl.semaphore_signal(barrier, inc=1, device_id=below, device_id_type=MESH)
        pl.semaphore_signal(barrier, inc=1, device_id=(low_z, 1, 1, 1), device_id_type=MESH)

    @pl.when(z < layers - 1)
    def _():
        pl.semaphore_signal(barrier, inc=1, device_id=above, device_id_type=MESH)

    others_z = [(lax.rem(z + k, layers), y, x, core) for k in range(1, layers)]
    for other in others_z:
        pl.semaphore_signal(barrier, inc=1, device_id=other, device_id_type=MESH)
    pl.semaphore_wait(
        barrier,
        6 + layers + jnp.where(z > 0, 1, 0) + jnp.where(z < layers - 1, 1, 0) + jnp.where(last, 8, 0),
    )

    def columns(p, rank):
        return w_mixer.at[:, pl.ds(pl.multiple_of(p * width + rank * wide, 128), wide)]

    def mixer_rows(layer, rank):
        return mixer.at[pl.ds(pl.multiple_of(layer * block + rank * rows, rows), rows)]

    mine = mixer_rows(z, me)
    owns = [
        pltpu.make_async_copy(columns(p, me), mine.at[:, pl.ds(p * wide, wide)], mixer_own.at[p])
        for p in range(4)
    ]
    for copy in owns:
        copy.start()
    for k in (2, 4, 6, 1, 3, 5, 7):
        for p in range(4):
            remote(
                columns(p, ranks[k]), mine.at[:, pl.ds(p * wide, wide)], mixer_sent.at[k],
                mixer_arrived.at[k], devices[k]
            ).start()

    def along(layer, rank, upward):
        place = mixer_rows(layer, rank)
        return remote(
            place, place, (up_sent if upward else down_sent).at[layer, rank],
            z_arrived.at[layer, rank], above if upward else below
        )

    def spread(rank):
        @pl.when(z < layers - 1)
        def _():
            along(z, rank, True).start()

        @pl.when(z > 0)
        def _():
            along(z, rank, False).start()

    for r in range(0, tokens.shape[0], 32):
        source = tokens[r : r + 32, :].astype(WIDE)
        scale = lax.rsqrt(jnp.mean(source * source, axis=-1, keepdims=True) + 1e-06)
        normed[r : r + 32, :] = (source * scale * gain[...]).astype(LOW)
    w_rates[...] = jnp.zeros_like(w_rates)
    w_rates[:, : own_rates.shape[1]] = own_rates[...]
    zeros[...] = jnp.zeros_like(zeros)
    gather_normed = Gather(normed, normed_all, *gather_semaphores)
    for copy in owns:
        copy.wait()
    spread(me)
    gather_normed.start()
    rate_copies = [
        remote(w_rates, rates.at[me, z], rates_z_sent.at[k], rates_z.at[k], other)
        for k, other in enumerate(others_z)
    ]
    for copy in rate_copies:
        copy.start()
    rate_own = pltpu.make_async_copy(w_rates, rates.at[me, z], rates_own)
    rate_own.start()

    def tails(a, b, c):
        k = (a * 2 + b) * 2 + c
        return remote(
            normed.at[pl.ds(normed.shape[0] - 16, 16)], tail, tail_sent.at[k], tail_arrived,
            (high_z, a, b, c)
        )

    @pl.when(last)
    def _():
        for a, b, c in flips:
            tails(a, b, c).start()

    for k in (1, 2, 4, 3, 5, 6, 7):
        place = mixer_rows(z, ranks[k])
        remote(place, place, mixer_sent.at[k], mixer_arrived.at[k], devices[k]).wait_recv()
        spread(ranks[k])

    def pass_on(far):
        @pl.loop(0, 8)
        def _(rank):
            @pl.when(z - far >= 0)
            def _():
                copy = along(jnp.maximum(z - far, 0), rank, True)
                copy.wait_recv()

                @pl.when(z < layers - 1)
                def _():
                    copy.start()

            @pl.when(z + far <= layers - 1)
            def _():
                copy = along(jnp.minimum(z + far, layers - 1), rank, False)
                copy.wait_recv()

                @pl.when(z > 0)
                def _():
                    copy.start()

    here = pl.ds(pl.multiple_of(me * rows, rows), rows)

    def shares(chip, t):
        found = []
        for half, later in enumerate(laters):
            begin, size, slot = units_of(hidden, t, half)
            first = pl.multiple_of(chip * per_chip + begin, 128)
            up = pl.multiple_of(hidden + first, 128)
            found += [
                (w_gate_up.at[:, pl.ds(first, size)], later.at[here, pl.ds(0, size)]),
                (w_gate_up.at[:, pl.ds(up, size)], later.at[here, pl.ds(slot, size)]),
                (w_down.at[:, pl.ds(first, size)], later.at[here, pl.ds(2 * slot, size)]),
            ]
        return found

    def later_wait(t, semaphore, arrival):
        for half, later in enumerate(laters):
            place = later.at[pl.ds(0, rows), pl.ds(0, 3 * units_of(hidden, t, half)[1])]
            copy = remote(place, place, semaphore.at[half], semaphore.at[half], sibling)
            if arrival:
                copy.wait_recv()
            else:
                copy.wait_send()

    def send_later(f, t):
        a, b = f >> 1, f & 1
        for i, (source, target) in enumerate(shares(turned(y, a) * 2 + turned(x, b), t)):
            remote(
                source, target, later_sent.at[f, t, i // 3], later_arrived.at[f, core, i // 3],
                (z, turned(y, a), turned(x, b), t)
            ).start()

    for f in (1, 2, 3):
        for t in range(2):
            send_later(f, t)
    for t in range(2):

        @pl.when(core == t)
        def _():
            for i, (source, target) in enumerate(shares(y * 2 + x, t)):
                pltpu.make_async_copy(source, target, later_own.at[i]).start()

        @pl.when(core != t)
        def _():
            send_later(0, t)

    _, least, slot = units_of(hidden, 1, 1)
    pads = [
        pltpu.make_async_copy(
            zeros, later_b.at[:, pl.ds(i * slot + least, slot - least)], zero_sem.at[i]
        )
        for i in range(3)
    ]

    @pl.when(core == 1)
    def _():
        for copy in pads:
            copy.start()

    pass_on(1)
    project_copies = [
        remote(w_project, shelf.at[z], project_sent.at[k], shelf_arrived.at[z], other)
        for k, other in enumerate(others_z)
    ]
    project_kept = pltpu.make_async_copy(w_project, shelf.at[z], project_own.at[0])
    project_kept.start()
    for copy in project_copies:
        copy.start()
    gather_normed.forward()
    pass_on(2)
    rate_own.wait()
    for copy in rate_copies:
        copy.wait_recv()
    for k in range(1, 8):
        place = rates.at[me]
        copy = remote(place, place, rates_sent.at[k], rates_arrived.at[k], devices[k])
        copy.start()
        rate_copies.append(copy)
    gather_normed.finish()
    own_j, keeps = 2 * x + core, core == y
    rows_of = lambda j: project.at[pl.ds(pl.multiple_of(j * rows, rows), rows)]

    def hand_on(l):
        return remote(
            shelf.at[l], rows_of(own_j), project_sent.at[layers - 1 + l], project_arrived.at[own_j],
            (z, l // 2, l % 2, y)
        )

    kept_here = pltpu.make_async_copy(shelf.at[2 * y + x], rows_of(own_j), project_own.at[1])
    project_kept.wait()
    for l in range(layers):
        is_own = keeps & (l == 2 * y + x)

        @pl.when(z != l)
        def _():
            remote(
                shelf.at[l], shelf.at[l], project_sent.at[0], shelf_arrived.at[l], sibling
            ).wait_recv()

        @pl.when(is_own)
        def _():
            kept_here.start()

        @pl.when(jnp.logical_not(is_own))
        def _():
            hand_on(l).start()

    pass_on(3)
    for j in range(4):

        @pl.when(jnp.logical_not(keeps & (own_j == j)))
        def _():
            remote(
                rows_of(j), rows_of(j), project_sent.at[0], project_arrived.at[j], sibling
            ).wait_recv()

    @pl.when(keeps)
    def _():
        kept_here.wait()

    for copy in project_copies:
        copy.wait_send()
    for l in range(layers):

        @pl.when(jnp.logical_not(keeps & (l == 2 * y + x)))
        def _():
            hand_on(l).wait_send()

    for t in range(2):

        @pl.when(core == t)
        def _():
            for f in range(4):
                for s in range(2):
                    if f or s != t:
                        later_wait(t, later_arrived.at[f, s], True)
            for i, (source, target) in enumerate(shares(y * 2 + x, t)):
                pltpu.make_async_copy(source, target, later_own.at[i]).wait()

    @pl.when(core == 1)
    def _():
        for copy in pads:
            copy.wait()

    for t in range(2):
        for f in range(1, 4):
            later_wait(t, later_sent.at[f, t], False)

        @pl.when(core != t)
        def _():
            later_wait(t, later_sent.at[0, t], False)

    for k in range(1, 8):
        remote(mine, mine, mixer_sent.at[k], mixer_arrived.at[k], devices[k]).wait_send()
        place = rates.at[ranks[k]]
        remote(place, place, rates_sent.at[k], rates_arrived.at[k], devices[k]).wait_recv()
    for copy in rate_copies:
        copy.wait_send()

    @pl.when(z == 0)
    def _():
        tail[...] = jnp.zeros_like(tail)

    @pl.when(z > 0)
    def _():
        tails(0, 0, 0).wait_recv()

    @pl.when(last)
    def _():
        for a, b, c in flips:
            tails(a, b, c).wait_send()

    for layer in range(4):

        @pl.loop(0, 8)
        def _(rank):
            @pl.when((z < layers - 1) & (layer <= z))
            def _():
                along(layer, rank, True).wait_send()

            @pl.when((z > 0) & (layer >= z))
            def _():
                along(layer, rank, False).wait_send()


def front(w_mixer, w_gate_up, w_down, w_project, w_rates, tokens, gain, place):
    rows, columns = w_mixer.shape
    layers = lax.axis_size("z")
    hidden = w_down.shape[1]
    _, least, slot = units_of(hidden, 1, 1)
    length, width = tokens.shape
    like = jax.ShapeDtypeStruct
    any_, vmem = pl.BlockSpec(memory_space=pl.ANY), pl.BlockSpec(memory_space=pltpu.VMEM)
    return pl.pallas_call(
        front_kernel,
        out_shape=[
            like((8 * layers * rows, columns // 8), LOW),
            like((8 * rows, 3 * slot), LOW),
            like((8 * rows, 3 * slot), LOW),
            like((4 * rows, w_project.shape[1]), LOW),
            like((8, length, width), LOW),
            like((16, width), LOW),
            like((8, layers, rows, 128), LOW),
        ],
        in_specs=[any_, any_, any_, any_, vmem, vmem, vmem],
        out_specs=[any_, any_, any_, any_, vmem, vmem, vmem],
        scratch_shapes=[
            pltpu.VMEM((length, width), LOW),
            pltpu.VMEM((8 * rows, slot - least), LOW),
            pltpu.VMEM((rows, 128), LOW),
            pltpu.VMEM((layers, rows, width), LOW),
            DMA((2,)), DMA((2 * layers - 1,)), DMA((layers,)), DMA((4,)),
            DMA, DMA((layers - 1,)), DMA((layers - 1,)), DMA((8,)), DMA((8,)),
            DMA((4,)), DMA((8,)), DMA((8,)), DMA((4, 8)), DMA((4, 8)), DMA((4, 8)),
            DMA((6,)), DMA((4, 2, 2)), DMA((4, 2, 2)), DMA((3,)), DMA((8,)), DMA,
        ]
        + GATHER_SEMAPHORES,
        compiler_params=pltpu.CompilerParams(
            collective_id=place, has_side_effects=True, vmem_limit_bytes=VMEM_MOST
        ),
        cost_estimate=pl.CostEstimate(flops=0, bytes_accessed=250_000_000, transcendentals=0),
        name="front",
    )(
        w_mixer, w_gate_up, w_down, w_project, tokens, gain[None], w_rates
    )


def scatter_steps(
    terms, out, held, from_core, over_a, over_b, side_x, side_y, core_sent, core_arrived,
    across_sent, across_arrived, sent, arrived
):
    z, y, x, core, over_x, over_y, sibling = neighbours()
    rows = terms.shape[1]
    half, step = rows // 2, 16
    chunks = lambda c: [
        rank_of(1 - y, 1 - x, c), rank_of(y, 1 - x, c), rank_of(1 - y, x, c), rank_of(y, x, c)
    ]
    mine, theirs = chunks(core), chunks(1 - core)
    to_core = [
        remote(terms.at[theirs[i]], from_core.at[i], core_sent.at[i], core_arrived.at[i], sibling)
        for i in range(4)
    ]
    for copy in to_core:
        copy.start()
    yield

    def add(target, at, count, more=None):
        @pl.loop(0, count, step=step)
        def _(r):
            here = pl.ds(pl.multiple_of(at + r, step), step)
            total = terms[mine[target], here, :].astype(WIDE) + from_core[target, here, :].astype(WIDE)
            if more is not None:
                total = total + more[pl.ds(pl.multiple_of(r, step), step), :].astype(WIDE)
            held[target, here, :] = total.astype(LOW)

    top, bottom = pl.ds(0, half), pl.ds(half, half)
    to_core[0].wait_recv()
    add(0, 0, rows)
    top_y = remote(held.at[0, top], over_a, across_sent.at[0], across_arrived.at[0], over_y)
    bottom_x = remote(held.at[0, bottom], over_b, across_sent.at[1], across_arrived.at[1], over_x)
    top_y.start()
    bottom_x.start()
    yield
    to_core[1].wait_recv()
    add(1, half, half)
    x_bottom = remote(held.at[1, bottom], side_x.at[bottom], sent.at[0, 1], arrived.at[0, 1], over_x)
    x_bottom.start()
    to_core[2].wait_recv()
    add(2, 0, half)
    y_top = remote(held.at[2, top], side_y.at[top], sent.at[1, 0], arrived.at[1, 0], over_y)
    y_top.start()
    yield
    top_y.wait_recv()
    add(1, 0, half, over_a)
    x_top = remote(held.at[1, top], side_x.at[top], sent.at[0, 0], arrived.at[0, 0], over_x)
    x_top.start()
    bottom_x.wait_recv()
    add(2, half, half, over_b)
    y_bottom = remote(held.at[2, bottom], side_y.at[bottom], sent.at[1, 1], arrived.at[1, 1], over_y)
    y_bottom.start()
    yield
    to_core[3].wait_recv()
    for copy in (x_bottom, y_top, x_top, y_bottom):
        copy.wait_recv()

    @pl.loop(0, rows, step=step)
    def _(r):
        here = pl.ds(pl.multiple_of(r, step), step)
        out[here, :] = (
            terms[mine[3], here, :].astype(WIDE)
            + from_core[3, here, :].astype(WIDE)
            + (side_x[here, :].astype(WIDE) + side_y[here, :].astype(WIDE))
        )

    for copy in to_core + [top_y, bottom_x, x_bottom, y_top, x_top, y_bottom]:
        copy.wait_send()


def scatter_kernel(*refs):
    greet(neighbours()[4:])
    for _ in scatter_steps(*refs):
        pass


def scatter_scratch(rows, width):
    block = lambda *shape: pltpu.VMEM(shape, LOW)
    return [
        block(3, rows, width),
        block(4, rows, width),
        block(rows // 2, width),
        block(rows // 2, width),
        block(rows, width),
        block(rows, width),
        DMA((4,)),
        DMA((4,)),
        DMA((2,)),
        DMA((2,)),
        DMA((2, 2)),
        DMA((2, 2)),
    ]


def behind(kernel, count):
    return lambda *refs: kernel(*refs[count:])


def plane_scatter(terms, place, after=()):
    rows, width = terms.shape[0] // 8, terms.shape[1]
    return pl.pallas_call(
        behind(scatter_kernel, len(after)),
        out_shape=jax.ShapeDtypeStruct((rows, width), WIDE),
        in_specs=[pl.BlockSpec(memory_space=pl.ANY)] * len(after)
        + [pl.BlockSpec(memory_space=pltpu.VMEM)],
        out_specs=pl.BlockSpec(memory_space=pltpu.VMEM),
        scratch_shapes=scatter_scratch(rows, width),
        compiler_params=pltpu.CompilerParams(
            collective_id=place, has_side_effects=True, vmem_limit_bytes=VMEM_MOST
        ),
        cost_estimate=pl.CostEstimate(flops=0, bytes_accessed=80_000_000, transcendentals=0),
        name="plane_scatter",
    )(*after, terms.reshape(8, rows, width))


def feed_forward_kernel(normed, cotangent, weights, *rest):
    before, (inner, grad_swiglu, back, out) = rest[:-4], rest[-4:]
    slot = inner.shape[1]
    gate_up, down = weights.at[:, : 2 * slot], weights.at[:, 2 * slot :]
    both = once(normed[...], gate_up[...])
    given = once(cotangent[...], down[...])
    a, b = both[:, :slot], both[:, slot:]
    open_ = jax.nn.sigmoid(a)
    active = a * open_
    inner_low = (active * b).astype(LOW)
    swiglu = jnp.concatenate(
        [given * b * open_ * (1.0 + a * (1.0 - open_)), given * active], 1
    ).astype(LOW)
    inner[...] = inner_low
    grad_swiglu[...] = swiglu
    terms = [once(swiglu, gate_up[...], NT), once(inner_low, down[...], NT)]
    for i, target in enumerate((back, out)):
        term = terms[i] + before[i][...] if before else terms[i]
        target[...] = term.astype(target.dtype)


def feed_forward(normed, cotangent, weights, before=()):
    tokens, width = normed.shape
    slot = weights.shape[1] // 3
    step = 256
    like = jax.ShapeDtypeStruct
    kind = LOW if before else WIDE
    return pl.pallas_call(
        feed_forward_kernel,
        grid=(tokens // step,),
        in_specs=[rows_spec((step, width)), rows_spec((step, width)), whole_spec(weights.shape)]
        + [rows_spec((step, width))] * len(before),
        out_specs=[
            rows_spec((step, slot)),
            rows_spec((step, 2 * slot)),
            rows_spec((step, width)),
            rows_spec((step, width)),
        ],
        out_shape=[
            like((tokens, slot), LOW),
            like((tokens, 2 * slot), LOW),
            like((tokens, width), kind),
            like((tokens, width), kind),
        ],
        compiler_params=pltpu.CompilerParams(vmem_limit_bytes=VMEM_MOST),
        cost_estimate=cost(2 * tokens * width * 6 * slot, 3e7),
        name="feed_forward",
    )(normed, cotangent, weights, *before)


def later_terms_kernel(normed, cotangent, swiglu, inner, out):
    both = swiglu.shape[1]
    out[:, :both] = once(normed[...], swiglu[...], TN).astype(LOW)
    out[:, both:] = once(cotangent[...], inner[...], TN).astype(LOW)


def later_terms(normed, cotangent, swiglu, inner):
    tokens, rows = normed.shape
    columns = swiglu.shape[1] + inner.shape[1]
    step = 256
    return pl.pallas_call(
        later_terms_kernel,
        grid=(rows // step,),
        in_specs=[pl.BlockSpec((tokens, step), lambda i: (0, i))] * 2
        + [whole_spec(swiglu.shape), whole_spec(inner.shape)],
        out_specs=rows_spec((step, columns)),
        out_shape=jax.ShapeDtypeStruct((rows, columns), LOW),
        compiler_params=pltpu.CompilerParams(vmem_limit_bytes=VMEM_MOST),
        cost_estimate=cost(2 * tokens * rows * columns, 2e7),
        name="later_terms",
    )(normed, cotangent, swiglu, inner)


def mixer_terms_kernel(slots, normed, mixed, out):
    rows, columns = normed.shape[1], mixed.shape[1]
    few = slots.shape[1]
    out[0, :rows, :] = once(normed[...], mixed[...], TN).astype(LOW)
    for half in range(2):
        out[0, rows + half * few : rows + (half + 1) * few, :] = slots[
            0, :, half * columns : (half + 1) * columns
        ]


def mixer_terms(slots, normed, mixed):
    tokens, rows = normed.shape
    columns = mixed.shape[1]
    layers, few, width = slots.shape
    share = rows // layers + 2 * few
    return pl.pallas_call(
        mixer_terms_kernel,
        grid=(layers,),
        in_specs=[
            rows_spec((1, few, width)),
            pl.BlockSpec((tokens, rows // layers), lambda i: (0, i)),
            whole_spec(mixed.shape),
        ],
        out_specs=rows_spec((1, share, columns)),
        out_shape=jax.ShapeDtypeStruct((layers, share, columns), LOW),
        compiler_params=pltpu.CompilerParams(vmem_limit_bytes=VMEM_MOST),
        cost_estimate=cost(2 * tokens * rows * columns, 2e7),
        name="mixer_terms",
    )(slots, normed, mixed)


def chain_kernel(reverse, whole, term, out, arriving, leaving, sent, arrived):
    z, y, x, core = (lax.axis_index(name) for name in ALL)
    layers = lax.axis_size("z")
    at = layers - 1 - z if reverse else z
    nearer = jnp.clip(z + (1 if reverse else -1), 0, layers - 1)
    further = jnp.clip(z + (-1 if reverse else 1), 0, layers - 1)
    barrier = pltpu.get_barrier_semaphore()

    @pl.when(at > 0)
    def _():
        pl.semaphore_signal(barrier, inc=1, device_id=(nearer, y, x, core), device_id_type=MESH)

    copy = remote(leaving, arriving, sent, arrived, (further, y, x, core))
    size = out.shape[1]
    factor = whole.at[:, :size]
    if not reverse:
        term = whole.at[:, size:]

    @pl.when(at == 0)
    def _():
        out[...] = jnp.zeros_like(out)
        leaving[...] = term[...].astype(LOW)

    @pl.when(at > 0)
    def _():
        copy.wait_recv()
        out[...] = arriving[...].astype(WIDE)

    @pl.when((at > 0) & (at < layers - 1))
    def _():
        for h in range(2):
            rows = slice(h * 128, (h + 1) * 128)
            moved = thrice(factor[rows, :], out[rows, :], TN if reverse else NN)
            leaving[rows, :] = (moved + term[rows, :]).astype(LOW)

    @pl.when(at < layers - 1)
    def _():
        pl.semaphore_wait(barrier, 1)
        copy.start()
        copy.wait_send()


def back_chain_kernel(
    whole, term, terms, out, slots, arriving, leaving, sent, arrived, kept, slot_sent, slot_arrived
):
    z, y, x, core, over_x, over_y, sibling = neighbours()
    layers = lax.axis_size("z")
    rows = slots.shape[1]
    at = layers - 1 - z
    nearer = (jnp.minimum(z + 1, layers - 1), y, x, core)
    further = (jnp.maximum(z - 1, 0), y, x, core)
    own_j, keeps = 2 * x + core, core == y
    barrier = pltpu.get_barrier_semaphore()

    @pl.when(at > 0)
    def _():
        pl.semaphore_signal(barrier, inc=1, device_id=nearer, device_id_type=MESH)

    for l in range(layers):

        @pl.when(jnp.logical_not(keeps & (l == 2 * y + x)))
        def _():
            pl.semaphore_signal(
                barrier, inc=1, device_id=(z, l // 2, l % 2, y), device_id_type=MESH
            )

    pl.semaphore_wait(
        barrier, layers - jnp.where(keeps, 1, 0) + jnp.where(at < layers - 1, 1, 0)
    )
    chain_copy = remote(leaving, arriving, sent, arrived, further)
    mine = slots.at[2 * y + x]

    def pass_terms(j):
        return remote(
            terms.at[pl.ds(j * rows, rows)], mine, slot_sent.at[j], slot_arrived.at[2 * y + x],
            (z, core, j // 2, j % 2)
        )

    kept_copy = pltpu.make_async_copy(
        terms.at[pl.ds(pl.multiple_of(own_j * rows, rows), rows)], mine, kept
    )

    @pl.when(at == 0)
    def _():
        out[...] = jnp.zeros_like(out)
        leaving[...] = term[...].astype(LOW)
        chain_copy.start()

    for j in range(4):

        @pl.when(jnp.logical_not(keeps & (own_j == j)))
        def _():
            pass_terms(j).start()

    @pl.when(keeps)
    def _():
        kept_copy.start()

    @pl.when(at > 0)
    def _():
        chain_copy.wait_recv()
        out[...] = arriving[...].astype(WIDE)

    @pl.when((at > 0) & (at < layers - 1))
    def _():
        size = out.shape[1]
        for h in range(2):
            here = slice(h * 128, (h + 1) * 128)
            moved = thrice(whole[here, :size], out[here, :], TN)
            leaving[here, :] = (moved + term[here, :]).astype(LOW)
        chain_copy.start()

    for l in range(layers):

        @pl.when(jnp.logical_not(keeps & (l == 2 * y + x)))
        def _():
            remote(
                slots.at[l], slots.at[l], slot_sent.at[0], slot_arrived.at[l], sibling
            ).wait_recv()

    @pl.when(keeps)
    def _():
        kept_copy.wait()

    for j in range(4):

        @pl.when(jnp.logical_not(keeps & (own_j == j)))
        def _():
            pass_terms(j).wait_send()

    @pl.when(at < layers - 1)
    def _():
        chain_copy.wait_send()


def back_chain(whole, term, terms, place):
    shape = (whole.shape[0], whole.shape[1] // 2)
    layers = lax.axis_size("z")
    rows, width = terms.shape[0] // 4, terms.shape[1]
    like = jax.ShapeDtypeStruct
    return pl.pallas_call(
        back_chain_kernel,
        out_shape=[like(shape, WIDE), like((layers, rows, width), LOW)],
        in_specs=[pl.BlockSpec(memory_space=pltpu.VMEM)] * 3,
        out_specs=[pl.BlockSpec(memory_space=pltpu.VMEM)] * 2,
        scratch_shapes=[
            pltpu.VMEM(shape, LOW), pltpu.VMEM(shape, LOW), DMA, DMA, DMA, DMA((4,)), DMA((layers,)),
        ],
        compiler_params=pltpu.CompilerParams(
            collective_id=place, has_side_effects=True, vmem_limit_bytes=VMEM_MOST
        ),
        cost_estimate=pl.CostEstimate(flops=0, bytes_accessed=50_000_000, transcendentals=0),
        name="back_chain",
    )(whole, term, terms)


def chain(whole, term, reverse, place):
    shape = (whole.shape[0], whole.shape[1] // 2)
    return pl.pallas_call(
        partial(chain_kernel, reverse),
        out_shape=jax.ShapeDtypeStruct(shape, WIDE),
        in_specs=[pl.BlockSpec(memory_space=pltpu.VMEM)] * 2,
        out_specs=pl.BlockSpec(memory_space=pltpu.VMEM),
        scratch_shapes=[pltpu.VMEM(shape, LOW), pltpu.VMEM(shape, LOW), DMA, DMA],
        compiler_params=pltpu.CompilerParams(
            collective_id=place, has_side_effects=True, vmem_limit_bytes=VMEM_MOST
        ),
        cost_estimate=pl.CostEstimate(flops=0, bytes_accessed=40_000_000, transcendentals=0),
        name="chain",
    )(whole, term)


def later_back_steps(sums_a, sums_b, gate_up, down, own_sem, sent, arrived):
    z, y, x, core, over_x, over_y, sibling = neighbours()
    rows, hidden = down.shape
    per_chip = hidden // 4
    me = rank_of(y, x, core)
    flips = [(k >> 2, (k >> 1) & 1, k & 1) for k in range(8)]
    devices = [(z, turned(y, a), turned(x, b), turned(core, c)) for a, b, c in flips]
    ranks = [rank_of(*device[1:]) for device in devices]

    def parts(rank, t):
        chip = y * 2 + x
        here = pl.ds(pl.multiple_of(rank * rows, rows), rows)
        found = []
        for half, sums in enumerate((sums_a, sums_b)):
            begin, size, slot = units_of(hidden, t, half)
            first = pl.multiple_of(chip * per_chip + begin, 128)
            up = pl.multiple_of(hidden + first, 128)
            found += [
                (sums.at[here, pl.ds(0, size)], gate_up.at[:, pl.ds(first, size)]),
                (sums.at[here, pl.ds(slot, size)], gate_up.at[:, pl.ds(up, size)]),
                (sums.at[here, pl.ds(2 * slot, size)], down.at[:, pl.ds(first, size)]),
            ]
        return found

    def amount(t):
        return [
            down.at[:, pl.ds(0, 3 * units_of(hidden, t, half)[1])] for half in range(2)
        ]

    for t in range(2):

        @pl.when(core == t)
        def _():
            for k in (2, 4, 6, 3, 5, 7, 1):
                for i, (source, target) in enumerate(parts(ranks[k], t)):
                    remote(
                        source, target, sent.at[k, i // 3], arrived.at[k, i // 3], devices[k]
                    ).start()
            for i, (source, target) in enumerate(parts(me, t)):
                pltpu.make_async_copy(source, target, own_sem.at[i]).start()

    for _ in range(5):
        yield
    for t in range(2):

        @pl.when(core == t)
        def _():
            for i, (source, target) in enumerate(parts(me, t)):
                pltpu.make_async_copy(source, target, own_sem.at[i]).wait()

    for k in range(1, 8):
        for t in range(2):
            @pl.when(turned(core, k & 1) == t)
            def _():
                for half, place in enumerate(amount(t)):
                    remote(
                        place, place, sent.at[k, half], arrived.at[k, half], devices[k]
                    ).wait_recv()

            @pl.when(core == t)
            def _():
                for half, place in enumerate(amount(t)):
                    remote(
                        place, place, sent.at[k, half], arrived.at[k, half], devices[k]
                    ).wait_send()


def small_steps(small, low, layers_in, gathered, z_sent, z_arrived, sent, arrived, patience=2):
    z, y, x, core, over_x, over_y, sibling = neighbours()
    layers = layers_in.shape[0]
    me = rank_of(y, x, core)
    flips = [(k >> 2, (k >> 1) & 1, k & 1) for k in range(8)]
    devices = [(z, turned(y, a), turned(x, b), turned(core, c)) for a, b, c in flips]
    ranks = [rank_of(*device[1:]) for device in devices]
    low[...] = small[...].astype(LOW)
    to_layers = [
        remote(
            low, layers_in.at[z], z_sent.at[k], z_arrived.at[k], (lax.rem(z + k, layers), y, x, core)
        )
        for k in range(1, layers)
    ]
    for copy in to_layers:
        copy.start()
    layers_in[z] = low[...]
    for _ in range(patience):
        yield
    for copy in to_layers:
        copy.wait_recv()
    total = layers_in[0].astype(WIDE)
    for k in range(1, layers):
        total = total + layers_in[k].astype(WIDE)
    gathered[me] = total
    spread = [
        remote(gathered.at[me], gathered.at[me], sent.at[k], arrived.at[k], devices[k])
        for k in range(1, 8)
    ]
    for copy in spread:
        copy.start()
    for _ in range(patience):
        yield
    for k in range(1, 8):
        place = gathered.at[ranks[k]]
        remote(place, place, sent.at[k], arrived.at[k], devices[k]).wait_recv()
    for copy in to_layers + spread:
        copy.wait_send()


def small_scratch(shape, layers):
    return [
        pltpu.VMEM(shape, WIDE),
        pltpu.VMEM(shape, LOW),
        pltpu.VMEM((layers,) + shape, LOW),
        pltpu.VMEM((8,) + shape, WIDE),
        DMA((layers,)),
        DMA((layers,)),
        DMA((8,)),
        DMA((8,)),
    ]


def together(running):
    while running:
        for steps in list(running):
            if next(steps, running) is running:
                running.remove(steps)


def others_of(z, y, x, core):
    flips = [(k >> 2, (k >> 1) & 1, k & 1) for k in range(1, 8)]
    layers = lax.axis_size("z")
    return [(z, turned(y, a), turned(x, b), turned(core, c)) for a, b, c in flips] + [
        (lax.rem(z + k, layers), y, x, core) for k in range(1, layers)
    ]


def source_steps(terms, out, tokens, small, scatter_parts, small_parts):
    yield from scatter_steps(terms, out, *scatter_parts)
    total = jnp.zeros((1, out.shape[1]), WIDE)
    for first in range(0, out.shape[0], 32):
        source = tokens[first : first + 32, :].astype(WIDE)
        scale = lax.rsqrt(jnp.mean(source * source, axis=-1, keepdims=True) + 1e-06)
        total = total + jnp.sum(
            out[first : first + 32, :] * source * scale, axis=0, keepdims=True
        )
    step = small.shape[1]
    for row in range(small.shape[0]):
        small[row : row + 1, :] = total[:, row * step : (row + 1) * step]
    yield from small_steps(small, *small_parts, patience=1)


def return_all_kernel(
    terms_a, terms_b, sums_a, sums_b, tokens, grad_kernel, decays, head_gain, gain_mlp, rate_terms,
    out_a, out_b, gate_up, down, all_kernel, all_decays, all_head, all_mlp, all_rates, all_mixer,
    *rest
):
    z, y, x, core, over_x, over_y, sibling = neighbours()
    barrier = pltpu.get_barrier_semaphore()
    others = others_of(z, y, x, core)
    for other in others:
        pl.semaphore_signal(barrier, inc=1, device_id=other, device_id_type=MESH)
    small, gathered = rest[0], rest[3]
    high = 6 * 128
    wide = 256
    small[...] = jnp.zeros_like(small)
    small[0:4, :high] = grad_kernel[0:4, :]
    small[0:1, high : high + 128] = decays[0:1, :]
    small[0:1, high + 128 :] = decays[1:2, :]
    small[1:2, high : high + 128] = head_gain[0:1, :]
    small[4:6, :] = gain_mlp[...]
    half = small.shape[1]
    small[8:12, :] = rate_terms[0:4, :half]
    small[12:16, :] = rate_terms[0:4, half:]
    pl.semaphore_wait(barrier, len(others))
    gain_parts, scratch = rest[8:16], rest[16:]
    count = (len(scratch) - 3) // 2
    together([
        source_steps(
            terms_a, out_a, tokens, gain_parts[0], scratch[:count], gain_parts[1:]
        ),
        scatter_steps(terms_b, out_b, *scratch[count : 2 * count]),
        later_back_steps(sums_a, sums_b, gate_up, down, *scratch[2 * count :]),
        small_steps(*rest[:8]),
    ])
    gains = gain_parts[3]
    whole = gains[0]
    for r in range(1, 8):
        whole = whole + gains[r]
    all_mixer[...] = whole
    whole = gathered[0]
    for r in range(8):
        for part in range(3):
            all_kernel[0:4, part * 8 * wide + r * wide : part * 8 * wide + (r + 1) * wide] = (
                gathered[r, 0:4, part * wide : (part + 1) * wide]
            )
        all_decays[r : r + 1, :] = gathered[r, 0:1, high:]
        all_rates[r] = gathered[r, 8:16, :]
        if r:
            whole = whole + gathered[r]
    all_head[...] = whole[1:2, high : high + 128]
    all_mlp[...] = whole[4:6, :]


def return_all(terms_a, terms_b, sums_a, sums_b, tokens, smalls, hidden, place, after=()):
    rows, width = terms_a.shape[0] // 8, terms_a.shape[1]
    owned = sums_a.shape[0] // 8
    layers = lax.axis_size("z")
    any_, vmem = pl.BlockSpec(memory_space=pl.ANY), pl.BlockSpec(memory_space=pltpu.VMEM)
    like = jax.ShapeDtypeStruct
    return pl.pallas_call(
        behind(return_all_kernel, len(after)),
        out_shape=[
            like((rows, width), WIDE),
            like((rows, width), WIDE),
            like((owned, 2 * hidden), LOW),
            like((owned, hidden), LOW),
            like((4, 6 * 1024), WIDE),
            like((8, 256), WIDE),
            like((1, 128), WIDE),
            like((2, 1024), WIDE),
            like((8, 8, 1024), WIDE),
            like((16, 128), WIDE),
        ],
        in_specs=[any_] * len(after) + [vmem, vmem, any_, any_] + [vmem] * 6,
        out_specs=[vmem, vmem, any_, any_] + [vmem] * 6,
        scratch_shapes=small_scratch((16, 1024), layers)
        + small_scratch((16, 128), layers)
        + scatter_scratch(rows, width) * 2
        + [DMA((6,)), DMA((8, 2)), DMA((8, 2))],
        compiler_params=pltpu.CompilerParams(
            collective_id=place, has_side_effects=True, vmem_limit_bytes=VMEM_MOST
        ),
        cost_estimate=pl.CostEstimate(flops=0, bytes_accessed=200_000_000, transcendentals=0),
        name="return_all",
    )(
        *after, terms_a.reshape(8, rows, width), terms_b.reshape(8, rows, width), sums_a, sums_b,
        tokens, *smalls
    )


def mixer_back_steps(sums, mixer, own_sem, sent, arrived):
    z, y, x, core, over_x, over_y, sibling = neighbours()
    rows, columns = mixer.shape
    wide, width = columns // 32, columns // 4
    me = rank_of(y, x, core)
    flips = [(k >> 2, (k >> 1) & 1, k & 1) for k in range(8)]
    devices = [(z, turned(y, a), turned(x, b), turned(core, c)) for a, b, c in flips]
    ranks = [rank_of(*device[1:]) for device in devices]

    def parts(rank):
        here = pl.ds(pl.multiple_of(rank * rows, rows), rows)
        return [
            (
                sums.at[here, pl.ds(p * wide, wide)],
                mixer.at[:, pl.ds(pl.multiple_of(p * width + me * wide, 128), wide)],
            )
            for p in range(4)
        ]

    for k in (2, 4, 6, 3, 5, 7, 1):
        for source, target in parts(ranks[k]):
            remote(source, target, sent.at[k], arrived.at[k], devices[k]).start()
    owns = [
        pltpu.make_async_copy(source, target, own_sem.at[i])
        for i, (source, target) in enumerate(parts(me))
    ]
    for copy in owns:
        copy.start()
    yield
    yield
    for copy in owns:
        copy.wait()
    place = mixer.at[:, pl.ds(0, 4 * wide)]
    for k in range(1, 8):
        remote(place, place, sent.at[k], arrived.at[k], devices[k]).wait()


def last_kernel(sums, mixer, *rest):
    z, y, x, core, over_x, over_y, sibling = neighbours()
    greet(others_of(z, y, x, core)[:7])
    together([mixer_back_steps(sums, mixer, *rest)])


def last(sums, rows, place, after=()):
    columns = sums.shape[1]
    any_ = pl.BlockSpec(memory_space=pl.ANY)
    return pl.pallas_call(
        behind(last_kernel, len(after)),
        out_shape=jax.ShapeDtypeStruct((rows, 8 * columns), LOW),
        in_specs=[any_] * (len(after) + 1),
        out_specs=any_,
        scratch_shapes=[DMA((4,)), DMA((8,)), DMA((8,))],
        compiler_params=pltpu.CompilerParams(
            collective_id=place, has_side_effects=True, vmem_limit_bytes=VMEM_MOST
        ),
        cost_estimate=pl.CostEstimate(flops=0, bytes_accessed=60_000_000, transcendentals=0),
        name="last",
    )(*after, sums)


def heads_on_plane(
    tokens,
    w_mixer,
    w_rates,
    w_project,
    w_gate_up,
    w_down,
    conv_kernel,
    decay_log,
    decay_bias,
    head_gain,
    gain_mixer,
    gain_mlp,
    cotangent,
):
    length, width = tokens.shape
    size = head_gain.shape[0]
    rows = w_mixer.shape[0]
    hidden = w_down.shape[1]
    layers = lax.axis_size("z")
    ranks = lax.axis_size(ALL) // layers
    own = decay_log.shape[0] // ranks
    layer, rank = lax.axis_index("z"), lax.axis_index(PLANE)
    low = jnp.bfloat16
    wide = own * size

    def over_layers(terms):
        return lax.psum_scatter(terms, "z", scatter_dimension=0, tiled=True)

    gather = plane_gather

    def scatter(terms, place, after=()):
        return plane_scatter(terms.astype(low), place, after)

    source = tokens.astype(jnp.float32)
    norm_pull = jax.vjp(norm_scale, source, gain_mixer)[1]
    mixer, later_a, later_b, project, normed_all, tail, all_rates = front(
        w_mixer, w_gate_up, w_down, w_project, w_rates, tokens, gain_mixer, 1
    )
    total = length * ranks
    normed_all = normed_all.reshape(total, width)
    later_a = lax.all_gather(later_a, "z", axis=0, tiled=True)
    later_b = lax.all_gather(later_b, "z", axis=0, tiled=True)
    slot = later_a.shape[1] // 3
    all_rates = jnp.swapaxes(all_rates, 0, 1).reshape(width, 128)
    head_at = jnp.arange(2 * own) // own * (ranks * own) + jnp.arange(2 * own) % own + rank * own
    pick = jnp.pad(
        jax.nn.one_hot(head_at, 128, axis=0, dtype=low), ((0, 0), (0, 128 - 2 * own))
    )
    kernel = lax.dynamic_index_in_dim(
        conv_kernel.reshape(4, 3, ranks, wide), rank, 2, False
    ).reshape(4, 3 * wide)
    kernel = jnp.pad(kernel, ((0, 4), (0, 0)))
    log_rate = lax.dynamic_slice_in_dim(decay_log, rank * own, own)
    bias = lax.dynamic_slice_in_dim(decay_bias, rank * own, own)

    downward = [(z + 1, z) for z in range(layers - 1)]
    head_gains = jnp.broadcast_to(head_gain, (8, size))
    pads = ((0, 7), (2, 124))
    rates = jnp.pad(-jnp.exp(log_rate)[None], pads) + jnp.roll(jnp.pad(bias[None], pads), 1, 0)
    (
        mixed_low, gates, rate_in, ue, inverse, scores, steps, before, qk, columns, whole, rate_weight
    ) = prepare(normed_all, mixer, all_rates, pick, tail, kernel, rates)
    start = chain(whole, whole, False, 7)
    branch, gated_low, fresh, states, outputs = finish(
        start, before, ue, scores, qk, columns, gates, head_gains, project
    )
    hidden_state = source + scatter(branch, 2)
    normed_two, norm_two_pull = jax.vjp(norm_scale, hidden_state, gain_mlp)
    normed_two_all = gather(normed_two.astype(low), 3)
    cotangent_all = gather(cotangent, 4, (normed_two_all,))
    sums_of, terms_so_far = [], ()
    for weights in (later_a, later_b):
        inner, grad_swiglu, *terms_so_far = feed_forward(
            normed_two_all, cotangent_all, weights, terms_so_far
        )
        sums_of.append(
            over_layers(later_terms(normed_two_all, cotangent_all, grad_swiglu, inner))
        )
    back_terms, out_terms = terms_so_far
    later_sum_a, later_sum_b = sums_of
    grad_hidden_part, grad_gain_mlp = norm_two_pull(scatter(back_terms, 5))
    grad_hidden = cotangent.astype(jnp.float32) + grad_hidden_part
    grad_branch = gather(grad_hidden.astype(low), 6)
    grad_out, back_scores, returns, grad_gate, local, grad_head_gain = give_back(
        grad_branch, project, gates, head_gains, outputs, scores, ue, qk, columns, steps
    )
    project_terms = dot_tn(gated_low, grad_branch).astype(low)
    later_state, slots = back_chain(whole, local, project_terms, 8)
    grad_mixed, grad_rates, grad_kernel, sums, first_rows, edge = gradients(
        later_state, returns, steps, grad_out, back_scores, fresh, states, inverse, scores, qk, columns,
        mixed_low, rate_in, grad_gate, kernel, rates, (later_sum_a,)
    )
    following = lax.ppermute(first_rows[:3].astype(low), "z", downward).astype(jnp.float32)
    late = [
        sum(kernel[j] * following[r - j] for j in range(r + 1)) for r in range(3)
    ]
    edge = jnp.concatenate([edge[:13], edge[13:] + jnp.stack(late)], 0).astype(low)
    grad_mixed = lax.dynamic_update_slice(grad_mixed, edge, (total - 16, 0))
    terms = mixer_terms(slots, normed_all, grad_mixed)
    rate_terms = dot_tn(grad_rates, normed_all)
    mixer_sum = lax.psum_scatter(terms, "z", scatter_dimension=0)
    source_terms = dot_nt(grad_mixed, mixer) + dot_nt(grad_rates, rate_weight)
    smalls = (grad_kernel, sums, grad_head_gain, grad_gain_mlp.reshape(2, -1), rate_terms)
    (
        from_source, from_inner, grad_gate_up, grad_down, grad_kernel, decays, grad_head_gain,
        grad_gain_mlp, rate_sums, grad_gain_mixer
    ) = return_all(
        source_terms.astype(low), out_terms, later_sum_a, later_sum_b, tokens, smalls, hidden, 10,
        (terms,)
    )
    grad_source = norm_pull(from_source)[0]
    grad_tokens = (grad_hidden + grad_source).astype(low)
    result = (hidden_state + from_inner).astype(low)
    grad_gate_up, grad_down = grad_gate_up.astype(jnp.float32), grad_down.astype(jnp.float32)
    rate_sums = jnp.swapaxes(rate_sums.reshape(ranks, 2, 2 * own, -1, rows), 1, 2)
    rate_sums = rate_sums.reshape(ranks, 2, own, -1, rows)
    grad_rates = lax.dynamic_index_in_dim(rate_sums, layer * ranks + rank, 3, False)
    grad_rates = jnp.transpose(grad_rates, (3, 1, 0, 2)).reshape(rows, -1)
    few = (ranks + 1) * rows
    grad_project = jnp.concatenate(
        [mixer_sum[ranks * rows : few], mixer_sum[few:]], 1
    ).astype(jnp.float32)
    grad_mixer = last(
        mixer_sum, rows, 11,
        (grad_gate_up, grad_down, result, grad_tokens, grad_rates, grad_gain_mixer),
    )
    return (
        result,
        grad_tokens,
        grad_mixer.astype(jnp.float32),
        grad_rates,
        grad_project,
        grad_gate_up,
        grad_down,
        grad_kernel,
        decays[:, 128 + own : 128 + 2 * own].reshape(-1),
        decays[:, own : 2 * own].reshape(-1),
        grad_head_gain[0],
        grad_gain_mixer.reshape(-1),
        grad_gain_mlp.reshape(-1),
    )


def by_planes(mesh, members):
    seq, core = mesh.shape["seq"], mesh.shape["fsdp"]
    layers, ranks = seq // 4, 4 * core
    heads, size = members[7].shape[0], members[9].shape[0]
    return (
        core == 2
        and layers == 4
        and members[0].shape[0] == seq * core * size
        and heads % ranks == 0
        and members[5].shape[1] % (4 * 128) == 0
    )


def solution(mesh):
    rows, copied = P(("seq", "fsdp"), None), P()

    def run(*members):
        if by_planes(mesh, members):
            places = Mesh(mesh.devices.reshape(-1, 2, 2, 2), ALL)
            split, body = P(ALL, None), heads_on_plane
        else:
            places, split, body = mesh, rows, on_device
        return jax.shard_map(
            body,
            mesh=places,
            in_specs=(split,) * 6 + (copied,) * 6 + (split,),
            out_specs=(split,) * 7 + (copied,) * 6,
            check_vma=False,
        )(*members)

    return run
```
